32 devices in a mesh: stream: 2 (over core), dp: 16 (over z, y, x).
Axes of the slice: x: 2, y: 2, z: 4, core: 2. Of those that a mesh axis runs over, the one named last changes fastest.
Arguments:
- hidden: float32 [2, 8192, 768], P('stream', 'dp'), may hold values from -6 to 6
- features: bfloat16 [256, 257, 1408], P('dp'), may hold values from -6 to 6
- caption_lengths: int32 [16, 32], P('dp'), may hold values from 1 to 32, 512 in all within a row
- caption_image: int32 [16, 32], P('dp'), may hold values from 0 to 15, as said below
- out_grad: float32 [2, 8192, 768], P('stream', 'dp'), may hold values from -6 to 6
- attn_project: float32 [3, 768, 768], P(None, 'dp'), may hold values from -0.21875 to 0.21875
- attn_output: float32 [2, 768, 768], P(None, 'dp'), may hold values from -0.625 to 0.625
- cross_query: float32 [768, 768], P('dp'), may hold values from -0.21875 to 0.21875
- cross_vision: float32 [2, 1408, 768], P(None, 'dp'), may hold values from -0.15625 to 0.15625
- feed_expand: float32 [2, 3072, 768], P('stream', 'dp'), may hold values from -0.21875 to 0.21875
- feed_reduce: float32 [2, 3072, 768], P('stream', 'dp'), may hold values from -0.109375 to 0.109375
- norm_gains: float32 [4, 768], P(None, 'dp'), may hold values from 0.3 to 2.4, as said below
- first_project: float32 [3, 768, 768], P(None, 'dp'), may hold values from -0.00018310547 to 0.00018310547
- second_project: float32 [3, 768, 768], P(None, 'dp'), may hold values from 6.6041964e-11 to 2.6416785e-10
- first_output: float32 [2, 768, 768], P(None, 'dp'), may hold values from -0.00018310547 to 0.00018310547
- second_output: float32 [2, 768, 768], P(None, 'dp'), may hold values from 6.6041964e-11 to 2.6416785e-10
- first_query: float32 [768, 768], P('dp'), may hold values from -0.00018310547 to 0.00018310547
- second_query: float32 [768, 768], P('dp'), may hold values from 6.6041964e-11 to 2.6416785e-10
- first_vision: float32 [2, 1408, 768], P(None, 'dp'), may hold values from -0.00018310547 to 0.00018310547
- second_vision: float32 [2, 1408, 768], P(None, 'dp'), may hold values from 6.6041964e-11 to 2.6416785e-10
- first_expand: float32 [2, 3072, 768], P('stream', 'dp'), may hold values from -0.00018310547 to 0.00018310547
- second_expand: float32 [2, 3072, 768], P('stream', 'dp'), may hold values from 6.6041964e-11 to 2.6416785e-10
- first_reduce: float32 [2, 3072, 768], P('stream', 'dp'), may hold values from -0.00018310547 to 0.00018310547
- second_reduce: float32 [2, 3072, 768], P('stream', 'dp'), may hold values from 6.6041964e-11 to 2.6416785e-10
- first_gains: float32 [4, 768], P(None, 'dp'), may hold values from -0.0007324219 to 0.0007324219
- second_gains: float32 [4, 768], P(None, 'dp'), may hold values from 1.0566714e-09 to 4.2266857e-09
Outputs:
- layer_output: float32 [2, 8192, 768], P('stream', 'dp')
- hidden_grad: float32 [2, 8192, 768], P('stream', 'dp')
- grad_norm: float32 [], replicated
- rms_values: float32 [2, 4], replicated
- fresh_project: float32 [3, 768, 768], P(None, 'dp')
- mean_project: float32 [3, 768, 768], P(None, 'dp')
- square_project: float32 [3, 768, 768], P(None, 'dp')
- fresh_output: float32 [2, 768, 768], P(None, 'dp')
- mean_output: float32 [2, 768, 768], P(None, 'dp')
- square_output: float32 [2, 768, 768], P(None, 'dp')
- fresh_query: float32 [768, 768], P('dp')
- mean_query: float32 [768, 768], P('dp')
- square_query: float32 [768, 768], P('dp')
- fresh_vision: float32 [2, 1408, 768], P(None, 'dp')
- mean_vision: float32 [2, 1408, 768], P(None, 'dp')
- square_vision: float32 [2, 1408, 768], P(None, 'dp')
- fresh_expand: float32 [2, 3072, 768], P('stream', 'dp')
- mean_expand: float32 [2, 3072, 768], P('stream', 'dp')
- square_expand: float32 [2, 3072, 768], P('stream', 'dp')
- fresh_reduce: float32 [2, 3072, 768], P('stream', 'dp')
- mean_reduce: float32 [2, 3072, 768], P('stream', 'dp')
- square_reduce: float32 [2, 3072, 768], P('stream', 'dp')
- fresh_gains: float32 [4, 768], P(None, 'dp')
- mean_gains: float32 [4, 768], P(None, 'dp')
- square_gains: float32 [4, 768], P(None, 'dp')
- gain_grads: float32 [4, 768], P(None, 'dp')
- copy_project: bfloat16 [3, 768, 768], P(None, 'dp')
- copy_output: bfloat16 [2, 768, 768], P(None, 'dp')
- copy_query: bfloat16 [768, 768], P('dp')
- copy_vision: bfloat16 [2, 1408, 768], P(None, 'dp')
- copy_expand: bfloat16 [2, 3072, 768], P('stream', 'dp')
- copy_reduce: bfloat16 [2, 3072, 768], P('stream', 'dp')
The draws below stay inside these ranges and needn't reach their ends.
Inputs may be any that keep to these rules, and one draw needn't show every extreme that they name: `caption_lengths`: one index of dp's caption lengths fill its 512 text rows exactly, and one caption of each index has 32 tokens. `caption_image`: never falls along one index's captions; every image of an index has 1 to 5 captions, and some image of every index has 5. `norm_gains`: positive gains.
All inputs are finite; a program needn't handle non-finite values.
Results may differ from the reference program's by a relative error of at most 0.023.
Values may be sent and summed in bfloat16 or wider, within the bound.
A program may use at most 256 MiB of HBM per device.

```python
import math
import jax
import jax.numpy as jnp
import numpy as np
from jax import lax

D = 768
HEADS = 12
HD = 64
FF = 3072
DV = 1408
NF = 257
NQ = 32
IMG_DEV = 16
LMAX = 32
STEP = 10
ROWS_DEV = 512
CAPS_DEV = 32
IMAGES = 256
ROWS = 8192
NPARAM = 15141888
N_DP = 16


def draw_caption_image(key, part):
    key = jax.random.fold_in(key, 7)
    extra = jnp.concatenate([jnp.full((IMG_DEV // 8,), 4, jnp.int32), jnp.full((IMG_DEV // 8,), 2, jnp.int32), jnp.full((IMG_DEV // 4,), 1, jnp.int32), jnp.zeros((IMG_DEV // 2,), jnp.int32)])

    def one_device(device_key):
        counts = jax.random.permutation(device_key, extra) + 1
        caption_ends = jnp.cumsum(counts)
        caption_index = jnp.arange(CAPS_DEV, dtype=jnp.int32)
        return jnp.sum((caption_index[:, None] >= caption_ends[None, :]).astype(jnp.int32), axis=1)
    return jax.vmap(one_device)(jax.random.split(key, N_DP))


def draw_norm_gains(key, part):
    key = jax.random.fold_in(key, 11)
    position = jnp.arange(D, dtype=jnp.float32) / (D - 1)
    lowest = 0.6
    ratio = 3.0
    ramp = lowest * jnp.power(ratio, position)
    jitter = jax.random.uniform(key, (4, D), jnp.float32, 0.85, 1.15)
    return ramp[None, :] * jitter


def block_levels(rng, extent, pieces, least, largest):
    level = 1.0
    for axis_at, shards_of in pieces:
        heights = jax.random.uniform(jax.random.fold_in(jax.random.fold_in(rng, 6), axis_at), (shards_of,), jnp.float32, least / len(pieces), largest / len(pieces))
        level = level * jnp.repeat(jnp.exp(heights), extent[axis_at] // shards_of).reshape((-1,) + (1,) * (len(extent) - 1 - axis_at))
    return level


def profile(amount, total, reach, skew):
    weights = [(1 << 20) // math.isqrt(rank ** skew) + 1 for rank in range(2, amount + 1)]
    spare, given = total - reach - (amount - 1), [1] * (amount - 1)
    while spare > 0:
        movable = [i for i in range(amount - 1) if given[i] < reach]
        mass, remaining = sum([weights[i] for i in movable]), spare
        for i in movable:
            more = min(reach - given[i], max(1, remaining * weights[i] // mass), spare)
            given[i] = given[i] + more
            spare = spare - more
    return np.array([reach] + given)


def ragged_sizes(key, amount, total, reach, slope):
    if amount == 2:
        one = jax.random.randint(key, (), max(1, total - reach), min(reach, total - 1) + 1)
        return jnp.stack([one, total - one])
    sizes = jnp.asarray(profile(amount, total, reach, slope), jnp.int32)
    couples = (amount - 1) // 2
    donor, receiver = sizes[1:1 + 2 * couples:2], sizes[2:2 + 2 * couples:2]
    slack = jnp.minimum(donor - 1, reach - receiver)
    shifted = jax.random.randint(jax.random.fold_in(key, 1), (couples,), 0, 1 << 20) % (slack + 1)
    sizes = sizes.at[1:1 + 2 * couples:2].set(donor - shifted).at[2:2 + 2 * couples:2].set(receiver + shifted)
    return sizes[jax.random.permutation(jax.random.fold_in(key, 2), amount)]


def noise(stream_key, shape, width, most, pieces=(), kind=jnp.bfloat16):
    values = jax.random.normal(stream_key, shape, jnp.float32) * width
    if len(pieces) > 0:
        values = block_levels(stream_key, shape, pieces, -0.22, 0.18) * values
    return jnp.clip(values, min=-most, max=most).astype(kind)


def setup_inputs(seed: int = 0) -> dict:
    streams_of = jax.random.split(jax.random.key(seed), 27)
    hidden = noise(streams_of[0], (2, ROWS, D), 1.0, 6.0, ((0, 2), (1, 16)), jnp.float32)
    features = noise(streams_of[1], (IMAGES, NF, DV), 1.0, 6.0, ((0, 16),))
    caption_lengths = jax.vmap(lambda own: ragged_sizes(own, CAPS_DEV, ROWS_DEV, LMAX, 2))(jax.random.split(streams_of[2], N_DP)).reshape((N_DP, CAPS_DEV)).astype(jnp.int32)
    caption_image = draw_caption_image(jax.random.fold_in(streams_of[26], 71), 0)
    out_grad = noise(streams_of[4], (2, ROWS, D), 1.0, 6.0, ((0, 2), (1, 16)), jnp.float32)
    attn_project = noise(streams_of[5], (3, D, D), D ** -0.5, 0.21875, ((1, 16),), jnp.float32)
    attn_output = noise(streams_of[6], (2, D, D), (D // 8) ** -0.5, 0.625, ((1, 16),), jnp.float32)
    cross_query = noise(streams_of[7], (D, D), D ** -0.5, 0.21875, ((0, 16),), jnp.float32)
    cross_vision = noise(streams_of[8], (2, DV, D), DV ** -0.5, 0.15625, ((1, 16),), jnp.float32)
    feed_expand = noise(streams_of[9], (2, FF, D), D ** -0.5, 0.21875, ((0, 2), (1, 16)), jnp.float32)
    feed_reduce = noise(streams_of[10], (2, FF, D), FF ** -0.5, 0.109375, ((0, 2), (1, 16)), jnp.float32)
    norm_gains = draw_norm_gains(jax.random.fold_in(streams_of[26], 71), 0)
    first_project = noise(streams_of[12], (3, D, D), (0.11 / NPARAM ** 0.5), 0.00018310547, ((1, 16),), jnp.float32)
    second_project = jnp.clip(jnp.exp(math.log(2.6416785425809053e-10) - 1.3862944 * jax.random.uniform(streams_of[13], (3, D, D), jnp.float32) ** block_levels(streams_of[13], (3, D, D), ((1, 16),), -0.2, 0.2)), 6.604196356452263e-11, 2.6416785425809053e-10)
    first_output = noise(streams_of[14], (2, D, D), (0.11 / NPARAM ** 0.5), 0.00018310547, ((1, 16),), jnp.float32)
    second_output = jnp.clip(jnp.exp(math.log(2.6416785425809053e-10) - 1.3862944 * jax.random.uniform(streams_of[15], (2, D, D), jnp.float32) ** block_levels(streams_of[15], (2, D, D), ((1, 16),), -0.2, 0.2)), 6.604196356452263e-11, 2.6416785425809053e-10)
    first_query = noise(streams_of[16], (D, D), (0.11 / NPARAM ** 0.5), 0.00018310547, ((0, 16),), jnp.float32)
    second_query = jnp.clip(jnp.exp(math.log(2.6416785425809053e-10) - 1.3862944 * jax.random.uniform(streams_of[17], (D, D), jnp.float32) ** block_levels(streams_of[17], (D, D), ((0, 16),), -0.2, 0.2)), 6.604196356452263e-11, 2.6416785425809053e-10)
    first_vision = noise(streams_of[18], (2, DV, D), (0.11 / NPARAM ** 0.5), 0.00018310547, ((1, 16),), jnp.float32)
    second_vision = jnp.clip(jnp.exp(math.log(2.6416785425809053e-10) - 1.3862944 * jax.random.uniform(streams_of[19], (2, DV, D), jnp.float32) ** block_levels(streams_of[19], (2, DV, D), ((1, 16),), -0.2, 0.2)), 6.604196356452263e-11, 2.6416785425809053e-10)
    first_expand = noise(streams_of[20], (2, FF, D), (0.11 / NPARAM ** 0.5), 0.00018310547, ((0, 2), (1, 16)), jnp.float32)
    second_expand = jnp.clip(jnp.exp(math.log(2.6416785425809053e-10) - 1.3862944 * jax.random.uniform(streams_of[21], (2, FF, D), jnp.float32) ** block_levels(streams_of[21], (2, FF, D), ((0, 2), (1, 16)), -0.2, 0.2)), 6.604196356452263e-11, 2.6416785425809053e-10)
    first_reduce = noise(streams_of[22], (2, FF, D), (0.11 / NPARAM ** 0.5), 0.00018310547, ((0, 2), (1, 16)), jnp.float32)
    second_reduce = jnp.clip(jnp.exp(math.log(2.6416785425809053e-10) - 1.3862944 * jax.random.uniform(streams_of[23], (2, FF, D), jnp.float32) ** block_levels(streams_of[23], (2, FF, D), ((0, 2), (1, 16)), -0.2, 0.2)), 6.604196356452263e-11, 2.6416785425809053e-10)
    first_gains = noise(streams_of[24], (4, D), (0.44 / NPARAM ** 0.5), 0.0007324219, ((1, 16),), jnp.float32)
    second_gains = jnp.clip(jnp.exp(math.log(4.2266856681294485e-09) - 1.3862944 * jax.random.uniform(streams_of[25], (4, D), jnp.float32) ** block_levels(streams_of[25], (4, D), ((1, 16),), -0.2, 0.2)), 1.0566714170323621e-09, 4.2266856681294485e-09)
    return {"hidden": hidden, "features": features, "caption_lengths": caption_lengths, "caption_image": caption_image, "out_grad": out_grad, "attn_project": attn_project, "attn_output": attn_output, "cross_query": cross_query, "cross_vision": cross_vision, "feed_expand": feed_expand, "feed_reduce": feed_reduce, "norm_gains": norm_gains, "first_project": first_project, "second_project": second_project, "first_output": first_output, "second_output": second_output, "first_query": first_query, "second_query": second_query, "first_vision": first_vision, "second_vision": second_vision, "first_expand": first_expand, "second_expand": second_expand, "first_reduce": first_reduce, "second_reduce": second_reduce, "first_gains": first_gains, "second_gains": second_gains}


epsilon = 1e-06
masked_value = -1e+30
beta_first = 0.9
beta_second = 0.999
rate_matrix = 0.05
rate_gains = 1.0
decay_rate = 0.01
adam_floor = 1e-08
clip_norm = 1.0
highest = lax.Precision.HIGHEST

@jax.custom_vjp
def low(v):
    return lax.optimization_barrier(v.astype(jnp.bfloat16)).astype(jnp.float32)

@jax.custom_vjp
def low_back(v):
    return v

def low_keep(v):
    return (low(v), None)

def low_pass(kept, grad):
    return (grad,)

def back_keep(v):
    return (v, None)

def back_low(kept, grad):
    return (low(grad),)
low.defvjp(low_keep, low_pass)
low_back.defvjp(back_keep, back_low)

def matmul(left, right):
    return jnp.dot(left, right, precision=highest, preferred_element_type=jnp.float32)

def matmul_trans(left, right):
    return lax.dot_general(left, right, (((1,), (1,)), ((), ())), precision=highest, preferred_element_type=jnp.float32)

def norm_rows(values, gain):
    return values * lax.rsqrt(lax.optimization_barrier(jnp.mean(values * values, axis=-1, keepdims=True)) + epsilon) * gain

def square_rows(values):
    return jnp.sum(lax.optimization_barrier(jnp.mean(values * values, axis=-1)))

def layout(lengths, owners, row_count, per_image):
    caption_ends = jnp.cumsum(lengths).astype(jnp.int32)
    caption_starts = caption_ends - lengths
    row_index = jnp.arange(row_count, dtype=jnp.int32)
    inside = (row_index[:, None] >= caption_starts[None, :]) & (row_index[:, None] < caption_ends[None, :])
    caption = lax.optimization_barrier(jnp.sum(jnp.where(inside, jnp.arange(lengths.shape[0], dtype=jnp.int32)[None, :], 0), axis=1))
    text_image = lax.optimization_barrier(jnp.sum(jnp.where(inside, owners[None, :], 0), axis=1))
    query_image = row_index // per_image
    query_allow = query_image[:, None] == query_image[None, :]
    own_caption = (caption[:, None] == caption[None, :]) & (row_index[None, :] <= row_index[:, None])
    text_allow = jnp.concatenate([text_image[:, None] == query_image[None, :], own_caption], axis=1)
    return (query_allow, text_allow)

def attend(query_rows, key_rows, value_rows, allowed):
    batch_count, query_count, width_all = query_rows.shape
    query_heads = query_rows.reshape(batch_count, query_count, HEADS, HD)
    key_heads = key_rows.reshape(batch_count, key_rows.shape[1], HEADS, HD)
    value_heads = value_rows.reshape(batch_count, value_rows.shape[1], HEADS, HD)
    scores = jnp.einsum('bqhd,bkhd->bhqk', query_heads, key_heads, precision=highest) * HD ** (-0.5)
    scores = low_back(scores)
    if allowed is not None:
        scores = jnp.where(allowed[:, None], scores, masked_value)
    weights = jnp.exp(scores - lax.optimization_barrier(jnp.max(scores, axis=-1, keepdims=True)))
    probability = low(weights / lax.optimization_barrier(jnp.sum(weights, axis=-1, keepdims=True)))
    context = jnp.einsum('bhqk,bkhd->bqhd', probability, value_heads, precision=highest)
    return context.reshape(batch_count, query_count, width_all)

def feed_forward(values, gain, expand_weight, reduce_weight):
    normed = low(norm_rows(values, gain))
    before = low_back(matmul_trans(normed, expand_weight))
    active = low(jax.nn.gelu(before, approximate=False))
    return low_back(matmul(active, reduce_weight))

def shard_forward(params, query_in, text_in, feature_block, lengths, owners):
    project, output, cross_weight, vision, expand_weight, reduce_weight, gains = params
    row_count = query_in.shape[0]
    query_allow, text_allow = layout(lengths, owners, row_count, NQ)
    normed_query = low(norm_rows(query_in, gains[0]))
    normed_text = low(norm_rows(text_in, gains[0]))
    query_q = low_back(low(matmul(normed_query, project[0])))
    query_key_value = low(matmul(normed_query, project[1]))
    query_value_value = low(matmul(normed_query, project[2]))
    text_q = low_back(low(matmul(normed_text, project[0])))
    text_k = low_back(low(matmul(normed_text, project[1])))
    text_v = low_back(low(matmul(normed_text, project[2])))
    context_query = attend(query_q[None], low_back(query_key_value)[None], low_back(query_value_value)[None], query_allow[None])[0]
    keys_text = jnp.concatenate([low_back(query_key_value), text_k], axis=0)
    values_text = jnp.concatenate([low_back(query_value_value), text_v], axis=0)
    context_text = attend(text_q[None], keys_text[None], values_text[None], text_allow[None])[0]
    branch_query = low_back(matmul(low_back(low(context_query)), output[0]))
    after_query = query_in + branch_query
    normed_cross = low(norm_rows(after_query, gains[1]))
    cross_q = low_back(low(matmul(normed_cross, cross_weight)))
    vision_pair = low_back(low(jnp.einsum('inv,kvd->kind', feature_block.astype(jnp.float32), vision, precision=highest)))
    context_cross = attend(cross_q.reshape(IMG_DEV, NQ, D), vision_pair[0], vision_pair[1], None).reshape(row_count, D)
    branch_cross = low_back(matmul(low_back(low(context_cross)), output[1]))
    crossed = after_query + branch_cross
    feed_query = feed_forward(crossed, gains[2], expand_weight[0], reduce_weight[0])
    out_query = crossed + feed_query
    branch_text = low_back(matmul(low_back(low(context_text)), output[0]))
    after_text = text_in + branch_text
    feed_text = feed_forward(after_text, gains[3], expand_weight[1], reduce_weight[1])
    out_text = after_text + feed_text
    statistics = jnp.stack([jnp.stack([square_rows(query_in), square_rows(branch_query), square_rows(feed_query), square_rows(out_query)]), jnp.stack([square_rows(text_in), square_rows(branch_text), square_rows(feed_text), square_rows(out_text)])])
    return (jnp.stack([out_query, out_text]), statistics)

def adam_step(weight, gradient, first, second, factor, rate, decay):
    clipped = gradient * factor
    mean_new = beta_first * first + (1.0 - beta_first) * clipped
    square_new = beta_second * second + (1.0 - beta_second) * clipped * clipped
    corrected_mean = mean_new / (1.0 - beta_first ** STEP)
    corrected_square = square_new / (1.0 - beta_second ** STEP)
    fresh = weight - rate * (corrected_mean / (jnp.sqrt(corrected_square) + adam_floor) + decay * weight)
    return (fresh, mean_new, square_new)

def reference(hidden, features, caption_lengths, caption_image, out_grad, attn_project, attn_output, cross_query, cross_vision, feed_expand, feed_reduce, norm_gains, first_project, second_project, first_output, second_output, first_query, second_query, first_vision, second_vision, first_expand, second_expand, first_reduce, second_reduce, first_gains, second_gains):
    params = (attn_project, attn_output, cross_query, cross_vision, feed_expand, feed_reduce, norm_gains)
    blocks = features.reshape(N_DP, IMG_DEV, NF, DV)

    def forward(weights, inputs):
        lowered = tuple((low(weight) for weight in weights))
        paired_rows = inputs.reshape(2, N_DP, ROWS_DEV, D).transpose(1, 0, 2, 3)

        def one_shard(packed):
            shard_rows, feature_block, lengths, owners = packed
            return shard_forward(lowered, shard_rows[0], shard_rows[1], feature_block, lengths, owners)
        outputs, statistics = lax.map(jax.checkpoint(one_shard), (paired_rows, blocks, caption_lengths, caption_image))
        return (outputs.transpose(1, 0, 2, 3).reshape(2, ROWS, D), lax.optimization_barrier(jnp.sum(statistics, axis=0)))
    layer_output, pullback, stat_sums = jax.vjp(forward, params, hidden, has_aux=True)
    grads, hidden_grad = pullback(out_grad)
    total_square = jnp.float32(0.0)
    for gradient in grads:
        total_square = total_square + jnp.sum(gradient * gradient)
    grad_norm = jnp.sqrt(total_square)
    rms_values = jnp.sqrt(stat_sums / ROWS)
    factor = clip_norm / jnp.maximum(grad_norm, clip_norm)
    gain_grads = grads[6] * factor
    firsts = (first_project, first_output, first_query, first_vision, first_expand, first_reduce, first_gains)
    seconds = (second_project, second_output, second_query, second_vision, second_expand, second_reduce, second_gains)
    updated = []
    for index in range(7):
        rate = rate_gains if index == 6 else rate_matrix
        decay = 0.0 if index == 6 else decay_rate
        updated.append(adam_step(params[index], grads[index], firsts[index], seconds[index], factor, rate, decay))
    fresh_project, mean_project, square_project = updated[0]
    fresh_output, mean_output, square_output = updated[1]
    fresh_query, mean_query, square_query = updated[2]
    fresh_vision, mean_vision, square_vision = updated[3]
    fresh_expand, mean_expand, square_expand = updated[4]
    fresh_reduce, mean_reduce, square_reduce = updated[5]
    fresh_gains, mean_gains, square_gains = updated[6]
    return (layer_output, hidden_grad, grad_norm, rms_values, fresh_project, mean_project, square_project, fresh_output, mean_output, square_output, fresh_query, mean_query, square_query, fresh_vision, mean_vision, square_vision, fresh_expand, mean_expand, square_expand, fresh_reduce, mean_reduce, square_reduce, fresh_gains, mean_gains, square_gains, gain_grads, fresh_project.astype(jnp.bfloat16), fresh_output.astype(jnp.bfloat16), fresh_query.astype(jnp.bfloat16), fresh_vision.astype(jnp.bfloat16), fresh_expand.astype(jnp.bfloat16), fresh_reduce.astype(jnp.bfloat16))
```

```python
import jax
import jax.numpy as jnp
from jax import lax
from jax.experimental import pallas as pl
from jax.experimental.pallas import tpu as pltpu
from jax.sharding import PartitionSpec as P

HEADS = 12
HD = 64
NQ = 32
STEP = 10


epsilon = 1e-06
masked_value = -1e30
beta_first = 0.9
beta_second = 0.999
rate_matrix = 0.05
rate_gains = 1.0
decay_rate = 0.01
adam_floor = 1e-08
clip_norm = 1.0


def shifted(block, axis, distance):
    devices = range(lax.axis_size(axis))
    route = [(i - distance, i) for i in devices if i - distance in devices]
    return lax.ppermute(block, axis, route)


def to_half(values):
    return values.astype(jnp.bfloat16)


def product(left, right):
    return jnp.dot(left, right, preferred_element_type=jnp.float32)


def left_product(left, right):
    return lax.dot_general(
        left, right, (((0,), (0,)), ((), ())), preferred_element_type=jnp.float32
    )


def right_product(left, right):
    return lax.dot_general(
        left, right, (((1,), (1,)), ((), ())), preferred_element_type=jnp.float32
    )


def norm_rows(values, gain):
    return values * lax.rsqrt(jnp.mean(values * values, axis=-1, keepdims=True) + epsilon) * gain


def exact_gelu(values):
    return jax.nn.gelu(values, approximate=False)


def square_rows(values):
    return jnp.sum(jnp.mean(values * values, axis=-1))


def layout(lengths, owners, row_count, per_image):
    caption_ends = jnp.cumsum(lengths)
    caption_starts = caption_ends - lengths
    row_index = jnp.arange(row_count, dtype=jnp.int32)
    inside = (row_index[:, None] >= caption_starts[None, :]) & (
        row_index[:, None] < caption_ends[None, :]
    )
    caption = jnp.sum(
        jnp.where(inside, jnp.arange(lengths.shape[0], dtype=jnp.int32)[None, :], 0), axis=1
    )
    text_image = jnp.sum(jnp.where(inside, owners[None, :], 0), axis=1)
    query_image = row_index // per_image
    query_allow = query_image[:, None] == query_image[None, :]
    own_caption = (caption[:, None] == caption[None, :]) & (
        row_index[None, :] <= row_index[:, None]
    )
    text_allow = jnp.concatenate([text_image[:, None] == query_image[None, :], own_caption], axis=1)
    return (query_allow, text_allow)


def attention_scores(query_rows, key_rows, allowed):
    batch_count, query_count, width_all = query_rows.shape
    query_heads = query_rows.reshape(batch_count, query_count, HEADS, HD)
    key_heads = key_rows.reshape(batch_count, key_rows.shape[1], HEADS, HD)
    scores = jnp.einsum(
        "bqhd,bkhd->bhqk", query_heads, key_heads, preferred_element_type=jnp.float32
    ) * HD ** (-0.5)
    if allowed is not None:
        scores = jnp.where(allowed[:, None], scores, masked_value)
    return (scores, query_heads, key_heads)


def attend(query_rows, key_rows, value_rows, allowed):
    scores, query_heads, key_heads = attention_scores(query_rows, key_rows, allowed)
    value_heads = value_rows.reshape(key_heads.shape)
    row_max = jnp.max(scores, axis=-1, keepdims=True)
    weights = jnp.exp(scores - row_max)
    denominator = jnp.sum(weights, axis=-1, keepdims=True)
    probability = to_half(weights / denominator)
    context = jnp.einsum(
        "bhqk,bkhd->bqhd", probability, value_heads, preferred_element_type=jnp.float32
    )
    return (context.reshape(query_rows.shape), (row_max + jnp.log(denominator))[..., 0])


def attend_back(query_rows, key_rows, value_rows, allowed, log_total, grad_context):
    scores, query_heads, key_heads = attention_scores(query_rows, key_rows, allowed)
    value_heads = value_rows.reshape(key_heads.shape)
    probability = jnp.exp(scores - log_total[..., None])
    grad_heads = grad_context.reshape(query_heads.shape)
    grad_prob = jnp.einsum(
        "bqhd,bkhd->bhqk", grad_heads, value_heads, preferred_element_type=jnp.float32
    )
    grad_value = jnp.einsum(
        "bhqk,bqhd->bkhd", to_half(probability), grad_heads, preferred_element_type=jnp.float32
    )
    grad_score = to_half(
        probability * (grad_prob - jnp.sum(grad_prob * probability, axis=-1, keepdims=True))
    )
    grad_query = jnp.einsum(
        "bhqk,bkhd->bqhd", grad_score, key_heads, preferred_element_type=jnp.float32
    ) * HD ** (-0.5)
    grad_key = jnp.einsum(
        "bhqk,bqhd->bkhd", grad_score, query_heads, preferred_element_type=jnp.float32
    ) * HD ** (-0.5)
    return (
        grad_query.reshape(query_rows.shape),
        grad_key.reshape(key_rows.shape),
        grad_value.reshape(value_rows.shape),
    )


def project_vision(feature_block, vision_weights):
    return to_half(
        jnp.einsum(
            "inv,kvd->kind", feature_block, vision_weights, preferred_element_type=jnp.float32
        )
    )


def vision_grad(feature_block, grad_pair):
    return jnp.einsum("inv,kind->kvd", feature_block, grad_pair, preferred_element_type=jnp.float32)


def adam_step(weight, gradient, first, second, factor, rate, decay):
    clipped = gradient * factor
    mean_new = beta_first * first + (1.0 - beta_first) * clipped
    square_new = beta_second * second + (1.0 - beta_second) * clipped * clipped
    corrected_mean = mean_new / (1.0 - beta_first**STEP)
    corrected_square = square_new / (1.0 - beta_second**STEP)
    fresh = weight - rate * (
        corrected_mean / (jnp.sqrt(corrected_square) + adam_floor) + decay * weight
    )
    return (fresh, mean_new, square_new)


MESH = pl.DeviceIdType.MESH
VMEM_LIMIT = 60 * 2**20


def coordinates():
    c = lax.axis_index("stream")
    d = lax.axis_index("dp")
    return c, d // 4, (d // 2) % 2, d % 2


def device(c, z, y, x):
    return (c, z * 4 + y * 2 + x)


def meet(c, z, y, x):
    barrier = pltpu.get_barrier_semaphore()
    others = [device(1 - c, z, y, x), device(c, z, 1 - y, x), device(c, z, y, 1 - x)]
    others += [device(c, (z + k) % 4, y, x) for k in (1, 2, 3)]
    for other in others:
        pl.semaphore_signal(barrier, inc=1, device_id=other, device_id_type=MESH)
    pl.semaphore_wait(barrier, len(others))


ORDERS = {
    ("late", 0): ("z", "y", "x"),
    ("late", 1): ("z", "x", "y"),
    ("early", 0): ("x", "z", "y"),
    ("early", 1): ("y", "z", "x"),
}


def gather_kernel(
    first, vision, expand, reduce, gains,
    all_first, all_vision, all_expand, all_reduce, all_gains,
    send_sem, recv_sem, local_sem,
):
    c, z, y, x = coordinates()
    half = expand.shape[0] // 2
    low, high = pl.ds(0, half), pl.ds(half, half)
    chunks = [
        (gains, lambda *at: all_gains.at[at], "late", False),
        (first.at[0], lambda *at: all_first.at[(c, 0) + at], "early", True),
        (first.at[1], lambda *at: all_first.at[(c, 1) + at], "early", True),
        (first.at[2], lambda *at: all_first.at[(c, 2) + at], "early", True),
        (vision, lambda *at: all_vision.at[(c,) + at], "early", True),
        (expand.at[low], lambda *at: all_expand.at[at + (low,)], "late", False),
        (expand.at[high], lambda *at: all_expand.at[at + (high,)], "late", False),
        (reduce.at[low], lambda *at: all_reduce.at[at + (low,)], "late", False),
        (reduce.at[high], lambda *at: all_reduce.at[at + (high,)], "late", False),
    ]
    own = {"z": z, "y": y, "x": x}

    def remote(source, target, index, where):
        return pltpu.make_async_remote_copy(
            src_ref=source, dst_ref=target, send_sem=send_sem.at[index],
            recv_sem=recv_sem.at[index], device_id=where, device_id_type=MESH,
        )

    def sends(number, stage, core):
        source, target, kind, _ = chunks[number]
        order = ORDERS[kind, core]
        done, axis = order[:stage], order[stage]
        at = tuple(slice(None) if a in done else own[a] for a in "zyx")
        block = target(*at)
        here = source if stage == 0 else block
        base = (number * 3 + stage) * 3
        if axis == "z":
            return [
                remote(here, block, base + k - 1, device(c, (z + k) % 4, y, x)) for k in (1, 2, 3)
            ]
        where = device(c, z, 1 - y, x) if axis == "y" else device(c, z, y, 1 - x)
        return [remote(here, block, base, where)]

    def place(number):
        source, target, _, _ = chunks[number]
        return pltpu.make_async_copy(source, target(z, y, x), local_sem.at[number])

    def across(number):
        _, target, _, _ = chunks[number]
        block = target(slice(None), slice(None), slice(None))
        return remote(block, block, len(chunks) * 9 + number, device(1 - c, z, y, x))

    def run(core):
        count = len(chunks)
        for tick in range(count + 3):
            for stage in (3, 2, 1, 0):
                number = tick - stage
                if not 0 <= number < count:
                    continue
                if stage > 0:
                    for copy in sends(number, stage - 1, core):
                        copy.wait_recv()
                if stage == 1:
                    place(number).wait()
                if stage < 3:
                    for copy in sends(number, stage, core):
                        copy.start()
                    if stage == 0:
                        place(number).start()
                elif chunks[number][3]:
                    across(number).start()
        for number in range(count):
            for stage in range(3):
                for copy in sends(number, stage, core):
                    copy.wait_send()
            if chunks[number][3]:
                across(number).wait()

    meet(c, z, y, x)

    @pl.when(c == 0)
    def _():
        run(0)

    @pl.when(c == 1)
    def _():
        run(1)


def gather_all(first, vision, expand, reduce, gains):
    half = jnp.bfloat16
    width = first.shape[-1]
    shapes = [
        (2, 3, 4, 2, 2) + first.shape[1:],
        (2, 4, 2, 2) + vision.shape,
        (4, 2, 2) + expand.shape,
        (4, 2, 2) + reduce.shape,
        (4, 2, 2) + gains.shape,
    ]
    count = 9
    anywhere = pl.BlockSpec(memory_space=pl.ANY)
    return pl.pallas_call(
        gather_kernel,
        out_shape=[jax.ShapeDtypeStruct(shape, half) for shape in shapes],
        in_specs=[anywhere] * 5,
        out_specs=[anywhere] * 5,
        scratch_shapes=[
            pltpu.SemaphoreType.DMA((count * 10,)),
            pltpu.SemaphoreType.DMA((count * 10,)),
            pltpu.SemaphoreType.DMA((count,)),
        ],
        compiler_params=pltpu.CompilerParams(
            collective_id=0, has_side_effects=True, vmem_limit_bytes=VMEM_LIMIT
        ),
        name="gather_weights",
    )(first, vision, expand, reduce, gains)


def wide(block):
    return block.astype(jnp.float32)


def scatter_kernel(
    part_first, part_vision, part_expand, part_reduce, part_gains, part_stats,
    sum_first, sum_vision, sum_expand, sum_reduce, sum_gains, totals,
    held_first, held_vision, held_expand, held_reduce,
    pair_first, pair_vision,
    got_a0, got_a1, got_a2, got_b0, got_b1, got_b2, got_c0, got_c1, got_c2,
    gains_now, gains_got, gains_z, stats_now, stats_got, stats_z,
    send_sem, recv_sem, local_sem,
):
    c, z, y, x = coordinates()
    half = sum_expand.shape[0] // 2
    low, high = pl.ds(0, half), pl.ds(half, half)
    own = {"z": z, "y": y, "x": x}
    chunks = []
    for number, (held, total) in enumerate([(held_expand, sum_expand), (held_reduce, sum_reduce)]):
        for part, rows in enumerate((low, high)):
            slot = number * 2 + part
            chunks.append((
                lambda at, held=held, rows=rows: at + (rows,), held,
                (got_a0.at[slot], got_a1.at[slot], got_a2.at[slot]), "late",
                (total, (rows,)), None,
            ))
    for j in range(3):
        chunks.append((
            lambda at, j=j: (j,) + at, held_first,
            (got_b0.at[j], got_b1.at[j], got_b2.at[j]), "early",
            (sum_first, (c, j)), (pair_first, j),
        ))
    chunks.append((
        lambda at: at, held_vision, (got_c0, got_c1, got_c2), "early",
        (sum_vision, (c,)), (pair_vision, None),
    ))
    count = len(chunks)

    def remote(source, target, index, where):
        return pltpu.make_async_remote_copy(
            src_ref=source, dst_ref=target, send_sem=send_sem.at[index],
            recv_sem=recv_sem.at[index], device_id=where, device_id_type=MESH,
        )

    def load(number):
        result = [
            (part_expand.at[:, :, :, low], held_expand.at[:, :, :, low]),
            (part_expand.at[:, :, :, high], held_expand.at[:, :, :, high]),
            (part_reduce.at[:, :, :, low], held_reduce.at[:, :, :, low]),
            (part_reduce.at[:, :, :, high], held_reduce.at[:, :, :, high]),
        ]
        result += [(part_first.at[c, j], held_first.at[j]) for j in range(3)]
        result += [(part_vision.at[c], held_vision)]
        source, target = result[number]
        return pltpu.make_async_copy(source, target, local_sem.at[number])

    def pair_copy(number):
        buffer, j = chunks[number][5]
        if j is None:
            source, target = part_vision.at[1 - c], buffer
        else:
            source, target = part_first.at[1 - c, j], buffer.at[j]
        return remote(source, target, count * 9 + number, device(1 - c, z, y, x))

    def sends(number, stage, core):
        address, held, got, kind, _, _ = chunks[number]
        order = ORDERS[kind, core][::-1]
        done, axis = order[:stage], order[stage]
        base = (number * 3 + stage) * 3

        def block(there):
            at = tuple(
                there if a == axis else own[a] if a in done else slice(None) for a in "zyx"
            )
            return held.at[address(at)]

        if axis == "z":
            return [
                remote(
                    block((z + k) % 4), got[stage].at[k - 1], base + k - 1,
                    device(c, (z + k) % 4, y, x),
                )
                for k in (1, 2, 3)
            ]
        where = device(c, z, 1 - y, x) if axis == "y" else device(c, z, y, 1 - x)
        return [remote(block(1 - own[axis]), got[stage], base, where)]

    def absorb(number, stage, core):
        address, held, got, kind, total, _ = chunks[number]
        order = ORDERS[kind, core][::-1]
        done, axis = order[: stage + 1], order[stage]
        free = [a for a in "zyx" if a not in done]
        sizes = [4 if a == "z" else 2 for a in free]
        steps = 1
        for size in sizes:
            steps *= size

        def step(i, carry):
            index = {}
            for a, size in reversed(list(zip(free, sizes))):
                index[a] = i % size
                i = i // size
            at = address(tuple(index[a] if a in index else own[a] for a in "zyx"))
            inner = tuple(index[a] for a in free)
            value = wide(held[at])
            if axis == "z":
                for k in range(3):
                    value = value + wide(got[stage][(k,) + inner])
            else:
                value = value + wide(got[stage][inner] if inner else got[stage][...])
            if stage == 2:
                target, where = total
                target[where] = value
            else:
                held[at] = value.astype(jnp.bfloat16)
            return carry

        if steps == 1:
            step(0, 0)
        else:
            lax.fori_loop(0, steps, step, 0)

    def add_pair(number):
        address, held, _, _, _, (buffer, j) = chunks[number]

        def step(i, carry):
            at = (i // 4, (i // 2) % 2, i % 2)
            here = address(at)
            value = wide(held[here]) + wide(buffer[at if j is None else (j,) + at])
            held[here] = value.astype(jnp.bfloat16)
            return carry

        lax.fori_loop(0, 16, step, 0)

    small_base = count * 10

    def small(stage, now, got, got_z, base):
        if stage < 3:
            where = (device(1 - c, z, y, x), device(c, z, 1 - y, x), device(c, z, y, 1 - x))[stage]
            return [remote(now.at[stage], got.at[stage], base + stage, where)]
        return [
            remote(now.at[3], got_z.at[z], base + 2 + k, device(c, (z + k) % 4, y, x))
            for k in (1, 2, 3)
        ]

    def small_step(stage, now, got, got_z, base):
        if stage > 0:
            for copy in small(stage - 1, now, got, got_z, base):
                copy.wait()
            if stage < 4:
                now[stage] = now[stage - 1] + got[stage - 1]
            else:
                got_z[z] = now[3]
                now[4] = (got_z[0] + got_z[1]) + (got_z[2] + got_z[3])
        if stage < 4:
            for copy in small(stage, now, got, got_z, base):
                copy.start()

    gains_base, stats_base = small_base, small_base + 6

    def run(core):
        for tick in range(count + 3):
            if tick < 5:
                small_step(tick, gains_now, gains_got, gains_z, gains_base)
            for stage in (3, 2, 1, 0):
                number = tick - stage
                if not 0 <= number < count:
                    continue
                if stage == 0:
                    load(number).wait()
                    if chunks[number][5] is not None:
                        pair_copy(number).wait()
                        add_pair(number)
                else:
                    for copy in sends(number, stage - 1, core):
                        copy.wait_recv()
                    absorb(number, stage - 1, core)
                if stage < 3:
                    for copy in sends(number, stage, core):
                        copy.start()
        for number in range(count):
            for stage in range(3):
                for copy in sends(number, stage, core):
                    copy.wait_send()

    meet(c, z, y, x)
    for number in range(count):
        load(number).start()
    for number in range(count):
        if chunks[number][5] is not None:
            pair_copy(number).start()
    gains_now[0] = part_gains[...]

    @pl.when(c == 0)
    def _():
        run(0)

    @pl.when(c == 1)
    def _():
        run(1)

    back = [
        remote(sum_first.at[c], sum_first.at[c], stats_base + 6, device(1 - c, z, y, x)),
        remote(sum_vision.at[c], sum_vision.at[c], stats_base + 7, device(1 - c, z, y, x)),
    ]
    for copy in back:
        copy.start()

    def squares(block):
        rows = block.shape[0]
        return jnp.sum((block * block).reshape(rows // 8, 8, block.shape[1]), axis=0)

    gains = gains_now[4]
    sum_gains[...] = gains
    count_gains = jnp.where((c == 0) & (z + y + x == 0), 1.0, 0.0)
    mass = count_gains * (gains * gains)
    for j in range(3):
        mass = mass + squares(sum_first[c, j])
    mass = mass + squares(sum_vision[c])
    mass = mass + squares(sum_expand[...]) + squares(sum_reduce[...])
    folded = mass[:, 0:128]
    for k in range(1, mass.shape[1] // 128):
        folded = folded + mass[:, k * 128 : (k + 1) * 128]
    stats_now[0, 0:8] = folded
    stats_now[0, 8:16] = part_stats[...]
    for stage in range(5):
        small_step(stage, stats_now, stats_got, stats_z, stats_base)
    totals[...] = stats_now[4]
    for copy in back:
        copy.wait()


def scatter_all(part_first, part_vision, part_expand, part_reduce, part_gains, part_stats):
    rows_first, width = part_first.shape[-2:]
    rows_vision = part_vision.shape[-2]
    rows_feed = part_expand.shape[-2]
    half_feed = rows_feed // 2
    half, single = jnp.bfloat16, jnp.float32
    anywhere = pl.BlockSpec(memory_space=pl.ANY)
    vmem = pl.BlockSpec(memory_space=pltpu.VMEM)
    count = 8

    def late(rows):
        return [(4, 2, rows, width), (4, rows, width), (3, rows, width)]

    def early(rows):
        return [(4, 2, rows, width), (3, 2, rows, width), (rows, width)]

    scratch = [
        pltpu.VMEM(part_first.shape[1:], half),
        pltpu.VMEM(part_vision.shape[1:], half),
        pltpu.VMEM(part_expand.shape, half),
        pltpu.VMEM(part_reduce.shape, half),
        pltpu.VMEM(part_first.shape[1:], half),
        pltpu.VMEM(part_vision.shape[1:], half),
    ]
    scratch += [pltpu.VMEM((4,) + shape, half) for shape in late(half_feed)]
    scratch += [pltpu.VMEM((3,) + shape, half) for shape in early(rows_first)]
    scratch += [pltpu.VMEM(shape, half) for shape in early(rows_vision)]
    for shape in (part_gains.shape, (16, 128)):
        scratch += [pltpu.VMEM((number,) + shape, single) for number in (5, 3, 4)]
    scratch += [
        pltpu.SemaphoreType.DMA((count * 10 + 14,)),
        pltpu.SemaphoreType.DMA((count * 10 + 14,)),
        pltpu.SemaphoreType.DMA((count,)),
    ]
    return pl.pallas_call(
        scatter_kernel,
        out_shape=[
            jax.ShapeDtypeStruct((2, 3, rows_first, width), single),
            jax.ShapeDtypeStruct((2, rows_vision, width), single),
            jax.ShapeDtypeStruct((rows_feed, width), single),
            jax.ShapeDtypeStruct((rows_feed, width), single),
            jax.ShapeDtypeStruct(part_gains.shape, single),
            jax.ShapeDtypeStruct((16, 128), single),
        ],
        in_specs=[anywhere] * 4 + [vmem] * 2,
        out_specs=[vmem] * 6,
        scratch_shapes=scratch,
        compiler_params=pltpu.CompilerParams(
            collective_id=1, has_side_effects=True, vmem_limit_bytes=VMEM_LIMIT
        ),
        name="scatter_grads",
    )(part_first, part_vision, part_expand, part_reduce, part_gains, part_stats)


def body(
    hidden,
    features,
    caption_lengths,
    caption_image,
    out_grad,
    attn_project,
    attn_output,
    cross_query,
    cross_vision,
    feed_expand,
    feed_reduce,
    norm_gains,
    first_project,
    second_project,
    first_output,
    second_output,
    first_query,
    second_query,
    first_vision,
    second_vision,
    first_expand,
    second_expand,
    first_reduce,
    second_reduce,
    first_gains,
    second_gains,
):
    stream = lax.axis_index("stream")
    direct = lax.axis_size("dp") == 16
    if direct:
        halves = [
            to_half(value)
            for value in (attn_project, attn_output, cross_query, cross_vision, feed_expand[0], feed_reduce[0])
        ]
        project_half, output_half, query_half_weight, vision_half, expand_half, reduce_half = halves
        first = jnp.where(
            stream == 0, project_half, jnp.concatenate([output_half, query_half_weight[None]], axis=0)
        )
        vision_own = jnp.where(stream == 0, vision_half[0], vision_half[1])
        gains_tile = jnp.pad(to_half(norm_gains), ((0, 12), (0, 80)))
        all_first, all_vision, all_expand, all_reduce, all_gains = gather_all(
            first, vision_own, expand_half, reduce_half, gains_tile
        )
        width = attn_project.shape[-1]
        full_first = all_first.reshape(2, 3, width, width)
        full_project = full_first[0]
        full_output = full_first[1, :2]
        full_query = full_first[1, 2]
        full_vision = all_vision.reshape(2, -1, width)
        full_expand = all_expand.reshape(1, -1, width)
        full_reduce = all_reduce.reshape(1, -1, width)
        full_gains = (
            all_gains.reshape(16, 16, 128)[:, :4, : norm_gains.shape[1]].transpose(1, 0, 2).reshape(4, width)
        )
    else:
        full_project, full_output, full_query, full_vision, full_expand, full_reduce, full_gains = (
            lax.all_gather(to_half(attn_project), "dp", axis=1, tiled=True),
            lax.all_gather(to_half(attn_output), "dp", axis=1, tiled=True),
            lax.all_gather(to_half(cross_query), "dp", axis=0, tiled=True),
            lax.all_gather(to_half(cross_vision), "dp", axis=1, tiled=True),
            lax.all_gather(to_half(feed_expand), "dp", axis=1, tiled=True),
            lax.all_gather(to_half(feed_reduce), "dp", axis=1, tiled=True),
            lax.all_gather(to_half(norm_gains), "dp", axis=1, tiled=True),
        )
    gain_rows = full_gains.astype(jnp.float32)
    gain_self = gain_rows[0]
    gain_cross = gain_rows[1]
    gain_feed = lax.dynamic_index_in_dim(gain_rows, 2 + stream, 0, keepdims=False)
    source = hidden[0]
    row_count = source.shape[0]
    feature_width = source.shape[1]
    image_count = features.shape[0]
    query_allow, text_allow = layout(caption_lengths[0], caption_image[0], row_count, NQ)
    normed_self = to_half(norm_rows(source, gain_self))
    query_half = to_half(product(normed_self, full_project[0]))
    key_half = to_half(product(normed_self, full_project[1]))
    value_half = to_half(product(normed_self, full_project[2]))
    empty_half = jnp.zeros((row_count, feature_width), jnp.bfloat16)
    far_key, far_value = shifted((key_half, value_half), "stream", 1)
    text_keys = jnp.concatenate([far_key, key_half], axis=0)
    text_values = jnp.concatenate([far_value, value_half], axis=0)

    def self_query():
        return attend(query_half[None], key_half[None], value_half[None], query_allow[None])

    def self_text():
        return attend(query_half[None], text_keys[None], text_values[None], text_allow[None])

    context_self, total_self = lax.cond(stream == 0, self_query, self_text)
    context_half = to_half(context_self[0])
    branch_self = product(context_half, full_output[0])
    after_self = source + branch_self

    def cross_on():
        normed_cross = to_half(norm_rows(after_self, gain_cross))
        cross_half = to_half(product(normed_cross, full_query))
        vision_pair = project_vision(features, full_vision)
        context_cross, total_cross = attend(
            cross_half.reshape(image_count, NQ, feature_width), vision_pair[0], vision_pair[1], None
        )
        context_cross_half = to_half(context_cross.reshape(row_count, feature_width))
        branch = product(context_cross_half, full_output[1])
        return (branch, total_cross, vision_pair, normed_cross, cross_half, context_cross_half)

    def cross_off():
        return (
            jnp.zeros((row_count, feature_width), jnp.float32),
            jnp.zeros((image_count, HEADS, NQ), jnp.float32),
            jnp.zeros((2, image_count, features.shape[1], feature_width), jnp.bfloat16),
            empty_half,
            empty_half,
            empty_half,
        )

    branch_cross, total_cross, vision_pair, normed_cross, cross_half, context_cross_half = lax.cond(
        stream == 0, cross_on, cross_off
    )
    after_cross = after_self + branch_cross
    normed_feed = to_half(norm_rows(after_cross, gain_feed))
    before = right_product(normed_feed, full_expand[0])
    active_half = to_half(exact_gelu(before))
    branch_feed = product(active_half, full_reduce[0])
    result = after_cross + branch_feed
    grad_result = out_grad[0]
    grad_feed_half = to_half(grad_result)
    grad_reduce = left_product(active_half, grad_feed_half)
    grad_active = right_product(grad_feed_half, full_reduce[0])
    grad_before = to_half(jax.vjp(exact_gelu, before)[1](grad_active)[0])
    grad_expand = left_product(grad_before, normed_feed)
    grad_normed_feed = product(grad_before, full_expand[0])
    feed_in, grad_gain_feed = jax.vjp(norm_rows, after_cross, gain_feed)[1](grad_normed_feed)
    grad_cross = grad_result + feed_in

    def cross_back_on():
        grad_branch_half = to_half(grad_cross)
        grad_out_cross = left_product(context_cross_half, grad_branch_half)
        grad_context = to_half(right_product(grad_branch_half, full_output[1]))
        grad_cq, grad_ck, grad_cv = attend_back(
            cross_half.reshape(image_count, NQ, feature_width),
            vision_pair[0],
            vision_pair[1],
            None,
            total_cross,
            grad_context.reshape(image_count, NQ, feature_width),
        )
        grad_cq_half = to_half(grad_cq.reshape(row_count, feature_width))
        grad_pair = to_half(jnp.stack([grad_ck, grad_cv]))
        grad_cross_weight = left_product(normed_cross, grad_cq_half)
        grad_normed_cross = right_product(grad_cq_half, full_query)
        cross_in, grad_gain_cross = jax.vjp(norm_rows, after_self, gain_cross)[1](grad_normed_cross)
        vision_term = vision_grad(features, grad_pair)
        return (cross_in, grad_gain_cross, grad_out_cross, grad_cross_weight, vision_term)

    def cross_back_off():
        square_zero = jnp.zeros((feature_width, feature_width), jnp.float32)
        vision_term = jnp.zeros((2, features.shape[2], feature_width), jnp.float32)
        return (
            jnp.zeros((row_count, feature_width), jnp.float32),
            jnp.zeros((feature_width,), jnp.float32),
            square_zero,
            square_zero,
            vision_term,
        )

    cross_in, grad_gain_cross, grad_out_cross, grad_cross_weight, vision_term = lax.cond(
        stream == 0, cross_back_on, cross_back_off
    )
    grad_after_self = grad_cross + cross_in
    grad_branch_half = to_half(grad_after_self)
    grad_out_self = left_product(context_half, grad_branch_half)
    grad_context_self = to_half(right_product(grad_branch_half, full_output[0]))

    def self_back_query():
        grad_sq, grad_sk, grad_sv = attend_back(
            query_half[None],
            key_half[None],
            value_half[None],
            query_allow[None],
            total_self,
            grad_context_self[None],
        )
        empty_rows = jnp.zeros((row_count, feature_width), jnp.float32)
        return (grad_sq[0], grad_sk[0], grad_sv[0], empty_rows, empty_rows)

    def self_back_text():
        grad_sq, grad_sk, grad_sv = attend_back(
            query_half[None],
            text_keys[None],
            text_values[None],
            text_allow[None],
            total_self,
            grad_context_self[None],
        )
        return (
            grad_sq[0],
            grad_sk[0, row_count:],
            grad_sv[0, row_count:],
            grad_sk[0, :row_count],
            grad_sv[0, :row_count],
        )

    own_query, own_key, own_value, far_grad_key, far_grad_value = lax.cond(
        stream == 0, self_back_query, self_back_text
    )
    own_query = to_half(own_query)
    own_key = to_half(own_key)
    own_value = to_half(own_value)
    far_key_half = to_half(far_grad_key)
    far_value_half = to_half(far_grad_value)
    grad_normed = (
        right_product(own_query, full_project[0])
        + right_product(own_key, full_project[1])
        + right_product(own_value, full_project[2])
    )
    grad_key_weight = left_product(normed_self, own_key)
    grad_value_weight = left_product(normed_self, own_value)
    back_key, back_value = shifted((far_key_half, far_value_half), "stream", -1)
    grad_normed = (
        grad_normed
        + right_product(back_key, full_project[1])
        + right_product(back_value, full_project[2])
    )
    grad_key_weight = grad_key_weight + left_product(normed_self, back_key)
    grad_value_weight = grad_value_weight + left_product(normed_self, back_value)
    grad_project = jnp.stack(
        [left_product(normed_self, own_query), grad_key_weight, grad_value_weight]
    )
    source_in, grad_gain_self = jax.vjp(norm_rows, source, gain_self)[1](grad_normed)
    hidden_grad = grad_after_self + source_in
    zero_row = jnp.zeros_like(grad_gain_feed)
    gain_grads = jnp.stack(
        [
            grad_gain_self,
            grad_gain_cross,
            jnp.where(stream == 0, grad_gain_feed, zero_row),
            jnp.where(stream == 1, grad_gain_feed, zero_row),
        ]
    )
    shared_grads = (
        grad_project,
        jnp.stack([grad_out_self, grad_out_cross]),
        grad_cross_weight,
        vision_term,
        gain_grads,
    )
    stat_row = jnp.stack(
        [
            square_rows(source),
            square_rows(branch_self),
            square_rows(branch_feed),
            square_rows(result),
        ]
    )
    stat_local = jnp.where(
        jnp.arange(2, dtype=jnp.int32)[:, None] == stream, stat_row[None, :], 0.0
    )
    if direct:
        width = grad_project.shape[-1]
        rows = attn_project.shape[1]
        part_first = to_half(
            jnp.stack([grad_project, jnp.stack([grad_out_self, grad_out_cross, grad_cross_weight])])
        ).reshape(2, 3, 4, 2, 2, rows, width)
        part_vision = to_half(vision_term).reshape(2, 4, 2, 2, cross_vision.shape[1], width)
        part_expand = to_half(grad_expand).reshape(4, 2, 2, feed_expand.shape[1], width)
        part_reduce = to_half(grad_reduce).reshape(4, 2, 2, feed_reduce.shape[1], width)
        part_stats = jnp.pad(stat_local.reshape(8, 1), ((0, 0), (0, 127)))
        sum_first, sum_vision, sum_expand, sum_reduce, all_gain_sums, totals = scatter_all(
            part_first, part_vision, part_expand, part_reduce, jnp.pad(gain_grads, ((0, 4), (0, 0))), part_stats
        )
        sum_project = sum_first[0]
        sum_output = sum_first[1, :2]
        sum_query = sum_first[1, 2]
        parts_expand, parts_reduce = sum_expand[None], sum_reduce[None]
        own_gains = norm_gains.shape[1]
        sum_gains = lax.dynamic_slice_in_dim(
            all_gain_sums[:4], lax.axis_index("dp") * own_gains, own_gains, axis=1
        )
        total_square = jnp.sum(totals[:8])
        stat_sums = jnp.sum(totals[8:], axis=1).reshape(2, 4)
    else:
        (
            parts_project,
            parts_output,
            parts_query,
            parts_vision,
            parts_expand,
            parts_reduce,
            parts_gains,
        ) = (
            lax.psum_scatter(shared_grads[0], "dp", scatter_dimension=1, tiled=True),
            lax.psum_scatter(shared_grads[1], "dp", scatter_dimension=1, tiled=True),
            lax.psum_scatter(shared_grads[2], "dp", scatter_dimension=0, tiled=True),
            lax.psum_scatter(shared_grads[3], "dp", scatter_dimension=1, tiled=True),
            lax.psum_scatter(grad_expand[None], "dp", scatter_dimension=1, tiled=True),
            lax.psum_scatter(grad_reduce[None], "dp", scatter_dimension=1, tiled=True),
            lax.psum_scatter(shared_grads[4], "dp", scatter_dimension=1, tiled=True),
        )
        sum_project, sum_output, sum_query, sum_vision, sum_gains = (
            lax.psum(parts_project.astype(jnp.bfloat16), "stream").astype(jnp.float32),
            lax.psum(parts_output.astype(jnp.bfloat16), "stream").astype(jnp.float32),
            lax.psum(parts_query.astype(jnp.bfloat16), "stream").astype(jnp.float32),
            lax.psum(parts_vision.astype(jnp.bfloat16), "stream").astype(jnp.float32),
            lax.psum(parts_gains.astype(jnp.bfloat16), "stream").astype(jnp.float32),
        )
        shared_square = (
            jnp.sum(sum_project * sum_project)
            + jnp.sum(sum_output * sum_output)
            + jnp.sum(sum_query * sum_query)
            + jnp.sum(sum_vision * sum_vision)
            + jnp.sum(sum_gains * sum_gains)
        )
        local_square = (
            0.5 * shared_square
            + jnp.sum(parts_expand * parts_expand)
            + jnp.sum(parts_reduce * parts_reduce)
        )
        total_square, stat_sums = lax.psum((local_square, stat_local), ("stream", "dp"))
    grad_norm = jnp.sqrt(total_square)
    rms_values = jnp.sqrt(stat_sums / (row_count * lax.axis_size("dp")))
    factor = clip_norm / jnp.maximum(grad_norm, clip_norm)
    clipped_gains = sum_gains * factor
    fresh_expand, mean_expand, square_expand = adam_step(
        feed_expand, parts_expand, first_expand, second_expand, factor, rate_matrix, decay_rate
    )
    fresh_reduce, mean_reduce, square_reduce = adam_step(
        feed_reduce, parts_reduce, first_reduce, second_reduce, factor, rate_matrix, decay_rate
    )
    weights_shared = (attn_project, attn_output, cross_query, cross_vision, norm_gains)
    firsts_shared = (first_project, first_output, first_query, first_vision, first_gains)
    seconds_shared = (second_project, second_output, second_query, second_vision, second_gains)
    summed_shared = (sum_project, sum_output, sum_query, sum_vision, sum_gains)
    updated = []
    for index in range(5):
        rate = rate_gains if index == 4 else rate_matrix
        decay = 0.0 if index == 4 else decay_rate
        weight = weights_shared[index]
        first = firsts_shared[index]
        second = seconds_shared[index]
        updated.append(adam_step(weight, summed_shared[index], first, second, factor, rate, decay))
    fresh_project, mean_project, square_project = updated[0]
    fresh_output, mean_output, square_output = updated[1]
    fresh_query, mean_query, square_query = updated[2]
    fresh_vision, mean_vision, square_vision = updated[3]
    fresh_gains, mean_gains, square_gains = updated[4]
    return (
        result[None],
        hidden_grad[None],
        grad_norm,
        rms_values,
        fresh_project,
        mean_project,
        square_project,
        fresh_output,
        mean_output,
        square_output,
        fresh_query,
        mean_query,
        square_query,
        fresh_vision,
        mean_vision,
        square_vision,
        fresh_expand,
        mean_expand,
        square_expand,
        fresh_reduce,
        mean_reduce,
        square_reduce,
        fresh_gains,
        mean_gains,
        square_gains,
        clipped_gains,
        to_half(fresh_project),
        to_half(fresh_output),
        to_half(fresh_query),
        to_half(fresh_vision),
        to_half(fresh_expand),
        to_half(fresh_reduce),
    )


def solution(mesh):
    return jax.shard_map(
        body,
        mesh=mesh,
        in_specs=(
            P("stream", "dp", None),
            P("dp", None, None),
            P("dp", None),
            P("dp", None),
            P("stream", "dp", None),
            P(None, "dp", None),
            P(None, "dp", None),
            P("dp", None),
            P(None, "dp", None),
            P("stream", "dp", None),
            P("stream", "dp", None),
            P(None, "dp"),
            P(None, "dp", None),
            P(None, "dp", None),
            P(None, "dp", None),
            P(None, "dp", None),
            P("dp", None),
            P("dp", None),
            P(None, "dp", None),
            P(None, "dp", None),
            P("stream", "dp", None),
            P("stream", "dp", None),
            P("stream", "dp", None),
            P("stream", "dp", None),
            P(None, "dp"),
            P(None, "dp"),
        ),
        out_specs=(
            P("stream", "dp", None),
            P("stream", "dp", None),
            P(),
            P(),
            P(None, "dp", None),
            P(None, "dp", None),
            P(None, "dp", None),
            P(None, "dp", None),
            P(None, "dp", None),
            P(None, "dp", None),
            P("dp", None),
            P("dp", None),
            P("dp", None),
            P(None, "dp", None),
            P(None, "dp", None),
            P(None, "dp", None),
            P("stream", "dp", None),
            P("stream", "dp", None),
            P("stream", "dp", None),
            P("stream", "dp", None),
            P("stream", "dp", None),
            P("stream", "dp", None),
            P(None, "dp"),
            P(None, "dp"),
            P(None, "dp"),
            P(None, "dp"),
            P(None, "dp", None),
            P(None, "dp", None),
            P("dp", None),
            P(None, "dp", None),
            P("stream", "dp", None),
            P("stream", "dp", None),
        ),
        check_vma=False,
    )
```

```python
import functools

import jax
import jax.numpy as jnp
from jax import lax
from jax.experimental import pallas as pl
from jax.experimental.pallas import tpu as pltpu
from jax.sharding import PartitionSpec as P

HEADS = 12
HD = 64
NQ = 32
STEP = 10


epsilon = 1e-06
masked_value = -1e30
beta_first = 0.9
beta_second = 0.999
rate_matrix = 0.05
rate_gains = 1.0
decay_rate = 0.01
adam_floor = 1e-08
clip_norm = 1.0


def shifted(block, axis, distance):
    devices = range(lax.axis_size(axis))
    route = [(i - distance, i) for i in devices if i - distance in devices]
    return lax.ppermute(block, axis, route)


def to_half(values):
    return values.astype(jnp.bfloat16)


def product(left, right):
    return jnp.dot(left, right, preferred_element_type=jnp.float32)


def left_product(left, right):
    return lax.dot_general(
        left, right, (((0,), (0,)), ((), ())), preferred_element_type=jnp.float32
    )


def right_product(left, right):
    return lax.dot_general(
        left, right, (((1,), (1,)), ((), ())), preferred_element_type=jnp.float32
    )


def norm_rows(values, gain):
    return values * lax.rsqrt(jnp.mean(values * values, axis=-1, keepdims=True) + epsilon) * gain


def exact_gelu(values):
    return jax.nn.gelu(values, approximate=False)


def square_rows(values):
    return jnp.sum(jnp.mean(values * values, axis=-1))


def layout(lengths, owners, row_count, per_image):
    caption_ends = jnp.cumsum(lengths)
    caption_starts = caption_ends - lengths
    row_index = jnp.arange(row_count, dtype=jnp.int32)
    inside = (row_index[:, None] >= caption_starts[None, :]) & (
        row_index[:, None] < caption_ends[None, :]
    )
    caption = jnp.sum(
        jnp.where(inside, jnp.arange(lengths.shape[0], dtype=jnp.int32)[None, :], 0), axis=1
    )
    text_image = jnp.sum(jnp.where(inside, owners[None, :], 0), axis=1)
    query_image = row_index // per_image
    query_allow = query_image[:, None] == query_image[None, :]
    own_caption = (caption[:, None] == caption[None, :]) & (
        row_index[None, :] <= row_index[:, None]
    )
    text_allow = jnp.concatenate([text_image[:, None] == query_image[None, :], own_caption], axis=1)
    return (query_allow, text_allow)


def attention_scores(query_rows, key_rows, allowed):
    batch_count, query_count, width_all = query_rows.shape
    query_heads = query_rows.reshape(batch_count, query_count, HEADS, HD)
    key_heads = key_rows.reshape(batch_count, key_rows.shape[1], HEADS, HD)
    scores = jnp.einsum(
        "bqhd,bkhd->bhqk", query_heads, key_heads, preferred_element_type=jnp.float32
    ) * HD ** (-0.5)
    if allowed is not None:
        scores = jnp.where(allowed[:, None], scores, masked_value)
    return (scores, query_heads, key_heads)


def attend(query_rows, key_rows, value_rows, allowed):
    scores, query_heads, key_heads = attention_scores(query_rows, key_rows, allowed)
    value_heads = value_rows.reshape(key_heads.shape)
    row_max = jnp.max(scores, axis=-1, keepdims=True)
    weights = jnp.exp(scores - row_max)
    denominator = jnp.sum(weights, axis=-1, keepdims=True)
    probability = to_half(weights / denominator)
    context = jnp.einsum(
        "bhqk,bkhd->bqhd", probability, value_heads, preferred_element_type=jnp.float32
    )
    return (context.reshape(query_rows.shape), (row_max + jnp.log(denominator))[..., 0])


def attend_back(query_rows, key_rows, value_rows, allowed, log_total, grad_context):
    scores, query_heads, key_heads = attention_scores(query_rows, key_rows, allowed)
    value_heads = value_rows.reshape(key_heads.shape)
    probability = jnp.exp(scores - log_total[..., None])
    grad_heads = grad_context.reshape(query_heads.shape)
    grad_prob = jnp.einsum(
        "bqhd,bkhd->bhqk", grad_heads, value_heads, preferred_element_type=jnp.float32
    )
    grad_value = jnp.einsum(
        "bhqk,bqhd->bkhd", to_half(probability), grad_heads, preferred_element_type=jnp.float32
    )
    grad_score = to_half(
        probability * (grad_prob - jnp.sum(grad_prob * probability, axis=-1, keepdims=True))
    )
    grad_query = jnp.einsum(
        "bhqk,bkhd->bqhd", grad_score, key_heads, preferred_element_type=jnp.float32
    ) * HD ** (-0.5)
    grad_key = jnp.einsum(
        "bhqk,bqhd->bkhd", grad_score, query_heads, preferred_element_type=jnp.float32
    ) * HD ** (-0.5)
    return (
        grad_query.reshape(query_rows.shape),
        grad_key.reshape(key_rows.shape),
        grad_value.reshape(value_rows.shape),
    )


def project_vision(feature_block, vision_weights):
    return to_half(
        jnp.einsum(
            "inv,kvd->kind", feature_block, vision_weights, preferred_element_type=jnp.float32
        )
    )


def vision_grad(feature_block, grad_pair):
    return jnp.einsum("inv,kind->kvd", feature_block, grad_pair, preferred_element_type=jnp.float32)


def adam_step(weight, gradient, first, second, factor, rate, decay):
    clipped = gradient * factor
    mean_new = beta_first * first + (1.0 - beta_first) * clipped
    square_new = beta_second * second + (1.0 - beta_second) * clipped * clipped
    corrected_mean = mean_new / (1.0 - beta_first**STEP)
    corrected_square = square_new / (1.0 - beta_second**STEP)
    fresh = weight - rate * (
        corrected_mean / (jnp.sqrt(corrected_square) + adam_floor) + decay * weight
    )
    return (fresh, mean_new, square_new)


MESH = pl.DeviceIdType.MESH
VMEM_LIMIT = 60 * 2**20


def coordinates():
    c = lax.axis_index("stream")
    d = lax.axis_index("dp")
    return c, d // 4, (d // 2) % 2, d % 2


def device(c, z, y, x):
    return (c, z * 4 + y * 2 + x)


def meet(c, z, y, x):
    barrier = pltpu.get_barrier_semaphore()
    others = [device(1 - c, z, y, x), device(c, z, 1 - y, x), device(c, z, y, 1 - x)]
    others += [device(c, (z + k) % 4, y, x) for k in (1, 2, 3)]
    for other in others:
        pl.semaphore_signal(barrier, inc=1, device_id=other, device_id_type=MESH)
    pl.semaphore_wait(barrier, len(others))


ORDERS = {
    ("late", 0): ("z", "y", "x"),
    ("late", 1): ("z", "x", "y"),
    ("early", 0): ("x", "z", "y"),
    ("early", 1): ("y", "z", "x"),
    ("right", 0): ("y", "z", "x"),
    ("right", 1): ("y", "z", "x"),
    ("vision", 0): ("x", "z", "y"),
    ("vision", 1): ("x", "z", "y"),
}


PARTS = 4


def wide(block):
    return block.astype(jnp.float32)


def nn(left, right):
    return lax.dot_general(
        left, right, (((1,), (0,)), ((), ())), preferred_element_type=jnp.float32
    )


def nt(left, right):
    return lax.dot_general(
        left, right, (((1,), (1,)), ((), ())), preferred_element_type=jnp.float32
    )


def tn(left, right):
    return lax.dot_general(
        left, right, (((0,), (0,)), ((), ())), preferred_element_type=jnp.float32
    )


def span(index, size):
    return pl.ds(pl.multiple_of(index * size, size), size)


def loop(count, step):
    def body(index, carry):
        step(index)
        return carry

    lax.fori_loop(0, count, body, 0)


def row_sum(values):
    return jnp.sum(values, axis=0, keepdims=True)


def norm_back(values, gain, grad):
    scale = lax.rsqrt(jnp.mean(values * values, axis=-1, keepdims=True) + epsilon)
    unit = values * scale
    grad_unit = grad * gain
    mean = jnp.mean(grad_unit * unit, axis=-1, keepdims=True)
    return scale * (grad_unit - unit * mean), row_sum(grad * unit)


def lane_masks(rows):
    lane = lax.broadcasted_iota(jnp.int32, (rows, 2 * HD), 1)
    left = jnp.where(lane < HD, 1.0, 0.0)
    return to_half(left), to_half(1.0 - left)


def head_pair(block, masks):
    return jnp.concatenate([block * masks[0], block * masks[1]], axis=0)


def pair_join(both):
    rows = both.shape[0] // 2
    lane = lax.broadcasted_iota(jnp.int32, (rows, 2 * HD), 1)
    return jnp.where(lane < HD, both[:rows], both[rows:])


def diagonal(full, rows):
    lane = lax.broadcasted_iota(jnp.int32, (rows, 2 * HD), 1)
    tiles = []
    for t in range(HEADS // 2):
        tile = full[:, t * 2 * HD : (t + 1) * 2 * HD]
        left = tile[2 * t * rows : (2 * t + 1) * rows]
        right = tile[(2 * t + 1) * rows : (2 * t + 2) * rows]
        tiles.append(jnp.where(lane < HD, left, right))
    return jnp.concatenate(tiles, axis=1)


def head_mask(rows, width):
    row = lax.broadcasted_iota(jnp.int32, (HEADS * rows, width), 0) // rows
    lane = lax.broadcasted_iota(jnp.int32, (HEADS * rows, width), 1) // HD
    return to_half(jnp.where(row == lane, 1.0, 0.0))


def caption_layout(lengths, owners, row_count):
    count = lengths.shape[1]
    size = wide(lengths)
    owner = wide(owners)
    sub = lax.broadcasted_iota(jnp.int32, (count, count), 0)
    lane = lax.broadcasted_iota(jnp.int32, (count, count), 1)
    starts = jnp.sum(jnp.where(lane < sub, size, 0.0), axis=1, keepdims=True)
    owner_down = jnp.sum(jnp.where(lane == sub, owner, 0.0), axis=1, keepdims=True)
    row = wide(lax.broadcasted_iota(jnp.int32, (count, row_count), 1))
    begun = starts <= row
    start = jnp.max(jnp.where(begun, starts, 0.0), axis=0, keepdims=True)
    image = jnp.max(jnp.where(begun, owner_down, 0.0), axis=0, keepdims=True)
    return start, image


def text_bias(rb, start, image, far_rows, window, bias):
    begin = jnp.maximum(rb - 1, 0) * 128
    far = lax.broadcasted_iota(jnp.int32, (far_rows, 128), 0) // NQ
    far_bias = jnp.where(wide(far) == image, 0.0, masked_value)
    key = lax.broadcasted_iota(jnp.int32, (window, 128), 0) + begin
    row = lax.broadcasted_iota(jnp.int32, (window, 128), 1) + rb * 128
    seen = (wide(key) >= start) & (key <= row)
    own_bias = jnp.where(seen, 0.0, masked_value)
    bias[0:far_rows] = jnp.concatenate([far_bias, far_bias], axis=1)
    bias[far_rows : far_rows + window] = jnp.concatenate([own_bias, own_bias], axis=1)


def query_bias(bias):
    key = lax.broadcasted_iota(jnp.int32, (128, 256), 0) // NQ
    row = (lax.broadcasted_iota(jnp.int32, (128, 256), 1) % 128) // NQ
    bias[0:128] = jnp.where(key == row, 0.0, masked_value)


def forward_kernel(
    first, vision, expand, reduce, gains,
    hidden_in, out_grad_in, features, lengths, owners,
    out_result, out_grad_cross, part_expand, part_reduce, gain_feed_out, stats,
    keep_first, keep_gains, keep_normed, keep_query, keep_key, keep_value, keep_far_key, keep_far_value,
    keep_context, keep_after_self, keep_cross_query, keep_cross_context, keep_vision, keep_images, total_self, total_cross,
    all_first, raw_vision, all_vision, all_expand, all_reduce, all_gains, gain_rows,
    hidden, out_grad, images, vision_pair, normed, query, key, value, far_key, far_value, context, after_self,
    cross_query, cross_context, after_cross, normed_feed, grad_feed, sum_branch, sum_normed, bias, mask,
    layout_rows, send_sem, recv_sem, local_sem,
):
    c, z, y, x = coordinates()
    own = {"z": z, "y": y, "x": x}
    row_count, width = hidden.shape
    image_count = total_cross.shape[0]
    padded = vision_pair.shape[0] // image_count
    feature_rows = features.shape[0] // (2 * image_count)
    feature_width = features.shape[1]
    part_rows = expand.shape[0] // PARTS
    far_rows, window = far_key.shape[0], 256
    cross_rows = image_count * NQ

    chunks = [(gains, lambda *at: all_gains.at[at], "late", False, 1)]
    for j, kind in enumerate(("late", "early", "late")):
        chunks.append((first.at[j], lambda *at, j=j: all_first.at[(c, j) + at], kind, True, 1))
    chunks.append((vision, lambda *at: raw_vision.at[(c,) + at], "late", True, 2))
    for p in range(PARTS):
        rows = pl.ds(p * part_rows, part_rows)
        kinds = ("early", "late") if p % 2 == 0 else ("late", "early")
        for (source, whole), kind in zip(((expand, all_expand), (reduce, all_reduce)), kinds):
            target = lambda *at, p=p, whole=whole: whole.at[(p,) + at]
            chunks.append((source.at[rows], target, kind, False, 2))
    count = len(chunks)
    events = [
        (number + stage * chunk[4], -stage, number)
        for number, chunk in enumerate(chunks)
        for stage in range(4)
    ]

    def remote(source, target, index, where):
        return pltpu.make_async_remote_copy(
            src_ref=source, dst_ref=target, send_sem=send_sem.at[index],
            recv_sem=recv_sem.at[index], device_id=where, device_id_type=MESH,
        )

    def sends(number, stage, core):
        source, target, kind = chunks[number][:3]
        order = ORDERS[kind, core]
        done, axis = order[:stage], order[stage]
        at = tuple(slice(None) if a in done else own[a] for a in "zyx")
        block = target(*at)
        here = source if stage == 0 else block
        base = (number * 3 + stage) * 3
        if axis == "z":
            return [
                remote(here, block, base + k - 1, device(c, (z + k) % 4, y, x)) for k in (1, 2, 3)
            ]
        where = device(c, z, 1 - y, x) if axis == "y" else device(c, z, y, 1 - x)
        return [remote(here, block, base, where)]

    def place(number):
        source, target = chunks[number][:2]
        return pltpu.make_async_copy(source, target(z, y, x), local_sem.at[number])

    pair = device(1 - c, z, y, x)

    def across(number):
        target = chunks[number][1]
        block = target(slice(None), slice(None), slice(None))
        return remote(block, block, count * 9 + number, pair)

    def tick_core(tick, core):
        for when, negative, number in sorted(events):
            stage = -negative
            if when != tick:
                continue
            if stage > 0:
                for copy in sends(number, stage - 1, core):
                    copy.wait_recv()
            if stage == 1:
                place(number).wait()
            if stage < 3:
                for copy in sends(number, stage, core):
                    copy.start()
                if stage == 0:
                    place(number).start()
            elif chunks[number][3]:
                across(number).start()

    def both(step):
        @pl.when(c == 0)
        def _():
            step(0)

        @pl.when(c == 1)
        def _():
            step(1)

    def tick(number):
        both(lambda core: tick_core(number, core))

    def sent(number):
        def step(core):
            for stage in range(3):
                for copy in sends(number, stage, core):
                    copy.wait_send()

        both(step)

    swap_base = count * 10
    swaps = {
        "key": (key, far_key),
        "value": (value, far_value),
        "query": (cross_query.at[pl.ds(cross_rows, cross_rows)], cross_query.at[pl.ds(0, cross_rows)]),
        "context": (cross_context.at[pl.ds(0, cross_rows)], cross_context.at[pl.ds(cross_rows, cross_rows)]),
    }

    def swap(name):
        source, target = swaps[name]
        return remote(source, target, swap_base + list(swaps).index(name), pair)

    local_base = count
    loads = [
        (hidden_in, hidden),
        (out_grad_in, out_grad),
    ]
    step_rows = 2 * image_count * 32
    whole_steps = feature_rows // 32
    half_rows = whole_steps // 2 * step_rows
    for begin, size in ((0, half_rows), (half_rows, features.shape[0] - half_rows)):
        staged = vision_pair.at[pl.ds(0, size), pl.ds(0, feature_width)]
        loads.append((features.at[pl.ds(begin, size)], staged))
    keeps = {
        "first": (all_first, keep_first),
        "gains": (gain_rows, keep_gains),
        "normed": (normed, keep_normed),
        "query": (query, keep_query),
        "key": (key, keep_key),
        "value": (value, keep_value),
        "far_key": (far_key, keep_far_key),
        "far_value": (far_value, keep_far_value),
        "context": (context, keep_context),
        "after_self": (after_self, keep_after_self),
        "cross_query": (cross_query.at[pl.ds(0, cross_rows)], keep_cross_query),
        "cross_context": (cross_context, keep_cross_context),
        "vision": (vision_pair, keep_vision),
        "images": (images, keep_images),
        "result": (sum_branch, out_result),
        "grad_cross": (sum_normed, out_grad_cross),
    }
    for p in range(PARTS):
        keeps["expand", p] = (all_expand.at[p], part_expand.at[p])
        keeps["reduce", p] = (all_reduce.at[p], part_reduce.at[p])

    def load(k):
        source, target = loads[k]
        return pltpu.make_async_copy(source, target, local_sem.at[local_base + k])

    def keep(name):
        source, target = keeps[name]
        index = local_base + len(loads) + list(keeps).index(name)
        return pltpu.make_async_copy(source, target, local_sem.at[index])

    def weight(plane, j):
        return all_first[plane, j].reshape(width, width)

    def gain(k):
        return gain_rows[pl.ds(k, 1), :]

    def stat(k, amount):
        row = pl.ds(c * 4 + k, 1)
        stats[row, :] = stats[row, :] + amount


    def start():
        stats[...] = jnp.zeros_like(stats)
        mask[...] = head_mask(NQ, width)
        first_row, image = caption_layout(lengths[...], owners[...], row_count)
        layout_rows[0:1] = first_row
        layout_rows[1:2] = image

    def read_gains():
        total = jnp.zeros(gain_rows.shape, jnp.float32)
        per = width // 16
        for k in range(16):
            lane = lax.broadcasted_iota(jnp.int32, (128, width), 0)
            column = lax.broadcasted_iota(jnp.int32, (128, width), 1)
            pick = to_half(jnp.where((column == lane + k * per) & (lane < per), 1.0, 0.0))
            total = total + nn(all_gains[k // 4, (k // 2) % 2, k % 2], pick)
        gain_rows[...] = total

    def self_in():
        def step(i):
            rows = span(i, 256)
            source = hidden[rows, :]
            stat(0, row_sum(source * source))
            part = to_half(norm_rows(source, gain(0)))
            normed[rows, :] = part
            query[rows, :] = to_half(nn(part, weight(0, 0))) * jnp.bfloat16(HD**-0.5)
            key[rows, :] = to_half(nn(part, weight(0, 1)))
            value[rows, :] = to_half(nn(part, weight(0, 2)))

        loop(row_count // 256, step)

    def attend_pair(rb, t, parts):
        lanes, rows = span(t, 128), span(rb, 128)
        queries = head_pair(query[rows, lanes], lane_masks(128))
        scores, most = [], None
        for keys, _, where, _ in parts:
            score = nt(keys, queries) + bias[where, :]
            scores.append(score)
            top = jnp.max(score, axis=0, keepdims=True)
            most = top if most is None else jnp.maximum(most, top)
        weights = [jnp.exp(score - most) for score in scores]
        total = sum(row_sum(part) for part in weights)
        inverse = 1.0 / total
        result = sum(
            tn(to_half(part * inverse), values) for part, (_, values, _, _) in zip(weights, parts)
        )
        context[rows, lanes] = to_half(pair_join(result))
        total_self[rb, t] = most + jnp.log(total)

    def self_query():
        query_bias(bias)

        def step(i):
            rb, t = i // 6, i % 6
            rows, lanes = span(rb, 128), span(t, 128)
            attend_pair(rb, t, [(key[rows, lanes], value[rows, lanes], pl.ds(0, 128), None)])

        loop(row_count // 128 * 6, step)

    def self_text():
        def outer(rb):
            rows = span(rb, 128)
            text_bias(rb, layout_rows[0:1, rows], layout_rows[1:2, rows], far_rows, window, bias)
            near = pl.ds(pl.multiple_of(jnp.maximum(rb - 1, 0) * 128, 128), window)

            def inner(t):
                lanes = span(t, 128)
                attend_pair(rb, t, [
                    (far_key[:, lanes], far_value[:, lanes], pl.ds(0, far_rows), None),
                    (key[near, lanes], value[near, lanes], pl.ds(far_rows, window), None),
                ])

            loop(6, inner)

        loop(row_count // 128, outer)

    def self_out():
        def step(i):
            rows = span(i, 256)
            branch = nn(context[rows, :], weight(1, 0))
            stat(1, row_sum(branch * branch))
            after_self[rows, :] = hidden[rows, :] + branch

        loop(row_count // 256, step)

    def cross_in():
        def step(i):
            rows = span(i, 256)
            part = to_half(norm_rows(after_self[rows, :], gain(1)))
            result = to_half(nn(part, weight(1, 2))) * jnp.bfloat16(HD**-0.5)
            cross_query[rows, :] = result

        loop(row_count // 256, step)

    def pack_vision():
        def step(i):
            plane, z_at, y_at = i // 8, (i // 2) % 4, i % 2
            left = wide(raw_vision[plane, z_at, y_at, 0])
            right = wide(raw_vision[plane, z_at, y_at, 1])
            size = 2 * left.shape[0]
            all_vision[plane, span(z_at * 2 + y_at, size), :] = to_half(
                jnp.concatenate([left, right], axis=0)
            )

        loop(16, step)

    def sort_rows(begin, rows, base):
        size = rows // (2 * image_count)
        block = max(size, 16)
        out = lax.broadcasted_iota(jnp.int32, (image_count * block, rows), 0)
        column = lax.broadcasted_iota(jnp.int32, (image_count * block, rows), 1)
        source = (out % block) * (2 * image_count) + c * image_count + out // block
        pick = to_half(jnp.where((column == source) & (out % block < size), 1.0, 0.0))
        sorted_rows = to_half(nn(pick, vision_pair[begin, 0:feature_width]))
        for j in range(image_count):
            where = pl.ds(pl.multiple_of(j * padded + base, 16), block)
            images[where, :] = sorted_rows[j * block : (j + 1) * block]

    def sort_images(part):
        def step(i):
            sort_rows(span(i, step_rows), step_rows, 32 * (i + part * (whole_steps // 2)))

        loop(whole_steps // 2, step)
        if part == 1:
            rest = feature_rows % 32 * 2 * image_count
            sort_rows(pl.ds(whole_steps // 2 * step_rows, rest), rest, whole_steps * 32)

    def project_images(begin, end):
        def step(i):
            rows = pl.ds(pl.multiple_of((i + begin) * padded, 16), padded)
            image = images[rows, :]
            vision_pair[rows, 0:width] = to_half(nn(image, all_vision[0]))
            vision_pair[rows, width : 2 * width] = to_half(nn(image, all_vision[1]))

        loop(end - begin, step)

    def cross_attend(begin, end):
        def step(i):
            i = i + begin
            rows = pl.ds(pl.multiple_of(i * padded, 16), padded)
            own_rows = span(i, NQ)
            part = cross_query[own_rows, :]
            queries = jnp.concatenate([part] * HEADS, axis=0) * mask[...]
            score = nt(vision_pair[rows, 0:width], queries)
            key_row = lax.broadcasted_iota(jnp.int32, score.shape, 0)
            score = jnp.where(key_row < feature_rows, score, masked_value)
            most = jnp.max(score, axis=0, keepdims=True)
            weights = jnp.exp(score - most)
            total = row_sum(weights)
            total_cross[i] = most + jnp.log(total)
            full = tn(to_half(weights * (1.0 / total)), vision_pair[rows, width : 2 * width])
            cross_context[own_rows, :] = to_half(diagonal(full, NQ))

        loop(end - begin, step)

    def cross_out():
        def step(i):
            rows = span(i, 256)
            after_cross[rows, :] = after_self[rows, :] + nn(cross_context[rows, :], weight(1, 1))

        loop(row_count // 256, step)

    def feed_in():
        def step(i):
            rows = span(i, 128)
            normed_feed[rows, :] = to_half(norm_rows(after_cross[rows, :], gain(2 + c)))
            grad_feed[rows, :] = to_half(out_grad[rows, :])
            sum_branch[rows, :] = jnp.zeros((128, width), jnp.float32)
            sum_normed[rows, :] = jnp.zeros((128, width), jnp.float32)

        loop(row_count // 128, step)

    def feed_part(p):
        size = all_expand.shape[2] * all_expand.shape[3] * part_rows

        def step(s):
            at = pl.ds(2 * s, 2)
            shape = (2,) + all_expand.shape[2:]
            up = all_expand[p, at].reshape(2 * size, width)
            down = all_reduce[p, at].reshape(2 * size, width)
            before = nt(normed_feed[...], up)
            share = 0.5 * (1.0 + lax.erf(before * (0.5**0.5)))
            density = jnp.exp(before * before * -0.5) * (0.5 / jnp.pi) ** 0.5
            active = to_half(before * share)
            slope = share + before * density
            sum_branch[...] += nn(active, down)
            grad_before = to_half(nt(grad_feed[...], down) * slope)
            sum_normed[...] += nn(grad_before, up)
            all_reduce[p, at] = to_half(tn(active, grad_feed[...])).reshape(shape)
            all_expand[p, at] = to_half(tn(grad_before, normed_feed[...])).reshape(shape)

        loop(2, step)

    def feed_out():
        gain_feed_out[...] = jnp.zeros_like(gain_feed_out)

        def step(i):
            rows = span(i, 128)
            source = after_cross[rows, :]
            branch = sum_branch[rows, :]
            result = source + branch
            stat(2, row_sum(branch * branch))
            stat(3, row_sum(result * result))
            sum_branch[rows, :] = result
            back, gain_part = norm_back(source, gain(2 + c), sum_normed[rows, :])
            gain_feed_out[0:1, :] = gain_feed_out[0:1, :] + gain_part
            sum_normed[rows, :] = out_grad[rows, :] + back

        loop(row_count // 128, step)

    for k in range(3):
        load(k).start()
    meet(c, z, y, x)
    tick(0)
    start()
    tick(1)
    tick(2)
    load(2).wait()
    sort_images(0)
    load(3).start()
    tick(3)
    read_gains()
    keep("gains").start()
    tick(4)
    load(3).wait()
    sort_images(1)
    keep("images").start()
    tick(5)
    tick(6)
    for number in (1, 2, 3):
        across(number).wait_recv()
    load(0).wait()
    self_in()
    for name in ("normed", "query", "key", "value"):
        keep(name).start()

    @pl.when(c == 0)
    def _():
        swap("key").start()
        swap("value").start()

    tick(7)
    keep("first").start()

    @pl.when(c == 0)
    def _():
        self_query()

    @pl.when(c == 1)
    def _():
        swap("key").wait_recv()
        swap("value").wait_recv()
        self_text()
        keep("far_key").start()
        keep("far_value").start()

    tick(8)
    keep("context").start()
    self_out()
    keep("after_self").start()

    @pl.when(c == 0)
    def _():
        cross_in()
        swap("query").start()

    tick(9)
    tick(10)
    across(4).wait_recv()
    pack_vision()
    project_images(0, image_count // 2)
    tick(11)
    project_images(image_count // 2, image_count)
    keep("vision").start()
    tick(12)

    @pl.when(c == 1)
    def _():
        swap("query").wait_recv()

    cross_attend(0, image_count)
    tick(13)

    @pl.when(c == 1)
    def _():
        swap("context").start()
        after_cross[...] = after_self[...]

    @pl.when(c == 0)
    def _():
        swap("context").wait_recv()
        cross_out()

    keep("cross_query").start()
    keep("cross_context").start()
    load(1).wait()
    feed_in()
    for p in range(PARTS):
        sent(5 + 2 * p)
        sent(6 + 2 * p)
        feed_part(p)
        keep(("expand", p)).start()
        keep(("reduce", p)).start()
        for number in {0: (14,), 1: (15, 16), 2: (17, 18)}.get(p, ()):
            tick(number)
    feed_out()
    keep("result").start()
    keep("grad_cross").start()
    for number in range(5):
        sent(number)
    for number in range(1, 5):
        across(number).wait_send()

    @pl.when(c == 0)
    def _():
        swap("key").wait_send()
        swap("value").wait_send()
        swap("query").wait_send()

    @pl.when(c == 1)
    def _():
        swap("context").wait_send()

    for name in keeps:
        if name in ("far_key", "far_value"):

            @pl.when(c == 1)
            def _(name=name):
                keep(name).wait()

        else:
            keep(name).wait()


def forward_all(first, vision, expand, reduce, gains, hidden, out_grad, features, lengths, owners):
    half, single = jnp.bfloat16, jnp.float32
    row_count, width = hidden.shape
    image_count, feature_rows, feature_width = features.shape
    image_count = image_count // 2
    features = features.transpose(1, 0, 2).reshape(-1, feature_width)
    padded = -(-feature_rows // 16) * 16
    cross_rows = image_count * NQ
    part_rows = expand.shape[0] // PARTS
    anywhere = pl.BlockSpec(memory_space=pl.ANY)
    vmem = pl.BlockSpec(memory_space=pltpu.VMEM)
    rows_half = jax.ShapeDtypeStruct((row_count, width), half)
    rows_single = jax.ShapeDtypeStruct((row_count, width), single)
    all_first = (2,) + first.shape[:1] + (4, 2, 2) + first.shape[1:]
    all_feed = (PARTS, 4, 2, 2, part_rows, width)
    gain_shape = (16, width)
    pair_shape = (image_count * padded, 2 * width)
    outs = {
        "result": (rows_single, anywhere),
        "grad_cross": (rows_single, anywhere),
        "part_expand": (jax.ShapeDtypeStruct(all_feed, half), anywhere),
        "part_reduce": (jax.ShapeDtypeStruct(all_feed, half), anywhere),
        "gain_feed": (jax.ShapeDtypeStruct((8, width), single), vmem),
        "stats": (jax.ShapeDtypeStruct((8, width), single), vmem),
        "first": (jax.ShapeDtypeStruct(all_first, half), anywhere),
        "gains": (jax.ShapeDtypeStruct(gain_shape, single), anywhere),
        "normed": (rows_half, anywhere),
        "query": (rows_half, anywhere),
        "key": (rows_half, anywhere),
        "value": (rows_half, anywhere),
        "far_key": (rows_half, anywhere),
        "far_value": (rows_half, anywhere),
        "context": (rows_half, anywhere),
        "after_self": (rows_single, anywhere),
        "cross_query": (jax.ShapeDtypeStruct((cross_rows, width), half), anywhere),
        "cross_context": (rows_half, anywhere),
        "vision": (jax.ShapeDtypeStruct(pair_shape, half), anywhere),
        "images": (jax.ShapeDtypeStruct((image_count * padded, feature_width), half), anywhere),
        "total_self": (jax.ShapeDtypeStruct((row_count // 128, HEADS // 2, 1, 256), single), vmem),
        "total_cross": (jax.ShapeDtypeStruct((image_count, 1, HEADS * NQ), single), vmem),
    }
    halves = (row_count, width)
    scratch = [
        pltpu.VMEM(all_first, half),
        pltpu.VMEM((2, 4, 2, 2) + vision.shape, half),
        pltpu.VMEM((2, feature_width, width), half),
        pltpu.VMEM(all_feed, half),
        pltpu.VMEM(all_feed, half),
        pltpu.VMEM((4, 2, 2) + gains.shape, half),
        pltpu.VMEM(gain_shape, single),
        pltpu.VMEM(halves, single),
        pltpu.VMEM(halves, single),
        pltpu.VMEM((image_count * padded, feature_width), half),
        pltpu.VMEM(pair_shape, half),
    ]
    scratch += [pltpu.VMEM(halves, half)] * 7
    scratch += [
        pltpu.VMEM(halves, single),
        pltpu.VMEM(halves, half),
        pltpu.VMEM(halves, half),
        pltpu.VMEM(halves, single),
        pltpu.VMEM(halves, half),
        pltpu.VMEM(halves, half),
        pltpu.VMEM(halves, single),
        pltpu.VMEM(halves, single),
        pltpu.VMEM((row_count + 256, 256), single),
        pltpu.VMEM((HEADS * NQ, width), half),
        pltpu.VMEM((8, row_count), single),
        pltpu.SemaphoreType.DMA((13 * 10 + 4,)),
        pltpu.SemaphoreType.DMA((13 * 10 + 4,)),
        pltpu.SemaphoreType.DMA((13 + 4 + 16 + 2 * PARTS,)),
    ]
    values = pl.pallas_call(
        forward_kernel,
        out_shape=[shape for shape, _ in outs.values()],
        in_specs=[anywhere] * 8 + [vmem] * 2,
        out_specs=[spec for _, spec in outs.values()],
        scratch_shapes=scratch,
        compiler_params=pltpu.CompilerParams(
            collective_id=2, has_side_effects=True, vmem_limit_bytes=VMEM_LIMIT
        ),
        name="forward_layer",
    )(first, vision, expand, reduce, gains, hidden, out_grad, features, lengths, owners)
    return dict(zip(outs, values))


def add_events(chunks):
    return sorted(
        (number + stage * chunk["gap"] + chunk["begin"], -stage, number)
        for number, chunk in enumerate(chunks)
        for stage in range(4)
    )


def scatter_engine(chunks, send_sem, recv_sem):
    c, z, y, x = coordinates()
    own = {"z": z, "y": y, "x": x}
    events = add_events(chunks)

    def remote(source, target, index, where):
        return pltpu.make_async_remote_copy(
            src_ref=source, dst_ref=target, send_sem=send_sem.at[index],
            recv_sem=recv_sem.at[index], device_id=where, device_id_type=MESH,
        )

    def sends(number, stage, core):
        chunk = chunks[number]
        held, got = chunk["held"], chunk["got"][stage]
        order = ORDERS[chunk["kind"], core][::-1]
        done, axis = order[:stage], order[stage]
        base = (number * 3 + stage) * 3

        def block(there):
            return held.at[
                tuple(there if a == axis else own[a] if a in done else slice(None) for a in "zyx")
            ]

        if axis == "z":
            return [
                remote(
                    block((z + k) % 4), got.at[k - 1], base + k - 1, device(c, (z + k) % 4, y, x)
                )
                for k in (1, 2, 3)
            ]
        where = device(c, z, 1 - y, x) if axis == "y" else device(c, z, y, 1 - x)
        return [remote(block(1 - own[axis]), got, base, where)]

    def absorb(number, stage, core):
        chunk = chunks[number]
        held, got = chunk["held"], chunk["got"][stage]
        order = ORDERS[chunk["kind"], core][::-1]
        done, axis = order[: stage + 1], order[stage]
        free = [a for a in "zyx" if a not in done]
        sizes = [4 if a == "z" else 2 for a in free]
        steps = 1
        for size in sizes:
            steps *= size

        def step(i):
            index = {}
            for a, size in reversed(list(zip(free, sizes))):
                index[a] = i % size
                i = i // size
            at = tuple(index[a] if a in index else own[a] for a in "zyx")
            inner = tuple(index[a] for a in free)
            value = wide(held[at])
            if axis == "z":
                for k in range(3):
                    value = value + wide(got[(k,) + inner])
            else:
                value = value + wide(got[inner] if inner else got[...])
            if stage == 2:
                chunk["total"][...] = value
            else:
                held[at] = to_half(value)

        if steps == 1:
            step(0)
        else:
            loop(steps, step)

    def tick_core(now, core):
        for when, negative, number in events:
            stage = -negative
            if when != now:
                continue
            if stage == 0:
                chunks[number]["ready"]()
            else:
                for copy in sends(number, stage - 1, core):
                    copy.wait_recv()
                absorb(number, stage - 1, core)
            if stage < 3:
                for copy in sends(number, stage, core):
                    copy.start()

    def each_core(step):
        @pl.when(c == 0)
        def _():
            step(0)

        @pl.when(c == 1)
        def _():
            step(1)

    def tick(now):
        each_core(lambda core: tick_core(now, core))

    def wait_sent():
        def step(core):
            for number in range(len(chunks)):
                for stage in range(3):
                    for copy in sends(number, stage, core):
                        copy.wait_send()

        each_core(step)

    return tick, wait_sent, remote, events[-1][0]


def got_shapes(kind, rows, width):
    if kind == "late":
        return [(4, 2, rows, width), (4, rows, width), (3, rows, width)]
    return [(4, 2, rows, width), (3, 2, rows, width), (rows, width)]


FEED_KINDS = ("late", "early", "late", "late", "early", "late", "late", "early")


def backward_kernel(
    feature_rows,
    part_expand, part_reduce, grad_cross_in, hidden_in, after_self_in, first_in, gains_in,
    normed_in, query_in, key_in, value_in, far_key_in, far_value_in, context_in,
    cross_query_in, cross_context_in, vision_in, images_in, lengths, owners, total_self, total_cross, gain_feed,
    hidden_grad_out, part_first, part_vision, sum_expand, sum_reduce, gain_parts,
    held_expand, held_reduce, got_l0, got_l1, got_l2, got_e0, got_e1, got_e2,
    first, pair, images, grad_vision, cross_context, after_self, hidden, grad_after, grad_normed, gain_rows,
    cross_query, grad_context, grad_query, far_grad, bias, mask, sum_far_key, sum_far_value, sum_key, sum_value,
    layout_rows, send_sem, recv_sem, local_sem,
):
    c, z, y, x = coordinates()
    row_count, width = hidden.shape
    image_count = total_cross.shape[0]
    padded = pair.shape[0] // image_count
    feature_width = images.shape[1]
    cross_rows = image_count * NQ
    part_rows = held_expand.shape[-2]
    far_rows, window = row_count, 256
    scale = HD**-0.5
    other = device(1 - c, z, y, x)

    def shelf(buffer, number):
        at = pl.ds(number // 2 * row_count, row_count), pl.ds(number % 2 * width, width)
        return buffer.at[at[0], at[1]]

    names = ("normed", "query", "key", "value", "far_key", "far_value", "context", "grad_context")
    normed, query, key, value, far_key, far_value, context, grad_context_self = (
        shelf(pair, number) for number in range(len(names))
    )
    own_query, own_key, own_value = (shelf(images, 2 * number) for number in range(3))

    loads = {
        "expand": (part_expand, held_expand),
        "reduce": (part_reduce, held_reduce),
        "grad_cross": (grad_cross_in, grad_after),
        "first": (first_in, first),
        "gains": (gains_in, gain_rows),
        "cross_context": (cross_context_in, cross_context),
        "cross_query": (cross_query_in, cross_query),
        "vision": (vision_in, pair),
        "images": (images_in, images),
        "after_self": (after_self_in, after_self),
        "hidden": (hidden_in, hidden),
        "normed": (normed_in, normed),
        "query": (query_in, query),
        "key": (key_in, key),
        "value": (value_in, value),
        "far_key": (far_key_in, far_key),
        "far_value": (far_value_in, far_value),
        "context": (context_in, context),
        "out_hidden": (grad_after, hidden_grad_out),
        "out_first": (first, part_first),
        "out_vision": (grad_vision, part_vision),
    }

    def local(name):
        source, target = loads[name]
        return pltpu.make_async_copy(source, target, local_sem.at[list(loads).index(name)])

    chunks, slots = [], {"late": 0, "early": 0}
    for number, kind in enumerate(FEED_KINDS):
        p = number // 2
        held, total, name = (
            (held_expand, sum_expand, "expand"), (held_reduce, sum_reduce, "reduce")
        )[number % 2]
        slot = slots[kind]
        slots[kind] += 1
        got = (got_l0, got_l1, got_l2) if kind == "late" else (got_e0, got_e1, got_e2)
        chunks.append({
            "held": held.at[p], "got": [part.at[slot] for part in got], "kind": kind,
            "total": total.at[pl.ds(p * part_rows, part_rows)], "gap": 2, "begin": 0,
            "ready": (lambda name=name: local(name).wait()) if p == 0 else (lambda: None),
        })
    tick, wait_sent, remote, last = scatter_engine(chunks, send_sem, recv_sem)

    swap_base = len(chunks) * 9
    own_rows, other_rows = pl.ds(0, cross_rows), pl.ds(cross_rows, cross_rows)
    swaps = {
        "context": (grad_context.at[other_rows], grad_context.at[own_rows]),
        "query": (grad_query.at[own_rows], grad_query.at[other_rows]),
        "far_key": (far_grad.at[0], far_grad.at[0]),
        "far_value": (far_grad.at[1], far_grad.at[1]),
    }

    def swap(name):
        source, target = swaps[name]
        return remote(source, target, swap_base + list(swaps).index(name), other)

    def weight(plane, j):
        return first[plane, j].reshape(width, width)

    def gain(k):
        return gain_rows[pl.ds(k, 1), :]

    def store_weight_grad(plane, j, value):
        first[plane, j] = to_half(value).reshape(first.shape[2:])


    def start():
        gain_parts[...] = jnp.zeros_like(gain_parts)
        gain_parts[pl.ds(2 + c, 1), :] = gain_feed[0:1, :]
        mask[...] = head_mask(NQ, width)
        first_row, image = caption_layout(lengths[...], owners[...], row_count)
        layout_rows[0:1] = first_row
        layout_rows[1:2] = image

    def cross_out_back():
        def step(i):
            rows = span(i, 256)
            part = to_half(grad_after[rows, :])
            grad_query[rows, :] = part
            grad_context[rows, :] = to_half(nt(part, weight(1, 1)))

        loop(row_count // 256, step)
        store_weight_grad(1, 1, tn(cross_context[...], grad_query[...]))
        swap("context").start()

    def cross_back(begin, end):
        def step(i):
            i = i + begin
            rows = pl.ds(pl.multiple_of(i * padded, 16), padded)
            at = span(i, NQ)
            queries = jnp.concatenate([cross_query[at, :]] * HEADS, axis=0) * mask[...]
            grads = jnp.concatenate([grad_context[at, :]] * HEADS, axis=0) * mask[...]
            keys, values = pair[rows, 0:width], pair[rows, width : 2 * width]
            score = nt(keys, queries)
            key_row = lax.broadcasted_iota(jnp.int32, score.shape, 0)
            seen = key_row < feature_rows
            probability = jnp.exp(jnp.where(seen, score, masked_value) - total_cross[i])
            grad_prob = nt(values, grads)
            inner = row_sum(grad_prob * probability)
            grad_score = to_half(probability * (grad_prob - inner))
            full = tn(grad_score, keys)
            pair[rows, 0:width] = to_half(nn(grad_score, queries))
            pair[rows, width : 2 * width] = to_half(nn(to_half(probability), grads))
            grad_query[at, :] = to_half(diagonal(full, NQ) * scale)

        loop(end - begin, step)


    def vision_back(begin, end):
        def step(i):
            i = i + begin
            lanes = span(i, 128)
            both = to_half(tn(images[:, lanes], pair[...]))
            grad_vision[0, lanes, :] = both[:, 0:width]
            grad_vision[1, lanes, :] = both[:, width : 2 * width]

        loop(end - begin, step)

    def cross_in_back():
        def step(i):
            rows = span(i, 128)
            source = after_self[rows, :]
            grad = nt(grad_query[rows, :], weight(1, 2))
            back, part = norm_back(source, gain(1), grad)
            gain_parts[1:2, :] = gain_parts[1:2, :] + part
            grad_after[rows, :] = grad_after[rows, :] + back
            grad_context[rows, :] = to_half(norm_rows(source, gain(1)))

        loop(row_count // 128, step)
        store_weight_grad(1, 2, tn(grad_context[...], grad_query[...]))

    def self_out_back():
        def step(i):
            rows = span(i, 256)
            part = to_half(grad_after[rows, :])
            grad_context[rows, :] = part
            grad_context_self[rows, :] = to_half(nt(part, weight(1, 0)))

        loop(row_count // 256, step)
        store_weight_grad(1, 0, tn(context[...], grad_context[...]))

    def attend_pair_back(rb, t, parts):
        rows, lanes = span(rb, 128), span(t, 128)
        masks = lane_masks(128)
        queries = head_pair(query[rows, lanes], masks)
        grads = head_pair(grad_context_self[rows, lanes], masks)
        kept, inner = [], 0.0
        for keys, values, where in parts:
            score = nt(keys, queries) + wide(where)
            probability = jnp.exp(score - total_self[rb, t])
            grad_prob = nt(values, grads)
            inner = inner + row_sum(grad_prob * probability)
            kept.append((probability, grad_prob))
        result, back = [], 0.0
        for (keys, values, _), (probability, grad_prob) in zip(parts, kept):
            grad_score = to_half(probability * (grad_prob - inner))
            result.append((nn(grad_score, queries), nn(to_half(probability), grads)))
            back = back + tn(grad_score, keys)
        own_query[rows, lanes] = to_half(pair_join(back) * scale)
        return result

    def self_query_back(begin, end):
        def step(i):
            rb, t = i // 6, i % 6
            rows, lanes = span(rb, 128), span(t, 128)
            parts = [(key[rows, lanes], value[rows, lanes], bias[0, 0:128])]
            ((grad_key, grad_value),) = attend_pair_back(rb, t, parts)
            own_key[rows, lanes] = to_half(grad_key)
            own_value[rows, lanes] = to_half(grad_value)

        blocks = row_count // 128

        def shifted_step(i):
            step(i + begin * blocks)

        loop((end - begin) * blocks, shifted_step)

    def text_biases():
        def step(rb):
            rows = span(rb, 128)
            start_row, image = layout_rows[0:1, rows], layout_rows[1:2, rows]
            begin = jnp.maximum(rb - 1, 0) * 128
            far = lax.broadcasted_iota(jnp.int32, (far_rows, 128), 0) // NQ
            far_bias = jnp.where(wide(far) == image, 0.0, masked_value)
            key_row = lax.broadcasted_iota(jnp.int32, (window, 128), 0) + begin
            row = lax.broadcasted_iota(jnp.int32, (window, 128), 1) + rb * 128
            seen = (wide(key_row) >= start_row) & (key_row <= row)
            own_bias = jnp.where(seen, 0.0, masked_value)
            bias[rb, 0:far_rows] = to_half(jnp.concatenate([far_bias, far_bias], axis=1))
            bias[rb, far_rows : far_rows + window] = to_half(
                jnp.concatenate([own_bias, own_bias], axis=1)
            )

        loop(row_count // 128, step)

    def query_biases():
        key_row = lax.broadcasted_iota(jnp.int32, (128, 256), 0) // NQ
        row = (lax.broadcasted_iota(jnp.int32, (128, 256), 1) % 128) // NQ
        bias[0, 0:128] = to_half(jnp.where(key_row == row, 0.0, masked_value))

    def self_text_back(begin, end):
        def outer(t):
            t = t + begin
            lanes = span(t, 128)
            for total in (sum_far_key, sum_far_value, sum_key, sum_value):
                total[...] = jnp.zeros_like(total)

            def inner(rb):
                near = pl.ds(pl.multiple_of(jnp.maximum(rb - 1, 0) * 128, 128), window)
                parts = [
                    (far_key[:, lanes], far_value[:, lanes], bias[rb, 0:far_rows]),
                    (key[near, lanes], value[near, lanes], bias[rb, far_rows : far_rows + window]),
                ]
                far_part, near_part = attend_pair_back(rb, t, parts)
                sum_far_key[...] += far_part[0]
                sum_far_value[...] += far_part[1]
                sum_key[near, :] = sum_key[near, :] + near_part[0]
                sum_value[near, :] = sum_value[near, :] + near_part[1]

            loop(row_count // 128, inner)
            far_grad[0, :, lanes] = to_half(sum_far_key[...])
            far_grad[1, :, lanes] = to_half(sum_far_value[...])
            own_key[:, lanes] = to_half(sum_key[...])
            own_value[:, lanes] = to_half(sum_value[...])

        loop(end - begin, outer)

    def self_in_back():
        def step(i):
            rows = span(i, 256)
            grad = nt(own_query[rows, :], weight(0, 0))
            grad = grad + nt(own_key[rows, :], weight(0, 1))
            grad = grad + nt(own_value[rows, :], weight(0, 2))
            grad_normed[rows, :] = grad

        loop(row_count // 256, step)

    def far_in_back():
        def step(i):
            rows = span(i, 256)
            grad = nt(far_grad[0, rows, :], weight(0, 1)) + nt(far_grad[1, rows, :], weight(0, 2))
            grad_normed[rows, :] = grad_normed[rows, :] + grad

        loop(row_count // 256, step)

    def project_back(far):
        rows = normed[...]
        store_weight_grad(0, 0, tn(rows, own_query[...]))
        grad_key, grad_value = tn(rows, own_key[...]), tn(rows, own_value[...])
        if far:
            grad_key = grad_key + tn(rows, far_grad[0])
            grad_value = grad_value + tn(rows, far_grad[1])
        store_weight_grad(0, 1, grad_key)
        store_weight_grad(0, 2, grad_value)

    def hidden_back():
        def step(i):
            rows = span(i, 128)
            back, part = norm_back(hidden[rows, :], gain(0), grad_normed[rows, :])
            gain_parts[0:1, :] = gain_parts[0:1, :] + part
            grad_after[rows, :] = grad_after[rows, :] + back

        loop(row_count // 128, step)

    for name in ("expand", "reduce", "grad_cross", "first", "cross_context", "vision", "cross_query",
                 "images", "after_self", "gains", "hidden"):
        local(name).start()
    meet(c, z, y, x)
    tick(0)
    start()
    local("grad_cross").wait()
    local("first").wait()
    local("cross_context").wait()

    @pl.when(c == 0)
    def _():
        cross_out_back()

    @pl.when(c == 1)
    def _():
        first[1, 1] = jnp.zeros(first.shape[2:], jnp.bfloat16)
        first[1, 2] = jnp.zeros(first.shape[2:], jnp.bfloat16)
        swap("context").wait_recv()

    tick(1)
    local("vision").wait()
    local("cross_query").wait()
    quarter = image_count // 4
    for k in range(4):
        cross_back(k * quarter, (k + 1) * quarter)
        tick(2 + k)

    @pl.when(c == 1)
    def _():
        swap("query").start()

    local("images").wait()
    tiles = feature_width // 128
    vision_back(0, tiles // 2)
    tick(6)
    vision_back(tiles // 2, tiles)
    local("out_vision").start()
    for name in names[:-1]:
        local(name).start()
    tick(7)
    local("after_self").wait()
    local("gains").wait()

    @pl.when(c == 0)
    def _():
        swap("query").wait_recv()
        swap("context").wait_send()
        cross_in_back()

    for name in names[:-1]:
        local(name).wait()
    self_out_back()
    tick(8)

    @pl.when(c == 0)
    def _():
        query_biases()
        self_query_back(0, 6)

    @pl.when(c == 1)
    def _():
        text_biases()
        self_text_back(0, 2)

    tick(9)

    @pl.when(c == 1)
    def _():
        self_text_back(2, 4)

    tick(10)

    @pl.when(c == 1)
    def _():
        self_text_back(4, 6)
        swap("far_key").start()
        swap("far_value").start()

    tick(11)
    self_in_back()
    tick(12)

    @pl.when(c == 0)
    def _():
        swap("far_key").wait_recv()
        swap("far_value").wait_recv()
        far_in_back()
        project_back(True)

    @pl.when(c == 1)
    def _():
        project_back(False)

    tick(13)
    local("out_first").start()
    local("hidden").wait()
    hidden_back()
    local("out_hidden").start()
    assert last == 13
    wait_sent()

    @pl.when(c == 1)
    def _():
        swap("query").wait_send()
        swap("far_key").wait_send()
        swap("far_value").wait_send()

    for name in ("out_hidden", "out_first", "out_vision"):
        local(name).wait()


def backward_all(kept, hidden, lengths, owners, feature_rows):
    half, single = jnp.bfloat16, jnp.float32
    row_count, width = hidden.shape
    feature_width = kept["images"].shape[1]
    parts = kept["part_expand"].shape
    part_rows = parts[-2]
    cross_rows = kept["cross_query"].shape[0]
    anywhere = pl.BlockSpec(memory_space=pl.ANY)
    vmem = pl.BlockSpec(memory_space=pltpu.VMEM)
    rows_half, rows_single = pltpu.VMEM((row_count, width), half), pltpu.VMEM((row_count, width), single)
    outs = {
        "hidden_grad": (jax.ShapeDtypeStruct((row_count, width), single), anywhere),
        "first": (jax.ShapeDtypeStruct(kept["first"].shape, half), anywhere),
        "vision": (jax.ShapeDtypeStruct((2, feature_width, width), half), anywhere),
        "expand": (jax.ShapeDtypeStruct((PARTS * part_rows, width), single), vmem),
        "reduce": (jax.ShapeDtypeStruct((PARTS * part_rows, width), single), vmem),
        "gains": (jax.ShapeDtypeStruct((8, width), single), vmem),
    }
    scratch = [pltpu.VMEM(parts, half)] * 2
    for kind in ("late", "early"):
        number = FEED_KINDS.count(kind)
        scratch += [
            pltpu.VMEM((number,) + shape, half) for shape in got_shapes(kind, part_rows, width)
        ]
    scratch += [
        pltpu.VMEM(kept["first"].shape, half),
        pltpu.VMEM(kept["vision"].shape, half),
        pltpu.VMEM(kept["images"].shape, half),
        pltpu.VMEM((2, feature_width, width), half),
        rows_half,
        rows_single,
        rows_single,
        rows_single,
        rows_single,
        pltpu.VMEM((16, width), single),
        pltpu.VMEM((cross_rows, width), half),
        rows_half,
        rows_half,
        pltpu.VMEM((2, row_count, width), half),
        pltpu.VMEM((row_count // 128, row_count + 256, 256), half),
        pltpu.VMEM((HEADS * NQ, width), half),
    ]
    scratch += [pltpu.VMEM((row_count, 128), single)] * 4
    scratch += [
        pltpu.VMEM((8, row_count), single),
        pltpu.SemaphoreType.DMA((len(FEED_KINDS) * 9 + 4,)),
        pltpu.SemaphoreType.DMA((len(FEED_KINDS) * 9 + 4,)),
        pltpu.SemaphoreType.DMA((21,)),
    ]
    order = ("part_expand", "part_reduce", "grad_cross", None, "after_self", "first", "gains", "normed",
             "query", "key", "value", "far_key", "far_value", "context", "cross_query", "cross_context",
             "vision", "images")
    values = pl.pallas_call(
        functools.partial(backward_kernel, feature_rows),
        out_shape=[shape for shape, _ in outs.values()],
        in_specs=[anywhere] * len(order) + [vmem] * 5,
        out_specs=[spec for _, spec in outs.values()],
        scratch_shapes=scratch,
        compiler_params=pltpu.CompilerParams(
            collective_id=3, has_side_effects=True, vmem_limit_bytes=VMEM_LIMIT
        ),
        name="backward_layer",
    )(
        *[hidden if name is None else kept[name] for name in order],
        lengths, owners, kept["total_self"], kept["total_cross"], kept["gain_feed"],
    )
    return dict(zip(outs, values))


SHARED_KINDS = ("late", "early", "late", "late")


def reduce_kernel(
    part_first, part_vision, sum_expand, sum_reduce, part_gains, part_stats,
    sum_first, sum_vision, sum_gains, totals,
    held_first, held_vision, own_vision, pair_first, pair_vision,
    got_l0, got_l1, got_l2, got_e0, got_e1, got_e2, got_v0, got_v1, got_v2,
    gains_now, gains_got, gains_z, stats_now, stats_got, stats_z, send_sem, recv_sem, local_sem,
):
    c, z, y, x = coordinates()
    other = device(1 - c, z, y, x)
    rows_vision = held_vision.shape[-2]
    chunks, slots = [], {"late": 0, "early": 0}

    def load(k):
        if k == 3:
            return pltpu.make_async_copy(part_vision.at[c], own_vision, local_sem.at[k])
        return pltpu.make_async_copy(part_first.at[c, k], held_first.at[k], local_sem.at[k])

    def pair_copy(k):
        if k == 3:
            return remote(part_vision.at[1 - c], pair_vision, pair_base + k, other)
        return remote(part_first.at[1 - c, k], pair_first.at[k], pair_base + k, other)

    def ready_first(j):
        load(j).wait()
        pair_copy(j).wait()

        def step(i):
            at = (j, i // 4, (i // 2) % 2, i % 2)
            held_first[at] = to_half(wide(held_first[at]) + wide(pair_first[at]))

        loop(16, step)

    def ready_vision():
        load(3).wait()
        pair_copy(3).wait()

        def step(i):
            rows = span(i, 2 * rows_vision)
            value = wide(own_vision[rows, :]) + wide(pair_vision[rows, :])
            held_vision[i // 2, i % 2, 0] = to_half(value[:rows_vision])
            held_vision[i // 2, i % 2, 1] = to_half(value[rows_vision:])

        loop(8, step)

    for j in range(3):
        kind = SHARED_KINDS[j]
        slot = slots[kind]
        slots[kind] += 1
        got = (got_l0, got_l1, got_l2) if kind == "late" else (got_e0, got_e1, got_e2)
        chunks.append({
            "held": held_first.at[j], "got": [part.at[slot] for part in got], "kind": kind,
            "total": sum_first.at[c, j], "gap": 2, "begin": 0, "ready": lambda j=j: ready_first(j),
        })
    chunks.append({
        "held": held_vision, "got": [got_v0, got_v1, got_v2], "kind": SHARED_KINDS[3],
        "total": sum_vision.at[c], "gap": 2, "begin": 0, "ready": ready_vision,
    })
    tick, wait_sent, remote, last = scatter_engine(chunks, send_sem, recv_sem)
    pair_base = len(chunks) * 9
    gains_base, stats_base = pair_base + 4, pair_base + 10

    def small(stage, now, got, got_z, base):
        if stage < 3:
            where = (other, device(c, z, 1 - y, x), device(c, z, y, 1 - x))[stage]
            return [remote(now.at[stage], got.at[stage], base + stage, where)]
        return [
            remote(now.at[3], got_z.at[z], base + 2 + k, device(c, (z + k) % 4, y, x))
            for k in (1, 2, 3)
        ]

    def small_step(stage, now, got, got_z, base):
        if stage > 0:
            for copy in small(stage - 1, now, got, got_z, base):
                copy.wait()
            if stage < 4:
                now[stage] = now[stage - 1] + got[stage - 1]
            else:
                got_z[z] = now[3]
                now[4] = (got_z[0] + got_z[1]) + (got_z[2] + got_z[3])
        if stage < 4:
            for copy in small(stage, now, got, got_z, base):
                copy.start()

    def folded(values):
        total = values[:, 0:128]
        for k in range(1, values.shape[1] // 128):
            total = total + values[:, k * 128 : (k + 1) * 128]
        return total

    def squares(block):
        return jnp.sum((block * block).reshape(-1, 8, block.shape[1]), axis=0)

    for k in range(4):
        load(k).start()
    meet(c, z, y, x)
    for k in range(4):
        pair_copy(k).start()
    gains_now[0] = part_gains[...]
    for now in range(last + 1):
        if now < 5:
            small_step(now, gains_now, gains_got, gains_z, gains_base)
        tick(now)
    back = [
        remote(sum_first.at[c], sum_first.at[c], stats_base + 6, other),
        remote(sum_vision.at[c], sum_vision.at[c], stats_base + 7, other),
    ]
    for copy in back:
        copy.start()
    gains = gains_now[4]
    sum_gains[...] = gains
    mass = jnp.where((c == 0) & (z + y + x == 0), 1.0, 0.0) * (gains * gains)
    for j in range(3):
        mass = mass + squares(sum_first[c, j])
    mass = mass + squares(sum_vision[c])
    mass = mass + squares(sum_expand[...]) + squares(sum_reduce[...])
    stats_now[0, 0:8] = folded(mass)
    stats_now[0, 8:16] = folded(part_stats[...])
    for stage in range(5):
        small_step(stage, stats_now, stats_got, stats_z, stats_base)
    totals[...] = stats_now[4]
    for copy in back:
        copy.wait()
    wait_sent()


def reduce_all(part_first, part_vision, sum_expand, sum_reduce, part_gains, part_stats):
    half, single = jnp.bfloat16, jnp.float32
    rows_first, width = part_first.shape[-2:]
    feature_width = part_vision.shape[1]
    rows_vision = feature_width // 16
    anywhere = pl.BlockSpec(memory_space=pl.ANY)
    vmem = pl.BlockSpec(memory_space=pltpu.VMEM)
    scratch = [
        pltpu.VMEM(part_first.shape[1:], half),
        pltpu.VMEM((4, 2, 2, rows_vision, width), half),
        pltpu.VMEM((feature_width, width), half),
        pltpu.VMEM(part_first.shape[1:], half),
        pltpu.VMEM((feature_width, width), half),
    ]
    for kind in ("late", "early"):
        number = SHARED_KINDS[:3].count(kind)
        scratch += [
            pltpu.VMEM((number,) + shape, half) for shape in got_shapes(kind, rows_first, width)
        ]
    scratch += [pltpu.VMEM(shape, half) for shape in got_shapes(SHARED_KINDS[3], rows_vision, width)]
    for shape in (part_gains.shape, (16, 128)):
        scratch += [pltpu.VMEM((number,) + shape, single) for number in (5, 3, 4)]
    scratch += [
        pltpu.SemaphoreType.DMA((4 * 9 + 4 + 14,)),
        pltpu.SemaphoreType.DMA((4 * 9 + 4 + 14,)),
        pltpu.SemaphoreType.DMA((4,)),
    ]
    return pl.pallas_call(
        reduce_kernel,
        out_shape=[
            jax.ShapeDtypeStruct((2, 3, rows_first, width), single),
            jax.ShapeDtypeStruct((2, rows_vision, width), single),
            jax.ShapeDtypeStruct(part_gains.shape, single),
            jax.ShapeDtypeStruct((16, 128), single),
        ],
        in_specs=[anywhere] * 2 + [vmem] * 4,
        out_specs=[vmem] * 4,
        scratch_shapes=scratch,
        compiler_params=pltpu.CompilerParams(
            collective_id=4, has_side_effects=True, vmem_limit_bytes=VMEM_LIMIT
        ),
        name="reduce_grads",
    )(part_first, part_vision, sum_expand, sum_reduce, part_gains, part_stats)


def general_grads(
    hidden,
    features,
    caption_lengths,
    caption_image,
    out_grad,
    attn_project,
    attn_output,
    cross_query,
    cross_vision,
    feed_expand,
    feed_reduce,
    norm_gains,
):
    stream = lax.axis_index("stream")
    full_project, full_output, full_query, full_vision, full_expand, full_reduce, full_gains = (
        lax.all_gather(to_half(attn_project), "dp", axis=1, tiled=True),
        lax.all_gather(to_half(attn_output), "dp", axis=1, tiled=True),
        lax.all_gather(to_half(cross_query), "dp", axis=0, tiled=True),
        lax.all_gather(to_half(cross_vision), "dp", axis=1, tiled=True),
        lax.all_gather(to_half(feed_expand), "dp", axis=1, tiled=True),
        lax.all_gather(to_half(feed_reduce), "dp", axis=1, tiled=True),
        lax.all_gather(to_half(norm_gains), "dp", axis=1, tiled=True),
    )
    gain_rows = full_gains.astype(jnp.float32)
    gain_self = gain_rows[0]
    gain_cross = gain_rows[1]
    gain_feed = lax.dynamic_index_in_dim(gain_rows, 2 + stream, 0, keepdims=False)
    source = hidden[0]
    row_count = source.shape[0]
    feature_width = source.shape[1]
    image_count = features.shape[0]
    query_allow, text_allow = layout(caption_lengths[0], caption_image[0], row_count, NQ)
    normed_self = to_half(norm_rows(source, gain_self))
    query_half = to_half(product(normed_self, full_project[0]))
    key_half = to_half(product(normed_self, full_project[1]))
    value_half = to_half(product(normed_self, full_project[2]))
    empty_half = jnp.zeros((row_count, feature_width), jnp.bfloat16)
    far_key, far_value = shifted((key_half, value_half), "stream", 1)
    text_keys = jnp.concatenate([far_key, key_half], axis=0)
    text_values = jnp.concatenate([far_value, value_half], axis=0)

    def self_query():
        return attend(query_half[None], key_half[None], value_half[None], query_allow[None])

    def self_text():
        return attend(query_half[None], text_keys[None], text_values[None], text_allow[None])

    context_self, total_self = lax.cond(stream == 0, self_query, self_text)
    context_half = to_half(context_self[0])
    branch_self = product(context_half, full_output[0])
    after_self = source + branch_self

    def cross_on():
        normed_cross = to_half(norm_rows(after_self, gain_cross))
        cross_half = to_half(product(normed_cross, full_query))
        vision_pair = project_vision(features, full_vision)
        context_cross, total_cross = attend(
            cross_half.reshape(image_count, NQ, feature_width), vision_pair[0], vision_pair[1], None
        )
        context_cross_half = to_half(context_cross.reshape(row_count, feature_width))
        branch = product(context_cross_half, full_output[1])
        return (branch, total_cross, vision_pair, normed_cross, cross_half, context_cross_half)

    def cross_off():
        return (
            jnp.zeros((row_count, feature_width), jnp.float32),
            jnp.zeros((image_count, HEADS, NQ), jnp.float32),
            jnp.zeros((2, image_count, features.shape[1], feature_width), jnp.bfloat16),
            empty_half,
            empty_half,
            empty_half,
        )

    branch_cross, total_cross, vision_pair, normed_cross, cross_half, context_cross_half = lax.cond(
        stream == 0, cross_on, cross_off
    )
    after_cross = after_self + branch_cross
    normed_feed = to_half(norm_rows(after_cross, gain_feed))
    before = right_product(normed_feed, full_expand[0])
    active_half = to_half(exact_gelu(before))
    branch_feed = product(active_half, full_reduce[0])
    result = after_cross + branch_feed
    grad_result = out_grad[0]
    grad_feed_half = to_half(grad_result)
    grad_reduce = left_product(active_half, grad_feed_half)
    grad_active = right_product(grad_feed_half, full_reduce[0])
    grad_before = to_half(jax.vjp(exact_gelu, before)[1](grad_active)[0])
    grad_expand = left_product(grad_before, normed_feed)
    grad_normed_feed = product(grad_before, full_expand[0])
    feed_in, grad_gain_feed = jax.vjp(norm_rows, after_cross, gain_feed)[1](grad_normed_feed)
    grad_cross = grad_result + feed_in

    def cross_back_on():
        grad_branch_half = to_half(grad_cross)
        grad_out_cross = left_product(context_cross_half, grad_branch_half)
        grad_context = to_half(right_product(grad_branch_half, full_output[1]))
        grad_cq, grad_ck, grad_cv = attend_back(
            cross_half.reshape(image_count, NQ, feature_width),
            vision_pair[0],
            vision_pair[1],
            None,
            total_cross,
            grad_context.reshape(image_count, NQ, feature_width),
        )
        grad_cq_half = to_half(grad_cq.reshape(row_count, feature_width))
        grad_pair = to_half(jnp.stack([grad_ck, grad_cv]))
        grad_cross_weight = left_product(normed_cross, grad_cq_half)
        grad_normed_cross = right_product(grad_cq_half, full_query)
        cross_in, grad_gain_cross = jax.vjp(norm_rows, after_self, gain_cross)[1](grad_normed_cross)
        vision_term = vision_grad(features, grad_pair)
        return (cross_in, grad_gain_cross, grad_out_cross, grad_cross_weight, vision_term)

    def cross_back_off():
        square_zero = jnp.zeros((feature_width, feature_width), jnp.float32)
        vision_term = jnp.zeros((2, features.shape[2], feature_width), jnp.float32)
        return (
            jnp.zeros((row_count, feature_width), jnp.float32),
            jnp.zeros((feature_width,), jnp.float32),
            square_zero,
            square_zero,
            vision_term,
        )

    cross_in, grad_gain_cross, grad_out_cross, grad_cross_weight, vision_term = lax.cond(
        stream == 0, cross_back_on, cross_back_off
    )
    grad_after_self = grad_cross + cross_in
    grad_branch_half = to_half(grad_after_self)
    grad_out_self = left_product(context_half, grad_branch_half)
    grad_context_self = to_half(right_product(grad_branch_half, full_output[0]))

    def self_back_query():
        grad_sq, grad_sk, grad_sv = attend_back(
            query_half[None],
            key_half[None],
            value_half[None],
            query_allow[None],
            total_self,
            grad_context_self[None],
        )
        empty_rows = jnp.zeros((row_count, feature_width), jnp.float32)
        return (grad_sq[0], grad_sk[0], grad_sv[0], empty_rows, empty_rows)

    def self_back_text():
        grad_sq, grad_sk, grad_sv = attend_back(
            query_half[None],
            text_keys[None],
            text_values[None],
            text_allow[None],
            total_self,
            grad_context_self[None],
        )
        return (
            grad_sq[0],
            grad_sk[0, row_count:],
            grad_sv[0, row_count:],
            grad_sk[0, :row_count],
            grad_sv[0, :row_count],
        )

    own_query, own_key, own_value, far_grad_key, far_grad_value = lax.cond(
        stream == 0, self_back_query, self_back_text
    )
    own_query = to_half(own_query)
    own_key = to_half(own_key)
    own_value = to_half(own_value)
    far_key_half = to_half(far_grad_key)
    far_value_half = to_half(far_grad_value)
    grad_normed = (
        right_product(own_query, full_project[0])
        + right_product(own_key, full_project[1])
        + right_product(own_value, full_project[2])
    )
    grad_key_weight = left_product(normed_self, own_key)
    grad_value_weight = left_product(normed_self, own_value)
    back_key, back_value = shifted((far_key_half, far_value_half), "stream", -1)
    grad_normed = (
        grad_normed
        + right_product(back_key, full_project[1])
        + right_product(back_value, full_project[2])
    )
    grad_key_weight = grad_key_weight + left_product(normed_self, back_key)
    grad_value_weight = grad_value_weight + left_product(normed_self, back_value)
    grad_project = jnp.stack(
        [left_product(normed_self, own_query), grad_key_weight, grad_value_weight]
    )
    source_in, grad_gain_self = jax.vjp(norm_rows, source, gain_self)[1](grad_normed)
    hidden_grad = grad_after_self + source_in
    zero_row = jnp.zeros_like(grad_gain_feed)
    gain_grads = jnp.stack(
        [
            grad_gain_self,
            grad_gain_cross,
            jnp.where(stream == 0, grad_gain_feed, zero_row),
            jnp.where(stream == 1, grad_gain_feed, zero_row),
        ]
    )
    shared_grads = (
        grad_project,
        jnp.stack([grad_out_self, grad_out_cross]),
        grad_cross_weight,
        vision_term,
        gain_grads,
    )
    (
        parts_project,
        parts_output,
        parts_query,
        parts_vision,
        parts_expand,
        parts_reduce,
        parts_gains,
    ) = (
        lax.psum_scatter(shared_grads[0], "dp", scatter_dimension=1, tiled=True),
        lax.psum_scatter(shared_grads[1], "dp", scatter_dimension=1, tiled=True),
        lax.psum_scatter(shared_grads[2], "dp", scatter_dimension=0, tiled=True),
        lax.psum_scatter(shared_grads[3], "dp", scatter_dimension=1, tiled=True),
        lax.psum_scatter(grad_expand[None], "dp", scatter_dimension=1, tiled=True),
        lax.psum_scatter(grad_reduce[None], "dp", scatter_dimension=1, tiled=True),
        lax.psum_scatter(shared_grads[4], "dp", scatter_dimension=1, tiled=True),
    )
    sum_project, sum_output, sum_query, sum_vision, sum_gains = (
        lax.psum(parts_project.astype(jnp.bfloat16), "stream").astype(jnp.float32),
        lax.psum(parts_output.astype(jnp.bfloat16), "stream").astype(jnp.float32),
        lax.psum(parts_query.astype(jnp.bfloat16), "stream").astype(jnp.float32),
        lax.psum(parts_vision.astype(jnp.bfloat16), "stream").astype(jnp.float32),
        lax.psum(parts_gains.astype(jnp.bfloat16), "stream").astype(jnp.float32),
    )
    shared_square = (
        jnp.sum(sum_project * sum_project)
        + jnp.sum(sum_output * sum_output)
        + jnp.sum(sum_query * sum_query)
        + jnp.sum(sum_vision * sum_vision)
        + jnp.sum(sum_gains * sum_gains)
    )
    local_square = (
        0.5 * shared_square
        + jnp.sum(parts_expand * parts_expand)
        + jnp.sum(parts_reduce * parts_reduce)
    )
    stat_row = jnp.stack(
        [
            square_rows(source),
            square_rows(branch_self),
            square_rows(branch_feed),
            square_rows(result),
        ]
    )
    stat_local = jnp.where(
        jnp.arange(2, dtype=jnp.int32)[:, None] == stream, stat_row[None, :], 0.0
    )
    total_square, stat_sums = lax.psum((local_square, stat_local), ("stream", "dp"))
    return (
        result, hidden_grad, total_square, stat_sums, parts_expand, parts_reduce,
        (sum_project, sum_output, sum_query, sum_vision, sum_gains),
    )


def direct_grads(
    hidden,
    features,
    caption_lengths,
    caption_image,
    out_grad,
    attn_project,
    attn_output,
    cross_query,
    cross_vision,
    feed_expand,
    feed_reduce,
    norm_gains,
):
    stream = lax.axis_index("stream")
    width = attn_project.shape[-1]
    row_count = hidden.shape[1]
    output_half, query_half = to_half(attn_output), to_half(cross_query)
    first = jnp.where(
        stream == 0, to_half(attn_project), jnp.concatenate([output_half, query_half[None]], axis=0)
    )
    vision = to_half(lax.dynamic_index_in_dim(cross_vision, stream, 0, keepdims=False))
    gains = jnp.pad(to_half(norm_gains), ((0, 12), (0, 128 - norm_gains.shape[1])))
    kept = forward_all(
        first, vision, to_half(feed_expand[0]), to_half(feed_reduce[0]), gains,
        hidden[0], out_grad[0], features, caption_lengths, caption_image,
    )
    back = backward_all(kept, hidden[0], caption_lengths, caption_image, features.shape[1])
    sum_first, sum_vision, gain_sums, totals = reduce_all(
        back["first"], back["vision"], back["expand"], back["reduce"], back["gains"], kept["stats"]
    )
    own_gains = norm_gains.shape[1]
    begin = lax.axis_index("dp") * own_gains
    sum_gains = lax.dynamic_slice_in_dim(gain_sums[:4], begin, own_gains, axis=1)
    total_square = jnp.sum(totals[:8])
    stat_sums = jnp.sum(totals[8:], axis=1).reshape(2, 4) / width
    return (
        kept["result"], back["hidden_grad"], total_square, stat_sums,
        back["expand"][None], back["reduce"][None],
        (sum_first[0], sum_first[1, :2], sum_first[1, 2], sum_vision, sum_gains),
    )


def body(
    hidden,
    features,
    caption_lengths,
    caption_image,
    out_grad,
    attn_project,
    attn_output,
    cross_query,
    cross_vision,
    feed_expand,
    feed_reduce,
    norm_gains,
    first_project,
    second_project,
    first_output,
    second_output,
    first_query,
    second_query,
    first_vision,
    second_vision,
    first_expand,
    second_expand,
    first_reduce,
    second_reduce,
    first_gains,
    second_gains,
):
    grads = direct_grads if lax.axis_size("dp") == 16 else general_grads
    row_count = hidden.shape[1]
    result, hidden_grad, total_square, stat_sums, parts_expand, parts_reduce, shared = grads(
        hidden, features, caption_lengths, caption_image, out_grad, attn_project,
        attn_output, cross_query, cross_vision, feed_expand, feed_reduce, norm_gains,
    )
    sum_project, sum_output, sum_query, sum_vision, sum_gains = shared
    grad_norm = jnp.sqrt(total_square)
    rms_values = jnp.sqrt(stat_sums / (row_count * lax.axis_size("dp")))
    factor = clip_norm / jnp.maximum(grad_norm, clip_norm)
    clipped_gains = sum_gains * factor
    fresh_expand, mean_expand, square_expand = adam_step(
        feed_expand, parts_expand, first_expand, second_expand, factor, rate_matrix, decay_rate
    )
    fresh_reduce, mean_reduce, square_reduce = adam_step(
        feed_reduce, parts_reduce, first_reduce, second_reduce, factor, rate_matrix, decay_rate
    )
    weights_shared = (attn_project, attn_output, cross_query, cross_vision, norm_gains)
    firsts_shared = (first_project, first_output, first_query, first_vision, first_gains)
    seconds_shared = (second_project, second_output, second_query, second_vision, second_gains)
    summed_shared = (sum_project, sum_output, sum_query, sum_vision, sum_gains)
    updated = []
    for index in range(5):
        rate = rate_gains if index == 4 else rate_matrix
        decay = 0.0 if index == 4 else decay_rate
        weight = weights_shared[index]
        first = firsts_shared[index]
        second = seconds_shared[index]
        updated.append(adam_step(weight, summed_shared[index], first, second, factor, rate, decay))
    fresh_project, mean_project, square_project = updated[0]
    fresh_output, mean_output, square_output = updated[1]
    fresh_query, mean_query, square_query = updated[2]
    fresh_vision, mean_vision, square_vision = updated[3]
    fresh_gains, mean_gains, square_gains = updated[4]
    return (
        result[None],
        hidden_grad[None],
        grad_norm,
        rms_values,
        fresh_project,
        mean_project,
        square_project,
        fresh_output,
        mean_output,
        square_output,
        fresh_query,
        mean_query,
        square_query,
        fresh_vision,
        mean_vision,
        square_vision,
        fresh_expand,
        mean_expand,
        square_expand,
        fresh_reduce,
        mean_reduce,
        square_reduce,
        fresh_gains,
        mean_gains,
        square_gains,
        clipped_gains,
        to_half(fresh_project),
        to_half(fresh_output),
        to_half(fresh_query),
        to_half(fresh_vision),
        to_half(fresh_expand),
        to_half(fresh_reduce),
    )


def solution(mesh):
    return jax.shard_map(
        body,
        mesh=mesh,
        in_specs=(
            P("stream", "dp", None),
            P("dp", None, None),
            P("dp", None),
            P("dp", None),
            P("stream", "dp", None),
            P(None, "dp", None),
            P(None, "dp", None),
            P("dp", None),
            P(None, "dp", None),
            P("stream", "dp", None),
            P("stream", "dp", None),
            P(None, "dp"),
            P(None, "dp", None),
            P(None, "dp", None),
            P(None, "dp", None),
            P(None, "dp", None),
            P("dp", None),
            P("dp", None),
            P(None, "dp", None),
            P(None, "dp", None),
            P("stream", "dp", None),
            P("stream", "dp", None),
            P("stream", "dp", None),
            P("stream", "dp", None),
            P(None, "dp"),
            P(None, "dp"),
        ),
        out_specs=(
            P("stream", "dp", None),
            P("stream", "dp", None),
            P(),
            P(),
            P(None, "dp", None),
            P(None, "dp", None),
            P(None, "dp", None),
            P(None, "dp", None),
            P(None, "dp", None),
            P(None, "dp", None),
            P("dp", None),
            P("dp", None),
            P("dp", None),
            P(None, "dp", None),
            P(None, "dp", None),
            P(None, "dp", None),
            P("stream", "dp", None),
            P("stream", "dp", None),
            P("stream", "dp", None),
            P("stream", "dp", None),
            P("stream", "dp", None),
            P("stream", "dp", None),
            P(None, "dp"),
            P(None, "dp"),
            P(None, "dp"),
            P(None, "dp"),
            P(None, "dp", None),
            P(None, "dp", None),
            P("dp", None),
            P(None, "dp", None),
            P("stream", "dp", None),
            P("stream", "dp", None),
        ),
        check_vma=False,
    )
```

```python
import functools

import jax
import jax.numpy as jnp
from jax import lax
from jax.experimental import pallas as pl
from jax.experimental.pallas import tpu as pltpu
from jax.sharding import PartitionSpec as P

HEADS = 12
HD = 64
NQ = 32
STEP = 10


epsilon = 1e-06
masked_value = -1e30
beta_first = 0.9
beta_second = 0.999
rate_matrix = 0.05
rate_gains = 1.0
decay_rate = 0.01
adam_floor = 1e-08
clip_norm = 1.0


def shifted(block, axis, distance):
    devices = range(lax.axis_size(axis))
    route = [(i - distance, i) for i in devices if i - distance in devices]
    return lax.ppermute(block, axis, route)


def to_half(values):
    return values.astype(jnp.bfloat16)


def product(left, right):
    return jnp.dot(left, right, preferred_element_type=jnp.float32)


def left_product(left, right):
    return lax.dot_general(
        left, right, (((0,), (0,)), ((), ())), preferred_element_type=jnp.float32
    )


def right_product(left, right):
    return lax.dot_general(
        left, right, (((1,), (1,)), ((), ())), preferred_element_type=jnp.float32
    )


def norm_rows(values, gain):
    return values * lax.rsqrt(jnp.mean(values * values, axis=-1, keepdims=True) + epsilon) * gain


def exact_gelu(values):
    return jax.nn.gelu(values, approximate=False)


def square_rows(values):
    return jnp.sum(jnp.mean(values * values, axis=-1))


def layout(lengths, owners, row_count, per_image):
    caption_ends = jnp.cumsum(lengths)
    caption_starts = caption_ends - lengths
    row_index = jnp.arange(row_count, dtype=jnp.int32)
    inside = (row_index[:, None] >= caption_starts[None, :]) & (
        row_index[:, None] < caption_ends[None, :]
    )
    caption = jnp.sum(
        jnp.where(inside, jnp.arange(lengths.shape[0], dtype=jnp.int32)[None, :], 0), axis=1
    )
    text_image = jnp.sum(jnp.where(inside, owners[None, :], 0), axis=1)
    query_image = row_index // per_image
    query_allow = query_image[:, None] == query_image[None, :]
    own_caption = (caption[:, None] == caption[None, :]) & (
        row_index[None, :] <= row_index[:, None]
    )
    text_allow = jnp.concatenate([text_image[:, None] == query_image[None, :], own_caption], axis=1)
    return (query_allow, text_allow)


def attention_scores(query_rows, key_rows, allowed):
    batch_count, query_count, width_all = query_rows.shape
    query_heads = query_rows.reshape(batch_count, query_count, HEADS, HD)
    key_heads = key_rows.reshape(batch_count, key_rows.shape[1], HEADS, HD)
    scores = jnp.einsum(
        "bqhd,bkhd->bhqk", query_heads, key_heads, preferred_element_type=jnp.float32
    ) * HD ** (-0.5)
    if allowed is not None:
        scores = jnp.where(allowed[:, None], scores, masked_value)
    return (scores, query_heads, key_heads)


def attend(query_rows, key_rows, value_rows, allowed):
    scores, query_heads, key_heads = attention_scores(query_rows, key_rows, allowed)
    value_heads = value_rows.reshape(key_heads.shape)
    row_max = jnp.max(scores, axis=-1, keepdims=True)
    weights = jnp.exp(scores - row_max)
    denominator = jnp.sum(weights, axis=-1, keepdims=True)
    probability = to_half(weights / denominator)
    context = jnp.einsum(
        "bhqk,bkhd->bqhd", probability, value_heads, preferred_element_type=jnp.float32
    )
    return (context.reshape(query_rows.shape), (row_max + jnp.log(denominator))[..., 0])


def attend_back(query_rows, key_rows, value_rows, allowed, log_total, grad_context):
    scores, query_heads, key_heads = attention_scores(query_rows, key_rows, allowed)
    value_heads = value_rows.reshape(key_heads.shape)
    probability = jnp.exp(scores - log_total[..., None])
    grad_heads = grad_context.reshape(query_heads.shape)
    grad_prob = jnp.einsum(
        "bqhd,bkhd->bhqk", grad_heads, value_heads, preferred_element_type=jnp.float32
    )
    grad_value = jnp.einsum(
        "bhqk,bqhd->bkhd", to_half(probability), grad_heads, preferred_element_type=jnp.float32
    )
    grad_score = to_half(
        probability * (grad_prob - jnp.sum(grad_prob * probability, axis=-1, keepdims=True))
    )
    grad_query = jnp.einsum(
        "bhqk,bkhd->bqhd", grad_score, key_heads, preferred_element_type=jnp.float32
    ) * HD ** (-0.5)
    grad_key = jnp.einsum(
        "bhqk,bqhd->bkhd", grad_score, query_heads, preferred_element_type=jnp.float32
    ) * HD ** (-0.5)
    return (
        grad_query.reshape(query_rows.shape),
        grad_key.reshape(key_rows.shape),
        grad_value.reshape(value_rows.shape),
    )


def project_vision(feature_block, vision_weights):
    return to_half(
        jnp.einsum(
            "inv,kvd->kind", feature_block, vision_weights, preferred_element_type=jnp.float32
        )
    )


def vision_grad(feature_block, grad_pair):
    return jnp.einsum("inv,kind->kvd", feature_block, grad_pair, preferred_element_type=jnp.float32)


def adam_step(weight, gradient, first, second, factor, rate, decay):
    clipped = gradient * factor
    mean_new = beta_first * first + (1.0 - beta_first) * clipped
    square_new = beta_second * second + (1.0 - beta_second) * clipped * clipped
    corrected_mean = mean_new / (1.0 - beta_first**STEP)
    corrected_square = square_new / (1.0 - beta_second**STEP)
    fresh = weight - rate * (
        corrected_mean / (jnp.sqrt(corrected_square) + adam_floor) + decay * weight
    )
    return (fresh, mean_new, square_new)


MESH = pl.DeviceIdType.MESH
VMEM_LIMIT = 62 * 2**20


def coordinates():
    c = lax.axis_index("stream")
    d = lax.axis_index("dp")
    return c, d // 4, (d // 2) % 2, d % 2


def device(c, z, y, x):
    return (c, z * 4 + y * 2 + x)


def meet(c, z, y, x):
    barrier = pltpu.get_barrier_semaphore()
    others = [device(1 - c, z, y, x), device(c, z, 1 - y, x), device(c, z, y, 1 - x)]
    others += [device(c, (z + k) % 4, y, x) for k in (1, 2, 3)]
    for other in others:
        pl.semaphore_signal(barrier, inc=1, device_id=other, device_id_type=MESH)
    pl.semaphore_wait(barrier, len(others))


ORDERS = {
    ("late", 0): ("z", "y", "x"),
    ("late", 1): ("z", "x", "y"),
    ("early", 0): ("x", "z", "y"),
    ("early", 1): ("y", "z", "x"),
    ("feed", 0): ("z", "o"),
    ("feed", 1): ("z", "o"),
}


PARTS = 2
PLANES = {
    "query": (0, 0), "key": (0, 1), "cross_output": (0, 2),
    "value": (1, 0), "self_output": (1, 1), "cross_query": (1, 2),
}


def wide(block):
    return block.astype(jnp.float32)


def nn(left, right):
    return lax.dot_general(
        left, right, (((1,), (0,)), ((), ())), preferred_element_type=jnp.float32
    )


def nt(left, right):
    return lax.dot_general(
        left, right, (((1,), (1,)), ((), ())), preferred_element_type=jnp.float32
    )


def tn(left, right):
    return lax.dot_general(
        left, right, (((0,), (0,)), ((), ())), preferred_element_type=jnp.float32
    )


def span(index, size):
    return pl.ds(pl.multiple_of(index * size, size), size)


def loop(count, step):
    def body(index, carry):
        step(index)
        return carry

    lax.fori_loop(0, count, body, 0)


def row_sum(values):
    return jnp.sum(values, axis=0, keepdims=True)


def norm_back(values, gain, grad):
    scale = lax.rsqrt(jnp.mean(values * values, axis=-1, keepdims=True) + epsilon)
    unit = values * scale
    grad_unit = grad * gain
    mean = jnp.mean(grad_unit * unit, axis=-1, keepdims=True)
    return scale * (grad_unit - unit * mean), row_sum(grad * unit)


def lane_masks(rows):
    lane = lax.broadcasted_iota(jnp.int32, (rows, 2 * HD), 1)
    left = jnp.where(lane < HD, 1.0, 0.0)
    return to_half(left), to_half(1.0 - left)


def head_pair(block, masks):
    return jnp.concatenate([block * masks[0], block * masks[1]], axis=0)


def pair_join(both):
    rows = both.shape[0] // 2
    lane = lax.broadcasted_iota(jnp.int32, (rows, 2 * HD), 1)
    return jnp.where(lane < HD, both[:rows], both[rows:])


def diagonal(full, rows):
    lane = lax.broadcasted_iota(jnp.int32, (rows, 2 * HD), 1)
    tiles = []
    for t in range(HEADS // 2):
        tile = full[:, t * 2 * HD : (t + 1) * 2 * HD]
        left = tile[2 * t * rows : (2 * t + 1) * rows]
        right = tile[(2 * t + 1) * rows : (2 * t + 2) * rows]
        tiles.append(jnp.where(lane < HD, left, right))
    return jnp.concatenate(tiles, axis=1)


def head_mask(rows, width):
    row = lax.broadcasted_iota(jnp.int32, (HEADS * rows, width), 0) // rows
    lane = lax.broadcasted_iota(jnp.int32, (HEADS * rows, width), 1) // HD
    return to_half(jnp.where(row == lane, 1.0, 0.0))


def caption_layout(lengths, owners, row_count):
    count = lengths.shape[1]
    size = wide(lengths)
    owner = wide(owners)
    sub = lax.broadcasted_iota(jnp.int32, (count, count), 0)
    lane = lax.broadcasted_iota(jnp.int32, (count, count), 1)
    starts = jnp.sum(jnp.where(lane < sub, size, 0.0), axis=1, keepdims=True)
    owner_down = jnp.sum(jnp.where(lane == sub, owner, 0.0), axis=1, keepdims=True)
    row = wide(lax.broadcasted_iota(jnp.int32, (count, row_count), 1))
    begun = starts <= row
    start = jnp.max(jnp.where(begun, starts, 0.0), axis=0, keepdims=True)
    image = jnp.max(jnp.where(begun, owner_down, 0.0), axis=0, keepdims=True)
    return start, image


def text_bias(rb, start, image, far_rows, window, bias):
    begin = jnp.maximum(rb - 1, 0) * 128
    far = lax.broadcasted_iota(jnp.int32, (far_rows, 128), 0) // NQ
    far_bias = jnp.where(wide(far) == image, 0.0, masked_value)
    key = lax.broadcasted_iota(jnp.int32, (window, 128), 0) + begin
    row = lax.broadcasted_iota(jnp.int32, (window, 128), 1) + rb * 128
    seen = (wide(key) >= start) & (key <= row)
    own_bias = jnp.where(seen, 0.0, masked_value)
    bias[0:far_rows] = jnp.concatenate([far_bias, far_bias], axis=1)
    bias[far_rows : far_rows + window] = jnp.concatenate([own_bias, own_bias], axis=1)


def query_bias(bias):
    key = lax.broadcasted_iota(jnp.int32, (128, 256), 0) // NQ
    row = (lax.broadcasted_iota(jnp.int32, (128, 256), 1) % 128) // NQ
    bias[0:128] = jnp.where(key == row, 0.0, masked_value)


def forward_kernel(
    first, vision, expand, reduce, gains,
    hidden_in, out_grad_in, features, lengths, owners,
    out_result, out_grad_cross, part_expand, part_reduce, gain_feed_out, stats,
    keep_first, keep_gains, keep_normed, keep_query, keep_key, keep_value, keep_far_key, keep_far_value,
    keep_context, keep_after_self, keep_cross_query, keep_cross_context, keep_vision, keep_images, total_self, total_cross,
    all_first, raw_vision, all_vision, all_expand, all_reduce, all_gains, gain_rows,
    hidden, out_grad, images, vision_pair, normed, query, key, value, far_key, far_value, context, after_self,
    cross_query, cross_context, after_cross, normed_feed, grad_feed, sum_branch, sum_normed, got_normed, got_branch, bias, mask,
    layout_rows, send_sem, recv_sem, local_sem,
):
    c, z, y, x = coordinates()
    row_count, width = hidden.shape
    image_count = total_cross.shape[0]
    padded = vision_pair.shape[0] // image_count
    feature_rows = features.shape[0] // (2 * image_count)
    feature_width = features.shape[1]
    part_rows = expand.shape[0] // PARTS
    far_rows, window = far_key.shape[0], 256
    cross_rows = image_count * NQ

    across_at = jnp.where(c == 0, y, x)
    own_at = {"z": z, "y": y, "x": x, "o": across_at}
    mate = (c, z * 4 + jnp.where(c == 0, y, 1 - y) * 2 + jnp.where(c == 0, 1 - x, x))
    beyond = (c, z * 4 + jnp.where(c == 0, 1 - y, y) * 2 + jnp.where(c == 0, x, 1 - x))

    chunks = [(gains, lambda *at: all_gains.at[at], "late", False, 3)]
    chunks.append((vision, lambda *at: raw_vision.at[(c,) + at], "late", True, 3))
    for j in range(3):
        chunks.append((first.at[j], lambda *at, j=j: all_first.at[(c, j) + at], "late", True, 3))
    for p in range(PARTS):
        rows = pl.ds(p * part_rows, part_rows)
        for source, whole in ((expand, all_expand), (reduce, all_reduce)):
            target = lambda *at, p=p, whole=whole: whole.at[(p,) + at]
            chunks.append((source.at[rows], target, "feed", False, 4))
    count = len(chunks)
    events = [
        (2 * number + stage * chunk[4], -stage, number)
        for number, chunk in enumerate(chunks)
        for stage in range(3 if chunk[2] == "feed" else 4)
    ]
    last_tick = max(events)[0]

    def axes_of(number):
        return "zo" if chunks[number][2] == "feed" else "zyx"

    def stages_of(number):
        return 2 if chunks[number][2] == "feed" else 3

    def remote(source, target, index, where):
        return pltpu.make_async_remote_copy(
            src_ref=source, dst_ref=target, send_sem=send_sem.at[index],
            recv_sem=recv_sem.at[index], device_id=where, device_id_type=MESH,
        )

    def sends(number, stage, core):
        source, target, kind = chunks[number][:3]
        order = ORDERS[kind, core]
        done, axis = order[:stage], order[stage]
        at = tuple(slice(None) if a in done else own_at[a] for a in axes_of(number))
        block = target(*at)
        here = source if stage == 0 else block
        base = (number * 3 + stage) * 3
        if axis == "z":
            return [
                remote(here, block, base + k - 1, device(c, (z + k) % 4, y, x)) for k in (1, 2, 3)
            ]
        where = {"y": device(c, z, 1 - y, x), "x": device(c, z, y, 1 - x), "o": beyond}[axis]
        return [remote(here, block, base, where)]

    def place(number):
        source, target = chunks[number][:2]
        at = [own_at[a] for a in axes_of(number)]
        return pltpu.make_async_copy(source, target(*at), local_sem.at[number])

    pair = device(1 - c, z, y, x)

    def across(number):
        target = chunks[number][1]
        block = target(slice(None), slice(None), slice(None))
        return remote(block, block, count * 9 + number, pair)

    def tick_core(tick, core):
        for when, negative, number in sorted(events):
            stage = -negative
            if when != tick:
                continue
            if stage > 0:
                for copy in sends(number, stage - 1, core):
                    copy.wait_recv()
            if stage == 1:
                place(number).wait()
            if stage < stages_of(number):
                for copy in sends(number, stage, core):
                    copy.start()
                if stage == 0:
                    place(number).start()
            elif chunks[number][3]:
                across(number).start()

    def both(step):
        @pl.when(c == 0)
        def _():
            step(0)

        @pl.when(c == 1)
        def _():
            step(1)

    def tick(number):
        both(lambda core: tick_core(number, core))

    def sent(number):
        def step(core):
            for stage in range(stages_of(number)):
                for copy in sends(number, stage, core):
                    copy.wait_send()

        both(step)

    swap_base = count * 10
    near_rows, far_away = pl.ds(0, row_count), pl.ds(row_count, row_count)
    active, grad_before = vision_pair.at[pl.ds(0, 2 * row_count)], vision_pair.at[pl.ds(2 * row_count, 2 * row_count)]
    send_normed = images.at[pl.ds(0, row_count), pl.ds(0, width)]
    send_branch = images.at[pl.ds(row_count, row_count), pl.ds(0, width)]
    swaps = {
        "key": (key, far_key),
        "value": (value, far_value),
        "query": (cross_query.at[pl.ds(cross_rows, cross_rows)], cross_query.at[pl.ds(0, cross_rows)]),
        "context": (cross_context.at[pl.ds(0, cross_rows)], cross_context.at[pl.ds(cross_rows, cross_rows)]),
        "grad_feed": (grad_feed.at[near_rows], grad_feed.at[far_away]),
        "normed_feed": (normed_feed.at[near_rows], normed_feed.at[far_away]),
        "sum_normed": (send_normed, got_normed),
        "sum_branch": (send_branch, got_branch),
    }
    with_mate = ("grad_feed", "normed_feed", "sum_normed", "sum_branch")

    def swap(name):
        source, target = swaps[name]
        where = mate if name in with_mate else pair
        return remote(source, target, swap_base + list(swaps).index(name), where)

    local_base = count
    loads = [
        (hidden_in, hidden),
        (out_grad_in, out_grad),
    ]
    step_rows = 2 * image_count * 32
    whole_steps = feature_rows // 32
    half_rows = whole_steps // 2 * step_rows
    for begin, size in ((0, half_rows), (half_rows, features.shape[0] - half_rows)):
        staged = vision_pair.at[pl.ds(0, size), pl.ds(0, feature_width)]
        loads.append((features.at[pl.ds(begin, size)], staged))
    keeps = {
        "first": (all_first, keep_first),
        "gains": (gain_rows, keep_gains),
        "normed": (normed, keep_normed),
        "query": (query, keep_query),
        "key": (key, keep_key),
        "value": (value, keep_value),
        "far_key": (far_key, keep_far_key),
        "far_value": (far_value, keep_far_value),
        "context": (context, keep_context),
        "after_self": (after_self, keep_after_self),
        "cross_query": (cross_query.at[pl.ds(0, cross_rows)], keep_cross_query),
        "cross_context": (cross_context, keep_cross_context),
        "vision": (vision_pair, keep_vision),
        "images": (images, keep_images),
        "result": (sum_branch.at[pl.ds(0, row_count)], out_result),
        "grad_cross": (sum_normed.at[pl.ds(0, row_count)], out_grad_cross),
    }
    for p in range(PARTS):
        keeps["expand", p] = (all_expand.at[p], part_expand.at[p])
        keeps["reduce", p] = (all_reduce.at[p], part_reduce.at[p])

    def load(k):
        source, target = loads[k]
        return pltpu.make_async_copy(source, target, local_sem.at[local_base + k])

    def keep(name):
        source, target = keeps[name]
        index = local_base + len(loads) + list(keeps).index(name)
        return pltpu.make_async_copy(source, target, local_sem.at[index])

    def weight(name):
        plane, j = PLANES[name]
        return all_first[plane, j].reshape(width, width)

    def gain(k):
        return gain_rows[pl.ds(k, 1), :]

    def stat(k, amount):
        row = pl.ds(c * 4 + k, 1)
        stats[row, :] = stats[row, :] + amount


    def start():
        stats[...] = jnp.zeros_like(stats)
        mask[...] = head_mask(NQ, width)
        first_row, image = caption_layout(lengths[...], owners[...], row_count)
        layout_rows[0:1] = first_row
        layout_rows[1:2] = image

    def read_gains():
        total = jnp.zeros(gain_rows.shape, jnp.float32)
        per = width // 16
        for k in range(16):
            lane = lax.broadcasted_iota(jnp.int32, (128, width), 0)
            column = lax.broadcasted_iota(jnp.int32, (128, width), 1)
            pick = to_half(jnp.where((column == lane + k * per) & (lane < per), 1.0, 0.0))
            total = total + nn(all_gains[k // 4, (k // 2) % 2, k % 2], pick)
        gain_rows[...] = total

    def self_in():
        def step(i):
            rows = span(i, 256)
            source = hidden[rows, :]
            stat(0, row_sum(source * source))
            part = to_half(norm_rows(source, gain(0)))
            normed[rows, :] = part
            query[rows, :] = to_half(nn(part, weight("query"))) * jnp.bfloat16(HD**-0.5)
            key[rows, :] = to_half(nn(part, weight("key")))
            value[rows, :] = to_half(nn(part, weight("value")))

        loop(row_count // 256, step)

    def attend_pair(rb, t, parts):
        lanes, rows = span(t, 128), span(rb, 128)
        queries = head_pair(query[rows, lanes], lane_masks(128))
        scores, most = [], None
        for keys, _, where, _ in parts:
            score = nt(keys, queries) + bias[where, :]
            scores.append(score)
            top = jnp.max(score, axis=0, keepdims=True)
            most = top if most is None else jnp.maximum(most, top)
        weights = [jnp.exp(score - most) for score in scores]
        total = sum(row_sum(part) for part in weights)
        inverse = 1.0 / total
        result = sum(
            tn(to_half(part * inverse), values) for part, (_, values, _, _) in zip(weights, parts)
        )
        context[rows, lanes] = to_half(pair_join(result))
        total_self[rb, t] = most + jnp.log(total)

    def self_query():
        query_bias(bias)

        def step(i):
            rb, t = i // 6, i % 6
            rows, lanes = span(rb, 128), span(t, 128)
            attend_pair(rb, t, [(key[rows, lanes], value[rows, lanes], pl.ds(0, 128), None)])

        loop(row_count // 128 * 6, step)

    def self_text(begin, end):
        def outer(rb):
            rb = rb + begin
            rows = span(rb, 128)
            text_bias(rb, layout_rows[0:1, rows], layout_rows[1:2, rows], far_rows, window, bias)
            near = pl.ds(pl.multiple_of(jnp.maximum(rb - 1, 0) * 128, 128), window)

            def inner(t):
                lanes = span(t, 128)
                attend_pair(rb, t, [
                    (far_key[:, lanes], far_value[:, lanes], pl.ds(0, far_rows), None),
                    (key[near, lanes], value[near, lanes], pl.ds(far_rows, window), None),
                ])

            loop(6, inner)

        loop(end - begin, outer)

    def self_out():
        def step(i):
            rows = span(i, 256)
            branch = nn(context[rows, :], weight("self_output"))
            stat(1, row_sum(branch * branch))
            after_self[rows, :] = hidden[rows, :] + branch

        loop(row_count // 256, step)

    def cross_in():
        def step(i):
            rows = span(i, 256)
            part = to_half(norm_rows(after_self[rows, :], gain(1)))
            result = to_half(nn(part, weight("cross_query"))) * jnp.bfloat16(HD**-0.5)
            cross_query[rows, :] = result

        loop(row_count // 256, step)

    def pack_vision():
        def step(i):
            plane, z_at, y_at = i // 8, (i // 2) % 4, i % 2
            left = wide(raw_vision[plane, z_at, y_at, 0])
            right = wide(raw_vision[plane, z_at, y_at, 1])
            size = 2 * left.shape[0]
            all_vision[plane, span(z_at * 2 + y_at, size), :] = to_half(
                jnp.concatenate([left, right], axis=0)
            )

        loop(16, step)

    def sort_rows(begin, rows, base):
        size = rows // (2 * image_count)
        block = max(size, 16)
        out = lax.broadcasted_iota(jnp.int32, (image_count * block, rows), 0)
        column = lax.broadcasted_iota(jnp.int32, (image_count * block, rows), 1)
        source = (out % block) * (2 * image_count) + c * image_count + out // block
        pick = to_half(jnp.where((column == source) & (out % block < size), 1.0, 0.0))
        sorted_rows = to_half(nn(pick, vision_pair[begin, 0:feature_width]))
        for j in range(image_count):
            where = pl.ds(pl.multiple_of(j * padded + base, 16), block)
            images[where, :] = sorted_rows[j * block : (j + 1) * block]

    def sort_images(part):
        def step(i):
            sort_rows(span(i, step_rows), step_rows, 32 * (i + part * (whole_steps // 2)))

        loop(whole_steps // 2, step)
        if part == 1:
            rest = feature_rows % 32 * 2 * image_count
            sort_rows(pl.ds(whole_steps // 2 * step_rows, rest), rest, whole_steps * 32)

    def project_images(begin, end):
        def step(i):
            rows = pl.ds(pl.multiple_of((i + begin) * padded, 16), padded)
            image = images[rows, :]
            vision_pair[rows, 0:width] = to_half(nn(image, all_vision[0]))
            vision_pair[rows, width : 2 * width] = to_half(nn(image, all_vision[1]))

        loop(end - begin, step)

    def cross_attend(begin, end):
        def step(i):
            i = i + begin
            rows = pl.ds(pl.multiple_of(i * padded, 16), padded)
            own_rows = span(i, NQ)
            part = cross_query[own_rows, :]
            queries = jnp.concatenate([part] * HEADS, axis=0) * mask[...]
            score = nt(vision_pair[rows, 0:width], queries)
            key_row = lax.broadcasted_iota(jnp.int32, score.shape, 0)
            score = jnp.where(key_row < feature_rows, score, masked_value)
            most = jnp.max(score, axis=0, keepdims=True)
            weights = jnp.exp(score - most)
            total = row_sum(weights)
            total_cross[i] = most + jnp.log(total)
            full = tn(to_half(weights * (1.0 / total)), vision_pair[rows, width : 2 * width])
            cross_context[own_rows, :] = to_half(diagonal(full, NQ))

        loop(end - begin, step)

    def cross_out():
        def step(i):
            rows = span(i, 256)
            after_cross[rows, :] = after_self[rows, :] + nn(cross_context[rows, :], weight("cross_output"))

        loop(row_count // 256, step)

    def round_out_grad():
        def step(i):
            rows = span(i, 128)
            grad_feed[rows, :] = to_half(out_grad[rows, :])

        loop(row_count // 128, step)

    def feed_in():
        def step(i):
            rows = span(i, 128)
            normed_feed[rows, :] = to_half(norm_rows(after_cross[rows, :], gain(2 + c)))

        loop(row_count // 128, step)

    half_parts = 2 * PARTS
    block = all_expand.shape[1] * all_expand.shape[2] * part_rows // 2

    def feed_weights(b):
        p, at = b // 2, pl.ds(all_expand.shape[1] // 2 * (b % 2), all_expand.shape[1] // 2)
        return p, at, all_expand[p, at].reshape(block, width), all_reduce[p, at].reshape(block, width)

    def feed_rows(side, b):
        rows = pl.ds(side * row_count, row_count)
        lanes = pl.ds(b * block, block)
        _, _, up, down = feed_weights(b)
        before = nt(normed_feed[rows, :], up)
        share = 0.5 * (1.0 + lax.erf(before * (0.5**0.5)))
        density = jnp.exp(before * before * -0.5) * (0.5 / jnp.pi) ** 0.5
        result = to_half(before * share)
        slope = share + before * density
        active[rows, lanes] = result
        total = nn(result, down)
        back = to_half(nt(grad_feed[rows, :], down) * slope)
        grad_before[rows, lanes] = back
        total_normed = nn(back, up)
        if b == 0:
            sum_branch[rows, :] = total
            sum_normed[rows, :] = total_normed
        else:
            sum_branch[rows, :] = sum_branch[rows, :] + total
            sum_normed[rows, :] = sum_normed[rows, :] + total_normed

    def feed_grads(b):
        lanes = pl.ds(b * block, block)
        p, at = b // 2, pl.ds(all_expand.shape[1] // 2 * (b % 2), all_expand.shape[1] // 2)
        shape = (all_expand.shape[1] // 2,) + all_expand.shape[2:]
        all_expand[p, at] = to_half(tn(grad_before[:, lanes], normed_feed[...])).reshape(shape)
        all_reduce[p, at] = to_half(tn(active[:, lanes], grad_feed[...])).reshape(shape)

    def send_partial(total, buffer, name):
        def step(i):
            rows = span(i, 128)
            buffer[rows, :] = to_half(total[pl.ds(pl.multiple_of(row_count + i * 128, 128), 128), :])

        loop(row_count // 128, step)
        swap(name).start()

    def feed_back():
        gain_feed_out[...] = jnp.zeros_like(gain_feed_out)

        def step(i):
            rows = span(i, 128)
            grad = sum_normed[rows, :] + wide(got_normed[rows, :])
            back, gain_part = norm_back(after_cross[rows, :], gain(2 + c), grad)
            gain_feed_out[0:1, :] = gain_feed_out[0:1, :] + gain_part
            sum_normed[rows, :] = out_grad[rows, :] + back

        loop(row_count // 128, step)

    def feed_out():
        def step(i):
            rows = span(i, 128)
            branch = sum_branch[rows, :] + wide(got_branch[rows, :])
            result = after_cross[rows, :] + branch
            stat(2, row_sum(branch * branch))
            stat(3, row_sum(result * result))
            sum_branch[rows, :] = result

        loop(row_count // 128, step)

    half_tick = [0]

    def ticks(until):
        while half_tick[0] <= until:
            tick(half_tick[0])
            half_tick[0] += 1

    for k in range(3):
        load(k).start()
    meet(c, z, y, x)
    ticks(0)
    start()
    ticks(2)
    load(1).wait()
    round_out_grad()
    swap("grad_feed").start()
    ticks(4)
    load(2).wait()
    sort_images(0)
    load(3).start()
    ticks(7)
    load(3).wait()
    sort_images(1)
    keep("images").start()
    ticks(9)
    read_gains()
    keep("gains").start()
    ticks(11)
    across(1).wait_recv()
    pack_vision()
    quarter = image_count // 4
    project_images(0, quarter)
    ticks(13)
    project_images(quarter, 2 * quarter)
    ticks(15)
    project_images(2 * quarter, 3 * quarter)
    ticks(17)
    for number in (2, 3, 4):
        across(number).wait_recv()
    load(0).wait()
    self_in()
    for name in ("normed", "query", "key", "value"):
        keep(name).start()

    @pl.when(c == 0)
    def _():
        swap("key").start()
        swap("value").start()

    project_images(3 * quarter, image_count)
    keep("vision").start()
    ticks(18)
    keep("first").start()
    blocks = row_count // 128

    @pl.when(c == 0)
    def _():
        self_query()
        self_out()
        cross_in()
        swap("query").start()

    @pl.when(c == 1)
    def _():
        swap("key").wait_recv()
        swap("value").wait_recv()
        self_text(0, blocks // 2)
        keep("far_key").start()
        keep("far_value").start()

    ticks(20)

    @pl.when(c == 1)
    def _():
        self_text(blocks // 2, blocks)
        self_out()

    @pl.when(c == 0)
    def _():
        cross_attend(0, image_count // 2)

    ticks(21)

    @pl.when(c == 1)
    def _():
        swap("query").wait_recv()
        cross_attend(0, image_count // 2)

    @pl.when(c == 0)
    def _():
        cross_attend(image_count // 2, image_count)

    keep("context").start()
    keep("after_self").start()
    ticks(22)

    @pl.when(c == 1)
    def _():
        cross_attend(image_count // 2, image_count)
        swap("context").start()
        after_cross[...] = after_self[...]

    ticks(23)

    @pl.when(c == 0)
    def _():
        swap("context").wait_recv()
        cross_out()

    keep("cross_query").start()
    keep("cross_context").start()
    feed_in()
    swap("normed_feed").start()
    ticks(last_tick)
    for name in ("vision", "images"):
        keep(name).wait()
    for b in range(half_parts):
        feed_rows(0, b)
    swap("grad_feed").wait_recv()
    swap("normed_feed").wait_recv()
    for b in range(half_parts):
        feed_rows(1, b)
    send_partial(sum_normed, send_normed, "sum_normed")
    send_partial(sum_branch, send_branch, "sum_branch")
    for p in range(PARTS):
        sent(5 + 2 * p)
        sent(6 + 2 * p)
        feed_grads(2 * p)
        feed_grads(2 * p + 1)
        keep(("expand", p)).start()
        keep(("reduce", p)).start()
    swap("sum_normed").wait_recv()
    feed_back()
    keep("grad_cross").start()
    swap("sum_branch").wait_recv()
    feed_out()
    keep("result").start()
    for number in range(5):
        sent(number)
    for number in range(1, 5):
        across(number).wait_send()
    for name in with_mate:
        swap(name).wait_send()

    @pl.when(c == 0)
    def _():
        swap("key").wait_send()
        swap("value").wait_send()
        swap("query").wait_send()

    @pl.when(c == 1)
    def _():
        swap("context").wait_send()

    for name in keeps:
        if name in ("vision", "images"):
            continue
        if name in ("far_key", "far_value"):

            @pl.when(c == 1)
            def _(name=name):
                keep(name).wait()

        else:
            keep(name).wait()


def forward_all(first, vision, expand, reduce, gains, hidden, out_grad, features, lengths, owners):
    half, single = jnp.bfloat16, jnp.float32
    row_count, width = hidden.shape
    image_count, feature_rows, feature_width = features.shape
    image_count = image_count // 2
    features = features.transpose(1, 0, 2).reshape(-1, feature_width)
    padded = -(-feature_rows // 16) * 16
    cross_rows = image_count * NQ
    part_rows = expand.shape[0] // PARTS
    anywhere = pl.BlockSpec(memory_space=pl.ANY)
    vmem = pl.BlockSpec(memory_space=pltpu.VMEM)
    rows_half = jax.ShapeDtypeStruct((row_count, width), half)
    rows_single = jax.ShapeDtypeStruct((row_count, width), single)
    all_first = (2,) + first.shape[:1] + (4, 2, 2) + first.shape[1:]
    all_feed = (PARTS, 4, 2, part_rows, width)
    gain_shape = (16, width)
    pair_shape = (image_count * padded, 2 * width)
    outs = {
        "result": (rows_single, anywhere),
        "grad_cross": (rows_single, anywhere),
        "part_expand": (jax.ShapeDtypeStruct(all_feed, half), anywhere),
        "part_reduce": (jax.ShapeDtypeStruct(all_feed, half), anywhere),
        "gain_feed": (jax.ShapeDtypeStruct((8, width), single), vmem),
        "stats": (jax.ShapeDtypeStruct((8, width), single), vmem),
        "first": (jax.ShapeDtypeStruct(all_first, half), anywhere),
        "gains": (jax.ShapeDtypeStruct(gain_shape, single), anywhere),
        "normed": (rows_half, anywhere),
        "query": (rows_half, anywhere),
        "key": (rows_half, anywhere),
        "value": (rows_half, anywhere),
        "far_key": (rows_half, anywhere),
        "far_value": (rows_half, anywhere),
        "context": (rows_half, anywhere),
        "after_self": (rows_single, anywhere),
        "cross_query": (jax.ShapeDtypeStruct((cross_rows, width), half), anywhere),
        "cross_context": (rows_half, anywhere),
        "vision": (jax.ShapeDtypeStruct(pair_shape, half), anywhere),
        "images": (jax.ShapeDtypeStruct((image_count * padded, feature_width), half), anywhere),
        "total_self": (jax.ShapeDtypeStruct((row_count // 128, HEADS // 2, 1, 256), single), vmem),
        "total_cross": (jax.ShapeDtypeStruct((image_count, 1, HEADS * NQ), single), vmem),
    }
    halves = (row_count, width)
    scratch = [
        pltpu.VMEM(all_first, half),
        pltpu.VMEM((2, 4, 2, 2) + vision.shape, half),
        pltpu.VMEM((2, feature_width, width), half),
        pltpu.VMEM(all_feed, half),
        pltpu.VMEM(all_feed, half),
        pltpu.VMEM((4, 2, 2) + gains.shape, half),
        pltpu.VMEM(gain_shape, single),
        pltpu.VMEM(halves, single),
        pltpu.VMEM(halves, single),
        pltpu.VMEM((image_count * padded, feature_width), half),
        pltpu.VMEM(pair_shape, half),
    ]
    scratch += [pltpu.VMEM(halves, half)] * 7
    scratch += [
        pltpu.VMEM(halves, single),
        pltpu.VMEM(halves, half),
        pltpu.VMEM(halves, half),
        pltpu.VMEM(halves, single),
        pltpu.VMEM((2 * row_count, width), half),
        pltpu.VMEM((2 * row_count, width), half),
        pltpu.VMEM((2 * row_count, width), single),
        pltpu.VMEM((2 * row_count, width), single),
        pltpu.VMEM(halves, half),
        pltpu.VMEM(halves, half),
        pltpu.VMEM((row_count + 256, 256), single),
        pltpu.VMEM((HEADS * NQ, width), half),
        pltpu.VMEM((8, row_count), single),
        pltpu.SemaphoreType.DMA(((5 + 2 * PARTS) * 10 + 8,)),
        pltpu.SemaphoreType.DMA(((5 + 2 * PARTS) * 10 + 8,)),
        pltpu.SemaphoreType.DMA((5 + 4 + 16 + 4 * PARTS,)),
    ]
    values = pl.pallas_call(
        forward_kernel,
        out_shape=[shape for shape, _ in outs.values()],
        in_specs=[anywhere] * 8 + [vmem] * 2,
        out_specs=[spec for _, spec in outs.values()],
        scratch_shapes=scratch,
        compiler_params=pltpu.CompilerParams(
            collective_id=2, has_side_effects=True, vmem_limit_bytes=VMEM_LIMIT
        ),
        name="forward_layer",
    )(first, vision, expand, reduce, gains, hidden, out_grad, features, lengths, owners)
    return dict(zip(outs, values))


def scatter_engine(chunks, send_sem, recv_sem):
    c, z, y, x = coordinates()
    own = {"z": z, "y": y, "x": x, "o": jnp.where(c == 0, y, x)}
    beyond = (c, z * 4 + jnp.where(c == 0, 1 - y, y) * 2 + jnp.where(c == 0, x, 1 - x))

    def axes_of(chunk):
        return "zo" if chunk["kind"] == "feed" else "zyx"

    def remote(source, target, index, where):
        return pltpu.make_async_remote_copy(
            src_ref=source, dst_ref=target, send_sem=send_sem.at[index],
            recv_sem=recv_sem.at[index], device_id=where, device_id_type=MESH,
        )

    def sends(number, stage, core):
        chunk = chunks[number]
        held, got = chunk["held"], chunk["got"][stage]
        order = ORDERS[chunk["kind"], core][::-1]
        done, axis = order[:stage], order[stage]
        base = (number * 3 + stage) * 3

        def block(there):
            return held.at[
                tuple(
                    there if a == axis else own[a] if a in done else slice(None)
                    for a in axes_of(chunk)
                )
            ]

        if axis == "z":
            return [
                remote(
                    block((z + k) % 4), got.at[k - 1], base + k - 1, device(c, (z + k) % 4, y, x)
                )
                for k in (1, 2, 3)
            ]
        where = {"y": device(c, z, 1 - y, x), "x": device(c, z, y, 1 - x), "o": beyond}[axis]
        return [remote(block(1 - own[axis]), got, base, where)]

    def absorb(number, stage, core):
        chunk = chunks[number]
        held, got = chunk["held"], chunk["got"][stage]
        order = ORDERS[chunk["kind"], core][::-1]
        done, axis = order[: stage + 1], order[stage]
        free = [a for a in axes_of(chunk) if a not in done]
        sizes = [4 if a == "z" else 2 for a in free]
        steps = 1
        for size in sizes:
            steps *= size

        def step(i):
            index = {}
            for a, size in reversed(list(zip(free, sizes))):
                index[a] = i % size
                i = i // size
            at = tuple(index[a] if a in index else own[a] for a in axes_of(chunk))
            inner = tuple(index[a] for a in free)
            value = wide(held[at])
            if axis == "z":
                for k in range(3):
                    value = value + wide(got[(k,) + inner])
            else:
                value = value + wide(got[inner] if inner else got[...])
            if stage == len(order) - 1:
                chunk["total"][...] = value
            else:
                held[at] = to_half(value)

        if steps == 1:
            step(0)
        else:
            loop(steps, step)

    def tick_core(now, core):
        for number, stage in [
            (number, stage)
            for stage in (3, 2, 1, 0)
            for number, chunk in enumerate(chunks)
            if stage < len(chunk["ticks"][core]) and chunk["ticks"][core][stage] == now
        ]:
            if stage == 0:
                chunks[number]["ready"](core)
            else:
                for copy in sends(number, stage - 1, core):
                    copy.wait_recv()
                absorb(number, stage - 1, core)
            if stage < len(chunks[number]["ticks"][core]) - 1:
                for copy in sends(number, stage, core):
                    copy.start()

    def each_core(step):
        @pl.when(c == 0)
        def _():
            step(0)

        @pl.when(c == 1)
        def _():
            step(1)

    def tick(now):
        each_core(lambda core: tick_core(now, core))

    def wait_sent():
        def step(core):
            for number, chunk in enumerate(chunks):
                for stage in range(len(chunk["ticks"][core]) - 1):
                    for copy in sends(number, stage, core):
                        copy.wait_send()

        each_core(step)

    last = max(max(ticks) for chunk in chunks for ticks in chunk["ticks"])
    return tick, wait_sent, remote, last


def got_shapes(kind, rows, width):
    if kind == "feed":
        return [(4, rows, width), (3, rows, width)]
    if kind == "late":
        return [(4, 2, rows, width), (4, rows, width), (3, rows, width)]
    return [(4, 2, rows, width), (3, 2, rows, width), (rows, width)]


FEED_CHUNKS = 2 * PARTS
FEED_TICKS = [(0, 2, 5), (2, 4, 7), (4, 6, 9), (6, 8, 11)]
PLANE_TICKS = (
    [(17, 18, 19, 20), (17, 18, 19, 20), (3, 5, 8, 11)],
    [(17, 18, 19, 20), (11, 13, 15, 16), (10, 12, 14, 15)],
)
VISION_TICKS = ((9, 12, 14, 16), (9, 12, 14, 16))


def backward_kernel(
    feature_rows,
    part_expand, part_reduce, grad_cross_in, hidden_in, after_self_in, first_in, gains_in,
    normed_in, query_in, key_in, value_in, far_key_in, far_value_in, context_in,
    cross_query_in, cross_context_in, vision_in, images_in, lengths, owners, total_self, total_cross, gain_feed,
    part_stats, hidden_grad_out, sum_expand, sum_reduce, sum_first, sum_vision, sum_gains, totals,
    held_expand, held_reduce, got_f0, got_f1, got_p0, got_p1, got_p2, got_v0, got_v1, got_v2,
    pair_first, pair_vision, held_vision, gains_now, gains_got, gains_z, stats_now, stats_got, stats_z,
    first, pair, images, grad_vision, cross_context, after_self, hidden, grad_after, gain_rows,
    cross_query, grad_context, grad_query, far_grad, bias, mask, sum_far_key, sum_far_value, sum_key, sum_value,
    layout_rows, gain_parts, send_sem, recv_sem, local_sem,
):
    c, z, y, x = coordinates()
    row_count, width = hidden.shape
    image_count = total_cross.shape[0]
    padded = pair.shape[0] // image_count
    feature_width = images.shape[1]
    cross_rows = image_count * NQ
    part_rows = held_expand.shape[-2]
    rows_vision = held_vision.shape[-2]
    grad_normed = after_self
    far_rows, window = row_count, 256
    scale = HD**-0.5
    other = device(1 - c, z, y, x)

    def shelf(buffer, number):
        at = pl.ds(number // 2 * row_count, row_count), pl.ds(number % 2 * width, width)
        return buffer.at[at[0], at[1]]

    names = ("normed", "query", "key", "value", "far_key", "far_value", "context", "grad_context")
    normed, query, key, value, far_key, far_value, context, grad_context_self = (
        shelf(pair, number) for number in range(len(names))
    )
    own_query, own_key, own_value = (shelf(images, 2 * number) for number in range(3))

    loads = {
        "expand": (part_expand, held_expand),
        "reduce": (part_reduce, held_reduce),
        "grad_cross": (grad_cross_in, grad_after),
        "first": (first_in, first),
        "gains": (gains_in, gain_rows),
        "cross_context": (cross_context_in, cross_context),
        "cross_query": (cross_query_in, cross_query),
        "vision": (vision_in, pair),
        "images": (images_in, images),
        "after_self": (after_self_in, after_self),
        "hidden": (hidden_in, hidden),
        "normed": (normed_in, normed),
        "query": (query_in, query),
        "key": (key_in, key),
        "value": (value_in, value),
        "far_key": (far_key_in, far_key),
        "far_value": (far_value_in, far_value),
        "context": (context_in, context),
        "out_hidden": (grad_after, hidden_grad_out),
    }

    def local(name):
        source, target = loads[name]
        return pltpu.make_async_copy(source, target, local_sem.at[list(loads).index(name)])

    def pair_copy(k):
        if k == 3:
            return remote(grad_vision.at[1 - c], pair_vision, pair_base + k, other)
        return remote(first.at[1 - c, k], pair_first.at[k], pair_base + k, other)

    def ready_first(j, core):
        pair_copy(j).wait_recv()

        def step(i):
            at = (i // 4, (i // 2) % 2, i % 2)
            value = wide(first[(core, j) + at]) + wide(pair_first[(j,) + at])
            first[(core, j) + at] = to_half(value)

        loop(16, step)

    def ready_vision(core):
        pair_copy(3).wait_recv()

        def step(i):
            rows = span(i, 2 * rows_vision)
            value = wide(grad_vision[core, rows, :]) + wide(pair_vision[rows, :])
            held_vision[i // 2, i % 2, 0] = to_half(value[:rows_vision])
            held_vision[i // 2, i % 2, 1] = to_half(value[rows_vision:])

        loop(8, step)

    chunks = []
    for number in range(FEED_CHUNKS):
        p = number // 2
        held, total, name = (
            (held_expand, sum_expand, "expand"), (held_reduce, sum_reduce, "reduce")
        )[number % 2]
        chunks.append({
            "held": held.at[p], "got": [got_f0.at[number], got_f1.at[number]], "kind": "feed",
            "total": total.at[pl.ds(p * part_rows, part_rows)], "ticks": (FEED_TICKS[number],) * 2,
            "ready": (lambda core, name=name: local(name).wait()) if p == 0 else (lambda core: None),
        })
    for j in range(3):
        chunks.append({
            "held": first.at[c, j], "got": [got_p0.at[j], got_p1.at[j], got_p2.at[j]], "kind": "late",
            "total": sum_first.at[c, j], "ticks": (PLANE_TICKS[0][j], PLANE_TICKS[1][j]),
            "ready": lambda core, j=j: ready_first(j, core),
        })
    chunks.append({
        "held": held_vision, "got": [got_v0, got_v1, got_v2], "kind": "late",
        "total": sum_vision.at[c], "ticks": VISION_TICKS, "ready": ready_vision,
    })
    tick, wait_sent, remote, last = scatter_engine(chunks, send_sem, recv_sem)
    pair_base = len(chunks) * 9
    gains_base, stats_base = pair_base + 4, pair_base + 10
    swap_base = stats_base + 8

    def small(stage, now, got, got_z, base):
        if stage < 3:
            where = (other, device(c, z, 1 - y, x), device(c, z, y, 1 - x))[stage]
            return [remote(now.at[stage], got.at[stage], base + stage, where)]
        return [
            remote(now.at[3], got_z.at[z], base + 2 + k, device(c, (z + k) % 4, y, x))
            for k in (1, 2, 3)
        ]

    def small_step(stage, now, got, got_z, base):
        if stage > 0:
            for copy in small(stage - 1, now, got, got_z, base):
                copy.wait()
            if stage < 4:
                now[stage] = now[stage - 1] + got[stage - 1]
            else:
                got_z[z] = now[3]
                now[4] = (got_z[0] + got_z[1]) + (got_z[2] + got_z[3])
        if stage < 4:
            for copy in small(stage, now, got, got_z, base):
                copy.start()

    def folded(values):
        total = values[:, 0:128]
        for k in range(1, values.shape[1] // 128):
            total = total + values[:, k * 128 : (k + 1) * 128]
        return total

    def squares(block):
        return jnp.sum((block * block).reshape(-1, 8, block.shape[1]), axis=0)

    own_rows, other_rows = pl.ds(0, cross_rows), pl.ds(cross_rows, cross_rows)
    swaps = {
        "context": (grad_context.at[other_rows], grad_context.at[own_rows]),
        "query": (grad_query.at[own_rows], grad_query.at[other_rows]),
        "far_key": (far_grad.at[0], far_grad.at[0]),
        "far_value": (far_grad.at[1], far_grad.at[1]),
    }

    def swap(name):
        source, target = swaps[name]
        return remote(source, target, swap_base + list(swaps).index(name), other)

    def weight(name):
        plane, j = PLANES[name]
        return first[plane, j].reshape(width, width)

    def gain(k):
        return gain_rows[pl.ds(k, 1), :]

    def store_weight_grad(name, value):
        plane, j = PLANES[name]
        first[plane, j] = to_half(value).reshape(first.shape[2:])


    def start():
        gain_parts[...] = jnp.zeros_like(gain_parts)
        gain_parts[pl.ds(2 + c, 1), :] = gain_feed[0:1, :]
        mask[...] = head_mask(NQ, width)
        first_row, image = caption_layout(lengths[...], owners[...], row_count)
        layout_rows[0:1] = first_row
        layout_rows[1:2] = image

    def cross_out_back():
        def step(i):
            rows = span(i, 256)
            part = to_half(grad_after[rows, :])
            grad_query[rows, :] = part
            grad_context[rows, :] = to_half(nt(part, weight("cross_output")))

        loop(row_count // 256, step)
        store_weight_grad("cross_output", tn(cross_context[...], grad_query[...]))
        swap("context").start()

    def cross_back(begin, end):
        def step(i):
            i = i + begin
            rows = pl.ds(pl.multiple_of(i * padded, 16), padded)
            at = span(i, NQ)
            queries = jnp.concatenate([cross_query[at, :]] * HEADS, axis=0) * mask[...]
            grads = jnp.concatenate([grad_context[at, :]] * HEADS, axis=0) * mask[...]
            keys, values = pair[rows, 0:width], pair[rows, width : 2 * width]
            score = nt(keys, queries)
            key_row = lax.broadcasted_iota(jnp.int32, score.shape, 0)
            seen = key_row < feature_rows
            probability = jnp.exp(jnp.where(seen, score, masked_value) - total_cross[i])
            grad_prob = nt(values, grads)
            inner = row_sum(grad_prob * probability)
            grad_score = to_half(probability * (grad_prob - inner))
            full = tn(grad_score, keys)
            pair[rows, 0:width] = to_half(nn(grad_score, queries))
            pair[rows, width : 2 * width] = to_half(nn(to_half(probability), grads))
            grad_query[at, :] = to_half(diagonal(full, NQ) * scale)

        loop(end - begin, step)


    def vision_back(begin, end):
        def step(i):
            i = i + begin
            lanes = span(i, 128)
            both = to_half(tn(images[:, lanes], pair[...]))
            grad_vision[0, lanes, :] = both[:, 0:width]
            grad_vision[1, lanes, :] = both[:, width : 2 * width]

        loop(end - begin, step)

    def cross_in_back():
        def step(i):
            rows = span(i, 128)
            source = after_self[rows, :]
            grad = nt(grad_query[rows, :], weight("cross_query"))
            back, part = norm_back(source, gain(1), grad)
            gain_parts[1:2, :] = gain_parts[1:2, :] + part
            grad_after[rows, :] = grad_after[rows, :] + back
            grad_context[rows, :] = to_half(norm_rows(source, gain(1)))

        loop(row_count // 128, step)
        store_weight_grad("cross_query", tn(grad_context[...], grad_query[...]))

    def self_out_back():
        def step(i):
            rows = span(i, 256)
            part = to_half(grad_after[rows, :])
            grad_context[rows, :] = part
            grad_context_self[rows, :] = to_half(nt(part, weight("self_output")))

        loop(row_count // 256, step)
        store_weight_grad("self_output", tn(context[...], grad_context[...]))

    def attend_pair_back(rb, t, parts):
        rows, lanes = span(rb, 128), span(t, 128)
        masks = lane_masks(128)
        queries = head_pair(query[rows, lanes], masks)
        grads = head_pair(grad_context_self[rows, lanes], masks)
        kept, inner = [], 0.0
        for keys, values, where in parts:
            score = nt(keys, queries) + wide(where)
            probability = jnp.exp(score - total_self[rb, t])
            grad_prob = nt(values, grads)
            inner = inner + row_sum(grad_prob * probability)
            kept.append((probability, grad_prob))
        result, back = [], 0.0
        for (keys, values, _), (probability, grad_prob) in zip(parts, kept):
            grad_score = to_half(probability * (grad_prob - inner))
            result.append((nn(grad_score, queries), nn(to_half(probability), grads)))
            back = back + tn(grad_score, keys)
        own_query[rows, lanes] = to_half(pair_join(back) * scale)
        return result

    def self_query_back(begin, end):
        def step(i):
            rb, t = i // 6, i % 6
            rows, lanes = span(rb, 128), span(t, 128)
            parts = [(key[rows, lanes], value[rows, lanes], bias[0, 0:128])]
            ((grad_key, grad_value),) = attend_pair_back(rb, t, parts)
            own_key[rows, lanes] = to_half(grad_key)
            own_value[rows, lanes] = to_half(grad_value)

        blocks = row_count // 128

        def shifted_step(i):
            step(i + begin * blocks)

        loop((end - begin) * blocks, shifted_step)

    def text_biases():
        def step(rb):
            rows = span(rb, 128)
            start_row, image = layout_rows[0:1, rows], layout_rows[1:2, rows]
            begin = jnp.maximum(rb - 1, 0) * 128
            far = lax.broadcasted_iota(jnp.int32, (far_rows, 128), 0) // NQ
            far_bias = jnp.where(wide(far) == image, 0.0, masked_value)
            key_row = lax.broadcasted_iota(jnp.int32, (window, 128), 0) + begin
            row = lax.broadcasted_iota(jnp.int32, (window, 128), 1) + rb * 128
            seen = (wide(key_row) >= start_row) & (key_row <= row)
            own_bias = jnp.where(seen, 0.0, masked_value)
            bias[rb, 0:far_rows] = to_half(jnp.concatenate([far_bias, far_bias], axis=1))
            bias[rb, far_rows : far_rows + window] = to_half(
                jnp.concatenate([own_bias, own_bias], axis=1)
            )

        loop(row_count // 128, step)

    def query_biases():
        key_row = lax.broadcasted_iota(jnp.int32, (128, 256), 0) // NQ
        row = (lax.broadcasted_iota(jnp.int32, (128, 256), 1) % 128) // NQ
        bias[0, 0:128] = to_half(jnp.where(key_row == row, 0.0, masked_value))

    def self_text_back(begin, end):
        def outer(t):
            t = t + begin
            lanes = span(t, 128)
            for total in (sum_far_key, sum_far_value, sum_key, sum_value):
                total[...] = jnp.zeros_like(total)

            def inner(rb):
                near = pl.ds(pl.multiple_of(jnp.maximum(rb - 1, 0) * 128, 128), window)
                parts = [
                    (far_key[:, lanes], far_value[:, lanes], bias[rb, 0:far_rows]),
                    (key[near, lanes], value[near, lanes], bias[rb, far_rows : far_rows + window]),
                ]
                far_part, near_part = attend_pair_back(rb, t, parts)
                sum_far_key[...] += far_part[0]
                sum_far_value[...] += far_part[1]
                sum_key[near, :] = sum_key[near, :] + near_part[0]
                sum_value[near, :] = sum_value[near, :] + near_part[1]

            loop(row_count // 128, inner)
            far_grad[0, :, lanes] = to_half(sum_far_key[...])
            far_grad[1, :, lanes] = to_half(sum_far_value[...])
            own_key[:, lanes] = to_half(sum_key[...])
            own_value[:, lanes] = to_half(sum_value[...])

        loop(end - begin, outer)

    def self_in_back():
        def step(i):
            rows = span(i, 256)
            grad = nt(own_query[rows, :], weight("query"))
            grad = grad + nt(own_key[rows, :], weight("key"))
            grad = grad + nt(own_value[rows, :], weight("value"))
            grad_normed[rows, :] = grad

        loop(row_count // 256, step)

    def far_in_back():
        def step(i):
            rows = span(i, 256)
            grad = nt(far_grad[0, rows, :], weight("key")) + nt(far_grad[1, rows, :], weight("value"))
            grad_normed[rows, :] = grad_normed[rows, :] + grad

        loop(row_count // 256, step)

    def project_back(far):
        rows = normed[...]
        store_weight_grad("query", tn(rows, own_query[...]))
        grad_key, grad_value = tn(rows, own_key[...]), tn(rows, own_value[...])
        if far:
            grad_key = grad_key + tn(rows, far_grad[0])
            grad_value = grad_value + tn(rows, far_grad[1])
        store_weight_grad("key", grad_key)
        store_weight_grad("value", grad_value)

    def hidden_back():
        def step(i):
            rows = span(i, 128)
            back, part = norm_back(hidden[rows, :], gain(0), grad_normed[rows, :])
            gain_parts[0:1, :] = gain_parts[0:1, :] + part
            grad_after[rows, :] = grad_after[rows, :] + back

        loop(row_count // 128, step)

    def send_pair(core, *names):
        @pl.when(c == core)
        def _():
            for name in names:
                plane, j = PLANES[name]
                if plane != core:
                    pair_copy(j).start()

    for name in ("expand", "reduce", "grad_cross", "first", "cross_context", "vision", "cross_query",
                 "images", "after_self", "gains", "hidden"):
        local(name).start()
    meet(c, z, y, x)
    tick(0)
    start()
    local("grad_cross").wait()
    local("first").wait()
    local("cross_context").wait()

    @pl.when(c == 0)
    def _():
        cross_out_back()

    @pl.when(c == 1)
    def _():
        plane, j = PLANES["cross_output"]
        first[plane, j] = jnp.zeros(first.shape[2:], jnp.bfloat16)
        plane, j = PLANES["cross_query"]
        first[plane, j] = jnp.zeros(first.shape[2:], jnp.bfloat16)
        swap("context").wait_recv()

    send_pair(1, "cross_output")
    tick(1)
    local("vision").wait()
    local("cross_query").wait()
    quarter = image_count // 4
    for k in range(4):
        cross_back(k * quarter, (k + 1) * quarter)
        tick(2 + k)

    @pl.when(c == 1)
    def _():
        swap("query").start()

    local("images").wait()
    tiles = feature_width // 128
    vision_back(0, tiles // 3)
    tick(6)
    vision_back(tiles // 3, 2 * tiles // 3)
    tick(7)
    vision_back(2 * tiles // 3, tiles)
    pair_copy(3).start()
    for name in names[:-1]:
        local(name).start()
    tick(8)
    local("after_self").wait()
    local("gains").wait()

    @pl.when(c == 0)
    def _():
        swap("query").wait_recv()
        swap("context").wait_send()
        cross_in_back()

    send_pair(0, "cross_query")
    for name in names[:-1]:
        local(name).wait()
    self_out_back()
    send_pair(0, "self_output")
    tick(9)

    @pl.when(c == 0)
    def _():
        query_biases()
        self_query_back(0, 3)

    @pl.when(c == 1)
    def _():
        text_biases()

    for t in range(6):

        @pl.when(c == 1)
        def _(t=t):
            self_text_back(t, t + 1)

        if t == 1:

            @pl.when(c == 0)
            def _():
                self_query_back(3, 6)

        if t < 5:
            tick(10 + t)

    @pl.when(c == 1)
    def _():
        swap("far_key").start()
        swap("far_value").start()

    self_in_back()
    tick(15)

    @pl.when(c == 0)
    def _():
        swap("far_key").wait_recv()
        swap("far_value").wait_recv()
        far_in_back()
        project_back(True)

    @pl.when(c == 1)
    def _():
        project_back(False)

    send_pair(0, "value")
    send_pair(1, "query", "key")
    tick(16)
    local("hidden").wait()
    hidden_back()
    local("out_hidden").start()
    gains_now[0] = gain_parts[...]
    for now in range(17, last + 1):
        small_step(now - 17, gains_now, gains_got, gains_z, gains_base)
        tick(now)
    small_step(4, gains_now, gains_got, gains_z, gains_base)
    back = [
        remote(sum_first.at[c], sum_first.at[c], stats_base + 6, other),
        remote(sum_vision.at[c], sum_vision.at[c], stats_base + 7, other),
    ]
    for copy in back:
        copy.start()
    gains = gains_now[4]
    sum_gains[...] = gains
    mass = jnp.where((c == 0) & (z + y + x == 0), 1.0, 0.0) * (gains * gains)
    for j in range(3):
        mass = mass + squares(sum_first[c, j])
    mass = mass + squares(sum_vision[c])
    mass = mass + squares(sum_expand[...]) + squares(sum_reduce[...])
    stats_now[0, 0:8] = folded(mass)
    stats_now[0, 8:16] = folded(part_stats[...])
    for stage in range(5):
        small_step(stage, stats_now, stats_got, stats_z, stats_base)
    totals[...] = stats_now[4]
    for copy in back:
        copy.wait()
    assert last == 20
    wait_sent()
    for k in range(4):
        pair_copy(k).wait_send()

    @pl.when(c == 1)
    def _():
        swap("query").wait_send()
        swap("far_key").wait_send()
        swap("far_value").wait_send()

    local("out_hidden").wait()


def backward_all(kept, hidden, lengths, owners, feature_rows):
    half, single = jnp.bfloat16, jnp.float32
    row_count, width = hidden.shape
    feature_width = kept["images"].shape[1]
    parts = kept["part_expand"].shape
    part_rows = parts[-2]
    rows_first = kept["first"].shape[-2]
    rows_vision = feature_width // 16
    cross_rows = kept["cross_query"].shape[0]
    anywhere = pl.BlockSpec(memory_space=pl.ANY)
    vmem = pl.BlockSpec(memory_space=pltpu.VMEM)
    rows_half, rows_single = pltpu.VMEM((row_count, width), half), pltpu.VMEM((row_count, width), single)
    outs = {
        "hidden_grad": (jax.ShapeDtypeStruct((row_count, width), single), anywhere),
        "expand": (jax.ShapeDtypeStruct((PARTS * part_rows, width), single), vmem),
        "reduce": (jax.ShapeDtypeStruct((PARTS * part_rows, width), single), vmem),
        "first": (jax.ShapeDtypeStruct((2, 3, rows_first, width), single), vmem),
        "vision": (jax.ShapeDtypeStruct((2, rows_vision, width), single), vmem),
        "gains": (jax.ShapeDtypeStruct((8, width), single), vmem),
        "totals": (jax.ShapeDtypeStruct((16, 128), single), vmem),
    }
    scratch = [pltpu.VMEM(parts, half)] * 2
    scratch += [
        pltpu.VMEM((FEED_CHUNKS,) + shape, half) for shape in got_shapes("feed", part_rows, width)
    ]
    scratch += [pltpu.VMEM((3,) + shape, half) for shape in got_shapes("late", rows_first, width)]
    scratch += [pltpu.VMEM(shape, half) for shape in got_shapes("late", rows_vision, width)]
    scratch += [
        pltpu.VMEM(kept["first"].shape[1:], half),
        pltpu.VMEM((feature_width, width), half),
        pltpu.VMEM((4, 2, 2, rows_vision, width), half),
    ]
    for shape in ((8, width), (16, 128)):
        scratch += [pltpu.VMEM((number,) + shape, single) for number in (5, 3, 4)]
    scratch += [
        pltpu.VMEM(kept["first"].shape, half),
        pltpu.VMEM(kept["vision"].shape, half),
        pltpu.VMEM(kept["images"].shape, half),
        pltpu.VMEM((2, feature_width, width), half),
        rows_half,
        rows_single,
        rows_single,
        rows_single,
        pltpu.VMEM((16, width), single),
        pltpu.VMEM((cross_rows, width), half),
        rows_half,
        rows_half,
        pltpu.VMEM((2, row_count, width), half),
        pltpu.VMEM((row_count // 128, row_count + 256, 256), half),
        pltpu.VMEM((HEADS * NQ, width), half),
    ]
    scratch += [pltpu.VMEM((row_count, 128), single)] * 4
    scratch += [
        pltpu.VMEM((8, row_count), single),
        pltpu.VMEM((8, width), single),
        pltpu.SemaphoreType.DMA(((FEED_CHUNKS + 4) * 9 + 4 + 14 + 4,)),
        pltpu.SemaphoreType.DMA(((FEED_CHUNKS + 4) * 9 + 4 + 14 + 4,)),
        pltpu.SemaphoreType.DMA((19,)),
    ]
    order = ("part_expand", "part_reduce", "grad_cross", None, "after_self", "first", "gains", "normed",
             "query", "key", "value", "far_key", "far_value", "context", "cross_query", "cross_context",
             "vision", "images")
    values = pl.pallas_call(
        functools.partial(backward_kernel, feature_rows),
        out_shape=[shape for shape, _ in outs.values()],
        in_specs=[anywhere] * len(order) + [vmem] * 6,
        out_specs=[spec for _, spec in outs.values()],
        scratch_shapes=scratch,
        compiler_params=pltpu.CompilerParams(
            collective_id=3, has_side_effects=True, vmem_limit_bytes=VMEM_LIMIT
        ),
        name="backward_layer",
    )(
        *[hidden if name is None else kept[name] for name in order],
        lengths, owners, kept["total_self"], kept["total_cross"], kept["gain_feed"], kept["stats"],
    )
    return dict(zip(outs, values))


def general_grads(
    hidden,
    features,
    caption_lengths,
    caption_image,
    out_grad,
    attn_project,
    attn_output,
    cross_query,
    cross_vision,
    feed_expand,
    feed_reduce,
    norm_gains,
):
    stream = lax.axis_index("stream")
    full_project, full_output, full_query, full_vision, full_expand, full_reduce, full_gains = (
        lax.all_gather(to_half(attn_project), "dp", axis=1, tiled=True),
        lax.all_gather(to_half(attn_output), "dp", axis=1, tiled=True),
        lax.all_gather(to_half(cross_query), "dp", axis=0, tiled=True),
        lax.all_gather(to_half(cross_vision), "dp", axis=1, tiled=True),
        lax.all_gather(to_half(feed_expand), "dp", axis=1, tiled=True),
        lax.all_gather(to_half(feed_reduce), "dp", axis=1, tiled=True),
        lax.all_gather(to_half(norm_gains), "dp", axis=1, tiled=True),
    )
    gain_rows = full_gains.astype(jnp.float32)
    gain_self = gain_rows[0]
    gain_cross = gain_rows[1]
    gain_feed = lax.dynamic_index_in_dim(gain_rows, 2 + stream, 0, keepdims=False)
    source = hidden[0]
    row_count = source.shape[0]
    feature_width = source.shape[1]
    image_count = features.shape[0]
    query_allow, text_allow = layout(caption_lengths[0], caption_image[0], row_count, NQ)
    normed_self = to_half(norm_rows(source, gain_self))
    query_half = to_half(product(normed_self, full_project[0]))
    key_half = to_half(product(normed_self, full_project[1]))
    value_half = to_half(product(normed_self, full_project[2]))
    empty_half = jnp.zeros((row_count, feature_width), jnp.bfloat16)
    far_key, far_value = shifted((key_half, value_half), "stream", 1)
    text_keys = jnp.concatenate([far_key, key_half], axis=0)
    text_values = jnp.concatenate([far_value, value_half], axis=0)

    def self_query():
        return attend(query_half[None], key_half[None], value_half[None], query_allow[None])

    def self_text():
        return attend(query_half[None], text_keys[None], text_values[None], text_allow[None])

    context_self, total_self = lax.cond(stream == 0, self_query, self_text)
    context_half = to_half(context_self[0])
    branch_self = product(context_half, full_output[0])
    after_self = source + branch_self

    def cross_on():
        normed_cross = to_half(norm_rows(after_self, gain_cross))
        cross_half = to_half(product(normed_cross, full_query))
        vision_pair = project_vision(features, full_vision)
        context_cross, total_cross = attend(
            cross_half.reshape(image_count, NQ, feature_width), vision_pair[0], vision_pair[1], None
        )
        context_cross_half = to_half(context_cross.reshape(row_count, feature_width))
        branch = product(context_cross_half, full_output[1])
        return (branch, total_cross, vision_pair, normed_cross, cross_half, context_cross_half)

    def cross_off():
        return (
            jnp.zeros((row_count, feature_width), jnp.float32),
            jnp.zeros((image_count, HEADS, NQ), jnp.float32),
            jnp.zeros((2, image_count, features.shape[1], feature_width), jnp.bfloat16),
            empty_half,
            empty_half,
            empty_half,
        )

    branch_cross, total_cross, vision_pair, normed_cross, cross_half, context_cross_half = lax.cond(
        stream == 0, cross_on, cross_off
    )
    after_cross = after_self + branch_cross
    normed_feed = to_half(norm_rows(after_cross, gain_feed))
    before = right_product(normed_feed, full_expand[0])
    active_half = to_half(exact_gelu(before))
    branch_feed = product(active_half, full_reduce[0])
    result = after_cross + branch_feed
    grad_result = out_grad[0]
    grad_feed_half = to_half(grad_result)
    grad_reduce = left_product(active_half, grad_feed_half)
    grad_active = right_product(grad_feed_half, full_reduce[0])
    grad_before = to_half(jax.vjp(exact_gelu, before)[1](grad_active)[0])
    grad_expand = left_product(grad_before, normed_feed)
    grad_normed_feed = product(grad_before, full_expand[0])
    feed_in, grad_gain_feed = jax.vjp(norm_rows, after_cross, gain_feed)[1](grad_normed_feed)
    grad_cross = grad_result + feed_in

    def cross_back_on():
        grad_branch_half = to_half(grad_cross)
        grad_out_cross = left_product(context_cross_half, grad_branch_half)
        grad_context = to_half(right_product(grad_branch_half, full_output[1]))
        grad_cq, grad_ck, grad_cv = attend_back(
            cross_half.reshape(image_count, NQ, feature_width),
            vision_pair[0],
            vision_pair[1],
            None,
            total_cross,
            grad_context.reshape(image_count, NQ, feature_width),
        )
        grad_cq_half = to_half(grad_cq.reshape(row_count, feature_width))
        grad_pair = to_half(jnp.stack([grad_ck, grad_cv]))
        grad_cross_weight = left_product(normed_cross, grad_cq_half)
        grad_normed_cross = right_product(grad_cq_half, full_query)
        cross_in, grad_gain_cross = jax.vjp(norm_rows, after_self, gain_cross)[1](grad_normed_cross)
        vision_term = vision_grad(features, grad_pair)
        return (cross_in, grad_gain_cross, grad_out_cross, grad_cross_weight, vision_term)

    def cross_back_off():
        square_zero = jnp.zeros((feature_width, feature_width), jnp.float32)
        vision_term = jnp.zeros((2, features.shape[2], feature_width), jnp.float32)
        return (
            jnp.zeros((row_count, feature_width), jnp.float32),
            jnp.zeros((feature_width,), jnp.float32),
            square_zero,
            square_zero,
            vision_term,
        )

    cross_in, grad_gain_cross, grad_out_cross, grad_cross_weight, vision_term = lax.cond(
        stream == 0, cross_back_on, cross_back_off
    )
    grad_after_self = grad_cross + cross_in
    grad_branch_half = to_half(grad_after_self)
    grad_out_self = left_product(context_half, grad_branch_half)
    grad_context_self = to_half(right_product(grad_branch_half, full_output[0]))

    def self_back_query():
        grad_sq, grad_sk, grad_sv = attend_back(
            query_half[None],
            key_half[None],
            value_half[None],
            query_allow[None],
            total_self,
            grad_context_self[None],
        )
        empty_rows = jnp.zeros((row_count, feature_width), jnp.float32)
        return (grad_sq[0], grad_sk[0], grad_sv[0], empty_rows, empty_rows)

    def self_back_text():
        grad_sq, grad_sk, grad_sv = attend_back(
            query_half[None],
            text_keys[None],
            text_values[None],
            text_allow[None],
            total_self,
            grad_context_self[None],
        )
        return (
            grad_sq[0],
            grad_sk[0, row_count:],
            grad_sv[0, row_count:],
            grad_sk[0, :row_count],
            grad_sv[0, :row_count],
        )

    own_query, own_key, own_value, far_grad_key, far_grad_value = lax.cond(
        stream == 0, self_back_query, self_back_text
    )
    own_query = to_half(own_query)
    own_key = to_half(own_key)
    own_value = to_half(own_value)
    far_key_half = to_half(far_grad_key)
    far_value_half = to_half(far_grad_value)
    grad_normed = (
        right_product(own_query, full_project[0])
        + right_product(own_key, full_project[1])
        + right_product(own_value, full_project[2])
    )
    grad_key_weight = left_product(normed_self, own_key)
    grad_value_weight = left_product(normed_self, own_value)
    back_key, back_value = shifted((far_key_half, far_value_half), "stream", -1)
    grad_normed = (
        grad_normed
        + right_product(back_key, full_project[1])
        + right_product(back_value, full_project[2])
    )
    grad_key_weight = grad_key_weight + left_product(normed_self, back_key)
    grad_value_weight = grad_value_weight + left_product(normed_self, back_value)
    grad_project = jnp.stack(
        [left_product(normed_self, own_query), grad_key_weight, grad_value_weight]
    )
    source_in, grad_gain_self = jax.vjp(norm_rows, source, gain_self)[1](grad_normed)
    hidden_grad = grad_after_self + source_in
    zero_row = jnp.zeros_like(grad_gain_feed)
    gain_grads = jnp.stack(
        [
            grad_gain_self,
            grad_gain_cross,
            jnp.where(stream == 0, grad_gain_feed, zero_row),
            jnp.where(stream == 1, grad_gain_feed, zero_row),
        ]
    )
    shared_grads = (
        grad_project,
        jnp.stack([grad_out_self, grad_out_cross]),
        grad_cross_weight,
        vision_term,
        gain_grads,
    )
    (
        parts_project,
        parts_output,
        parts_query,
        parts_vision,
        parts_expand,
        parts_reduce,
        parts_gains,
    ) = (
        lax.psum_scatter(shared_grads[0], "dp", scatter_dimension=1, tiled=True),
        lax.psum_scatter(shared_grads[1], "dp", scatter_dimension=1, tiled=True),
        lax.psum_scatter(shared_grads[2], "dp", scatter_dimension=0, tiled=True),
        lax.psum_scatter(shared_grads[3], "dp", scatter_dimension=1, tiled=True),
        lax.psum_scatter(grad_expand[None], "dp", scatter_dimension=1, tiled=True),
        lax.psum_scatter(grad_reduce[None], "dp", scatter_dimension=1, tiled=True),
        lax.psum_scatter(shared_grads[4], "dp", scatter_dimension=1, tiled=True),
    )
    sum_project, sum_output, sum_query, sum_vision, sum_gains = (
        lax.psum(parts_project.astype(jnp.bfloat16), "stream").astype(jnp.float32),
        lax.psum(parts_output.astype(jnp.bfloat16), "stream").astype(jnp.float32),
        lax.psum(parts_query.astype(jnp.bfloat16), "stream").astype(jnp.float32),
        lax.psum(parts_vision.astype(jnp.bfloat16), "stream").astype(jnp.float32),
        lax.psum(parts_gains.astype(jnp.bfloat16), "stream").astype(jnp.float32),
    )
    shared_square = (
        jnp.sum(sum_project * sum_project)
        + jnp.sum(sum_output * sum_output)
        + jnp.sum(sum_query * sum_query)
        + jnp.sum(sum_vision * sum_vision)
        + jnp.sum(sum_gains * sum_gains)
    )
    local_square = (
        0.5 * shared_square
        + jnp.sum(parts_expand * parts_expand)
        + jnp.sum(parts_reduce * parts_reduce)
    )
    stat_row = jnp.stack(
        [
            square_rows(source),
            square_rows(branch_self),
            square_rows(branch_feed),
            square_rows(result),
        ]
    )
    stat_local = jnp.where(
        jnp.arange(2, dtype=jnp.int32)[:, None] == stream, stat_row[None, :], 0.0
    )
    total_square, stat_sums = lax.psum((local_square, stat_local), ("stream", "dp"))
    return (
        result, hidden_grad, total_square, stat_sums, parts_expand, parts_reduce,
        (sum_project, sum_output, sum_query, sum_vision, sum_gains),
    )


def direct_grads(
    hidden,
    features,
    caption_lengths,
    caption_image,
    out_grad,
    attn_project,
    attn_output,
    cross_query,
    cross_vision,
    feed_expand,
    feed_reduce,
    norm_gains,
):
    stream = lax.axis_index("stream")
    width = attn_project.shape[-1]
    row_count = hidden.shape[1]
    first = to_half(
        jnp.where(
            stream == 0,
            jnp.stack([attn_project[0], attn_project[1], attn_output[1]]),
            jnp.stack([attn_project[2], attn_output[0], cross_query]),
        )
    )
    vision = to_half(lax.dynamic_index_in_dim(cross_vision, stream, 0, keepdims=False))
    gains = jnp.pad(to_half(norm_gains), ((0, 12), (0, 128 - norm_gains.shape[1])))
    kept = forward_all(
        first, vision, to_half(feed_expand[0]), to_half(feed_reduce[0]), gains,
        hidden[0], out_grad[0], features, caption_lengths, caption_image,
    )
    back = backward_all(kept, hidden[0], caption_lengths, caption_image, features.shape[1])
    sum_first, sum_vision, gain_sums, totals = (
        back[name] for name in ("first", "vision", "gains", "totals")
    )
    own_gains = norm_gains.shape[1]
    begin = lax.axis_index("dp") * own_gains
    sum_gains = lax.dynamic_slice_in_dim(gain_sums[:4], begin, own_gains, axis=1)
    total_square = jnp.sum(totals[:8])
    stat_sums = jnp.sum(totals[8:], axis=1).reshape(2, 4) / width
    return (
        kept["result"], back["hidden_grad"], total_square, stat_sums,
        back["expand"][None], back["reduce"][None],
        (
            jnp.stack([sum_first[0, 0], sum_first[0, 1], sum_first[1, 0]]),
            jnp.stack([sum_first[1, 1], sum_first[0, 2]]),
            sum_first[1, 2], sum_vision, sum_gains,
        ),
    )


def body(
    hidden,
    features,
    caption_lengths,
    caption_image,
    out_grad,
    attn_project,
    attn_output,
    cross_query,
    cross_vision,
    feed_expand,
    feed_reduce,
    norm_gains,
    first_project,
    second_project,
    first_output,
    second_output,
    first_query,
    second_query,
    first_vision,
    second_vision,
    first_expand,
    second_expand,
    first_reduce,
    second_reduce,
    first_gains,
    second_gains,
):
    grads = direct_grads if lax.axis_size("dp") == 16 else general_grads
    row_count = hidden.shape[1]
    result, hidden_grad, total_square, stat_sums, parts_expand, parts_reduce, shared = grads(
        hidden, features, caption_lengths, caption_image, out_grad, attn_project,
        attn_output, cross_query, cross_vision, feed_expand, feed_reduce, norm_gains,
    )
    sum_project, sum_output, sum_query, sum_vision, sum_gains = shared
    grad_norm = jnp.sqrt(total_square)
    rms_values = jnp.sqrt(stat_sums / (row_count * lax.axis_size("dp")))
    factor = clip_norm / jnp.maximum(grad_norm, clip_norm)
    clipped_gains = sum_gains * factor
    fresh_expand, mean_expand, square_expand = adam_step(
        feed_expand, parts_expand, first_expand, second_expand, factor, rate_matrix, decay_rate
    )
    fresh_reduce, mean_reduce, square_reduce = adam_step(
        feed_reduce, parts_reduce, first_reduce, second_reduce, factor, rate_matrix, decay_rate
    )
    weights_shared = (attn_project, attn_output, cross_query, cross_vision, norm_gains)
    firsts_shared = (first_project, first_output, first_query, first_vision, first_gains)
    seconds_shared = (second_project, second_output, second_query, second_vision, second_gains)
    summed_shared = (sum_project, sum_output, sum_query, sum_vision, sum_gains)
    updated = []
    for index in range(5):
        rate = rate_gains if index == 4 else rate_matrix
        decay = 0.0 if index == 4 else decay_rate
        weight = weights_shared[index]
        first = firsts_shared[index]
        second = seconds_shared[index]
        updated.append(adam_step(weight, summed_shared[index], first, second, factor, rate, decay))
    fresh_project, mean_project, square_project = updated[0]
    fresh_output, mean_output, square_output = updated[1]
    fresh_query, mean_query, square_query = updated[2]
    fresh_vision, mean_vision, square_vision = updated[3]
    fresh_gains, mean_gains, square_gains = updated[4]
    return (
        result[None],
        hidden_grad[None],
        grad_norm,
        rms_values,
        fresh_project,
        mean_project,
        square_project,
        fresh_output,
        mean_output,
        square_output,
        fresh_query,
        mean_query,
        square_query,
        fresh_vision,
        mean_vision,
        square_vision,
        fresh_expand,
        mean_expand,
        square_expand,
        fresh_reduce,
        mean_reduce,
        square_reduce,
        fresh_gains,
        mean_gains,
        square_gains,
        clipped_gains,
        to_half(fresh_project),
        to_half(fresh_output),
        to_half(fresh_query),
        to_half(fresh_vision),
        to_half(fresh_expand),
        to_half(fresh_reduce),
    )


def solution(mesh):
    return jax.shard_map(
        body,
        mesh=mesh,
        in_specs=(
            P("stream", "dp", None),
            P("dp", None, None),
            P("dp", None),
            P("dp", None),
            P("stream", "dp", None),
            P(None, "dp", None),
            P(None, "dp", None),
            P("dp", None),
            P(None, "dp", None),
            P("stream", "dp", None),
            P("stream", "dp", None),
            P(None, "dp"),
            P(None, "dp", None),
            P(None, "dp", None),
            P(None, "dp", None),
            P(None, "dp", None),
            P("dp", None),
            P("dp", None),
            P(None, "dp", None),
            P(None, "dp", None),
            P("stream", "dp", None),
            P("stream", "dp", None),
            P("stream", "dp", None),
            P("stream", "dp", None),
            P(None, "dp"),
            P(None, "dp"),
        ),
        out_specs=(
            P("stream", "dp", None),
            P("stream", "dp", None),
            P(),
            P(),
            P(None, "dp", None),
            P(None, "dp", None),
            P(None, "dp", None),
            P(None, "dp", None),
            P(None, "dp", None),
            P(None, "dp", None),
            P("dp", None),
            P("dp", None),
            P("dp", None),
            P(None, "dp", None),
            P(None, "dp", None),
            P(None, "dp", None),
            P("stream", "dp", None),
            P("stream", "dp", None),
            P("stream", "dp", None),
            P("stream", "dp", None),
            P("stream", "dp", None),
            P("stream", "dp", None),
            P(None, "dp"),
            P(None, "dp"),
            P(None, "dp"),
            P(None, "dp"),
            P(None, "dp", None),
            P(None, "dp", None),
            P("dp", None),
            P(None, "dp", None),
            P("stream", "dp", None),
            P("stream", "dp", None),
        ),
        check_vma=False,
    )
```

```python
import functools

import jax
import jax.numpy as jnp
from jax import lax
from jax.experimental import pallas as pl
from jax.experimental.pallas import tpu as pltpu
from jax.sharding import PartitionSpec as P

HEADS = 12
HD = 64
NQ = 32
STEP = 10


epsilon = 1e-06
masked_value = -1e30
beta_first = 0.9
beta_second = 0.999
rate_matrix = 0.05
rate_gains = 1.0
decay_rate = 0.01
adam_floor = 1e-08
clip_norm = 1.0


def shifted(block, axis, distance):
    devices = range(lax.axis_size(axis))
    route = [(i - distance, i) for i in devices if i - distance in devices]
    return lax.ppermute(block, axis, route)


def to_half(values):
    return values.astype(jnp.bfloat16)


def product(left, right):
    return jnp.dot(left, right, preferred_element_type=jnp.float32)


def left_product(left, right):
    return lax.dot_general(
        left, right, (((0,), (0,)), ((), ())), preferred_element_type=jnp.float32
    )


def right_product(left, right):
    return lax.dot_general(
        left, right, (((1,), (1,)), ((), ())), preferred_element_type=jnp.float32
    )


def norm_rows(values, gain):
    return values * lax.rsqrt(jnp.mean(values * values, axis=-1, keepdims=True) + epsilon) * gain


def exact_gelu(values):
    return jax.nn.gelu(values, approximate=False)


def square_rows(values):
    return jnp.sum(jnp.mean(values * values, axis=-1))


def layout(lengths, owners, row_count, per_image):
    caption_ends = jnp.cumsum(lengths)
    caption_starts = caption_ends - lengths
    row_index = jnp.arange(row_count, dtype=jnp.int32)
    inside = (row_index[:, None] >= caption_starts[None, :]) & (
        row_index[:, None] < caption_ends[None, :]
    )
    caption = jnp.sum(
        jnp.where(inside, jnp.arange(lengths.shape[0], dtype=jnp.int32)[None, :], 0), axis=1
    )
    text_image = jnp.sum(jnp.where(inside, owners[None, :], 0), axis=1)
    query_image = row_index // per_image
    query_allow = query_image[:, None] == query_image[None, :]
    own_caption = (caption[:, None] == caption[None, :]) & (
        row_index[None, :] <= row_index[:, None]
    )
    text_allow = jnp.concatenate([text_image[:, None] == query_image[None, :], own_caption], axis=1)
    return (query_allow, text_allow)


def attention_scores(query_rows, key_rows, allowed):
    batch_count, query_count, width_all = query_rows.shape
    query_heads = query_rows.reshape(batch_count, query_count, HEADS, HD)
    key_heads = key_rows.reshape(batch_count, key_rows.shape[1], HEADS, HD)
    scores = jnp.einsum(
        "bqhd,bkhd->bhqk", query_heads, key_heads, preferred_element_type=jnp.float32
    ) * HD ** (-0.5)
    if allowed is not None:
        scores = jnp.where(allowed[:, None], scores, masked_value)
    return (scores, query_heads, key_heads)


def attend(query_rows, key_rows, value_rows, allowed):
    scores, query_heads, key_heads = attention_scores(query_rows, key_rows, allowed)
    value_heads = value_rows.reshape(key_heads.shape)
    row_max = jnp.max(scores, axis=-1, keepdims=True)
    weights = jnp.exp(scores - row_max)
    denominator = jnp.sum(weights, axis=-1, keepdims=True)
    probability = to_half(weights / denominator)
    context = jnp.einsum(
        "bhqk,bkhd->bqhd", probability, value_heads, preferred_element_type=jnp.float32
    )
    return (context.reshape(query_rows.shape), (row_max + jnp.log(denominator))[..., 0])


def attend_back(query_rows, key_rows, value_rows, allowed, log_total, grad_context):
    scores, query_heads, key_heads = attention_scores(query_rows, key_rows, allowed)
    value_heads = value_rows.reshape(key_heads.shape)
    probability = jnp.exp(scores - log_total[..., None])
    grad_heads = grad_context.reshape(query_heads.shape)
    grad_prob = jnp.einsum(
        "bqhd,bkhd->bhqk", grad_heads, value_heads, preferred_element_type=jnp.float32
    )
    grad_value = jnp.einsum(
        "bhqk,bqhd->bkhd", to_half(probability), grad_heads, preferred_element_type=jnp.float32
    )
    grad_score = to_half(
        probability * (grad_prob - jnp.sum(grad_prob * probability, axis=-1, keepdims=True))
    )
    grad_query = jnp.einsum(
        "bhqk,bkhd->bqhd", grad_score, key_heads, preferred_element_type=jnp.float32
    ) * HD ** (-0.5)
    grad_key = jnp.einsum(
        "bhqk,bqhd->bkhd", grad_score, query_heads, preferred_element_type=jnp.float32
    ) * HD ** (-0.5)
    return (
        grad_query.reshape(query_rows.shape),
        grad_key.reshape(key_rows.shape),
        grad_value.reshape(value_rows.shape),
    )


def project_vision(feature_block, vision_weights):
    return to_half(
        jnp.einsum(
            "inv,kvd->kind", feature_block, vision_weights, preferred_element_type=jnp.float32
        )
    )


def vision_grad(feature_block, grad_pair):
    return jnp.einsum("inv,kind->kvd", feature_block, grad_pair, preferred_element_type=jnp.float32)


def adam_step(weight, gradient, first, second, factor, rate, decay):
    clipped = gradient * factor
    mean_new = beta_first * first + (1.0 - beta_first) * clipped
    square_new = beta_second * second + (1.0 - beta_second) * clipped * clipped
    corrected_mean = mean_new / (1.0 - beta_first**STEP)
    corrected_square = square_new / (1.0 - beta_second**STEP)
    fresh = weight - rate * (
        corrected_mean / (jnp.sqrt(corrected_square) + adam_floor) + decay * weight
    )
    return (fresh, mean_new, square_new)


MESH = pl.DeviceIdType.MESH
VMEM_LIMIT = 62 * 2**20


def coordinates():
    c = lax.axis_index("stream")
    d = lax.axis_index("dp")
    return c, d // 4, (d // 2) % 2, d % 2


def device(c, z, y, x):
    return (c, z * 4 + y * 2 + x)


def meet(c, z, y, x, layer=False):
    barrier = pltpu.get_barrier_semaphore()
    others = [device(1 - c, z, y, x), device(c, z, 1 - y, x), device(c, z, y, 1 - x)]
    others += [device(c, (z + k) % 4, y, x) for k in (1, 2, 3)]
    if layer:
        others += [device(1 - c, z, 1 - y, x), device(1 - c, z, y, 1 - x)]
        others += [device(c, z, 1 - y, 1 - x), device(1 - c, z, 1 - y, 1 - x)]
    for other in others:
        pl.semaphore_signal(barrier, inc=1, device_id=other, device_id_type=MESH)
    pl.semaphore_wait(barrier, len(others))


ORDERS = {
    ("late", 0): ("z", "y", "x"),
    ("late", 1): ("z", "x", "y"),
    ("early", 0): ("x", "z", "y"),
    ("early", 1): ("y", "z", "x"),
    ("feed", 0): ("z", "o"),
    ("feed", 1): ("z", "o"),
}


PARTS = 2
GATHER_TICKS = [(0, 3, 6, 9), (2, 5, 8, 11), (4, 7, 10, 13), (6, 9, 12, 15), (8, 11, 14, 17)]
GATHER_TICKS += [(10, 17, 24), (12, 18, 24), (14, 21, 24), (16, 23, 24)]
PLANES = {
    "query": (0, 0), "key": (0, 1), "cross_output": (0, 2),
    "value": (1, 0), "self_output": (1, 1), "cross_query": (1, 2),
}


def wide(block):
    return block.astype(jnp.float32)


def nn(left, right):
    return lax.dot_general(
        left, right, (((1,), (0,)), ((), ())), preferred_element_type=jnp.float32
    )


def nt(left, right):
    return lax.dot_general(
        left, right, (((1,), (1,)), ((), ())), preferred_element_type=jnp.float32
    )


def tn(left, right):
    return lax.dot_general(
        left, right, (((0,), (0,)), ((), ())), preferred_element_type=jnp.float32
    )


def span(index, size):
    return pl.ds(pl.multiple_of(index * size, size), size)


def loop(count, step):
    def body(index, carry):
        step(index)
        return carry

    lax.fori_loop(0, count, body, 0)


def row_sum(values):
    return jnp.sum(values, axis=0, keepdims=True)


def norm_back(values, gain, grad):
    scale = lax.rsqrt(jnp.mean(values * values, axis=-1, keepdims=True) + epsilon)
    unit = values * scale
    grad_unit = grad * gain
    mean = jnp.mean(grad_unit * unit, axis=-1, keepdims=True)
    return scale * (grad_unit - unit * mean), row_sum(grad * unit)


def lane_masks(rows):
    lane = lax.broadcasted_iota(jnp.int32, (rows, 2 * HD), 1)
    left = jnp.where(lane < HD, 1.0, 0.0)
    return to_half(left), to_half(1.0 - left)


def head_pair(block, masks):
    return jnp.concatenate([block * masks[0], block * masks[1]], axis=0)


def pair_join(both):
    rows = both.shape[0] // 2
    lane = lax.broadcasted_iota(jnp.int32, (rows, 2 * HD), 1)
    return jnp.where(lane < HD, both[:rows], both[rows:])


def diagonal(full, rows):
    lane = lax.broadcasted_iota(jnp.int32, (rows, 2 * HD), 1)
    tiles = []
    for t in range(HEADS // 2):
        tile = full[:, t * 2 * HD : (t + 1) * 2 * HD]
        left = tile[2 * t * rows : (2 * t + 1) * rows]
        right = tile[(2 * t + 1) * rows : (2 * t + 2) * rows]
        tiles.append(jnp.where(lane < HD, left, right))
    return jnp.concatenate(tiles, axis=1)


def head_mask(rows, width):
    row = lax.broadcasted_iota(jnp.int32, (HEADS * rows, width), 0) // rows
    lane = lax.broadcasted_iota(jnp.int32, (HEADS * rows, width), 1) // HD
    return to_half(jnp.where(row == lane, 1.0, 0.0))


def caption_layout(lengths, owners, row_count):
    count = lengths.shape[1]
    size = wide(lengths)
    owner = wide(owners)
    sub = lax.broadcasted_iota(jnp.int32, (count, count), 0)
    lane = lax.broadcasted_iota(jnp.int32, (count, count), 1)
    starts = jnp.sum(jnp.where(lane < sub, size, 0.0), axis=1, keepdims=True)
    owner_down = jnp.sum(jnp.where(lane == sub, owner, 0.0), axis=1, keepdims=True)
    row = wide(lax.broadcasted_iota(jnp.int32, (count, row_count), 1))
    begun = starts <= row
    start = jnp.max(jnp.where(begun, starts, 0.0), axis=0, keepdims=True)
    image = jnp.max(jnp.where(begun, owner_down, 0.0), axis=0, keepdims=True)
    return start, image


def text_bias(rb, start, image, far_rows, window, bias):
    begin = jnp.maximum(rb - 1, 0) * 128
    far = lax.broadcasted_iota(jnp.int32, (far_rows, 128), 0) // NQ
    far_bias = jnp.where(wide(far) == image, 0.0, masked_value)
    key = lax.broadcasted_iota(jnp.int32, (window, 128), 0) + begin
    row = lax.broadcasted_iota(jnp.int32, (window, 128), 1) + rb * 128
    seen = (wide(key) >= start) & (key <= row)
    own_bias = jnp.where(seen, 0.0, masked_value)
    bias[0:far_rows] = jnp.concatenate([far_bias, far_bias], axis=1)
    bias[far_rows : far_rows + window] = jnp.concatenate([own_bias, own_bias], axis=1)


def query_bias(bias):
    key = lax.broadcasted_iota(jnp.int32, (128, 256), 0) // NQ
    row = (lax.broadcasted_iota(jnp.int32, (128, 256), 1) % 128) // NQ
    bias[0:128] = jnp.where(key == row, 0.0, masked_value)


def forward_kernel(
    attn_project, attn_output, cross_query_weight, cross_vision, feed_expand, feed_reduce, gains,
    hidden_in, out_grad_in, features, lengths, owners,
    out_result, out_grad_cross, part_expand, part_reduce, gain_feed_out, stats,
    keep_first, keep_gains, keep_normed, keep_query, keep_key, keep_value, keep_far_key, keep_far_value,
    keep_context, keep_after_self, keep_cross_query, keep_cross_context, keep_vision, keep_images, total_self, total_cross,
    all_first, raw_vision, all_vision, all_expand, all_reduce, all_gains, gain_rows,
    hidden, out_grad, images, vision_pair, normed, query, key, value, far_key, far_value, context, after_self,
    cross_query, cross_context, after_cross, normed_feed, grad_feed, sum_branch, sum_normed, got_normed, got_branch, bias, mask,
    first, vision, expand, reduce, layout_rows, send_sem, recv_sem, local_sem,
):
    c, z, y, x = coordinates()
    row_count, width = hidden.shape
    image_count = total_cross.shape[0]
    padded = vision_pair.shape[0] // image_count
    feature_rows = features.shape[0] // (2 * image_count)
    feature_width = features.shape[1]
    part_rows = expand.shape[0] // PARTS
    far_rows, window = far_key.shape[0], 256
    cross_rows = image_count * NQ

    across_at = jnp.where(c == 0, y, x)
    own_at = {"z": z, "y": y, "x": x, "o": across_at}
    mate = (c, z * 4 + jnp.where(c == 0, y, 1 - y) * 2 + jnp.where(c == 0, 1 - x, x))
    beyond = (c, z * 4 + jnp.where(c == 0, 1 - y, y) * 2 + jnp.where(c == 0, x, 1 - x))

    chunks = [(gains, lambda *at: all_gains.at[at], "late", False)]
    chunks.append((vision, lambda *at: raw_vision.at[(c,) + at], "late", True))
    for j in range(3):
        chunks.append((first.at[j], lambda *at, j=j: all_first.at[(c, j) + at], "late", True))
    for p in range(PARTS):
        rows = pl.ds(p * part_rows, part_rows)
        for source, whole in ((expand, all_expand), (reduce, all_reduce)):
            target = lambda *at, p=p, whole=whole: whole.at[(p,) + at]
            chunks.append((source.at[rows], target, "feed", False))
    count = len(chunks)
    events = [
        (when, -stage, number)
        for number, times in enumerate(GATHER_TICKS)
        for stage, when in enumerate(times)
    ]
    last_tick = max(events)[0]

    def axes_of(number):
        return "zo" if chunks[number][2] == "feed" else "zyx"

    def stages_of(number):
        return 2 if chunks[number][2] == "feed" else 3

    def remote(source, target, index, where):
        return pltpu.make_async_remote_copy(
            src_ref=source, dst_ref=target, send_sem=send_sem.at[index],
            recv_sem=recv_sem.at[index], device_id=where, device_id_type=MESH,
        )

    def sends(number, stage, core):
        source, target, kind = chunks[number][:3]
        order = ORDERS[kind, core]
        done, axis = order[:stage], order[stage]
        at = tuple(slice(None) if a in done else own_at[a] for a in axes_of(number))
        block = target(*at)
        here = source if stage == 0 else block
        base = (number * 3 + stage) * 3
        if axis == "z":
            return [
                remote(here, block, base + k - 1, device(c, (z + k) % 4, y, x)) for k in (1, 2, 3)
            ]
        where = {"y": device(c, z, 1 - y, x), "x": device(c, z, y, 1 - x), "o": beyond}[axis]
        return [remote(here, block, base, where)]

    def place(number):
        source, target = chunks[number][:2]
        at = [own_at[a] for a in axes_of(number)]
        return pltpu.make_async_copy(source, target(*at), local_sem.at[number])

    pair = device(1 - c, z, y, x)

    def across(number):
        target = chunks[number][1]
        block = target(slice(None), slice(None), slice(None))
        return remote(block, block, count * 9 + number, pair)

    def tick_core(tick, core):
        for when, negative, number in sorted(events):
            stage = -negative
            if when != tick:
                continue
            if stage > 0:
                for copy in sends(number, stage - 1, core):
                    copy.wait_recv()
            if stage == 1:
                place(number).wait()
            if stage < stages_of(number):
                for copy in sends(number, stage, core):
                    copy.start()
                if stage == 0:
                    place(number).start()
            elif chunks[number][3]:
                across(number).start()

    def both(step):
        @pl.when(c == 0)
        def _():
            step(0)

        @pl.when(c == 1)
        def _():
            step(1)

    def tick(number):
        both(lambda core: tick_core(number, core))

    def sent(number):
        def step(core):
            for stage in range(stages_of(number)):
                for copy in sends(number, stage, core):
                    copy.wait_send()

        both(step)

    swap_base = count * 10
    near_rows, far_away = pl.ds(0, row_count), pl.ds(row_count, row_count)
    active, grad_before = vision_pair.at[pl.ds(0, 2 * row_count)], vision_pair.at[pl.ds(2 * row_count, 2 * row_count)]
    send_normed = images.at[pl.ds(0, row_count), pl.ds(0, width)]
    send_branch = images.at[pl.ds(row_count, row_count), pl.ds(0, width)]
    swaps = {
        "key": (key, far_key),
        "value": (value, far_value),
        "query": (cross_query.at[pl.ds(cross_rows, cross_rows)], cross_query.at[pl.ds(0, cross_rows)]),
        "context": (cross_context.at[pl.ds(0, cross_rows)], cross_context.at[pl.ds(cross_rows, cross_rows)]),
        "grad_feed": (grad_feed.at[near_rows], grad_feed.at[far_away]),
        "normed_feed": (normed_feed.at[near_rows], normed_feed.at[far_away]),
        "sum_normed": (send_normed, got_normed),
        "sum_branch": (send_branch, got_branch),
    }
    with_mate = ("grad_feed", "normed_feed", "sum_normed", "sum_branch")

    def swap(name):
        source, target = swaps[name]
        where = mate if name in with_mate else pair
        return remote(source, target, swap_base + list(swaps).index(name), where)

    local_base = count
    loads = [
        (hidden_in, hidden),
        (out_grad_in, out_grad),
    ]
    step_rows = 2 * image_count * 32
    whole_steps = feature_rows // 32
    half_rows = whole_steps // 2 * step_rows
    for begin, size in ((0, half_rows), (half_rows, features.shape[0] - half_rows)):
        staged = vision_pair.at[pl.ds(0, size), pl.ds(0, feature_width)]
        loads.append((features.at[pl.ds(begin, size)], staged))
    keeps = {
        "first": (all_first, keep_first),
        "gains": (gain_rows, keep_gains),
        "normed": (normed, keep_normed),
        "query": (query, keep_query),
        "key": (key, keep_key),
        "value": (value, keep_value),
        "far_key": (far_key, keep_far_key),
        "far_value": (far_value, keep_far_value),
        "context": (context, keep_context),
        "after_self": (after_self, keep_after_self),
        "cross_query": (cross_query.at[pl.ds(0, cross_rows)], keep_cross_query),
        "cross_context": (cross_context, keep_cross_context),
        "vision": (vision_pair, keep_vision),
        "images": (images, keep_images),
        "result": (sum_branch.at[pl.ds(0, row_count)], out_result),
        "grad_cross": (sum_normed.at[pl.ds(0, row_count)], out_grad_cross),
    }
    for p in range(PARTS):
        keeps["expand", p] = (all_expand.at[p], part_expand.at[p])
        keeps["reduce", p] = (all_reduce.at[p], part_reduce.at[p])

    shard_rows = first.shape[1]
    sources = {
        0: [attn_project.at[0], attn_project.at[1], attn_output.at[1]],
        1: [attn_project.at[2], attn_output.at[0], cross_query_weight],
    }
    shard_base = local_base + len(loads) + len(keeps)

    def shard_place(k):
        size = (shard_rows, shard_rows, shard_rows, vision.shape[0], expand.shape[0], reduce.shape[0])
        return pl.ds(sum(size[:k]), size[k])

    def shard_load(k, core):
        sources_now = sources[core] + [cross_vision.at[core], feed_expand, feed_reduce]
        target = sum_branch.at[shard_place(k)]
        return pltpu.make_async_copy(sources_now[k], target, local_sem.at[shard_base + k])

    def shard_start():
        both(lambda core: [shard_load(k, core).start() for k in range(6)] and None)

    def shard_round(k):
        both(lambda core: shard_load(k, core).wait())
        value = to_half(sum_branch[shard_place(k), :])
        if k < 3:
            first[k] = value
        else:
            (vision, expand, reduce)[k - 3][...] = value

    def load(k):
        source, target = loads[k]
        return pltpu.make_async_copy(source, target, local_sem.at[local_base + k])

    def keep(name):
        source, target = keeps[name]
        index = local_base + len(loads) + list(keeps).index(name)
        return pltpu.make_async_copy(source, target, local_sem.at[index])

    def weight(name):
        plane, j = PLANES[name]
        return all_first[plane, j].reshape(width, width)

    def gain(k):
        return gain_rows[pl.ds(k, 1), :]

    def stat(k, amount):
        row = pl.ds(c * 4 + k, 1)
        stats[row, :] = stats[row, :] + amount


    def start():
        stats[...] = jnp.zeros_like(stats)
        mask[...] = head_mask(NQ, width)
        first_row, image = caption_layout(lengths[...], owners[...], row_count)
        layout_rows[0:1] = first_row
        layout_rows[1:2] = image

    def read_gains():
        total = jnp.zeros(gain_rows.shape, jnp.float32)
        per = width // 16
        for k in range(16):
            lane = lax.broadcasted_iota(jnp.int32, (128, width), 0)
            column = lax.broadcasted_iota(jnp.int32, (128, width), 1)
            pick = to_half(jnp.where((column == lane + k * per) & (lane < per), 1.0, 0.0))
            total = total + nn(all_gains[k // 4, (k // 2) % 2, k % 2], pick)
        gain_rows[...] = total

    def self_in():
        def step(i):
            rows = span(i, 256)
            source = hidden[rows, :]
            stat(0, row_sum(source * source))
            part = to_half(norm_rows(source, gain(0)))
            normed[rows, :] = part
            query[rows, :] = to_half(nn(part, weight("query"))) * jnp.bfloat16(HD**-0.5)
            key[rows, :] = to_half(nn(part, weight("key")))
            value[rows, :] = to_half(nn(part, weight("value")))

        loop(row_count // 256, step)

    def attend_pair(rb, t, parts):
        lanes, rows = span(t, 128), span(rb, 128)
        queries = head_pair(query[rows, lanes], lane_masks(128))
        scores, most = [], None
        for keys, _, where, _ in parts:
            score = nt(keys, queries) + bias[where, :]
            scores.append(score)
            top = jnp.max(score, axis=0, keepdims=True)
            most = top if most is None else jnp.maximum(most, top)
        weights = [jnp.exp(score - most) for score in scores]
        total = sum(row_sum(part) for part in weights)
        inverse = 1.0 / total
        result = sum(
            tn(to_half(part * inverse), values) for part, (_, values, _, _) in zip(weights, parts)
        )
        context[rows, lanes] = to_half(pair_join(result))
        total_self[rb, t] = most + jnp.log(total)

    def self_query():
        query_bias(bias)

        def step(i):
            rb, t = i // 6, i % 6
            rows, lanes = span(rb, 128), span(t, 128)
            attend_pair(rb, t, [(key[rows, lanes], value[rows, lanes], pl.ds(0, 128), None)])

        loop(row_count // 128 * 6, step)

    def self_text(begin, end):
        def outer(rb):
            rb = rb + begin
            rows = span(rb, 128)
            text_bias(rb, layout_rows[0:1, rows], layout_rows[1:2, rows], far_rows, window, bias)
            near = pl.ds(pl.multiple_of(jnp.maximum(rb - 1, 0) * 128, 128), window)

            def inner(t):
                lanes = span(t, 128)
                attend_pair(rb, t, [
                    (far_key[:, lanes], far_value[:, lanes], pl.ds(0, far_rows), None),
                    (key[near, lanes], value[near, lanes], pl.ds(far_rows, window), None),
                ])

            loop(6, inner)

        loop(end - begin, outer)

    def self_out():
        def step(i):
            rows = span(i, 256)
            branch = nn(context[rows, :], weight("self_output"))
            stat(1, row_sum(branch * branch))
            after_self[rows, :] = hidden[rows, :] + branch

        loop(row_count // 256, step)

    def cross_in():
        def step(i):
            rows = span(i, 256)
            part = to_half(norm_rows(after_self[rows, :], gain(1)))
            result = to_half(nn(part, weight("cross_query"))) * jnp.bfloat16(HD**-0.5)
            cross_query[rows, :] = result

        loop(row_count // 256, step)

    def pack_vision():
        def step(i):
            plane, z_at, y_at = i // 8, (i // 2) % 4, i % 2
            left = wide(raw_vision[plane, z_at, y_at, 0])
            right = wide(raw_vision[plane, z_at, y_at, 1])
            size = 2 * left.shape[0]
            all_vision[plane, span(z_at * 2 + y_at, size), :] = to_half(
                jnp.concatenate([left, right], axis=0)
            )

        loop(16, step)

    def sort_rows(begin, rows, base):
        size = rows // (2 * image_count)
        block = max(size, 16)
        out = lax.broadcasted_iota(jnp.int32, (image_count * block, rows), 0)
        column = lax.broadcasted_iota(jnp.int32, (image_count * block, rows), 1)
        source = (out % block) * (2 * image_count) + c * image_count + out // block
        pick = to_half(jnp.where((column == source) & (out % block < size), 1.0, 0.0))
        sorted_rows = to_half(nn(pick, vision_pair[begin, 0:feature_width]))
        for j in range(image_count):
            where = pl.ds(pl.multiple_of(j * padded + base, 16), block)
            images[where, :] = sorted_rows[j * block : (j + 1) * block]

    def sort_images(part):
        def step(i):
            sort_rows(span(i, step_rows), step_rows, 32 * (i + part * (whole_steps // 2)))

        loop(whole_steps // 2, step)
        if part == 1:
            rest = feature_rows % 32 * 2 * image_count
            sort_rows(pl.ds(whole_steps // 2 * step_rows, rest), rest, whole_steps * 32)

    def project_images(begin, end):
        def step(i):
            rows = pl.ds(pl.multiple_of((i + begin) * padded, 16), padded)
            image = images[rows, :]
            vision_pair[rows, 0:width] = to_half(nn(image, all_vision[0]))
            vision_pair[rows, width : 2 * width] = to_half(nn(image, all_vision[1]))

        loop(end - begin, step)

    def cross_attend(begin, end):
        def step(i):
            i = i + begin
            rows = pl.ds(pl.multiple_of(i * padded, 16), padded)
            own_rows = span(i, NQ)
            part = cross_query[own_rows, :]
            queries = jnp.concatenate([part] * HEADS, axis=0) * mask[...]
            score = nt(vision_pair[rows, 0:width], queries)
            key_row = lax.broadcasted_iota(jnp.int32, score.shape, 0)
            score = jnp.where(key_row < feature_rows, score, masked_value)
            most = jnp.max(score, axis=0, keepdims=True)
            weights = jnp.exp(score - most)
            total = row_sum(weights)
            total_cross[i] = most + jnp.log(total)
            full = tn(to_half(weights * (1.0 / total)), vision_pair[rows, width : 2 * width])
            cross_context[own_rows, :] = to_half(diagonal(full, NQ))

        loop(end - begin, step)

    def cross_out():
        def step(i):
            rows = span(i, 256)
            after_cross[rows, :] = after_self[rows, :] + nn(cross_context[rows, :], weight("cross_output"))

        loop(row_count // 256, step)

    def round_out_grad():
        def step(i):
            rows = span(i, 128)
            grad_feed[rows, :] = to_half(out_grad[rows, :])

        loop(row_count // 128, step)

    def feed_in():
        def step(i):
            rows = span(i, 128)
            normed_feed[rows, :] = to_half(norm_rows(after_cross[rows, :], gain(2 + c)))

        loop(row_count // 128, step)

    half_parts = 2 * PARTS
    block = all_expand.shape[1] * all_expand.shape[2] * part_rows // 2

    def feed_weights(b):
        p, at = b // 2, pl.ds(all_expand.shape[1] // 2 * (b % 2), all_expand.shape[1] // 2)
        return p, at, all_expand[p, at].reshape(block, width), all_reduce[p, at].reshape(block, width)

    def feed_rows(side, b):
        rows = pl.ds(side * row_count, row_count)
        lanes = pl.ds(b * block, block)
        _, _, up, down = feed_weights(b)
        before = nt(normed_feed[rows, :], up)
        share = 0.5 * (1.0 + lax.erf(before * (0.5**0.5)))
        density = jnp.exp(before * before * -0.5) * (0.5 / jnp.pi) ** 0.5
        result = to_half(before * share)
        slope = share + before * density
        active[rows, lanes] = result
        total = nn(result, down)
        back = to_half(nt(grad_feed[rows, :], down) * slope)
        grad_before[rows, lanes] = back
        total_normed = nn(back, up)
        if b == 0:
            sum_branch[rows, :] = total
            sum_normed[rows, :] = total_normed
        else:
            sum_branch[rows, :] = sum_branch[rows, :] + total
            sum_normed[rows, :] = sum_normed[rows, :] + total_normed

    def feed_grads(b):
        lanes = pl.ds(b * block, block)
        p, at = b // 2, pl.ds(all_expand.shape[1] // 2 * (b % 2), all_expand.shape[1] // 2)
        shape = (all_expand.shape[1] // 2,) + all_expand.shape[2:]
        all_expand[p, at] = to_half(tn(grad_before[:, lanes], normed_feed[...])).reshape(shape)
        all_reduce[p, at] = to_half(tn(active[:, lanes], grad_feed[...])).reshape(shape)

    def send_partial(total, buffer, name):
        def step(i):
            rows = span(i, 128)
            buffer[rows, :] = to_half(total[pl.ds(pl.multiple_of(row_count + i * 128, 128), 128), :])

        loop(row_count // 128, step)
        swap(name).start()

    def feed_back():
        gain_feed_out[...] = jnp.zeros_like(gain_feed_out)

        def step(i):
            rows = span(i, 128)
            grad = sum_normed[rows, :] + wide(got_normed[rows, :])
            back, gain_part = norm_back(after_cross[rows, :], gain(2 + c), grad)
            gain_feed_out[0:1, :] = gain_feed_out[0:1, :] + gain_part
            sum_normed[rows, :] = out_grad[rows, :] + back

        loop(row_count // 128, step)

    def feed_out():
        def step(i):
            rows = span(i, 128)
            branch = sum_branch[rows, :] + wide(got_branch[rows, :])
            result = after_cross[rows, :] + branch
            stat(2, row_sum(branch * branch))
            stat(3, row_sum(result * result))
            sum_branch[rows, :] = result

        loop(row_count // 128, step)

    half_tick = [0]

    def ticks(until):
        while half_tick[0] <= until:
            tick(half_tick[0])
            half_tick[0] += 1

    shard_start()
    for k in range(3):
        load(k).start()
    meet(c, z, y, x)
    ticks(0)
    for k in (3, 0, 1, 2, 4, 5):
        shard_round(k)
    ticks(1)
    start()
    ticks(2)
    load(1).wait()
    round_out_grad()
    swap("grad_feed").start()
    ticks(4)
    load(2).wait()
    sort_images(0)
    load(3).start()
    ticks(7)
    load(3).wait()
    sort_images(1)
    keep("images").start()
    ticks(9)
    read_gains()
    keep("gains").start()
    ticks(11)
    across(1).wait_recv()
    pack_vision()
    quarter = image_count // 4
    project_images(0, quarter)
    ticks(13)
    project_images(quarter, 2 * quarter)
    ticks(15)
    project_images(2 * quarter, 3 * quarter)
    ticks(17)
    for number in (2, 3, 4):
        across(number).wait_recv()
    load(0).wait()
    self_in()
    for name in ("normed", "query", "key", "value"):
        keep(name).start()

    @pl.when(c == 0)
    def _():
        swap("key").start()
        swap("value").start()

    project_images(3 * quarter, image_count)
    keep("vision").start()
    ticks(18)
    keep("first").start()
    blocks = row_count // 128

    @pl.when(c == 0)
    def _():
        self_query()
        self_out()
        cross_in()
        swap("query").start()

    @pl.when(c == 1)
    def _():
        swap("key").wait_recv()
        swap("value").wait_recv()
        self_text(0, blocks // 2)
        keep("far_key").start()
        keep("far_value").start()

    ticks(20)

    @pl.when(c == 1)
    def _():
        self_text(blocks // 2, blocks)
        self_out()

    @pl.when(c == 0)
    def _():
        cross_attend(0, image_count // 2)

    ticks(21)

    @pl.when(c == 1)
    def _():
        swap("query").wait_recv()
        cross_attend(0, image_count // 2)

    @pl.when(c == 0)
    def _():
        cross_attend(image_count // 2, image_count)

    keep("context").start()
    keep("after_self").start()
    ticks(22)

    @pl.when(c == 1)
    def _():
        cross_attend(image_count // 2, image_count)
        swap("context").start()
        after_cross[...] = after_self[...]

    ticks(23)

    @pl.when(c == 0)
    def _():
        swap("context").wait_recv()
        cross_out()

    keep("cross_query").start()
    keep("cross_context").start()
    feed_in()
    swap("normed_feed").start()
    ticks(last_tick)
    for name in ("vision", "images"):
        keep(name).wait()
    for b in range(half_parts):
        feed_rows(0, b)
    swap("grad_feed").wait_recv()
    swap("normed_feed").wait_recv()
    for b in range(half_parts):
        feed_rows(1, b)
    send_partial(sum_normed, send_normed, "sum_normed")
    send_partial(sum_branch, send_branch, "sum_branch")
    for p in range(PARTS):
        sent(5 + 2 * p)
        sent(6 + 2 * p)
        feed_grads(2 * p)
        feed_grads(2 * p + 1)
        keep(("expand", p)).start()
        keep(("reduce", p)).start()
    swap("sum_normed").wait_recv()
    feed_back()
    keep("grad_cross").start()
    swap("sum_branch").wait_recv()
    feed_out()
    keep("result").start()
    for number in range(5):
        sent(number)
    for number in range(1, 5):
        across(number).wait_send()
    for name in with_mate:
        swap(name).wait_send()

    @pl.when(c == 0)
    def _():
        swap("key").wait_send()
        swap("value").wait_send()
        swap("query").wait_send()

    @pl.when(c == 1)
    def _():
        swap("context").wait_send()

    for name in keeps:
        if name in ("vision", "images"):
            continue
        if name in ("far_key", "far_value"):

            @pl.when(c == 1)
            def _(name=name):
                keep(name).wait()

        else:
            keep(name).wait()


def forward_all(weights, gains, hidden, out_grad, features, lengths, owners):
    project, _, _, vision, expand, reduce = weights
    first = jax.ShapeDtypeStruct((3,) + project.shape[1:], project.dtype)
    vision = jax.ShapeDtypeStruct(vision.shape[1:], vision.dtype)
    half, single = jnp.bfloat16, jnp.float32
    row_count, width = hidden.shape
    image_count, feature_rows, feature_width = features.shape
    image_count = image_count // 2
    features = features.transpose(1, 0, 2).reshape(-1, feature_width)
    padded = -(-feature_rows // 16) * 16
    cross_rows = image_count * NQ
    part_rows = expand.shape[0] // PARTS
    anywhere = pl.BlockSpec(memory_space=pl.ANY)
    vmem = pl.BlockSpec(memory_space=pltpu.VMEM)
    rows_half = jax.ShapeDtypeStruct((row_count, width), half)
    rows_single = jax.ShapeDtypeStruct((row_count, width), single)
    all_first = (2,) + first.shape[:1] + (4, 2, 2) + first.shape[1:]
    all_feed = (PARTS, 4, 2, part_rows, width)
    gain_shape = (16, width)
    pair_shape = (image_count * padded, 2 * width)
    outs = {
        "result": (rows_single, anywhere),
        "grad_cross": (rows_single, anywhere),
        "part_expand": (jax.ShapeDtypeStruct(all_feed, half), anywhere),
        "part_reduce": (jax.ShapeDtypeStruct(all_feed, half), anywhere),
        "gain_feed": (jax.ShapeDtypeStruct((8, width), single), vmem),
        "stats": (jax.ShapeDtypeStruct((8, width), single), vmem),
        "first": (jax.ShapeDtypeStruct(all_first, half), anywhere),
        "gains": (jax.ShapeDtypeStruct(gain_shape, single), anywhere),
        "normed": (rows_half, anywhere),
        "query": (rows_half, anywhere),
        "key": (rows_half, anywhere),
        "value": (rows_half, anywhere),
        "far_key": (rows_half, anywhere),
        "far_value": (rows_half, anywhere),
        "context": (rows_half, anywhere),
        "after_self": (rows_single, anywhere),
        "cross_query": (jax.ShapeDtypeStruct((cross_rows, width), half), anywhere),
        "cross_context": (rows_half, anywhere),
        "vision": (jax.ShapeDtypeStruct(pair_shape, half), anywhere),
        "images": (jax.ShapeDtypeStruct((image_count * padded, feature_width), half), anywhere),
        "total_self": (jax.ShapeDtypeStruct((row_count // 128, HEADS // 2, 1, 256), single), vmem),
        "total_cross": (jax.ShapeDtypeStruct((image_count, 1, HEADS * NQ), single), vmem),
    }
    halves = (row_count, width)
    scratch = [
        pltpu.VMEM(all_first, half),
        pltpu.VMEM((2, 4, 2, 2) + vision.shape, half),
        pltpu.VMEM((2, feature_width, width), half),
        pltpu.VMEM(all_feed, half),
        pltpu.VMEM(all_feed, half),
        pltpu.VMEM((4, 2, 2) + gains.shape, half),
        pltpu.VMEM(gain_shape, single),
        pltpu.VMEM(halves, single),
        pltpu.VMEM(halves, single),
        pltpu.VMEM((image_count * padded, feature_width), half),
        pltpu.VMEM(pair_shape, half),
    ]
    scratch += [pltpu.VMEM(halves, half)] * 7
    scratch += [
        pltpu.VMEM(halves, single),
        pltpu.VMEM(halves, half),
        pltpu.VMEM(halves, half),
        pltpu.VMEM(halves, single),
        pltpu.VMEM((2 * row_count, width), half),
        pltpu.VMEM((2 * row_count, width), half),
        pltpu.VMEM((2 * row_count, width), single),
        pltpu.VMEM((2 * row_count, width), single),
        pltpu.VMEM(halves, half),
        pltpu.VMEM(halves, half),
        pltpu.VMEM((row_count + 256, 256), single),
        pltpu.VMEM((HEADS * NQ, width), half),
        pltpu.VMEM(first.shape, half),
        pltpu.VMEM(vision.shape, half),
        pltpu.VMEM(expand.shape, half),
        pltpu.VMEM(reduce.shape, half),
        pltpu.VMEM((8, row_count), single),
        pltpu.SemaphoreType.DMA(((5 + 2 * PARTS) * 10 + 8,)),
        pltpu.SemaphoreType.DMA(((5 + 2 * PARTS) * 10 + 8,)),
        pltpu.SemaphoreType.DMA((5 + 4 + 16 + 4 * PARTS + 6,)),
    ]
    values = pl.pallas_call(
        forward_kernel,
        out_shape=[shape for shape, _ in outs.values()],
        in_specs=[anywhere] * 10 + [vmem] * 2,
        out_specs=[spec for _, spec in outs.values()],
        scratch_shapes=scratch,
        compiler_params=pltpu.CompilerParams(
            collective_id=2, has_side_effects=True, vmem_limit_bytes=VMEM_LIMIT
        ),
        name="forward_layer",
    )(*weights, gains, hidden, out_grad, features, lengths, owners)
    return dict(zip(outs, values))


def scatter_engine(chunks, send_sem, recv_sem):
    c, z, y, x = coordinates()
    own = {"z": z, "y": y, "x": x, "o": jnp.where(c == 0, y, x)}
    beyond = (c, z * 4 + jnp.where(c == 0, 1 - y, y) * 2 + jnp.where(c == 0, x, 1 - x))

    def axes_of(chunk):
        return "zo" if chunk["kind"] == "feed" else "zyx"

    def remote(source, target, index, where):
        return pltpu.make_async_remote_copy(
            src_ref=source, dst_ref=target, send_sem=send_sem.at[index],
            recv_sem=recv_sem.at[index], device_id=where, device_id_type=MESH,
        )

    def sends(number, stage, core):
        chunk = chunks[number]
        held, got = chunk["held"], chunk["got"][stage]
        order = ORDERS[chunk["kind"], core][::-1]
        done, axis = order[:stage], order[stage]
        base = (number * 3 + stage) * 3

        def block(there):
            return held.at[
                tuple(
                    there if a == axis else own[a] if a in done else slice(None)
                    for a in axes_of(chunk)
                )
            ]

        if axis == "z":
            return [
                remote(
                    block((z + k) % 4), got.at[k - 1], base + k - 1, device(c, (z + k) % 4, y, x)
                )
                for k in (1, 2, 3)
            ]
        where = {"y": device(c, z, 1 - y, x), "x": device(c, z, y, 1 - x), "o": beyond}[axis]
        return [remote(block(1 - own[axis]), got, base, where)]

    def absorb(number, stage, core):
        chunk = chunks[number]
        held, got = chunk["held"], chunk["got"][stage]
        order = ORDERS[chunk["kind"], core][::-1]
        done, axis = order[: stage + 1], order[stage]
        free = [a for a in axes_of(chunk) if a not in done]
        sizes = [4 if a == "z" else 2 for a in free]
        steps = 1
        for size in sizes:
            steps *= size

        def step(i):
            index = {}
            for a, size in reversed(list(zip(free, sizes))):
                index[a] = i % size
                i = i // size
            at = tuple(index[a] if a in index else own[a] for a in axes_of(chunk))
            inner = tuple(index[a] for a in free)
            value = wide(held[at])
            if axis == "z":
                for k in range(3):
                    value = value + wide(got[(k,) + inner])
            else:
                value = value + wide(got[inner] if inner else got[...])
            if stage == len(order) - 1:
                chunk["total"][...] = value
            else:
                held[at] = to_half(value)

        if steps == 1:
            step(0)
        else:
            loop(steps, step)

    def tick_core(now, core):
        for number, stage in [
            (number, stage)
            for stage in (3, 2, 1, 0)
            for number, chunk in enumerate(chunks)
            if stage < len(chunk["ticks"][core]) and chunk["ticks"][core][stage] == now
        ]:
            if stage == 0:
                chunks[number]["ready"](core)
            else:
                for copy in sends(number, stage - 1, core):
                    copy.wait_recv()
                absorb(number, stage - 1, core)
            if stage < len(chunks[number]["ticks"][core]) - 1:
                for copy in sends(number, stage, core):
                    copy.start()

    def each_core(step):
        @pl.when(c == 0)
        def _():
            step(0)

        @pl.when(c == 1)
        def _():
            step(1)

    def tick(now):
        each_core(lambda core: tick_core(now, core))

    def wait_sent():
        def step(core):
            for number, chunk in enumerate(chunks):
                for stage in range(len(chunk["ticks"][core]) - 1):
                    for copy in sends(number, stage, core):
                        copy.wait_send()

        each_core(step)

    last = max(max(ticks) for chunk in chunks for ticks in chunk["ticks"])
    return tick, wait_sent, remote, last


def got_shapes(kind, rows, width):
    if kind == "feed":
        return [(4, rows, width), (3, rows, width)]
    if kind == "late":
        return [(4, 2, rows, width), (4, rows, width), (3, rows, width)]
    return [(4, 2, rows, width), (3, 2, rows, width), (rows, width)]


FEED_CHUNKS = 2 * PARTS
FEED_TICKS = [(0, 2, 20), (1, 4, 20), (3, 6, 20), (5, 8, 20)]
PLANE_TICKS = (
    [(17, 18, 19, 20), (17, 18, 19, 20), (3, 5, 7, 20)],
    [(17, 18, 19, 20), (10, 12, 14, 20), (10, 12, 14, 20)],
)
VISION_TICKS = ((9, 11, 13, 20), (9, 11, 13, 20))


def backward_kernel(
    feature_rows,
    part_expand, part_reduce, grad_cross_in, hidden_in, after_self_in, first_in, gains_in,
    normed_in, query_in, key_in, value_in, far_key_in, far_value_in, context_in,
    cross_query_in, cross_context_in, vision_in, images_in, lengths, owners, total_self, total_cross, gain_feed,
    part_stats, hidden_grad_out, sum_expand, sum_reduce, sum_first, sum_vision, sum_gains, totals,
    held_expand, held_reduce, got_f0, got_f1, got_p0, got_p1, got_p2, got_v0, got_v1, got_v2,
    pair_first, pair_vision, held_vision, gains_now, gains_got, gains_z, stats_now, stats_got, stats_z,
    first, pair, images, grad_vision, cross_context, after_self, hidden, grad_after, gain_rows,
    cross_query, grad_context, grad_query, far_grad, bias, mask, sum_far_key, sum_far_value, sum_key, sum_value,
    layout_rows, gain_parts, send_sem, recv_sem, local_sem,
):
    c, z, y, x = coordinates()
    row_count, width = hidden.shape
    image_count = total_cross.shape[0]
    padded = pair.shape[0] // image_count
    feature_width = images.shape[1]
    cross_rows = image_count * NQ
    part_rows = held_expand.shape[-2]
    rows_vision = held_vision.shape[-2]
    grad_normed = after_self
    far_rows, window = row_count, 256
    scale = HD**-0.5
    other = device(1 - c, z, y, x)

    def shelf(buffer, number):
        at = pl.ds(number // 2 * row_count, row_count), pl.ds(number % 2 * width, width)
        return buffer.at[at[0], at[1]]

    names = ("normed", "query", "key", "value", "far_key", "far_value", "context", "grad_context")
    normed, query, key, value, far_key, far_value, context, grad_context_self = (
        shelf(pair, number) for number in range(len(names))
    )
    own_query, own_key, own_value = (shelf(images, 2 * number) for number in range(3))

    loads = {
        "expand": (part_expand, held_expand),
        "reduce": (part_reduce, held_reduce),
        "grad_cross": (grad_cross_in, grad_after),
        "first": (first_in, first),
        "gains": (gains_in, gain_rows),
        "cross_context": (cross_context_in, cross_context),
        "cross_query": (cross_query_in, cross_query),
        "vision": (vision_in, pair),
        "images": (images_in, images),
        "after_self": (after_self_in, after_self),
        "hidden": (hidden_in, hidden),
        "normed": (normed_in, normed),
        "query": (query_in, query),
        "key": (key_in, key),
        "value": (value_in, value),
        "far_key": (far_key_in, far_key),
        "far_value": (far_value_in, far_value),
        "context": (context_in, context),
        "out_hidden": (grad_after, hidden_grad_out),
    }

    def local(name):
        source, target = loads[name]
        return pltpu.make_async_copy(source, target, local_sem.at[list(loads).index(name)])

    def pair_copy(k):
        if k == 3:
            return remote(grad_vision.at[1 - c], pair_vision, pair_base + k, other)
        return remote(first.at[1 - c, k], pair_first.at[k], pair_base + k, other)

    def ready_first(j, core):
        pair_copy(j).wait_recv()

        def step(i):
            at = (i // 4, (i // 2) % 2, i % 2)
            value = wide(first[(core, j) + at]) + wide(pair_first[(j,) + at])
            first[(core, j) + at] = to_half(value)

        loop(16, step)

    def ready_vision(core):
        pair_copy(3).wait_recv()

        def step(i):
            rows = span(i, 2 * rows_vision)
            value = wide(grad_vision[core, rows, :]) + wide(pair_vision[rows, :])
            held_vision[i // 2, i % 2, 0] = to_half(value[:rows_vision])
            held_vision[i // 2, i % 2, 1] = to_half(value[rows_vision:])

        loop(8, step)

    chunks = []
    for number in range(FEED_CHUNKS):
        p = number // 2
        held, total, name = (
            (held_expand, sum_expand, "expand"), (held_reduce, sum_reduce, "reduce")
        )[number % 2]
        chunks.append({
            "held": held.at[p], "got": [got_f0.at[number], got_f1.at[number]], "kind": "feed",
            "total": total.at[pl.ds(p * part_rows, part_rows)], "ticks": (FEED_TICKS[number],) * 2,
            "ready": (lambda core, name=name: local(name).wait()) if p == 0 else (lambda core: None),
        })
    for j in range(3):
        chunks.append({
            "held": first.at[c, j], "got": [got_p0.at[j], got_p1.at[j], got_p2.at[j]], "kind": "late",
            "total": sum_first.at[c, j], "ticks": (PLANE_TICKS[0][j], PLANE_TICKS[1][j]),
            "ready": lambda core, j=j: ready_first(j, core),
        })
    chunks.append({
        "held": held_vision, "got": [got_v0, got_v1, got_v2], "kind": "late",
        "total": sum_vision.at[c], "ticks": VISION_TICKS, "ready": ready_vision,
    })
    tick, wait_sent, remote, last = scatter_engine(chunks, send_sem, recv_sem)
    pair_base = len(chunks) * 9
    gains_base, stats_base = pair_base + 4, pair_base + 14
    back_base = stats_base + 10
    swap_base = back_base + 2

    layer = c * 4 + y * 2 + x

    def small(stage, now, got, got_z, base):
        if stage == 0:
            return [
                remote(now.at[0], got.at[layer], base + k - 1, layer_device(layer, k))
                for k in range(1, 8)
            ]
        return [
            remote(now.at[1], got_z.at[z], base + 6 + k, device(c, (z + k) % 4, y, x))
            for k in (1, 2, 3)
        ]

    def layer_device(at, k):
        c_at, y_at, x_at = k // 4, (k // 2) % 2, k % 2
        flip = lambda value, bit: 1 - value if bit else value
        return device(flip(c, c_at), z, flip(y, y_at), flip(x, x_at))

    def small_step(stage, now, got, got_z, base):
        if stage > 0:
            for copy in small(stage - 1, now, got, got_z, base):
                copy.wait()
            if stage == 1:
                got[layer] = now[0]
                now[1] = sum(got[k] for k in range(8))
            else:
                got_z[z] = now[1]
                now[2] = (got_z[0] + got_z[1]) + (got_z[2] + got_z[3])
        if stage < 2:
            for copy in small(stage, now, got, got_z, base):
                copy.start()

    def folded(values):
        total = values[:, 0:128]
        for k in range(1, values.shape[1] // 128):
            total = total + values[:, k * 128 : (k + 1) * 128]
        return total

    def squares(block):
        return jnp.sum((block * block).reshape(-1, 8, block.shape[1]), axis=0)

    own_rows, other_rows = pl.ds(0, cross_rows), pl.ds(cross_rows, cross_rows)
    swaps = {
        "context": (grad_context.at[other_rows], grad_context.at[own_rows]),
        "query": (grad_query.at[own_rows], grad_query.at[other_rows]),
        "far_key": (far_grad.at[0], far_grad.at[0]),
        "far_value": (far_grad.at[1], far_grad.at[1]),
    }

    def swap(name):
        source, target = swaps[name]
        return remote(source, target, swap_base + list(swaps).index(name), other)

    def weight(name):
        plane, j = PLANES[name]
        return first[plane, j].reshape(width, width)

    def gain(k):
        return gain_rows[pl.ds(k, 1), :]

    def store_weight_grad(name, value):
        plane, j = PLANES[name]
        first[plane, j] = to_half(value).reshape(first.shape[2:])


    def start():
        gain_parts[...] = jnp.zeros_like(gain_parts)
        gain_parts[pl.ds(2 + c, 1), :] = gain_feed[0:1, :]
        mask[...] = head_mask(NQ, width)
        first_row, image = caption_layout(lengths[...], owners[...], row_count)
        layout_rows[0:1] = first_row
        layout_rows[1:2] = image

    def cross_out_back():
        def step(i):
            rows = span(i, 256)
            part = to_half(grad_after[rows, :])
            grad_query[rows, :] = part
            grad_context[rows, :] = to_half(nt(part, weight("cross_output")))

        loop(row_count // 256, step)
        store_weight_grad("cross_output", tn(cross_context[...], grad_query[...]))
        swap("context").start()

    def cross_back(begin, end):
        def step(i):
            i = i + begin
            rows = pl.ds(pl.multiple_of(i * padded, 16), padded)
            at = span(i, NQ)
            queries = jnp.concatenate([cross_query[at, :]] * HEADS, axis=0) * mask[...]
            grads = jnp.concatenate([grad_context[at, :]] * HEADS, axis=0) * mask[...]
            keys, values = pair[rows, 0:width], pair[rows, width : 2 * width]
            score = nt(keys, queries)
            key_row = lax.broadcasted_iota(jnp.int32, score.shape, 0)
            seen = key_row < feature_rows
            probability = jnp.exp(jnp.where(seen, score, masked_value) - total_cross[i])
            grad_prob = nt(values, grads)
            inner = row_sum(grad_prob * probability)
            grad_score = to_half(probability * (grad_prob - inner))
            full = tn(grad_score, keys)
            pair[rows, 0:width] = to_half(nn(grad_score, queries))
            pair[rows, width : 2 * width] = to_half(nn(to_half(probability), grads))
            grad_query[at, :] = to_half(diagonal(full, NQ) * scale)

        loop(end - begin, step)


    def vision_back(begin, end):
        def step(i):
            i = i + begin
            lanes = span(i, 128)
            both = to_half(tn(images[:, lanes], pair[...]))
            grad_vision[0, lanes, :] = both[:, 0:width]
            grad_vision[1, lanes, :] = both[:, width : 2 * width]

        loop(end - begin, step)

    def cross_in_back():
        def step(i):
            rows = span(i, 128)
            source = after_self[rows, :]
            grad = nt(grad_query[rows, :], weight("cross_query"))
            back, part = norm_back(source, gain(1), grad)
            gain_parts[1:2, :] = gain_parts[1:2, :] + part
            grad_after[rows, :] = grad_after[rows, :] + back
            grad_context[rows, :] = to_half(norm_rows(source, gain(1)))

        loop(row_count // 128, step)
        store_weight_grad("cross_query", tn(grad_context[...], grad_query[...]))

    def self_out_back():
        def step(i):
            rows = span(i, 256)
            part = to_half(grad_after[rows, :])
            grad_context[rows, :] = part
            grad_context_self[rows, :] = to_half(nt(part, weight("self_output")))

        loop(row_count // 256, step)
        store_weight_grad("self_output", tn(context[...], grad_context[...]))

    def attend_pair_back(rb, t, parts):
        rows, lanes = span(rb, 128), span(t, 128)
        masks = lane_masks(128)
        queries = head_pair(query[rows, lanes], masks)
        grads = head_pair(grad_context_self[rows, lanes], masks)
        kept, inner = [], 0.0
        for keys, values, where in parts:
            score = nt(keys, queries) + wide(where)
            probability = jnp.exp(score - total_self[rb, t])
            grad_prob = nt(values, grads)
            inner = inner + row_sum(grad_prob * probability)
            kept.append((probability, grad_prob))
        result, back = [], 0.0
        for (keys, values, _), (probability, grad_prob) in zip(parts, kept):
            grad_score = to_half(probability * (grad_prob - inner))
            result.append((nn(grad_score, queries), nn(to_half(probability), grads)))
            back = back + tn(grad_score, keys)
        own_query[rows, lanes] = to_half(pair_join(back) * scale)
        return result

    def self_query_back(begin, end):
        def step(i):
            rb, t = i // 6, i % 6
            rows, lanes = span(rb, 128), span(t, 128)
            parts = [(key[rows, lanes], value[rows, lanes], bias[0, 0:128])]
            ((grad_key, grad_value),) = attend_pair_back(rb, t, parts)
            own_key[rows, lanes] = to_half(grad_key)
            own_value[rows, lanes] = to_half(grad_value)

        blocks = row_count // 128

        def shifted_step(i):
            step(i + begin * blocks)

        loop((end - begin) * blocks, shifted_step)

    def text_biases():
        def step(rb):
            rows = span(rb, 128)
            start_row, image = layout_rows[0:1, rows], layout_rows[1:2, rows]
            begin = jnp.maximum(rb - 1, 0) * 128
            far = lax.broadcasted_iota(jnp.int32, (far_rows, 128), 0) // NQ
            far_bias = jnp.where(wide(far) == image, 0.0, masked_value)
            key_row = lax.broadcasted_iota(jnp.int32, (window, 128), 0) + begin
            row = lax.broadcasted_iota(jnp.int32, (window, 128), 1) + rb * 128
            seen = (wide(key_row) >= start_row) & (key_row <= row)
            own_bias = jnp.where(seen, 0.0, masked_value)
            bias[rb, 0:far_rows] = to_half(jnp.concatenate([far_bias, far_bias], axis=1))
            bias[rb, far_rows : far_rows + window] = to_half(
                jnp.concatenate([own_bias, own_bias], axis=1)
            )

        loop(row_count // 128, step)

    def query_biases():
        key_row = lax.broadcasted_iota(jnp.int32, (128, 256), 0) // NQ
        row = (lax.broadcasted_iota(jnp.int32, (128, 256), 1) % 128) // NQ
        bias[0, 0:128] = to_half(jnp.where(key_row == row, 0.0, masked_value))

    def self_text_back(begin, end):
        def outer(t):
            t = t + begin
            lanes = span(t, 128)
            for total in (sum_far_key, sum_far_value, sum_key, sum_value):
                total[...] = jnp.zeros_like(total)

            def inner(rb):
                near = pl.ds(pl.multiple_of(jnp.maximum(rb - 1, 0) * 128, 128), window)
                parts = [
                    (far_key[:, lanes], far_value[:, lanes], bias[rb, 0:far_rows]),
                    (key[near, lanes], value[near, lanes], bias[rb, far_rows : far_rows + window]),
                ]
                far_part, near_part = attend_pair_back(rb, t, parts)
                sum_far_key[...] += far_part[0]
                sum_far_value[...] += far_part[1]
                sum_key[near, :] = sum_key[near, :] + near_part[0]
                sum_value[near, :] = sum_value[near, :] + near_part[1]

            loop(row_count // 128, inner)
            far_grad[0, :, lanes] = to_half(sum_far_key[...])
            far_grad[1, :, lanes] = to_half(sum_far_value[...])
            own_key[:, lanes] = to_half(sum_key[...])
            own_value[:, lanes] = to_half(sum_value[...])

        loop(end - begin, outer)

    def self_in_back():
        def step(i):
            rows = span(i, 256)
            grad = nt(own_query[rows, :], weight("query"))
            grad = grad + nt(own_key[rows, :], weight("key"))
            grad = grad + nt(own_value[rows, :], weight("value"))
            grad_normed[rows, :] = grad

        loop(row_count // 256, step)

    def far_in_back():
        def step(i):
            rows = span(i, 256)
            grad = nt(far_grad[0, rows, :], weight("key")) + nt(far_grad[1, rows, :], weight("value"))
            grad_normed[rows, :] = grad_normed[rows, :] + grad

        loop(row_count // 256, step)

    def project_back(far):
        rows = normed[...]
        store_weight_grad("query", tn(rows, own_query[...]))
        grad_key, grad_value = tn(rows, own_key[...]), tn(rows, own_value[...])
        if far:
            grad_key = grad_key + tn(rows, far_grad[0])
            grad_value = grad_value + tn(rows, far_grad[1])
        store_weight_grad("key", grad_key)
        store_weight_grad("value", grad_value)

    def hidden_back():
        def step(i):
            rows = span(i, 128)
            back, part = norm_back(hidden[rows, :], gain(0), grad_normed[rows, :])
            gain_parts[0:1, :] = gain_parts[0:1, :] + part
            grad_after[rows, :] = grad_after[rows, :] + back

        loop(row_count // 128, step)

    def send_pair(core, *names):
        @pl.when(c == core)
        def _():
            for name in names:
                plane, j = PLANES[name]
                if plane != core:
                    pair_copy(j).start()

    for name in ("expand", "reduce", "grad_cross", "first", "cross_context", "vision", "cross_query",
                 "images", "after_self", "gains", "hidden"):
        local(name).start()
    meet(c, z, y, x, layer=True)
    tick(0)
    start()
    local("grad_cross").wait()
    local("first").wait()
    local("cross_context").wait()

    @pl.when(c == 0)
    def _():
        cross_out_back()

    @pl.when(c == 1)
    def _():
        plane, j = PLANES["cross_output"]
        first[plane, j] = jnp.zeros(first.shape[2:], jnp.bfloat16)
        plane, j = PLANES["cross_query"]
        first[plane, j] = jnp.zeros(first.shape[2:], jnp.bfloat16)
        swap("context").wait_recv()

    send_pair(1, "cross_output")
    tick(1)
    local("vision").wait()
    local("cross_query").wait()
    quarter = image_count // 4
    for k in range(4):
        cross_back(k * quarter, (k + 1) * quarter)
        tick(2 + k)

    @pl.when(c == 1)
    def _():
        swap("query").start()

    local("images").wait()
    tiles = feature_width // 128
    vision_back(0, tiles // 3)
    tick(6)
    vision_back(tiles // 3, 2 * tiles // 3)
    tick(7)
    vision_back(2 * tiles // 3, tiles)
    pair_copy(3).start()
    for name in names[:-1]:
        local(name).start()
    tick(8)
    local("after_self").wait()
    local("gains").wait()

    @pl.when(c == 0)
    def _():
        swap("query").wait_recv()
        swap("context").wait_send()
        cross_in_back()

    send_pair(0, "cross_query")
    for name in names[:-1]:
        local(name).wait()
    self_out_back()
    send_pair(0, "self_output")
    tick(9)

    @pl.when(c == 0)
    def _():
        query_biases()
        self_query_back(0, 3)

    @pl.when(c == 1)
    def _():
        text_biases()

    for t in range(6):

        @pl.when(c == 1)
        def _(t=t):
            self_text_back(t, t + 1)

        if t == 1:

            @pl.when(c == 0)
            def _():
                self_query_back(3, 6)

        if t < 5:
            tick(10 + t)

    @pl.when(c == 1)
    def _():
        swap("far_key").start()
        swap("far_value").start()

    self_in_back()
    tick(15)

    @pl.when(c == 0)
    def _():
        swap("far_key").wait_recv()
        swap("far_value").wait_recv()
        far_in_back()
        project_back(True)

    @pl.when(c == 1)
    def _():
        project_back(False)

    send_pair(0, "value")
    send_pair(1, "query", "key")
    tick(16)
    local("hidden").wait()
    hidden_back()
    local("out_hidden").start()
    gains_now[0] = gain_parts[...]
    for now in range(17, last + 1):
        if now < 20:
            small_step(now - 17, gains_now, gains_got, gains_z, gains_base)
        tick(now)
    back = [
        remote(sum_first.at[c], sum_first.at[c], back_base, other),
        remote(sum_vision.at[c], sum_vision.at[c], back_base + 1, other),
    ]
    for copy in back:
        copy.start()
    gains = gains_now[2]
    sum_gains[...] = gains
    mass = jnp.where((c == 0) & (z + y + x == 0), 1.0, 0.0) * (gains * gains)
    for j in range(3):
        mass = mass + squares(sum_first[c, j])
    mass = mass + squares(sum_vision[c])
    mass = mass + squares(sum_expand[...]) + squares(sum_reduce[...])
    stats_now[0, 0:8] = folded(mass)
    stats_now[0, 8:16] = folded(part_stats[...])
    for stage in range(3):
        small_step(stage, stats_now, stats_got, stats_z, stats_base)
    totals[...] = stats_now[2]
    for copy in back:
        copy.wait()
    assert last == 20
    wait_sent()
    for k in range(4):
        pair_copy(k).wait_send()

    @pl.when(c == 1)
    def _():
        swap("query").wait_send()
        swap("far_key").wait_send()
        swap("far_value").wait_send()

    local("out_hidden").wait()


def backward_all(kept, hidden, lengths, owners, feature_rows):
    half, single = jnp.bfloat16, jnp.float32
    row_count, width = hidden.shape
    feature_width = kept["images"].shape[1]
    parts = kept["part_expand"].shape
    part_rows = parts[-2]
    rows_first = kept["first"].shape[-2]
    rows_vision = feature_width // 16
    cross_rows = kept["cross_query"].shape[0]
    anywhere = pl.BlockSpec(memory_space=pl.ANY)
    vmem = pl.BlockSpec(memory_space=pltpu.VMEM)
    rows_half, rows_single = pltpu.VMEM((row_count, width), half), pltpu.VMEM((row_count, width), single)
    outs = {
        "hidden_grad": (jax.ShapeDtypeStruct((row_count, width), single), anywhere),
        "expand": (jax.ShapeDtypeStruct((PARTS * part_rows, width), single), vmem),
        "reduce": (jax.ShapeDtypeStruct((PARTS * part_rows, width), single), vmem),
        "first": (jax.ShapeDtypeStruct((2, 3, rows_first, width), single), vmem),
        "vision": (jax.ShapeDtypeStruct((2, rows_vision, width), single), vmem),
        "gains": (jax.ShapeDtypeStruct((8, width), single), vmem),
        "totals": (jax.ShapeDtypeStruct((16, 128), single), vmem),
    }
    scratch = [pltpu.VMEM(parts, half)] * 2
    scratch += [
        pltpu.VMEM((FEED_CHUNKS,) + shape, half) for shape in got_shapes("feed", part_rows, width)
    ]
    scratch += [pltpu.VMEM((3,) + shape, half) for shape in got_shapes("late", rows_first, width)]
    scratch += [pltpu.VMEM(shape, half) for shape in got_shapes("late", rows_vision, width)]
    scratch += [
        pltpu.VMEM(kept["first"].shape[1:], half),
        pltpu.VMEM((feature_width, width), half),
        pltpu.VMEM((4, 2, 2, rows_vision, width), half),
    ]
    for shape in ((8, width), (16, 128)):
        scratch += [pltpu.VMEM((number,) + shape, single) for number in (3, 8, 4)]
    scratch += [
        pltpu.VMEM(kept["first"].shape, half),
        pltpu.VMEM(kept["vision"].shape, half),
        pltpu.VMEM(kept["images"].shape, half),
        pltpu.VMEM((2, feature_width, width), half),
        rows_half,
        rows_single,
        rows_single,
        rows_single,
        pltpu.VMEM((16, width), single),
        pltpu.VMEM((cross_rows, width), half),
        rows_half,
        rows_half,
        pltpu.VMEM((2, row_count, width), half),
        pltpu.VMEM((row_count // 128, row_count + 256, 256), half),
        pltpu.VMEM((HEADS * NQ, width), half),
    ]
    scratch += [pltpu.VMEM((row_count, 128), single)] * 4
    scratch += [
        pltpu.VMEM((8, row_count), single),
        pltpu.VMEM((8, width), single),
        pltpu.SemaphoreType.DMA(((FEED_CHUNKS + 4) * 9 + 4 + 22 + 4,)),
        pltpu.SemaphoreType.DMA(((FEED_CHUNKS + 4) * 9 + 4 + 22 + 4,)),
        pltpu.SemaphoreType.DMA((19,)),
    ]
    order = ("part_expand", "part_reduce", "grad_cross", None, "after_self", "first", "gains", "normed",
             "query", "key", "value", "far_key", "far_value", "context", "cross_query", "cross_context",
             "vision", "images")
    values = pl.pallas_call(
        functools.partial(backward_kernel, feature_rows),
        out_shape=[shape for shape, _ in outs.values()],
        in_specs=[anywhere] * len(order) + [vmem] * 6,
        out_specs=[spec for _, spec in outs.values()],
        scratch_shapes=scratch,
        compiler_params=pltpu.CompilerParams(
            collective_id=3, has_side_effects=True, vmem_limit_bytes=VMEM_LIMIT
        ),
        name="backward_layer",
    )(
        *[hidden if name is None else kept[name] for name in order],
        lengths, owners, kept["total_self"], kept["total_cross"], kept["gain_feed"], kept["stats"],
    )
    return dict(zip(outs, values))


NAMES = ("project", "output", "query", "vision", "expand", "reduce")
SUM_OF = {
    "project": ("query", "key", "value"), "output": ("self_output", "cross_output"), "query": ("cross_query",),
}


def update_kernel(amount, totals, sum_gains, gains, first_gains, second_gains, *refs):
    count = len(NAMES)
    sums, refs = refs[:4], refs[4:]
    inputs, refs = [refs[k * count : (k + 1) * count] for k in range(3)], refs[3 * count :]
    outputs, refs = [refs[k * count : (k + 1) * count] for k in range(4)], refs[4 * count :]
    gain_outs, norm_out, rms_out, refs = refs[:4], refs[4], refs[5], refs[6:]
    held_sums, refs = refs[:4], refs[4:]
    held, refs = [refs[k * count : (k + 1) * count] for k in range(3)], refs[3 * count :]
    half, sems = refs[:count], refs[count]

    def load_sum(k):
        return pltpu.make_async_copy(sums[k], held_sums[k], sems.at[k])

    def load(k, n):
        return pltpu.make_async_copy(inputs[k][n], held[k][n], sems.at[4 + k * count + n])

    def store(k, n):
        source = half[n] if k == 3 else held[k][n]
        return pltpu.make_async_copy(source, outputs[k][n], sems.at[4 + (3 + k) * count + n])

    for k in range(4):
        load_sum(k).start()
    for n in range(count):
        for k in range(3):
            load(k, n).start()
    lanes = jnp.sum(totals[0:8], axis=1, keepdims=True)
    grad_norm = jnp.sqrt(jnp.sum(lanes, axis=0, keepdims=True))
    norm_out[...] = grad_norm
    factor = clip_norm / jnp.maximum(grad_norm, clip_norm)
    rms_out[...] = jnp.sqrt(jnp.sum(totals[8:16], axis=1, keepdims=True) / amount)
    clipped = sum_gains[...] * factor
    fresh, mean, square = adam_step(
        gains[...], sum_gains[...], first_gains[...], second_gains[...], factor, rate_gains, 0.0
    )
    for target, value in zip(gain_outs, (fresh, mean, square, clipped)):
        target[...] = value
    for k in range(4):
        load_sum(k).wait()
    for n, name in enumerate(NAMES):
        for k in range(3):
            load(k, n).wait()
        weight, first, second = (held[k][n] for k in range(3))
        pieces = weight.shape[0] if len(weight.shape) == 3 else 1
        for j in range(pieces):
            at = (j,) if len(weight.shape) == 3 else (Ellipsis,)
            if name in SUM_OF:
                gradient = held_sums[0][PLANES[SUM_OF[name][j]]]
            else:
                gradient = held_sums[NAMES.index(name) - 2][at]
            fresh, mean, square = adam_step(
                weight[at], gradient, first[at], second[at], factor, rate_matrix, decay_rate
            )
            weight[at], first[at], second[at] = fresh, mean, square
            half[n][at] = to_half(fresh)
        for k in range(4):
            store(k, n).start()
    for n in range(count):
        for k in range(4):
            store(k, n).wait()


def update_all(amount, totals, sum_gains, gain_state, sums, weights, firsts, seconds):
    single, half = jnp.float32, jnp.bfloat16
    anywhere, vmem = pl.BlockSpec(memory_space=pl.ANY), pl.BlockSpec(memory_space=pltpu.VMEM)
    count = len(NAMES)
    shapes = [weight.shape for weight in weights]
    out_shape = [jax.ShapeDtypeStruct(shape, single) for _ in range(3) for shape in shapes]
    out_shape += [jax.ShapeDtypeStruct(shape, half) for shape in shapes]
    out_shape += [jax.ShapeDtypeStruct(sum_gains.shape, single)] * 4
    out_shape += [jax.ShapeDtypeStruct((1, 1), single), jax.ShapeDtypeStruct((8, 1), single)]
    scratch = [pltpu.VMEM(value.shape, single) for value in sums]
    scratch += [pltpu.VMEM(shape, single) for _ in range(3) for shape in shapes]
    scratch += [pltpu.VMEM(shape, half) for shape in shapes]
    scratch += [pltpu.SemaphoreType.DMA((4 + 7 * count,))]
    values = pl.pallas_call(
        functools.partial(update_kernel, amount),
        out_shape=out_shape,
        in_specs=[vmem] * 5 + [anywhere] * (4 + 3 * count),
        out_specs=[anywhere] * (4 * count) + [vmem] * 6,
        scratch_shapes=scratch,
        compiler_params=pltpu.CompilerParams(vmem_limit_bytes=VMEM_LIMIT),
        name="update_weights",
    )(totals, sum_gains, *gain_state, *sums, *weights, *firsts, *seconds)
    fresh, mean, square, copies = (values[k * count : (k + 1) * count] for k in range(4))
    return fresh, mean, square, copies, values[4 * count : 4 * count + 4], values[-2], values[-1]


def general_grads(
    hidden,
    features,
    caption_lengths,
    caption_image,
    out_grad,
    attn_project,
    attn_output,
    cross_query,
    cross_vision,
    feed_expand,
    feed_reduce,
    norm_gains,
):
    stream = lax.axis_index("stream")
    full_project, full_output, full_query, full_vision, full_expand, full_reduce, full_gains = (
        lax.all_gather(to_half(attn_project), "dp", axis=1, tiled=True),
        lax.all_gather(to_half(attn_output), "dp", axis=1, tiled=True),
        lax.all_gather(to_half(cross_query), "dp", axis=0, tiled=True),
        lax.all_gather(to_half(cross_vision), "dp", axis=1, tiled=True),
        lax.all_gather(to_half(feed_expand), "dp", axis=1, tiled=True),
        lax.all_gather(to_half(feed_reduce), "dp", axis=1, tiled=True),
        lax.all_gather(to_half(norm_gains), "dp", axis=1, tiled=True),
    )
    gain_rows = full_gains.astype(jnp.float32)
    gain_self = gain_rows[0]
    gain_cross = gain_rows[1]
    gain_feed = lax.dynamic_index_in_dim(gain_rows, 2 + stream, 0, keepdims=False)
    source = hidden[0]
    row_count = source.shape[0]
    feature_width = source.shape[1]
    image_count = features.shape[0]
    query_allow, text_allow = layout(caption_lengths[0], caption_image[0], row_count, NQ)
    normed_self = to_half(norm_rows(source, gain_self))
    query_half = to_half(product(normed_self, full_project[0]))
    key_half = to_half(product(normed_self, full_project[1]))
    value_half = to_half(product(normed_self, full_project[2]))
    empty_half = jnp.zeros((row_count, feature_width), jnp.bfloat16)
    far_key, far_value = shifted((key_half, value_half), "stream", 1)
    text_keys = jnp.concatenate([far_key, key_half], axis=0)
    text_values = jnp.concatenate([far_value, value_half], axis=0)

    def self_query():
        return attend(query_half[None], key_half[None], value_half[None], query_allow[None])

    def self_text():
        return attend(query_half[None], text_keys[None], text_values[None], text_allow[None])

    context_self, total_self = lax.cond(stream == 0, self_query, self_text)
    context_half = to_half(context_self[0])
    branch_self = product(context_half, full_output[0])
    after_self = source + branch_self

    def cross_on():
        normed_cross = to_half(norm_rows(after_self, gain_cross))
        cross_half = to_half(product(normed_cross, full_query))
        vision_pair = project_vision(features, full_vision)
        context_cross, total_cross = attend(
            cross_half.reshape(image_count, NQ, feature_width), vision_pair[0], vision_pair[1], None
        )
        context_cross_half = to_half(context_cross.reshape(row_count, feature_width))
        branch = product(context_cross_half, full_output[1])
        return (branch, total_cross, vision_pair, normed_cross, cross_half, context_cross_half)

    def cross_off():
        return (
            jnp.zeros((row_count, feature_width), jnp.float32),
            jnp.zeros((image_count, HEADS, NQ), jnp.float32),
            jnp.zeros((2, image_count, features.shape[1], feature_width), jnp.bfloat16),
            empty_half,
            empty_half,
            empty_half,
        )

    branch_cross, total_cross, vision_pair, normed_cross, cross_half, context_cross_half = lax.cond(
        stream == 0, cross_on, cross_off
    )
    after_cross = after_self + branch_cross
    normed_feed = to_half(norm_rows(after_cross, gain_feed))
    before = right_product(normed_feed, full_expand[0])
    active_half = to_half(exact_gelu(before))
    branch_feed = product(active_half, full_reduce[0])
    result = after_cross + branch_feed
    grad_result = out_grad[0]
    grad_feed_half = to_half(grad_result)
    grad_reduce = left_product(active_half, grad_feed_half)
    grad_active = right_product(grad_feed_half, full_reduce[0])
    grad_before = to_half(jax.vjp(exact_gelu, before)[1](grad_active)[0])
    grad_expand = left_product(grad_before, normed_feed)
    grad_normed_feed = product(grad_before, full_expand[0])
    feed_in, grad_gain_feed = jax.vjp(norm_rows, after_cross, gain_feed)[1](grad_normed_feed)
    grad_cross = grad_result + feed_in

    def cross_back_on():
        grad_branch_half = to_half(grad_cross)
        grad_out_cross = left_product(context_cross_half, grad_branch_half)
        grad_context = to_half(right_product(grad_branch_half, full_output[1]))
        grad_cq, grad_ck, grad_cv = attend_back(
            cross_half.reshape(image_count, NQ, feature_width),
            vision_pair[0],
            vision_pair[1],
            None,
            total_cross,
            grad_context.reshape(image_count, NQ, feature_width),
        )
        grad_cq_half = to_half(grad_cq.reshape(row_count, feature_width))
        grad_pair = to_half(jnp.stack([grad_ck, grad_cv]))
        grad_cross_weight = left_product(normed_cross, grad_cq_half)
        grad_normed_cross = right_product(grad_cq_half, full_query)
        cross_in, grad_gain_cross = jax.vjp(norm_rows, after_self, gain_cross)[1](grad_normed_cross)
        vision_term = vision_grad(features, grad_pair)
        return (cross_in, grad_gain_cross, grad_out_cross, grad_cross_weight, vision_term)

    def cross_back_off():
        square_zero = jnp.zeros((feature_width, feature_width), jnp.float32)
        vision_term = jnp.zeros((2, features.shape[2], feature_width), jnp.float32)
        return (
            jnp.zeros((row_count, feature_width), jnp.float32),
            jnp.zeros((feature_width,), jnp.float32),
            square_zero,
            square_zero,
            vision_term,
        )

    cross_in, grad_gain_cross, grad_out_cross, grad_cross_weight, vision_term = lax.cond(
        stream == 0, cross_back_on, cross_back_off
    )
    grad_after_self = grad_cross + cross_in
    grad_branch_half = to_half(grad_after_self)
    grad_out_self = left_product(context_half, grad_branch_half)
    grad_context_self = to_half(right_product(grad_branch_half, full_output[0]))

    def self_back_query():
        grad_sq, grad_sk, grad_sv = attend_back(
            query_half[None],
            key_half[None],
            value_half[None],
            query_allow[None],
            total_self,
            grad_context_self[None],
        )
        empty_rows = jnp.zeros((row_count, feature_width), jnp.float32)
        return (grad_sq[0], grad_sk[0], grad_sv[0], empty_rows, empty_rows)

    def self_back_text():
        grad_sq, grad_sk, grad_sv = attend_back(
            query_half[None],
            text_keys[None],
            text_values[None],
            text_allow[None],
            total_self,
            grad_context_self[None],
        )
        return (
            grad_sq[0],
            grad_sk[0, row_count:],
            grad_sv[0, row_count:],
            grad_sk[0, :row_count],
            grad_sv[0, :row_count],
        )

    own_query, own_key, own_value, far_grad_key, far_grad_value = lax.cond(
        stream == 0, self_back_query, self_back_text
    )
    own_query = to_half(own_query)
    own_key = to_half(own_key)
    own_value = to_half(own_value)
    far_key_half = to_half(far_grad_key)
    far_value_half = to_half(far_grad_value)
    grad_normed = (
        right_product(own_query, full_project[0])
        + right_product(own_key, full_project[1])
        + right_product(own_value, full_project[2])
    )
    grad_key_weight = left_product(normed_self, own_key)
    grad_value_weight = left_product(normed_self, own_value)
    back_key, back_value = shifted((far_key_half, far_value_half), "stream", -1)
    grad_normed = (
        grad_normed
        + right_product(back_key, full_project[1])
        + right_product(back_value, full_project[2])
    )
    grad_key_weight = grad_key_weight + left_product(normed_self, back_key)
    grad_value_weight = grad_value_weight + left_product(normed_self, back_value)
    grad_project = jnp.stack(
        [left_product(normed_self, own_query), grad_key_weight, grad_value_weight]
    )
    source_in, grad_gain_self = jax.vjp(norm_rows, source, gain_self)[1](grad_normed)
    hidden_grad = grad_after_self + source_in
    zero_row = jnp.zeros_like(grad_gain_feed)
    gain_grads = jnp.stack(
        [
            grad_gain_self,
            grad_gain_cross,
            jnp.where(stream == 0, grad_gain_feed, zero_row),
            jnp.where(stream == 1, grad_gain_feed, zero_row),
        ]
    )
    shared_grads = (
        grad_project,
        jnp.stack([grad_out_self, grad_out_cross]),
        grad_cross_weight,
        vision_term,
        gain_grads,
    )
    (
        parts_project,
        parts_output,
        parts_query,
        parts_vision,
        parts_expand,
        parts_reduce,
        parts_gains,
    ) = (
        lax.psum_scatter(shared_grads[0], "dp", scatter_dimension=1, tiled=True),
        lax.psum_scatter(shared_grads[1], "dp", scatter_dimension=1, tiled=True),
        lax.psum_scatter(shared_grads[2], "dp", scatter_dimension=0, tiled=True),
        lax.psum_scatter(shared_grads[3], "dp", scatter_dimension=1, tiled=True),
        lax.psum_scatter(grad_expand[None], "dp", scatter_dimension=1, tiled=True),
        lax.psum_scatter(grad_reduce[None], "dp", scatter_dimension=1, tiled=True),
        lax.psum_scatter(shared_grads[4], "dp", scatter_dimension=1, tiled=True),
    )
    sum_project, sum_output, sum_query, sum_vision, sum_gains = (
        lax.psum(parts_project.astype(jnp.bfloat16), "stream").astype(jnp.float32),
        lax.psum(parts_output.astype(jnp.bfloat16), "stream").astype(jnp.float32),
        lax.psum(parts_query.astype(jnp.bfloat16), "stream").astype(jnp.float32),
        lax.psum(parts_vision.astype(jnp.bfloat16), "stream").astype(jnp.float32),
        lax.psum(parts_gains.astype(jnp.bfloat16), "stream").astype(jnp.float32),
    )
    shared_square = (
        jnp.sum(sum_project * sum_project)
        + jnp.sum(sum_output * sum_output)
        + jnp.sum(sum_query * sum_query)
        + jnp.sum(sum_vision * sum_vision)
        + jnp.sum(sum_gains * sum_gains)
    )
    local_square = (
        0.5 * shared_square
        + jnp.sum(parts_expand * parts_expand)
        + jnp.sum(parts_reduce * parts_reduce)
    )
    stat_row = jnp.stack(
        [
            square_rows(source),
            square_rows(branch_self),
            square_rows(branch_feed),
            square_rows(result),
        ]
    )
    stat_local = jnp.where(
        jnp.arange(2, dtype=jnp.int32)[:, None] == stream, stat_row[None, :], 0.0
    )
    total_square, stat_sums = lax.psum((local_square, stat_local), ("stream", "dp"))
    return (
        result, hidden_grad, total_square, stat_sums, parts_expand, parts_reduce,
        (sum_project, sum_output, sum_query, sum_vision, sum_gains),
    )


def direct_body(
    hidden,
    features,
    caption_lengths,
    caption_image,
    out_grad,
    attn_project,
    attn_output,
    cross_query,
    cross_vision,
    feed_expand,
    feed_reduce,
    norm_gains,
    first_project,
    second_project,
    first_output,
    second_output,
    first_query,
    second_query,
    first_vision,
    second_vision,
    first_expand,
    second_expand,
    first_reduce,
    second_reduce,
    first_gains,
    second_gains,
):
    width = attn_project.shape[-1]
    row_count = hidden.shape[1]
    gains = jnp.pad(to_half(norm_gains), ((0, 12), (0, 128 - norm_gains.shape[1])))
    weights = (
        attn_project, attn_output, cross_query, cross_vision, feed_expand[0], feed_reduce[0],
    )
    kept = forward_all(
        weights, gains, hidden[0], out_grad[0], features, caption_lengths, caption_image,
    )
    back = backward_all(kept, hidden[0], caption_lengths, caption_image, features.shape[1])
    own_gains = norm_gains.shape[1]
    begin = lax.axis_index("dp") * own_gains
    sum_gains = lax.dynamic_slice_in_dim(back["gains"][:4], begin, own_gains, axis=1)
    sums = [back[name] for name in ("first", "vision", "expand", "reduce")]
    firsts = (
        first_project, first_output, first_query, first_vision, first_expand[0], first_reduce[0],
    )
    seconds = (
        second_project, second_output, second_query, second_vision, second_expand[0], second_reduce[0],
    )
    amount = row_count * lax.axis_size("dp") * width
    fresh, mean, square, copies, gain_new, grad_norm, rms = update_all(
        amount, back["totals"], sum_gains, (norm_gains, first_gains, second_gains), sums,
        weights, firsts, seconds,
    )
    updated = []
    for n in range(6):
        step = [part[n] if n < 4 else part[n][None] for part in (fresh, mean, square, copies)]
        updated.append(step)
    steps = [value for step in updated for value in step[:3]]
    return (
        kept["result"][None],
        back["hidden_grad"][None],
        grad_norm.reshape(()),
        rms.reshape(2, 4),
        *steps,
        *gain_new,
        *[step[3] for step in updated],
    )


def body(
    hidden,
    features,
    caption_lengths,
    caption_image,
    out_grad,
    attn_project,
    attn_output,
    cross_query,
    cross_vision,
    feed_expand,
    feed_reduce,
    norm_gains,
    first_project,
    second_project,
    first_output,
    second_output,
    first_query,
    second_query,
    first_vision,
    second_vision,
    first_expand,
    second_expand,
    first_reduce,
    second_reduce,
    first_gains,
    second_gains,
):
    if lax.axis_size("dp") == 16:
        return direct_body(
            hidden, features, caption_lengths, caption_image, out_grad, attn_project, attn_output, cross_query,
            cross_vision, feed_expand, feed_reduce, norm_gains, first_project, second_project,
            first_output, second_output, first_query, second_query, first_vision, second_vision,
            first_expand, second_expand, first_reduce, second_reduce, first_gains, second_gains,
        )
    row_count = hidden.shape[1]
    result, hidden_grad, total_square, stat_sums, parts_expand, parts_reduce, shared = general_grads(
        hidden, features, caption_lengths, caption_image, out_grad, attn_project,
        attn_output, cross_query, cross_vision, feed_expand, feed_reduce, norm_gains,
    )
    sum_project, sum_output, sum_query, sum_vision, sum_gains = shared
    grad_norm = jnp.sqrt(total_square)
    rms_values = jnp.sqrt(stat_sums / (row_count * lax.axis_size("dp")))
    factor = clip_norm / jnp.maximum(grad_norm, clip_norm)
    clipped_gains = sum_gains * factor
    fresh_expand, mean_expand, square_expand = adam_step(
        feed_expand, parts_expand, first_expand, second_expand, factor, rate_matrix, decay_rate
    )
    fresh_reduce, mean_reduce, square_reduce = adam_step(
        feed_reduce, parts_reduce, first_reduce, second_reduce, factor, rate_matrix, decay_rate
    )
    weights_shared = (attn_project, attn_output, cross_query, cross_vision, norm_gains)
    firsts_shared = (first_project, first_output, first_query, first_vision, first_gains)
    seconds_shared = (second_project, second_output, second_query, second_vision, second_gains)
    summed_shared = (sum_project, sum_output, sum_query, sum_vision, sum_gains)
    updated = []
    for index in range(5):
        rate = rate_gains if index == 4 else rate_matrix
        decay = 0.0 if index == 4 else decay_rate
        weight = weights_shared[index]
        first = firsts_shared[index]
        second = seconds_shared[index]
        updated.append(adam_step(weight, summed_shared[index], first, second, factor, rate, decay))
    fresh_project, mean_project, square_project = updated[0]
    fresh_output, mean_output, square_output = updated[1]
    fresh_query, mean_query, square_query = updated[2]
    fresh_vision, mean_vision, square_vision = updated[3]
    fresh_gains, mean_gains, square_gains = updated[4]
    return (
        result[None],
        hidden_grad[None],
        grad_norm,
        rms_values,
        fresh_project,
        mean_project,
        square_project,
        fresh_output,
        mean_output,
        square_output,
        fresh_query,
        mean_query,
        square_query,
        fresh_vision,
        mean_vision,
        square_vision,
        fresh_expand,
        mean_expand,
        square_expand,
        fresh_reduce,
        mean_reduce,
        square_reduce,
        fresh_gains,
        mean_gains,
        square_gains,
        clipped_gains,
        to_half(fresh_project),
        to_half(fresh_output),
        to_half(fresh_query),
        to_half(fresh_vision),
        to_half(fresh_expand),
        to_half(fresh_reduce),
    )


def solution(mesh):
    return jax.shard_map(
        body,
        mesh=mesh,
        in_specs=(
            P("stream", "dp", None),
            P("dp", None, None),
            P("dp", None),
            P("dp", None),
            P("stream", "dp", None),
            P(None, "dp", None),
            P(None, "dp", None),
            P("dp", None),
            P(None, "dp", None),
            P("stream", "dp", None),
            P("stream", "dp", None),
            P(None, "dp"),
            P(None, "dp", None),
            P(None, "dp", None),
            P(None, "dp", None),
            P(None, "dp", None),
            P("dp", None),
            P("dp", None),
            P(None, "dp", None),
            P(None, "dp", None),
            P("stream", "dp", None),
            P("stream", "dp", None),
            P("stream", "dp", None),
            P("stream", "dp", None),
            P(None, "dp"),
            P(None, "dp"),
        ),
        out_specs=(
            P("stream", "dp", None),
            P("stream", "dp", None),
            P(),
            P(),
            P(None, "dp", None),
            P(None, "dp", None),
            P(None, "dp", None),
            P(None, "dp", None),
            P(None, "dp", None),
            P(None, "dp", None),
            P("dp", None),
            P("dp", None),
            P("dp", None),
            P(None, "dp", None),
            P(None, "dp", None),
            P(None, "dp", None),
            P("stream", "dp", None),
            P("stream", "dp", None),
            P("stream", "dp", None),
            P("stream", "dp", None),
            P("stream", "dp", None),
            P("stream", "dp", None),
            P(None, "dp"),
            P(None, "dp"),
            P(None, "dp"),
            P(None, "dp"),
            P(None, "dp", None),
            P(None, "dp", None),
            P("dp", None),
            P(None, "dp", None),
            P("stream", "dp", None),
            P("stream", "dp", None),
        ),
        check_vma=False,
    )
```

```python
import functools

import jax
import jax.numpy as jnp
from jax import lax
from jax.experimental import pallas as pl
from jax.experimental.pallas import tpu as pltpu
from jax.sharding import PartitionSpec as P

HEADS = 12
HD = 64
NQ = 32
STEP = 10


epsilon = 1e-06
masked_value = -1e30
beta_first = 0.9
beta_second = 0.999
rate_matrix = 0.05
rate_gains = 1.0
decay_rate = 0.01
adam_floor = 1e-08
clip_norm = 1.0


def shifted(block, axis, distance):
    devices = range(lax.axis_size(axis))
    route = [(i - distance, i) for i in devices if i - distance in devices]
    return lax.ppermute(block, axis, route)


def to_half(values):
    return values.astype(jnp.bfloat16)


def product(left, right):
    return jnp.dot(left, right, preferred_element_type=jnp.float32)


def left_product(left, right):
    return lax.dot_general(
        left, right, (((0,), (0,)), ((), ())), preferred_element_type=jnp.float32
    )


def right_product(left, right):
    return lax.dot_general(
        left, right, (((1,), (1,)), ((), ())), preferred_element_type=jnp.float32
    )


def norm_rows(values, gain):
    return values * lax.rsqrt(jnp.mean(values * values, axis=-1, keepdims=True) + epsilon) * gain


def exact_gelu(values):
    return jax.nn.gelu(values, approximate=False)


def square_rows(values):
    return jnp.sum(jnp.mean(values * values, axis=-1))


def layout(lengths, owners, row_count, per_image):
    caption_ends = jnp.cumsum(lengths)
    caption_starts = caption_ends - lengths
    row_index = jnp.arange(row_count, dtype=jnp.int32)
    inside = (row_index[:, None] >= caption_starts[None, :]) & (
        row_index[:, None] < caption_ends[None, :]
    )
    caption = jnp.sum(
        jnp.where(inside, jnp.arange(lengths.shape[0], dtype=jnp.int32)[None, :], 0), axis=1
    )
    text_image = jnp.sum(jnp.where(inside, owners[None, :], 0), axis=1)
    query_image = row_index // per_image
    query_allow = query_image[:, None] == query_image[None, :]
    own_caption = (caption[:, None] == caption[None, :]) & (
        row_index[None, :] <= row_index[:, None]
    )
    text_allow = jnp.concatenate([text_image[:, None] == query_image[None, :], own_caption], axis=1)
    return (query_allow, text_allow)


def attention_scores(query_rows, key_rows, allowed):
    batch_count, query_count, width_all = query_rows.shape
    query_heads = query_rows.reshape(batch_count, query_count, HEADS, HD)
    key_heads = key_rows.reshape(batch_count, key_rows.shape[1], HEADS, HD)
    scores = jnp.einsum(
        "bqhd,bkhd->bhqk", query_heads, key_heads, preferred_element_type=jnp.float32
    ) * HD ** (-0.5)
    if allowed is not None:
        scores = jnp.where(allowed[:, None], scores, masked_value)
    return (scores, query_heads, key_heads)


def attend(query_rows, key_rows, value_rows, allowed):
    scores, query_heads, key_heads = attention_scores(query_rows, key_rows, allowed)
    value_heads = value_rows.reshape(key_heads.shape)
    row_max = jnp.max(scores, axis=-1, keepdims=True)
    weights = jnp.exp(scores - row_max)
    denominator = jnp.sum(weights, axis=-1, keepdims=True)
    probability = to_half(weights / denominator)
    context = jnp.einsum(
        "bhqk,bkhd->bqhd", probability, value_heads, preferred_element_type=jnp.float32
    )
    return (context.reshape(query_rows.shape), (row_max + jnp.log(denominator))[..., 0])


def attend_back(query_rows, key_rows, value_rows, allowed, log_total, grad_context):
    scores, query_heads, key_heads = attention_scores(query_rows, key_rows, allowed)
    value_heads = value_rows.reshape(key_heads.shape)
    probability = jnp.exp(scores - log_total[..., None])
    grad_heads = grad_context.reshape(query_heads.shape)
    grad_prob = jnp.einsum(
        "bqhd,bkhd->bhqk", grad_heads, value_heads, preferred_element_type=jnp.float32
    )
    grad_value = jnp.einsum(
        "bhqk,bqhd->bkhd", to_half(probability), grad_heads, preferred_element_type=jnp.float32
    )
    grad_score = to_half(
        probability * (grad_prob - jnp.sum(grad_prob * probability, axis=-1, keepdims=True))
    )
    grad_query = jnp.einsum(
        "bhqk,bkhd->bqhd", grad_score, key_heads, preferred_element_type=jnp.float32
    ) * HD ** (-0.5)
    grad_key = jnp.einsum(
        "bhqk,bqhd->bkhd", grad_score, query_heads, preferred_element_type=jnp.float32
    ) * HD ** (-0.5)
    return (
        grad_query.reshape(query_rows.shape),
        grad_key.reshape(key_rows.shape),
        grad_value.reshape(value_rows.shape),
    )


def project_vision(feature_block, vision_weights):
    return to_half(
        jnp.einsum(
            "inv,kvd->kind", feature_block, vision_weights, preferred_element_type=jnp.float32
        )
    )


def vision_grad(feature_block, grad_pair):
    return jnp.einsum("inv,kind->kvd", feature_block, grad_pair, preferred_element_type=jnp.float32)


def adam_step(weight, gradient, first, second, factor, rate, decay):
    clipped = gradient * factor
    mean_new = beta_first * first + (1.0 - beta_first) * clipped
    square_new = beta_second * second + (1.0 - beta_second) * clipped * clipped
    corrected_mean = mean_new / (1.0 - beta_first**STEP)
    corrected_square = square_new / (1.0 - beta_second**STEP)
    fresh = weight - rate * (
        corrected_mean / (jnp.sqrt(corrected_square) + adam_floor) + decay * weight
    )
    return (fresh, mean_new, square_new)


MESH = pl.DeviceIdType.MESH
VMEM_LIMIT = 62 * 2**20


def coordinates():
    c = lax.axis_index("stream")
    d = lax.axis_index("dp")
    return c, d // 4, (d // 2) % 2, d % 2


def device(c, z, y, x):
    return (c, z * 4 + y * 2 + x)


def meet(c, z, y, x, layer=False):
    barrier = pltpu.get_barrier_semaphore()
    others = [device(1 - c, z, y, x), device(c, z, 1 - y, x), device(c, z, y, 1 - x)]
    others += [device(c, (z + k) % 4, y, x) for k in (1, 2, 3)]
    if layer:
        others += [device(1 - c, z, 1 - y, x), device(1 - c, z, y, 1 - x)]
        others += [device(c, z, 1 - y, 1 - x), device(1 - c, z, 1 - y, 1 - x)]
    for other in others:
        pl.semaphore_signal(barrier, inc=1, device_id=other, device_id_type=MESH)
    pl.semaphore_wait(barrier, len(others))


ORDERS = {
    ("late", 0): ("z", "y", "x"),
    ("late", 1): ("z", "x", "y"),
    ("early", 0): ("x", "z", "y"),
    ("early", 1): ("y", "z", "x"),
    ("feed", 0): ("z", "o"),
    ("feed", 1): ("z", "o"),
}


PARTS = 2
LMAX = 32
GATHER_TICKS = [(0, 3, 6, 9), (2, 5, 8, 11), (4, 7, 10, 13), (6, 9, 12, 15), (8, 11, 14, 17)]
GATHER_TICKS += [(10, 17, 24), (12, 18, 24), (14, 21, 24), (16, 23, 24)]
PLANES = {
    "query": (0, 0), "key": (0, 1), "cross_output": (0, 2),
    "value": (1, 0), "self_output": (1, 1), "cross_query": (1, 2),
}


def wide(block):
    return block.astype(jnp.float32)


def nn(left, right):
    return lax.dot_general(
        left, right, (((1,), (0,)), ((), ())), preferred_element_type=jnp.float32
    )


def nt(left, right):
    return lax.dot_general(
        left, right, (((1,), (1,)), ((), ())), preferred_element_type=jnp.float32
    )


def tn(left, right):
    return lax.dot_general(
        left, right, (((0,), (0,)), ((), ())), preferred_element_type=jnp.float32
    )


def span(index, size):
    return pl.ds(pl.multiple_of(index * size, size), size)


def loop(count, step):
    def body(index, carry):
        step(index)
        return carry

    lax.fori_loop(0, count, body, 0)


def row_sum(values):
    return jnp.sum(values, axis=0, keepdims=True)


def norm_back(values, gain, grad):
    scale = lax.rsqrt(jnp.mean(values * values, axis=-1, keepdims=True) + epsilon)
    unit = values * scale
    grad_unit = grad * gain
    mean = jnp.mean(grad_unit * unit, axis=-1, keepdims=True)
    return scale * (grad_unit - unit * mean), row_sum(grad * unit)


def lane_masks(rows):
    lane = lax.broadcasted_iota(jnp.int32, (rows, 2 * HD), 1)
    left = jnp.where(lane < HD, 1.0, 0.0)
    return to_half(left), to_half(1.0 - left)


def head_pair(block, masks):
    return jnp.concatenate([block * masks[0], block * masks[1]], axis=0)


def pair_join(both):
    rows = both.shape[0] // 2
    lane = lax.broadcasted_iota(jnp.int32, (rows, 2 * HD), 1)
    return jnp.where(lane < HD, both[:rows], both[rows:])


def diagonal(full, rows):
    lane = lax.broadcasted_iota(jnp.int32, (rows, 2 * HD), 1)
    tiles = []
    for t in range(HEADS // 2):
        tile = full[:, t * 2 * HD : (t + 1) * 2 * HD]
        left = tile[2 * t * rows : (2 * t + 1) * rows]
        right = tile[(2 * t + 1) * rows : (2 * t + 2) * rows]
        tiles.append(jnp.where(lane < HD, left, right))
    return jnp.concatenate(tiles, axis=1)


def head_mask(rows, width):
    row = lax.broadcasted_iota(jnp.int32, (HEADS * rows, width), 0) // rows
    lane = lax.broadcasted_iota(jnp.int32, (HEADS * rows, width), 1) // HD
    return to_half(jnp.where(row == lane, 1.0, 0.0))


def caption_layout(lengths, owners, row_count):
    count = lengths.shape[1]
    size = wide(lengths)
    owner = wide(owners)
    sub = lax.broadcasted_iota(jnp.int32, (count, count), 0)
    lane = lax.broadcasted_iota(jnp.int32, (count, count), 1)
    starts = jnp.sum(jnp.where(lane < sub, size, 0.0), axis=1, keepdims=True)
    owner_down = jnp.sum(jnp.where(lane == sub, owner, 0.0), axis=1, keepdims=True)
    row = wide(lax.broadcasted_iota(jnp.int32, (count, row_count), 1))
    begun = starts <= row
    start = jnp.max(jnp.where(begun, starts, 0.0), axis=0, keepdims=True)
    image = jnp.max(jnp.where(begun, owner_down, 0.0), axis=0, keepdims=True)
    return start, image


def text_bias(rb, start, image, far_rows, window, bias):
    begin = jnp.maximum(rb * 128 - LMAX, 0)
    far = lax.broadcasted_iota(jnp.int32, (far_rows, 128), 0) // NQ
    far_bias = jnp.where(wide(far) == image, 0.0, masked_value)
    key = lax.broadcasted_iota(jnp.int32, (window, 128), 0) + begin
    row = lax.broadcasted_iota(jnp.int32, (window, 128), 1) + rb * 128
    seen = (wide(key) >= start) & (key <= row)
    own_bias = jnp.where(seen, 0.0, masked_value)
    bias[0:far_rows] = jnp.concatenate([far_bias, far_bias], axis=1)
    bias[far_rows : far_rows + window] = jnp.concatenate([own_bias, own_bias], axis=1)


def query_bias(bias):
    key = lax.broadcasted_iota(jnp.int32, (128, 256), 0) // NQ
    row = (lax.broadcasted_iota(jnp.int32, (128, 256), 1) % 128) // NQ
    bias[0:128] = jnp.where(key == row, 0.0, masked_value)


def forward_kernel(
    attn_project, attn_output, cross_query_weight, cross_vision, feed_expand, feed_reduce, gains,
    hidden_in, out_grad_in, features, lengths, owners,
    keep_branch, keep_after_cross, keep_mate_branch, out_grad_cross, part_expand, part_reduce, gain_feed_out, stats,
    keep_first, keep_gains, keep_normed, keep_query, keep_key, keep_value, keep_far_key, keep_far_value,
    keep_context, keep_after_self, keep_cross_query, keep_cross_context, keep_vision, keep_images, total_self, total_cross,
    all_first, raw_vision, all_vision, all_expand, all_reduce, all_gains, gain_rows,
    hidden, out_grad, images, vision_pair, normed, query, key, value, far_key, far_value, context, after_self,
    cross_query, cross_context, after_cross, normed_feed, grad_feed, sum_branch, sum_normed, got_normed, bias, mask,
    first, vision, expand, reduce, layout_rows, send_sem, recv_sem, local_sem,
):
    c, z, y, x = coordinates()
    row_count, width = hidden.shape
    image_count = total_cross.shape[0]
    padded = vision_pair.shape[0] // image_count
    feature_rows = features.shape[0] // (2 * image_count)
    feature_width = features.shape[1]
    part_rows = expand.shape[0] // PARTS
    far_rows, window = far_key.shape[0], 128 + LMAX
    cross_rows = image_count * NQ

    across_at = jnp.where(c == 0, y, x)
    own_at = {"z": z, "y": y, "x": x, "o": across_at}
    mate = (c, z * 4 + jnp.where(c == 0, y, 1 - y) * 2 + jnp.where(c == 0, 1 - x, x))
    beyond = (c, z * 4 + jnp.where(c == 0, 1 - y, y) * 2 + jnp.where(c == 0, x, 1 - x))

    chunks = [(gains, lambda *at: all_gains.at[at], "late", False)]
    chunks.append((vision, lambda *at: raw_vision.at[(c,) + at], "late", True))
    for j in range(3):
        chunks.append((first.at[j], lambda *at, j=j: all_first.at[(c, j) + at], "late", True))
    for p in range(PARTS):
        rows = pl.ds(p * part_rows, part_rows)
        for source, whole in ((expand, all_expand), (reduce, all_reduce)):
            target = lambda *at, p=p, whole=whole: whole.at[(p,) + at]
            chunks.append((source.at[rows], target, "feed", False))
    count = len(chunks)
    events = [
        (when, -stage, number)
        for number, times in enumerate(GATHER_TICKS)
        for stage, when in enumerate(times)
    ]
    last_tick = max(events)[0]

    def axes_of(number):
        return "zo" if chunks[number][2] == "feed" else "zyx"

    def stages_of(number):
        return 2 if chunks[number][2] == "feed" else 3

    def remote(source, target, index, where):
        return pltpu.make_async_remote_copy(
            src_ref=source, dst_ref=target, send_sem=send_sem.at[index],
            recv_sem=recv_sem.at[index], device_id=where, device_id_type=MESH,
        )

    def sends(number, stage, core):
        source, target, kind = chunks[number][:3]
        order = ORDERS[kind, core]
        done, axis = order[:stage], order[stage]
        at = tuple(slice(None) if a in done else own_at[a] for a in axes_of(number))
        block = target(*at)
        here = source if stage == 0 else block
        base = (number * 3 + stage) * 3
        if axis == "z":
            return [
                remote(here, block, base + k - 1, device(c, (z + k) % 4, y, x)) for k in (1, 2, 3)
            ]
        where = {"y": device(c, z, 1 - y, x), "x": device(c, z, y, 1 - x), "o": beyond}[axis]
        return [remote(here, block, base, where)]

    def place(number):
        source, target = chunks[number][:2]
        at = [own_at[a] for a in axes_of(number)]
        return pltpu.make_async_copy(source, target(*at), local_sem.at[number])

    pair = device(1 - c, z, y, x)

    def across(number):
        target = chunks[number][1]
        block = target(slice(None), slice(None), slice(None))
        return remote(block, block, count * 9 + number, pair)

    def tick_core(tick, core):
        for when, negative, number in sorted(events):
            stage = -negative
            if when != tick:
                continue
            if stage > 0:
                for copy in sends(number, stage - 1, core):
                    copy.wait_recv()
            if stage == 1:
                place(number).wait()
            if stage < stages_of(number):
                for copy in sends(number, stage, core):
                    copy.start()
                if stage == 0:
                    place(number).start()
            elif chunks[number][3]:
                across(number).start()

    def both(step):
        @pl.when(c == 0)
        def _():
            step(0)

        @pl.when(c == 1)
        def _():
            step(1)

    def tick(number):
        both(lambda core: tick_core(number, core))

    def sent(number):
        def step(core):
            for stage in range(stages_of(number)):
                for copy in sends(number, stage, core):
                    copy.wait_send()

        both(step)

    swap_base = count * 10
    near_rows, far_away = pl.ds(0, row_count), pl.ds(row_count, row_count)
    active, grad_before = vision_pair.at[pl.ds(0, 2 * row_count)], vision_pair.at[pl.ds(2 * row_count, 2 * row_count)]
    send_normed = images.at[pl.ds(0, row_count), pl.ds(0, width)]
    send_branch = images.at[pl.ds(row_count, row_count), pl.ds(0, width)]
    swaps = {
        "key": (key, far_key),
        "value": (value, far_value),
        "query": (cross_query.at[pl.ds(cross_rows, cross_rows)], cross_query.at[pl.ds(0, cross_rows)]),
        "context": (cross_context.at[pl.ds(0, cross_rows)], cross_context.at[pl.ds(cross_rows, cross_rows)]),
        "grad_feed": (grad_feed.at[near_rows], grad_feed.at[far_away]),
        "normed_feed": (normed_feed.at[near_rows], normed_feed.at[far_away]),
        "sum_normed": (send_normed, got_normed),
    }
    with_mate = ("grad_feed", "normed_feed", "sum_normed")

    def swap(name):
        source, target = swaps[name]
        where = mate if name in with_mate else pair
        return remote(source, target, swap_base + list(swaps).index(name), where)

    local_base = count
    loads = [
        (hidden_in, hidden),
        (out_grad_in, out_grad),
    ]
    step_rows = 2 * image_count * 32
    whole_steps = feature_rows // 32
    half_rows = whole_steps // 2 * step_rows
    for begin, size in ((0, half_rows), (half_rows, features.shape[0] - half_rows)):
        staged = vision_pair.at[pl.ds(0, size), pl.ds(0, feature_width)]
        loads.append((features.at[pl.ds(begin, size)], staged))
    keeps = {
        "first": (all_first, keep_first),
        "gains": (gain_rows, keep_gains),
        "normed": (normed, keep_normed),
        "query": (query, keep_query),
        "key": (key, keep_key),
        "value": (value, keep_value),
        "far_key": (far_key, keep_far_key),
        "far_value": (far_value, keep_far_value),
        "context": (context, keep_context),
        "after_self": (after_self, keep_after_self),
        "cross_query": (cross_query.at[pl.ds(0, cross_rows)], keep_cross_query),
        "cross_context": (cross_context, keep_cross_context),
        "vision": (vision_pair, keep_vision),
        "images": (images, keep_images),
        "branch": (sum_branch.at[pl.ds(0, row_count)], keep_branch),
        "after_cross": (after_cross, keep_after_cross),
        "mate_branch": (images.at[pl.ds(row_count, row_count), pl.ds(0, width)], keep_mate_branch),
        "grad_cross": (sum_normed.at[pl.ds(0, row_count)], out_grad_cross),
    }
    for p in range(PARTS):
        keeps["expand", p] = (all_expand.at[p], part_expand.at[p])
        keeps["reduce", p] = (all_reduce.at[p], part_reduce.at[p])

    shard_rows = first.shape[1]
    sources = {
        0: [attn_project.at[0], attn_project.at[1], attn_output.at[1]],
        1: [attn_project.at[2], attn_output.at[0], cross_query_weight],
    }
    shard_base = local_base + len(loads) + len(keeps)

    def shard_place(k):
        size = (shard_rows, shard_rows, shard_rows, vision.shape[0], expand.shape[0], reduce.shape[0])
        return pl.ds(sum(size[:k]), size[k])

    def shard_load(k, core):
        sources_now = sources[core] + [cross_vision.at[core], feed_expand, feed_reduce]
        target = sum_branch.at[shard_place(k)]
        return pltpu.make_async_copy(sources_now[k], target, local_sem.at[shard_base + k])

    def shard_start():
        both(lambda core: [shard_load(k, core).start() for k in range(6)] and None)

    def shard_round(k):
        both(lambda core: shard_load(k, core).wait())
        value = to_half(sum_branch[shard_place(k), :])
        if k < 3:
            first[k] = value
        else:
            (vision, expand, reduce)[k - 3][...] = value

    def load(k):
        source, target = loads[k]
        return pltpu.make_async_copy(source, target, local_sem.at[local_base + k])

    def keep(name):
        source, target = keeps[name]
        index = local_base + len(loads) + list(keeps).index(name)
        return pltpu.make_async_copy(source, target, local_sem.at[index])

    def weight(name):
        plane, j = PLANES[name]
        return all_first[plane, j].reshape(width, width)

    def gain(k):
        return gain_rows[pl.ds(k, 1), :]

    def stat(k, amount):
        row = pl.ds(c * 4 + k, 1)
        stats[row, :] = stats[row, :] + amount


    def start():
        stats[...] = jnp.zeros_like(stats)
        mask[...] = head_mask(NQ, width)
        first_row, image = caption_layout(lengths[...], owners[...], row_count)
        layout_rows[0:1] = first_row
        layout_rows[1:2] = image

    def read_gains():
        total = jnp.zeros(gain_rows.shape, jnp.float32)
        per = width // 16
        for k in range(16):
            lane = lax.broadcasted_iota(jnp.int32, (128, width), 0)
            column = lax.broadcasted_iota(jnp.int32, (128, width), 1)
            pick = to_half(jnp.where((column == lane + k * per) & (lane < per), 1.0, 0.0))
            total = total + nn(all_gains[k // 4, (k // 2) % 2, k % 2], pick)
        gain_rows[...] = total

    def self_in():
        def step(i):
            rows = span(i, 256)
            source = hidden[rows, :]
            stat(0, row_sum(source * source))
            part = to_half(norm_rows(source, gain(0)))
            normed[rows, :] = part
            query[rows, :] = to_half(nn(part, weight("query"))) * jnp.bfloat16(HD**-0.5)
            key[rows, :] = to_half(nn(part, weight("key")))
            value[rows, :] = to_half(nn(part, weight("value")))

        loop(row_count // 256, step)

    def attend_pair(rb, t, parts):
        lanes, rows = span(t, 128), span(rb, 128)
        queries = head_pair(query[rows, lanes], lane_masks(128))
        scores, most = [], None
        for keys, _, where, _ in parts:
            score = nt(keys, queries) + bias[where, :]
            scores.append(score)
            top = jnp.max(score, axis=0, keepdims=True)
            most = top if most is None else jnp.maximum(most, top)
        weights = [jnp.exp(score - most) for score in scores]
        total = sum(row_sum(part) for part in weights)
        inverse = 1.0 / total
        result = sum(
            tn(to_half(part * inverse), values) for part, (_, values, _, _) in zip(weights, parts)
        )
        context[rows, lanes] = to_half(pair_join(result))
        total_self[rb, t] = most + jnp.log(total)

    def self_query():
        query_bias(bias)

        def step(i):
            rb, t = i // 6, i % 6
            rows, lanes = span(rb, 128), span(t, 128)
            attend_pair(rb, t, [(key[rows, lanes], value[rows, lanes], pl.ds(0, 128), None)])

        loop(row_count // 128 * 6, step)

    def self_text(begin, end):
        def outer(rb):
            rb = rb + begin
            rows = span(rb, 128)
            text_bias(rb, layout_rows[0:1, rows], layout_rows[1:2, rows], far_rows, window, bias)
            near = pl.ds(pl.multiple_of(jnp.maximum(rb * 128 - LMAX, 0), LMAX), window)

            def inner(t):
                lanes = span(t, 128)
                attend_pair(rb, t, [
                    (far_key[:, lanes], far_value[:, lanes], pl.ds(0, far_rows), None),
                    (key[near, lanes], value[near, lanes], pl.ds(far_rows, window), None),
                ])

            loop(6, inner)

        loop(end - begin, outer)

    def self_out():
        def step(i):
            rows = span(i, 256)
            branch = nn(context[rows, :], weight("self_output"))
            stat(1, row_sum(branch * branch))
            after_self[rows, :] = hidden[rows, :] + branch

        loop(row_count // 256, step)

    def cross_in():
        def step(i):
            rows = span(i, 256)
            part = to_half(norm_rows(after_self[rows, :], gain(1)))
            result = to_half(nn(part, weight("cross_query"))) * jnp.bfloat16(HD**-0.5)
            cross_query[rows, :] = result

        loop(row_count // 256, step)

    def pack_vision():
        def step(i):
            plane, z_at, y_at = i // 8, (i // 2) % 4, i % 2
            left = wide(raw_vision[plane, z_at, y_at, 0])
            right = wide(raw_vision[plane, z_at, y_at, 1])
            size = 2 * left.shape[0]
            all_vision[plane, span(z_at * 2 + y_at, size), :] = to_half(
                jnp.concatenate([left, right], axis=0)
            )

        loop(16, step)

    def sort_rows(begin, rows, base):
        size = rows // (2 * image_count)
        block = max(size, 16)
        out = lax.broadcasted_iota(jnp.int32, (image_count * block, rows), 0)
        column = lax.broadcasted_iota(jnp.int32, (image_count * block, rows), 1)
        source = (out % block) * (2 * image_count) + c * image_count + out // block
        pick = to_half(jnp.where((column == source) & (out % block < size), 1.0, 0.0))
        sorted_rows = to_half(nn(pick, vision_pair[begin, 0:feature_width]))
        for j in range(image_count):
            where = pl.ds(pl.multiple_of(j * padded + base, 16), block)
            images[where, :] = sorted_rows[j * block : (j + 1) * block]

    def sort_images(part):
        def step(i):
            sort_rows(span(i, step_rows), step_rows, 32 * (i + part * (whole_steps // 2)))

        loop(whole_steps // 2, step)
        if part == 1:
            rest = feature_rows % 32 * 2 * image_count
            sort_rows(pl.ds(whole_steps // 2 * step_rows, rest), rest, whole_steps * 32)

    def project_images(begin, end):
        def step(i):
            rows = pl.ds(pl.multiple_of((i + begin) * padded, 16), padded)
            image = images[rows, :]
            vision_pair[rows, 0:width] = to_half(nn(image, all_vision[0]))
            vision_pair[rows, width : 2 * width] = to_half(nn(image, all_vision[1]))

        loop(end - begin, step)

    def cross_attend(begin, end):
        def step(i):
            i = i + begin
            rows = pl.ds(pl.multiple_of(i * padded, 16), padded)
            own_rows = span(i, NQ)
            part = cross_query[own_rows, :]
            queries = jnp.concatenate([part] * HEADS, axis=0) * mask[...]
            score = nt(vision_pair[rows, 0:width], queries)
            key_row = lax.broadcasted_iota(jnp.int32, score.shape, 0)
            score = jnp.where(key_row < feature_rows, score, masked_value)
            most = jnp.max(score, axis=0, keepdims=True)
            weights = jnp.exp(score - most)
            total = row_sum(weights)
            total_cross[i] = most + jnp.log(total)
            full = tn(to_half(weights * (1.0 / total)), vision_pair[rows, width : 2 * width])
            cross_context[own_rows, :] = to_half(diagonal(full, NQ))

        loop(end - begin, step)

    def cross_out():
        def step(i):
            rows = span(i, 256)
            after_cross[rows, :] = after_self[rows, :] + nn(cross_context[rows, :], weight("cross_output"))

        loop(row_count // 256, step)

    def round_out_grad():
        def step(i):
            rows = span(i, 128)
            grad_feed[rows, :] = to_half(out_grad[rows, :])

        loop(row_count // 128, step)

    def feed_in():
        def step(i):
            rows = span(i, 128)
            normed_feed[rows, :] = to_half(norm_rows(after_cross[rows, :], gain(2 + c)))

        loop(row_count // 128, step)

    half_parts = 2 * PARTS
    block = all_expand.shape[1] * all_expand.shape[2] * part_rows // 2

    def feed_weights(b):
        p, at = b // 2, pl.ds(all_expand.shape[1] // 2 * (b % 2), all_expand.shape[1] // 2)
        return p, at, all_expand[p, at].reshape(block, width), all_reduce[p, at].reshape(block, width)

    def feed_rows(side, b):
        rows = pl.ds(side * row_count, row_count)
        lanes = pl.ds(b * block, block)
        _, _, up, down = feed_weights(b)
        before = nt(normed_feed[rows, :], up)
        share = 0.5 * (1.0 + lax.erf(before * (0.5**0.5)))
        density = jnp.exp(before * before * -0.5) * (0.5 / jnp.pi) ** 0.5
        result = to_half(before * share)
        slope = share + before * density
        active[rows, lanes] = result
        total = nn(result, down)
        back = to_half(nt(grad_feed[rows, :], down) * slope)
        grad_before[rows, lanes] = back
        total_normed = nn(back, up)
        if b == 0:
            sum_branch[rows, :] = total
            sum_normed[rows, :] = total_normed
        else:
            sum_branch[rows, :] = sum_branch[rows, :] + total
            sum_normed[rows, :] = sum_normed[rows, :] + total_normed

    def feed_grads(b):
        lanes = pl.ds(b * block, block)
        p, at = b // 2, pl.ds(all_expand.shape[1] // 2 * (b % 2), all_expand.shape[1] // 2)
        shape = (all_expand.shape[1] // 2,) + all_expand.shape[2:]
        all_expand[p, at] = to_half(tn(grad_before[:, lanes], normed_feed[...])).reshape(shape)
        all_reduce[p, at] = to_half(tn(active[:, lanes], grad_feed[...])).reshape(shape)

    def round_partial(total, buffer):
        def step(i):
            rows = span(i, 128)
            buffer[rows, :] = to_half(total[pl.ds(pl.multiple_of(row_count + i * 128, 128), 128), :])

        loop(row_count // 128, step)

    def feed_back():
        gain_feed_out[...] = jnp.zeros_like(gain_feed_out)

        def step(i):
            rows = span(i, 128)
            grad = sum_normed[rows, :] + wide(got_normed[rows, :])
            back, gain_part = norm_back(after_cross[rows, :], gain(2 + c), grad)
            gain_feed_out[0:1, :] = gain_feed_out[0:1, :] + gain_part
            sum_normed[rows, :] = out_grad[rows, :] + back

        loop(row_count // 128, step)

    half_tick = [0]

    def ticks(until):
        while half_tick[0] <= until:
            tick(half_tick[0])
            half_tick[0] += 1

    shard_start()
    for k in range(3):
        load(k).start()
    meet(c, z, y, x)
    ticks(0)
    for k in (3, 0, 1, 2, 4, 5):
        shard_round(k)
    ticks(1)
    start()
    ticks(2)
    load(1).wait()
    round_out_grad()
    swap("grad_feed").start()
    ticks(4)
    load(2).wait()
    sort_images(0)
    load(3).start()
    ticks(7)
    load(3).wait()
    sort_images(1)
    keep("images").start()
    ticks(9)
    read_gains()
    keep("gains").start()
    ticks(11)
    across(1).wait_recv()
    pack_vision()
    quarter = image_count // 4
    project_images(0, quarter)
    ticks(13)
    project_images(quarter, 2 * quarter)
    ticks(15)
    project_images(2 * quarter, 3 * quarter)
    ticks(17)
    for number in (2, 3, 4):
        across(number).wait_recv()
    load(0).wait()
    self_in()
    for name in ("normed", "query", "key", "value"):
        keep(name).start()

    @pl.when(c == 0)
    def _():
        swap("key").start()
        swap("value").start()

    project_images(3 * quarter, image_count)
    keep("vision").start()
    ticks(18)
    keep("first").start()
    blocks = row_count // 128

    @pl.when(c == 0)
    def _():
        self_query()
        self_out()
        cross_in()
        swap("query").start()

    @pl.when(c == 1)
    def _():
        swap("key").wait_recv()
        swap("value").wait_recv()
        self_text(0, blocks // 2)
        keep("far_key").start()
        keep("far_value").start()

    ticks(20)

    @pl.when(c == 1)
    def _():
        self_text(blocks // 2, blocks)
        self_out()

    @pl.when(c == 0)
    def _():
        cross_attend(0, image_count // 2)

    ticks(21)

    @pl.when(c == 1)
    def _():
        swap("query").wait_recv()
        cross_attend(0, image_count // 2)

    @pl.when(c == 0)
    def _():
        cross_attend(image_count // 2, image_count)

    keep("context").start()
    keep("after_self").start()
    ticks(22)

    @pl.when(c == 1)
    def _():
        cross_attend(image_count // 2, image_count)
        swap("context").start()
        after_cross[...] = after_self[...]

    ticks(23)

    @pl.when(c == 0)
    def _():
        swap("context").wait_recv()
        cross_out()

    keep("cross_query").start()
    keep("cross_context").start()
    keep("after_cross").start()
    feed_in()
    swap("normed_feed").start()
    ticks(last_tick)
    for name in ("vision", "images"):
        keep(name).wait()
    for b in range(half_parts):
        feed_rows(0, b)
    swap("grad_feed").wait_recv()
    swap("normed_feed").wait_recv()
    for b in range(half_parts):
        feed_rows(1, b)
    round_partial(sum_normed, send_normed)
    swap("sum_normed").start()
    round_partial(sum_branch, send_branch)
    keep("mate_branch").start()
    keep("branch").start()
    for p in range(PARTS):
        sent(5 + 2 * p)
        sent(6 + 2 * p)
        feed_grads(2 * p)
        feed_grads(2 * p + 1)
        keep(("expand", p)).start()
        keep(("reduce", p)).start()
    swap("sum_normed").wait_recv()
    feed_back()
    keep("grad_cross").start()
    for number in range(5):
        sent(number)
    for number in range(1, 5):
        across(number).wait_send()
    for name in with_mate:
        swap(name).wait_send()

    @pl.when(c == 0)
    def _():
        swap("key").wait_send()
        swap("value").wait_send()
        swap("query").wait_send()

    @pl.when(c == 1)
    def _():
        swap("context").wait_send()

    for name in keeps:
        if name in ("vision", "images"):
            continue
        if name in ("far_key", "far_value"):

            @pl.when(c == 1)
            def _(name=name):
                keep(name).wait()

        else:
            keep(name).wait()


def forward_all(weights, gains, hidden, out_grad, features, lengths, owners):
    project, _, _, vision, expand, reduce = weights
    first = jax.ShapeDtypeStruct((3,) + project.shape[1:], project.dtype)
    vision = jax.ShapeDtypeStruct(vision.shape[1:], vision.dtype)
    half, single = jnp.bfloat16, jnp.float32
    row_count, width = hidden.shape
    image_count, feature_rows, feature_width = features.shape
    image_count = image_count // 2
    features = features.transpose(1, 0, 2).reshape(-1, feature_width)
    padded = -(-feature_rows // 16) * 16
    cross_rows = image_count * NQ
    part_rows = expand.shape[0] // PARTS
    anywhere = pl.BlockSpec(memory_space=pl.ANY)
    vmem = pl.BlockSpec(memory_space=pltpu.VMEM)
    rows_half = jax.ShapeDtypeStruct((row_count, width), half)
    rows_single = jax.ShapeDtypeStruct((row_count, width), single)
    all_first = (2,) + first.shape[:1] + (4, 2, 2) + first.shape[1:]
    all_feed = (PARTS, 4, 2, part_rows, width)
    gain_shape = (16, width)
    pair_shape = (image_count * padded, 2 * width)
    outs = {
        "branch": (rows_single, anywhere),
        "after_cross": (rows_single, anywhere),
        "mate_branch": (rows_half, anywhere),
        "grad_cross": (rows_single, anywhere),
        "part_expand": (jax.ShapeDtypeStruct(all_feed, half), anywhere),
        "part_reduce": (jax.ShapeDtypeStruct(all_feed, half), anywhere),
        "gain_feed": (jax.ShapeDtypeStruct((8, width), single), vmem),
        "stats": (jax.ShapeDtypeStruct((8, width), single), vmem),
        "first": (jax.ShapeDtypeStruct(all_first, half), anywhere),
        "gains": (jax.ShapeDtypeStruct(gain_shape, single), anywhere),
        "normed": (rows_half, anywhere),
        "query": (rows_half, anywhere),
        "key": (rows_half, anywhere),
        "value": (rows_half, anywhere),
        "far_key": (rows_half, anywhere),
        "far_value": (rows_half, anywhere),
        "context": (rows_half, anywhere),
        "after_self": (rows_single, anywhere),
        "cross_query": (jax.ShapeDtypeStruct((cross_rows, width), half), anywhere),
        "cross_context": (rows_half, anywhere),
        "vision": (jax.ShapeDtypeStruct(pair_shape, half), anywhere),
        "images": (jax.ShapeDtypeStruct((image_count * padded, feature_width), half), anywhere),
        "total_self": (jax.ShapeDtypeStruct((row_count // 128, HEADS // 2, 1, 256), single), vmem),
        "total_cross": (jax.ShapeDtypeStruct((image_count, 1, HEADS * NQ), single), vmem),
    }
    halves = (row_count, width)
    scratch = [
        pltpu.VMEM(all_first, half),
        pltpu.VMEM((2, 4, 2, 2) + vision.shape, half),
        pltpu.VMEM((2, feature_width, width), half),
        pltpu.VMEM(all_feed, half),
        pltpu.VMEM(all_feed, half),
        pltpu.VMEM((4, 2, 2) + gains.shape, half),
        pltpu.VMEM(gain_shape, single),
        pltpu.VMEM(halves, single),
        pltpu.VMEM(halves, single),
        pltpu.VMEM((image_count * padded, feature_width), half),
        pltpu.VMEM(pair_shape, half),
    ]
    scratch += [pltpu.VMEM(halves, half)] * 7
    scratch += [
        pltpu.VMEM(halves, single),
        pltpu.VMEM(halves, half),
        pltpu.VMEM(halves, half),
        pltpu.VMEM(halves, single),
        pltpu.VMEM((2 * row_count, width), half),
        pltpu.VMEM((2 * row_count, width), half),
        pltpu.VMEM((2 * row_count, width), single),
        pltpu.VMEM((2 * row_count, width), single),
        pltpu.VMEM(halves, half),
        pltpu.VMEM((row_count + 128 + LMAX, 256), single),
        pltpu.VMEM((HEADS * NQ, width), half),
        pltpu.VMEM(first.shape, half),
        pltpu.VMEM(vision.shape, half),
        pltpu.VMEM(expand.shape, half),
        pltpu.VMEM(reduce.shape, half),
        pltpu.VMEM((8, row_count), single),
        pltpu.SemaphoreType.DMA(((5 + 2 * PARTS) * 10 + 8,)),
        pltpu.SemaphoreType.DMA(((5 + 2 * PARTS) * 10 + 8,)),
        pltpu.SemaphoreType.DMA((5 + 4 + 18 + 4 * PARTS + 6,)),
    ]
    values = pl.pallas_call(
        forward_kernel,
        out_shape=[shape for shape, _ in outs.values()],
        in_specs=[anywhere] * 10 + [vmem] * 2,
        out_specs=[spec for _, spec in outs.values()],
        scratch_shapes=scratch,
        compiler_params=pltpu.CompilerParams(
            collective_id=2, has_side_effects=True, vmem_limit_bytes=VMEM_LIMIT
        ),
        name="forward_layer",
    )(*weights, gains, hidden, out_grad, features, lengths, owners)
    return dict(zip(outs, values))


def scatter_engine(chunks, send_sem, recv_sem):
    c, z, y, x = coordinates()
    own = {"z": z, "y": y, "x": x, "o": jnp.where(c == 0, y, x)}
    beyond = (c, z * 4 + jnp.where(c == 0, 1 - y, y) * 2 + jnp.where(c == 0, x, 1 - x))

    def axes_of(chunk):
        return "zo" if chunk["kind"] == "feed" else "zyx"

    def remote(source, target, index, where):
        return pltpu.make_async_remote_copy(
            src_ref=source, dst_ref=target, send_sem=send_sem.at[index],
            recv_sem=recv_sem.at[index], device_id=where, device_id_type=MESH,
        )

    def sends(number, stage, core):
        chunk = chunks[number]
        held, got = chunk["held"], chunk["got"][stage]
        order = ORDERS[chunk["kind"], core][::-1]
        done, axis = order[:stage], order[stage]
        base = (number * 3 + stage) * 3

        def block(there):
            return held.at[
                tuple(
                    there if a == axis else own[a] if a in done else slice(None)
                    for a in axes_of(chunk)
                )
            ]

        if axis == "z":
            return [
                remote(
                    block((z + k) % 4), got.at[k - 1], base + k - 1, device(c, (z + k) % 4, y, x)
                )
                for k in (1, 2, 3)
            ]
        where = {"y": device(c, z, 1 - y, x), "x": device(c, z, y, 1 - x), "o": beyond}[axis]
        return [remote(block(1 - own[axis]), got, base, where)]

    def absorb(number, stage, core):
        chunk = chunks[number]
        held, got = chunk["held"], chunk["got"][stage]
        order = ORDERS[chunk["kind"], core][::-1]
        done, axis = order[: stage + 1], order[stage]
        free = [a for a in axes_of(chunk) if a not in done]
        sizes = [4 if a == "z" else 2 for a in free]
        steps = 1
        for size in sizes:
            steps *= size

        def step(i):
            index = {}
            for a, size in reversed(list(zip(free, sizes))):
                index[a] = i % size
                i = i // size
            at = tuple(index[a] if a in index else own[a] for a in axes_of(chunk))
            inner = tuple(index[a] for a in free)
            value = wide(held[at])
            if axis == "z":
                for k in range(3):
                    value = value + wide(got[(k,) + inner])
            else:
                value = value + wide(got[inner] if inner else got[...])
            if stage == len(order) - 1:
                chunk["total"][...] = value
            else:
                held[at] = to_half(value)

        if steps == 1:
            step(0)
        else:
            loop(steps, step)

    def tick_core(now, core):
        for number, stage in [
            (number, stage)
            for stage in (3, 2, 1, 0)
            for number, chunk in enumerate(chunks)
            if stage < len(chunk["ticks"][core]) and chunk["ticks"][core][stage] == now
        ]:
            if stage == 0:
                chunks[number]["ready"](core)
            else:
                for copy in sends(number, stage - 1, core):
                    copy.wait_recv()
                absorb(number, stage - 1, core)
            if stage < len(chunks[number]["ticks"][core]) - 1:
                for copy in sends(number, stage, core):
                    copy.start()

    def each_core(step):
        @pl.when(c == 0)
        def _():
            step(0)

        @pl.when(c == 1)
        def _():
            step(1)

    def tick(now):
        each_core(lambda core: tick_core(now, core))

    def wait_sent():
        def step(core):
            for number, chunk in enumerate(chunks):
                for stage in range(len(chunk["ticks"][core]) - 1):
                    for copy in sends(number, stage, core):
                        copy.wait_send()

        each_core(step)

    last = max(max(ticks) for chunk in chunks for ticks in chunk["ticks"])
    return tick, wait_sent, remote, last


def got_shapes(kind, rows, width):
    if kind == "feed":
        return [(4, rows, width), (3, rows, width)]
    if kind == "late":
        return [(4, 2, rows, width), (4, rows, width), (3, rows, width)]
    return [(4, 2, rows, width), (3, 2, rows, width), (rows, width)]


FEED_CHUNKS = 2 * PARTS
FEED_TICKS = [(0, 2, 19), (1, 4, 19), (3, 6, 19), (5, 8, 19)]
PLANE_TICKS = (
    [(15, 17, 19, 21), (16, 18, 20, 21), (3, 5, 8, 19)],
    [(16, 18, 20, 21), (10, 15, 18, 21), (10, 15, 18, 21)],
)
VISION_TICKS = ((9, 13, 17, 21), (9, 13, 17, 21))


def backward_kernel(
    feature_rows,
    part_expand, part_reduce, grad_cross_in, hidden_in, after_self_in, first_in, gains_in,
    normed_in, query_in, key_in, value_in, far_key_in, far_value_in, context_in,
    cross_query_in, cross_context_in, vision_in, images_in, branch_in, after_cross_in, mate_branch_in, lengths, owners, total_self, total_cross, gain_feed,
    part_stats, result_out, hidden_grad_out, sum_expand, sum_reduce, sum_first, sum_vision, sum_gains, totals,
    held_expand, held_reduce, got_f0, got_f1, got_p0, got_p1, got_p2, got_v0, got_v1, got_v2,
    pair_first, pair_vision, held_vision, gains_now, gains_got, gains_z, stats_now, stats_got, stats_z,
    first, pair, images, grad_vision, cross_context, after_self, hidden, grad_after, gain_rows,
    cross_query, grad_context, grad_query, far_grad, bias, mask, sum_far_key, sum_far_value, sum_key, sum_value,
    layout_rows, gain_parts, stats, send_sem, recv_sem, local_sem,
):
    c, z, y, x = coordinates()
    row_count, width = hidden.shape
    image_count = total_cross.shape[0]
    padded = pair.shape[0] // image_count
    feature_width = images.shape[1]
    cross_rows = image_count * NQ
    part_rows = held_expand.shape[-2]
    rows_vision = held_vision.shape[-2]
    grad_normed = after_self
    far_rows, window = row_count, 128 + LMAX
    scale = HD**-0.5
    other = device(1 - c, z, y, x)

    def shelf(buffer, number):
        at = pl.ds(number // 2 * row_count, row_count), pl.ds(number % 2 * width, width)
        return buffer.at[at[0], at[1]]

    names = ("normed", "query", "key", "value", "far_key", "far_value", "context", "grad_context")
    normed, query, key, value, far_key, far_value, context, grad_context_self = (
        shelf(pair, number) for number in range(len(names))
    )
    own_query, own_key, own_value = (shelf(images, 2 * number) for number in range(3))

    loads = {
        "expand": (part_expand, held_expand),
        "reduce": (part_reduce, held_reduce),
        "grad_cross": (grad_cross_in, grad_after),
        "first": (first_in, first),
        "gains": (gains_in, gain_rows),
        "cross_context": (cross_context_in, cross_context),
        "cross_query": (cross_query_in, cross_query),
        "vision": (vision_in, pair),
        "images": (images_in, images),
        "after_self": (after_self_in, after_self),
        "hidden": (hidden_in, hidden),
        "normed": (normed_in, normed),
        "query": (query_in, query),
        "key": (key_in, key),
        "value": (value_in, value),
        "far_key": (far_key_in, far_key),
        "far_value": (far_value_in, far_value),
        "context": (context_in, context),
        "out_hidden": (grad_after, hidden_grad_out),
        "branch": (branch_in, hidden),
        "after_cross": (after_cross_in, after_self),
        "mate_branch": (mate_branch_in, grad_vision.at[1, pl.ds(0, row_count)]),
        "out_result": (hidden, result_out),
    }

    def local(name):
        source, target = loads[name]
        return pltpu.make_async_copy(source, target, local_sem.at[list(loads).index(name)])

    def pair_copy(k):
        if k == 3:
            return remote(grad_vision.at[1 - c], pair_vision, pair_base + k, other)
        return remote(first.at[1 - c, k], pair_first.at[k], pair_base + k, other)

    def ready_first(j, core):
        pair_copy(j).wait_recv()

        def step(i):
            at = (i // 4, (i // 2) % 2, i % 2)
            value = wide(first[(core, j) + at]) + wide(pair_first[(j,) + at])
            first[(core, j) + at] = to_half(value)

        loop(16, step)

    def ready_vision(core):
        pair_copy(3).wait_recv()

        def step(i):
            rows = span(i, 2 * rows_vision)
            value = wide(grad_vision[core, rows, :]) + wide(pair_vision[rows, :])
            held_vision[i // 2, i % 2, 0] = to_half(value[:rows_vision])
            held_vision[i // 2, i % 2, 1] = to_half(value[rows_vision:])

        loop(8, step)

    chunks = []
    for number in range(FEED_CHUNKS):
        p = number // 2
        held, total, name = (
            (held_expand, sum_expand, "expand"), (held_reduce, sum_reduce, "reduce")
        )[number % 2]
        chunks.append({
            "held": held.at[p], "got": [got_f0.at[number], got_f1.at[number]], "kind": "feed",
            "total": total.at[pl.ds(p * part_rows, part_rows)], "ticks": (FEED_TICKS[number],) * 2,
            "ready": (lambda core, name=name: local(name).wait()) if p == 0 else (lambda core: None),
        })
    for j in range(3):
        chunks.append({
            "held": first.at[c, j], "got": [got_p0.at[j], got_p1.at[j], got_p2.at[j]], "kind": "late",
            "total": sum_first.at[c, j], "ticks": (PLANE_TICKS[0][j], PLANE_TICKS[1][j]),
            "ready": lambda core, j=j: ready_first(j, core),
        })
    chunks.append({
        "held": held_vision, "got": [got_v0, got_v1, got_v2], "kind": "late",
        "total": sum_vision.at[c], "ticks": VISION_TICKS, "ready": ready_vision,
    })
    tick, wait_sent, remote, last = scatter_engine(chunks, send_sem, recv_sem)
    pair_base = len(chunks) * 9
    gains_base, stats_base = pair_base + 4, pair_base + 14
    back_base = stats_base + 10
    swap_base = back_base + 2

    layer = c * 4 + y * 2 + x

    def small(stage, now, got, got_z, base):
        if stage == 0:
            return [
                remote(now.at[0], got.at[layer], base + k - 1, layer_device(layer, k))
                for k in range(1, 8)
            ]
        return [
            remote(now.at[1], got_z.at[z], base + 6 + k, device(c, (z + k) % 4, y, x))
            for k in (1, 2, 3)
        ]

    def layer_device(at, k):
        c_at, y_at, x_at = k // 4, (k // 2) % 2, k % 2
        flip = lambda value, bit: 1 - value if bit else value
        return device(flip(c, c_at), z, flip(y, y_at), flip(x, x_at))

    def small_step(stage, now, got, got_z, base):
        if stage > 0:
            for copy in small(stage - 1, now, got, got_z, base):
                copy.wait()
            if stage == 1:
                got[layer] = now[0]
                now[1] = sum(got[k] for k in range(8))
            else:
                got_z[z] = now[1]
                now[2] = (got_z[0] + got_z[1]) + (got_z[2] + got_z[3])
        if stage < 2:
            for copy in small(stage, now, got, got_z, base):
                copy.start()

    def folded(values):
        total = values[:, 0:128]
        for k in range(1, values.shape[1] // 128):
            total = total + values[:, k * 128 : (k + 1) * 128]
        return total

    def squares(block):
        return jnp.sum((block * block).reshape(-1, 8, block.shape[1]), axis=0)

    own_rows, other_rows = pl.ds(0, cross_rows), pl.ds(cross_rows, cross_rows)
    swaps = {
        "context": (grad_context.at[other_rows], grad_context.at[own_rows]),
        "query": (grad_query.at[own_rows], grad_query.at[other_rows]),
        "far_key": (far_grad.at[0], far_grad.at[0]),
        "far_value": (far_grad.at[1], far_grad.at[1]),
        "branch": (grad_vision.at[1, pl.ds(0, row_count)], grad_vision.at[0, pl.ds(0, row_count)]),
    }
    mate = (c, z * 4 + jnp.where(c == 0, y, 1 - y) * 2 + jnp.where(c == 0, 1 - x, x))

    def swap(name):
        source, target = swaps[name]
        where = mate if name == "branch" else other
        return remote(source, target, swap_base + list(swaps).index(name), where)

    def weight(name):
        plane, j = PLANES[name]
        return first[plane, j].reshape(width, width)

    def gain(k):
        return gain_rows[pl.ds(k, 1), :]

    def store_weight_grad(name, value):
        plane, j = PLANES[name]
        first[plane, j] = to_half(value).reshape(first.shape[2:])


    def start():
        gain_parts[...] = jnp.zeros_like(gain_parts)
        gain_parts[pl.ds(2 + c, 1), :] = gain_feed[0:1, :]
        mask[...] = head_mask(NQ, width)
        first_row, image = caption_layout(lengths[...], owners[...], row_count)
        layout_rows[0:1] = first_row
        layout_rows[1:2] = image

    def feed_out():
        stats[...] = part_stats[...]

        def step(i):
            rows = span(i, 128)
            branch = hidden[rows, :] + wide(grad_vision[0, rows, :])
            result = after_self[rows, :] + branch
            for k, amount in ((2, branch), (3, result)):
                at = pl.ds(c * 4 + k, 1)
                stats[at, :] = stats[at, :] + row_sum(amount * amount)
            hidden[rows, :] = result

        loop(row_count // 128, step)

    def cross_out_back():
        def step(i):
            rows = span(i, 256)
            part = to_half(grad_after[rows, :])
            grad_query[rows, :] = part
            grad_context[rows, :] = to_half(nt(part, weight("cross_output")))

        loop(row_count // 256, step)
        store_weight_grad("cross_output", tn(cross_context[...], grad_query[...]))
        swap("context").start()

    def cross_back(begin, end):
        def step(i):
            i = i + begin
            rows = pl.ds(pl.multiple_of(i * padded, 16), padded)
            at = span(i, NQ)
            queries = jnp.concatenate([cross_query[at, :]] * HEADS, axis=0) * mask[...]
            grads = jnp.concatenate([grad_context[at, :]] * HEADS, axis=0) * mask[...]
            keys, values = pair[rows, 0:width], pair[rows, width : 2 * width]
            score = nt(keys, queries)
            key_row = lax.broadcasted_iota(jnp.int32, score.shape, 0)
            seen = key_row < feature_rows
            probability = jnp.exp(jnp.where(seen, score, masked_value) - total_cross[i])
            grad_prob = nt(values, grads)
            inner = row_sum(grad_prob * probability)
            grad_score = to_half(probability * (grad_prob - inner))
            full = tn(grad_score, keys)
            pair[rows, 0:width] = to_half(nn(grad_score, queries))
            pair[rows, width : 2 * width] = to_half(nn(to_half(probability), grads))
            grad_query[at, :] = to_half(diagonal(full, NQ) * scale)

        loop(end - begin, step)


    def vision_back(begin, end):
        def step(i):
            i = i + begin
            lanes = span(i, 128)
            both = to_half(tn(images[:, lanes], pair[...]))
            grad_vision[0, lanes, :] = both[:, 0:width]
            grad_vision[1, lanes, :] = both[:, width : 2 * width]

        loop(end - begin, step)

    def cross_in_back():
        def step(i):
            rows = span(i, 128)
            source = after_self[rows, :]
            grad = nt(grad_query[rows, :], weight("cross_query"))
            back, part = norm_back(source, gain(1), grad)
            gain_parts[1:2, :] = gain_parts[1:2, :] + part
            grad_after[rows, :] = grad_after[rows, :] + back
            grad_context[rows, :] = to_half(norm_rows(source, gain(1)))

        loop(row_count // 128, step)
        store_weight_grad("cross_query", tn(grad_context[...], grad_query[...]))

    def self_out_back():
        def step(i):
            rows = span(i, 256)
            part = to_half(grad_after[rows, :])
            grad_context[rows, :] = part
            grad_context_self[rows, :] = to_half(nt(part, weight("self_output")))

        loop(row_count // 256, step)
        store_weight_grad("self_output", tn(context[...], grad_context[...]))

    def attend_pair_back(rb, t, parts):
        rows, lanes = span(rb, 128), span(t, 128)
        masks = lane_masks(128)
        queries = head_pair(query[rows, lanes], masks)
        grads = head_pair(grad_context_self[rows, lanes], masks)
        kept, inner = [], 0.0
        for keys, values, where in parts:
            score = nt(keys, queries) + wide(where)
            probability = jnp.exp(score - total_self[rb, t])
            grad_prob = nt(values, grads)
            inner = inner + row_sum(grad_prob * probability)
            kept.append((probability, grad_prob))
        result, back = [], 0.0
        for (keys, values, _), (probability, grad_prob) in zip(parts, kept):
            grad_score = to_half(probability * (grad_prob - inner))
            result.append((nn(grad_score, queries), nn(to_half(probability), grads)))
            back = back + tn(grad_score, keys)
        own_query[rows, lanes] = to_half(pair_join(back) * scale)
        return result

    def self_query_back(begin, end):
        def step(i):
            rb, t = i // 6, i % 6
            rows, lanes = span(rb, 128), span(t, 128)
            parts = [(key[rows, lanes], value[rows, lanes], bias[0, 0:128])]
            ((grad_key, grad_value),) = attend_pair_back(rb, t, parts)
            own_key[rows, lanes] = to_half(grad_key)
            own_value[rows, lanes] = to_half(grad_value)

        blocks = row_count // 128

        def shifted_step(i):
            step(i + begin * blocks)

        loop((end - begin) * blocks, shifted_step)

    def text_biases():
        def step(rb):
            rows = span(rb, 128)
            start_row, image = layout_rows[0:1, rows], layout_rows[1:2, rows]
            begin = jnp.maximum(rb * 128 - LMAX, 0)
            far = lax.broadcasted_iota(jnp.int32, (far_rows, 128), 0) // NQ
            far_bias = jnp.where(wide(far) == image, 0.0, masked_value)
            key_row = lax.broadcasted_iota(jnp.int32, (window, 128), 0) + begin
            row = lax.broadcasted_iota(jnp.int32, (window, 128), 1) + rb * 128
            seen = (wide(key_row) >= start_row) & (key_row <= row)
            own_bias = jnp.where(seen, 0.0, masked_value)
            bias[rb, 0:far_rows] = to_half(jnp.concatenate([far_bias, far_bias], axis=1))
            bias[rb, far_rows : far_rows + window] = to_half(
                jnp.concatenate([own_bias, own_bias], axis=1)
            )

        loop(row_count // 128, step)

    def query_biases():
        key_row = lax.broadcasted_iota(jnp.int32, (128, 256), 0) // NQ
        row = (lax.broadcasted_iota(jnp.int32, (128, 256), 1) % 128) // NQ
        bias[0, 0:128] = to_half(jnp.where(key_row == row, 0.0, masked_value))

    def self_text_back(begin, end):
        def outer(t):
            t = t + begin
            lanes = span(t, 128)
            for total in (sum_far_key, sum_far_value, sum_key, sum_value):
                total[...] = jnp.zeros_like(total)

            def inner(rb):
                near = pl.ds(pl.multiple_of(jnp.maximum(rb * 128 - LMAX, 0), LMAX), window)
                parts = [
                    (far_key[:, lanes], far_value[:, lanes], bias[rb, 0:far_rows]),
                    (key[near, lanes], value[near, lanes], bias[rb, far_rows : far_rows + window]),
                ]
                far_part, near_part = attend_pair_back(rb, t, parts)
                sum_far_key[...] += far_part[0]
                sum_far_value[...] += far_part[1]
                sum_key[near, :] = sum_key[near, :] + near_part[0]
                sum_value[near, :] = sum_value[near, :] + near_part[1]

            loop(row_count // 128, inner)
            far_grad[0, :, lanes] = to_half(sum_far_key[...])
            far_grad[1, :, lanes] = to_half(sum_far_value[...])
            own_key[:, lanes] = to_half(sum_key[...])
            own_value[:, lanes] = to_half(sum_value[...])

        loop(end - begin, outer)

    def self_in_back(name, own, far):
        def step(i):
            rows = span(i, 256)
            grad = nt(own[rows, :], weight(name))
            if far is not None:
                grad = grad + nt(far_grad[far, rows, :], weight(name))
            if name != "query":
                grad = grad_normed[rows, :] + grad
            grad_normed[rows, :] = grad

        loop(row_count // 256, step)

    def project_back(name, own, far):
        self_in_back(name, own, far)
        grad = tn(normed[...], own[...])
        if far is not None:
            grad = grad + tn(normed[...], far_grad[far])
        store_weight_grad(name, grad)

    def hidden_back():
        def step(i):
            rows = span(i, 128)
            back, part = norm_back(hidden[rows, :], gain(0), grad_normed[rows, :])
            gain_parts[0:1, :] = gain_parts[0:1, :] + part
            grad_after[rows, :] = grad_after[rows, :] + back

        loop(row_count // 128, step)

    def send_pair(core, *names):
        @pl.when(c == core)
        def _():
            for name in names:
                plane, j = PLANES[name]
                if plane != core:
                    pair_copy(j).start()

    for name in ("mate_branch", "expand", "reduce", "grad_cross", "first", "cross_context", "branch",
                 "after_cross", "vision", "cross_query", "images", "gains"):
        local(name).start()
    meet(c, z, y, x, layer=True)
    local("mate_branch").wait()
    swap("branch").start()
    tick(0)
    start()
    local("grad_cross").wait()
    local("first").wait()
    local("cross_context").wait()

    @pl.when(c == 0)
    def _():
        cross_out_back()

    @pl.when(c == 1)
    def _():
        plane, j = PLANES["cross_output"]
        first[plane, j] = jnp.zeros(first.shape[2:], jnp.bfloat16)
        plane, j = PLANES["cross_query"]
        first[plane, j] = jnp.zeros(first.shape[2:], jnp.bfloat16)
        swap("context").wait_recv()

    send_pair(1, "cross_output")
    tick(1)
    local("vision").wait()
    local("cross_query").wait()
    quarter = image_count // 4
    for k in range(4):
        cross_back(k * quarter, (k + 1) * quarter)
        if k == 1:
            local("branch").wait()
            local("after_cross").wait()
            swap("branch").wait_recv()
            feed_out()
            local("out_result").start()
            local("after_self").start()
        tick(2 + k)

    @pl.when(c == 1)
    def _():
        swap("query").start()

    local("images").wait()
    swap("branch").wait_send()
    local("out_result").wait()
    local("hidden").start()
    tiles = feature_width // 128
    vision_back(0, tiles // 3)
    tick(6)
    vision_back(tiles // 3, 2 * tiles // 3)
    tick(7)
    vision_back(2 * tiles // 3, tiles)
    pair_copy(3).start()
    for name in names[:-1]:
        local(name).start()
    tick(8)
    local("after_self").wait()
    local("gains").wait()

    @pl.when(c == 0)
    def _():
        swap("query").wait_recv()
        swap("context").wait_send()
        cross_in_back()

    send_pair(0, "cross_query")
    for name in names[:-1]:
        local(name).wait()
    self_out_back()
    send_pair(0, "self_output")
    tick(9)

    @pl.when(c == 0)
    def _():
        query_biases()
        self_query_back(0, 3)

    @pl.when(c == 1)
    def _():
        text_biases()

    for t in range(6):

        @pl.when(c == 1)
        def _(t=t):
            self_text_back(t, t + 1)

        if t == 1:

            @pl.when(c == 0)
            def _():
                self_query_back(3, 6)

        if t < 5:
            tick(10 + t)

    @pl.when(c == 1)
    def _():
        swap("far_key").start()
        swap("far_value").start()

    project_back("query", own_query, None)
    send_pair(1, "query")

    @pl.when(c == 0)
    def _():
        swap("far_key").wait_recv()
        swap("far_value").wait_recv()
        project_back("value", own_value, 1)

    @pl.when(c == 1)
    def _():
        project_back("key", own_key, None)

    send_pair(0, "value")
    send_pair(1, "key")
    tick(15)

    @pl.when(c == 0)
    def _():
        project_back("key", own_key, 0)

    @pl.when(c == 1)
    def _():
        project_back("value", own_value, None)

    tick(16)
    local("hidden").wait()
    hidden_back()
    local("out_hidden").start()
    gains_now[0] = gain_parts[...]
    for now in range(17, 21):
        if now < 20:
            small_step(now - 17, gains_now, gains_got, gains_z, gains_base)
        tick(now)
    gains = gains_now[2]
    sum_gains[...] = gains
    mass = jnp.where((c == 0) & (z + y + x == 0), 1.0, 0.0) * (gains * gains)
    mass = mass + squares(sum_expand[...]) + squares(sum_reduce[...])
    tick(21)
    back = [
        remote(sum_first.at[c], sum_first.at[c], back_base, other),
        remote(sum_vision.at[c], sum_vision.at[c], back_base + 1, other),
    ]
    for copy in back:
        copy.start()
    for j in range(3):
        mass = mass + squares(sum_first[c, j])
    mass = mass + squares(sum_vision[c])
    stats_now[0, 0:8] = folded(mass)
    stats_now[0, 8:16] = folded(stats[...])
    for stage in range(3):
        small_step(stage, stats_now, stats_got, stats_z, stats_base)
    totals[...] = stats_now[2]
    for copy in back:
        copy.wait()
    assert last == 21
    wait_sent()
    for k in range(4):
        pair_copy(k).wait_send()

    @pl.when(c == 1)
    def _():
        swap("query").wait_send()
        swap("far_key").wait_send()
        swap("far_value").wait_send()

    local("out_hidden").wait()


def backward_all(kept, hidden, lengths, owners, feature_rows):
    half, single = jnp.bfloat16, jnp.float32
    row_count, width = hidden.shape
    feature_width = kept["images"].shape[1]
    parts = kept["part_expand"].shape
    part_rows = parts[-2]
    rows_first = kept["first"].shape[-2]
    rows_vision = feature_width // 16
    cross_rows = kept["cross_query"].shape[0]
    anywhere = pl.BlockSpec(memory_space=pl.ANY)
    vmem = pl.BlockSpec(memory_space=pltpu.VMEM)
    rows_half, rows_single = pltpu.VMEM((row_count, width), half), pltpu.VMEM((row_count, width), single)
    outs = {
        "result": (jax.ShapeDtypeStruct((row_count, width), single), anywhere),
        "hidden_grad": (jax.ShapeDtypeStruct((row_count, width), single), anywhere),
        "expand": (jax.ShapeDtypeStruct((PARTS * part_rows, width), single), vmem),
        "reduce": (jax.ShapeDtypeStruct((PARTS * part_rows, width), single), vmem),
        "first": (jax.ShapeDtypeStruct((2, 3, rows_first, width), single), vmem),
        "vision": (jax.ShapeDtypeStruct((2, rows_vision, width), single), vmem),
        "gains": (jax.ShapeDtypeStruct((8, width), single), vmem),
        "totals": (jax.ShapeDtypeStruct((16, 128), single), vmem),
    }
    scratch = [pltpu.VMEM(parts, half)] * 2
    scratch += [
        pltpu.VMEM((FEED_CHUNKS,) + shape, half) for shape in got_shapes("feed", part_rows, width)
    ]
    scratch += [pltpu.VMEM((3,) + shape, half) for shape in got_shapes("late", rows_first, width)]
    scratch += [pltpu.VMEM(shape, half) for shape in got_shapes("late", rows_vision, width)]
    scratch += [
        pltpu.VMEM(kept["first"].shape[1:], half),
        pltpu.VMEM((feature_width, width), half),
        pltpu.VMEM((4, 2, 2, rows_vision, width), half),
    ]
    for shape in ((8, width), (16, 128)):
        scratch += [pltpu.VMEM((number,) + shape, single) for number in (3, 8, 4)]
    scratch += [
        pltpu.VMEM(kept["first"].shape, half),
        pltpu.VMEM(kept["vision"].shape, half),
        pltpu.VMEM(kept["images"].shape, half),
        pltpu.VMEM((2, feature_width, width), half),
        rows_half,
        rows_single,
        rows_single,
        rows_single,
        pltpu.VMEM((16, width), single),
        pltpu.VMEM((cross_rows, width), half),
        rows_half,
        rows_half,
        pltpu.VMEM((2, row_count, width), half),
        pltpu.VMEM((row_count // 128, row_count + 128 + LMAX, 256), half),
        pltpu.VMEM((HEADS * NQ, width), half),
    ]
    scratch += [pltpu.VMEM((row_count, 128), single)] * 4
    scratch += [
        pltpu.VMEM((8, row_count), single),
        pltpu.VMEM((8, width), single),
        pltpu.VMEM((8, width), single),
        pltpu.SemaphoreType.DMA(((FEED_CHUNKS + 4) * 9 + 4 + 22 + 5,)),
        pltpu.SemaphoreType.DMA(((FEED_CHUNKS + 4) * 9 + 4 + 22 + 5,)),
        pltpu.SemaphoreType.DMA((23,)),
    ]
    order = ("part_expand", "part_reduce", "grad_cross", None, "after_self", "first", "gains", "normed",
             "query", "key", "value", "far_key", "far_value", "context", "cross_query", "cross_context",
             "vision", "images", "branch", "after_cross", "mate_branch")
    values = pl.pallas_call(
        functools.partial(backward_kernel, feature_rows),
        out_shape=[shape for shape, _ in outs.values()],
        in_specs=[anywhere] * len(order) + [vmem] * 6,
        out_specs=[spec for _, spec in outs.values()],
        scratch_shapes=scratch,
        compiler_params=pltpu.CompilerParams(
            collective_id=3, has_side_effects=True, vmem_limit_bytes=VMEM_LIMIT
        ),
        name="backward_layer",
    )(
        *[hidden if name is None else kept[name] for name in order],
        lengths, owners, kept["total_self"], kept["total_cross"], kept["gain_feed"], kept["stats"],
    )
    return dict(zip(outs, values))


NAMES = ("project", "output", "query", "vision", "expand", "reduce")
SUM_OF = {
    "project": ("query", "key", "value"), "output": ("self_output", "cross_output"), "query": ("cross_query",),
}


def update_kernel(amount, totals, sum_gains, gains, first_gains, second_gains, *refs):
    count = len(NAMES)
    sums, refs = refs[:4], refs[4:]
    inputs, refs = [refs[k * count : (k + 1) * count] for k in range(3)], refs[3 * count :]
    outputs, refs = [refs[k * count : (k + 1) * count] for k in range(4)], refs[4 * count :]
    gain_outs, norm_out, rms_out, refs = refs[:4], refs[4], refs[5], refs[6:]
    held_sums, refs = refs[:4], refs[4:]
    held, refs = [refs[k * count : (k + 1) * count] for k in range(3)], refs[3 * count :]
    half, sems = refs[:count], refs[count]

    def load_sum(k):
        return pltpu.make_async_copy(sums[k], held_sums[k], sems.at[k])

    def load(k, n):
        return pltpu.make_async_copy(inputs[k][n], held[k][n], sems.at[4 + k * count + n])

    def store(k, n):
        source = half[n] if k == 3 else held[k][n]
        return pltpu.make_async_copy(source, outputs[k][n], sems.at[4 + (3 + k) * count + n])

    for k in range(4):
        load_sum(k).start()
    for n in range(count):
        for k in range(3):
            load(k, n).start()
    lanes = jnp.sum(totals[0:8], axis=1, keepdims=True)
    grad_norm = jnp.sqrt(jnp.sum(lanes, axis=0, keepdims=True))
    norm_out[...] = grad_norm
    factor = clip_norm / jnp.maximum(grad_norm, clip_norm)
    rms_out[...] = jnp.sqrt(jnp.sum(totals[8:16], axis=1, keepdims=True) / amount)
    clipped = sum_gains[...] * factor
    fresh, mean, square = adam_step(
        gains[...], sum_gains[...], first_gains[...], second_gains[...], factor, rate_gains, 0.0
    )
    for target, value in zip(gain_outs, (fresh, mean, square, clipped)):
        target[...] = value
    for k in range(4):
        load_sum(k).wait()
    for n, name in enumerate(NAMES):
        for k in range(3):
            load(k, n).wait()
        weight, first, second = (held[k][n] for k in range(3))
        pieces = weight.shape[0] if len(weight.shape) == 3 else 1
        for j in range(pieces):
            at = (j,) if len(weight.shape) == 3 else (Ellipsis,)
            if name in SUM_OF:
                gradient = held_sums[0][PLANES[SUM_OF[name][j]]]
            else:
                gradient = held_sums[NAMES.index(name) - 2][at]
            fresh, mean, square = adam_step(
                weight[at], gradient, first[at], second[at], factor, rate_matrix, decay_rate
            )
            weight[at], first[at], second[at] = fresh, mean, square
            half[n][at] = to_half(fresh)
        for k in range(4):
            store(k, n).start()
    for n in range(count):
        for k in range(4):
            store(k, n).wait()


def update_all(amount, totals, sum_gains, gain_state, sums, weights, firsts, seconds):
    single, half = jnp.float32, jnp.bfloat16
    anywhere, vmem = pl.BlockSpec(memory_space=pl.ANY), pl.BlockSpec(memory_space=pltpu.VMEM)
    count = len(NAMES)
    shapes = [weight.shape for weight in weights]
    out_shape = [jax.ShapeDtypeStruct(shape, single) for _ in range(3) for shape in shapes]
    out_shape += [jax.ShapeDtypeStruct(shape, half) for shape in shapes]
    out_shape += [jax.ShapeDtypeStruct(sum_gains.shape, single)] * 4
    out_shape += [jax.ShapeDtypeStruct((1, 1), single), jax.ShapeDtypeStruct((8, 1), single)]
    scratch = [pltpu.VMEM(value.shape, single) for value in sums]
    scratch += [pltpu.VMEM(shape, single) for _ in range(3) for shape in shapes]
    scratch += [pltpu.VMEM(shape, half) for shape in shapes]
    scratch += [pltpu.SemaphoreType.DMA((4 + 7 * count,))]
    values = pl.pallas_call(
        functools.partial(update_kernel, amount),
        out_shape=out_shape,
        in_specs=[vmem] * 5 + [anywhere] * (4 + 3 * count),
        out_specs=[anywhere] * (4 * count) + [vmem] * 6,
        scratch_shapes=scratch,
        compiler_params=pltpu.CompilerParams(vmem_limit_bytes=VMEM_LIMIT),
        name="update_weights",
    )(totals, sum_gains, *gain_state, *sums, *weights, *firsts, *seconds)
    fresh, mean, square, copies = (values[k * count : (k + 1) * count] for k in range(4))
    return fresh, mean, square, copies, values[4 * count : 4 * count + 4], values[-2], values[-1]


def general_grads(
    hidden,
    features,
    caption_lengths,
    caption_image,
    out_grad,
    attn_project,
    attn_output,
    cross_query,
    cross_vision,
    feed_expand,
    feed_reduce,
    norm_gains,
):
    stream = lax.axis_index("stream")
    full_project, full_output, full_query, full_vision, full_expand, full_reduce, full_gains = (
        lax.all_gather(to_half(attn_project), "dp", axis=1, tiled=True),
        lax.all_gather(to_half(attn_output), "dp", axis=1, tiled=True),
        lax.all_gather(to_half(cross_query), "dp", axis=0, tiled=True),
        lax.all_gather(to_half(cross_vision), "dp", axis=1, tiled=True),
        lax.all_gather(to_half(feed_expand), "dp", axis=1, tiled=True),
        lax.all_gather(to_half(feed_reduce), "dp", axis=1, tiled=True),
        lax.all_gather(to_half(norm_gains), "dp", axis=1, tiled=True),
    )
    gain_rows = full_gains.astype(jnp.float32)
    gain_self = gain_rows[0]
    gain_cross = gain_rows[1]
    gain_feed = lax.dynamic_index_in_dim(gain_rows, 2 + stream, 0, keepdims=False)
    source = hidden[0]
    row_count = source.shape[0]
    feature_width = source.shape[1]
    image_count = features.shape[0]
    query_allow, text_allow = layout(caption_lengths[0], caption_image[0], row_count, NQ)
    normed_self = to_half(norm_rows(source, gain_self))
    query_half = to_half(product(normed_self, full_project[0]))
    key_half = to_half(product(normed_self, full_project[1]))
    value_half = to_half(product(normed_self, full_project[2]))
    empty_half = jnp.zeros((row_count, feature_width), jnp.bfloat16)
    far_key, far_value = shifted((key_half, value_half), "stream", 1)
    text_keys = jnp.concatenate([far_key, key_half], axis=0)
    text_values = jnp.concatenate([far_value, value_half], axis=0)

    def self_query():
        return attend(query_half[None], key_half[None], value_half[None], query_allow[None])

    def self_text():
        return attend(query_half[None], text_keys[None], text_values[None], text_allow[None])

    context_self, total_self = lax.cond(stream == 0, self_query, self_text)
    context_half = to_half(context_self[0])
    branch_self = product(context_half, full_output[0])
    after_self = source + branch_self

    def cross_on():
        normed_cross = to_half(norm_rows(after_self, gain_cross))
        cross_half = to_half(product(normed_cross, full_query))
        vision_pair = project_vision(features, full_vision)
        context_cross, total_cross = attend(
            cross_half.reshape(image_count, NQ, feature_width), vision_pair[0], vision_pair[1], None
        )
        context_cross_half = to_half(context_cross.reshape(row_count, feature_width))
        branch = product(context_cross_half, full_output[1])
        return (branch, total_cross, vision_pair, normed_cross, cross_half, context_cross_half)

    def cross_off():
        return (
            jnp.zeros((row_count, feature_width), jnp.float32),
            jnp.zeros((image_count, HEADS, NQ), jnp.float32),
            jnp.zeros((2, image_count, features.shape[1], feature_width), jnp.bfloat16),
            empty_half,
            empty_half,
            empty_half,
        )

    branch_cross, total_cross, vision_pair, normed_cross, cross_half, context_cross_half = lax.cond(
        stream == 0, cross_on, cross_off
    )
    after_cross = after_self + branch_cross
    normed_feed = to_half(norm_rows(after_cross, gain_feed))
    before = right_product(normed_feed, full_expand[0])
    active_half = to_half(exact_gelu(before))
    branch_feed = product(active_half, full_reduce[0])
    result = after_cross + branch_feed
    grad_result = out_grad[0]
    grad_feed_half = to_half(grad_result)
    grad_reduce = left_product(active_half, grad_feed_half)
    grad_active = right_product(grad_feed_half, full_reduce[0])
    grad_before = to_half(jax.vjp(exact_gelu, before)[1](grad_active)[0])
    grad_expand = left_product(grad_before, normed_feed)
    grad_normed_feed = product(grad_before, full_expand[0])
    feed_in, grad_gain_feed = jax.vjp(norm_rows, after_cross, gain_feed)[1](grad_normed_feed)
    grad_cross = grad_result + feed_in

    def cross_back_on():
        grad_branch_half = to_half(grad_cross)
        grad_out_cross = left_product(context_cross_half, grad_branch_half)
        grad_context = to_half(right_product(grad_branch_half, full_output[1]))
        grad_cq, grad_ck, grad_cv = attend_back(
            cross_half.reshape(image_count, NQ, feature_width),
            vision_pair[0],
            vision_pair[1],
            None,
            total_cross,
            grad_context.reshape(image_count, NQ, feature_width),
        )
        grad_cq_half = to_half(grad_cq.reshape(row_count, feature_width))
        grad_pair = to_half(jnp.stack([grad_ck, grad_cv]))
        grad_cross_weight = left_product(normed_cross, grad_cq_half)
        grad_normed_cross = right_product(grad_cq_half, full_query)
        cross_in, grad_gain_cross = jax.vjp(norm_rows, after_self, gain_cross)[1](grad_normed_cross)
        vision_term = vision_grad(features, grad_pair)
        return (cross_in, grad_gain_cross, grad_out_cross, grad_cross_weight, vision_term)

    def cross_back_off():
        square_zero = jnp.zeros((feature_width, feature_width), jnp.float32)
        vision_term = jnp.zeros((2, features.shape[2], feature_width), jnp.float32)
        return (
            jnp.zeros((row_count, feature_width), jnp.float32),
            jnp.zeros((feature_width,), jnp.float32),
            square_zero,
            square_zero,
            vision_term,
        )

    cross_in, grad_gain_cross, grad_out_cross, grad_cross_weight, vision_term = lax.cond(
        stream == 0, cross_back_on, cross_back_off
    )
    grad_after_self = grad_cross + cross_in
    grad_branch_half = to_half(grad_after_self)
    grad_out_self = left_product(context_half, grad_branch_half)
    grad_context_self = to_half(right_product(grad_branch_half, full_output[0]))

    def self_back_query():
        grad_sq, grad_sk, grad_sv = attend_back(
            query_half[None],
            key_half[None],
            value_half[None],
            query_allow[None],
            total_self,
            grad_context_self[None],
        )
        empty_rows = jnp.zeros((row_count, feature_width), jnp.float32)
        return (grad_sq[0], grad_sk[0], grad_sv[0], empty_rows, empty_rows)

    def self_back_text():
        grad_sq, grad_sk, grad_sv = attend_back(
            query_half[None],
            text_keys[None],
            text_values[None],
            text_allow[None],
            total_self,
            grad_context_self[None],
        )
        return (
            grad_sq[0],
            grad_sk[0, row_count:],
            grad_sv[0, row_count:],
            grad_sk[0, :row_count],
            grad_sv[0, :row_count],
        )

    own_query, own_key, own_value, far_grad_key, far_grad_value = lax.cond(
        stream == 0, self_back_query, self_back_text
    )
    own_query = to_half(own_query)
    own_key = to_half(own_key)
    own_value = to_half(own_value)
    far_key_half = to_half(far_grad_key)
    far_value_half = to_half(far_grad_value)
    grad_normed = (
        right_product(own_query, full_project[0])
        + right_product(own_key, full_project[1])
        + right_product(own_value, full_project[2])
    )
    grad_key_weight = left_product(normed_self, own_key)
    grad_value_weight = left_product(normed_self, own_value)
    back_key, back_value = shifted((far_key_half, far_value_half), "stream", -1)
    grad_normed = (
        grad_normed
        + right_product(back_key, full_project[1])
        + right_product(back_value, full_project[2])
    )
    grad_key_weight = grad_key_weight + left_product(normed_self, back_key)
    grad_value_weight = grad_value_weight + left_product(normed_self, back_value)
    grad_project = jnp.stack(
        [left_product(normed_self, own_query), grad_key_weight, grad_value_weight]
    )
    source_in, grad_gain_self = jax.vjp(norm_rows, source, gain_self)[1](grad_normed)
    hidden_grad = grad_after_self + source_in
    zero_row = jnp.zeros_like(grad_gain_feed)
    gain_grads = jnp.stack(
        [
            grad_gain_self,
            grad_gain_cross,
            jnp.where(stream == 0, grad_gain_feed, zero_row),
            jnp.where(stream == 1, grad_gain_feed, zero_row),
        ]
    )
    shared_grads = (
        grad_project,
        jnp.stack([grad_out_self, grad_out_cross]),
        grad_cross_weight,
        vision_term,
        gain_grads,
    )
    (
        parts_project,
        parts_output,
        parts_query,
        parts_vision,
        parts_expand,
        parts_reduce,
        parts_gains,
    ) = (
        lax.psum_scatter(shared_grads[0], "dp", scatter_dimension=1, tiled=True),
        lax.psum_scatter(shared_grads[1], "dp", scatter_dimension=1, tiled=True),
        lax.psum_scatter(shared_grads[2], "dp", scatter_dimension=0, tiled=True),
        lax.psum_scatter(shared_grads[3], "dp", scatter_dimension=1, tiled=True),
        lax.psum_scatter(grad_expand[None], "dp", scatter_dimension=1, tiled=True),
        lax.psum_scatter(grad_reduce[None], "dp", scatter_dimension=1, tiled=True),
        lax.psum_scatter(shared_grads[4], "dp", scatter_dimension=1, tiled=True),
    )
    sum_project, sum_output, sum_query, sum_vision, sum_gains = (
        lax.psum(parts_project.astype(jnp.bfloat16), "stream").astype(jnp.float32),
        lax.psum(parts_output.astype(jnp.bfloat16), "stream").astype(jnp.float32),
        lax.psum(parts_query.astype(jnp.bfloat16), "stream").astype(jnp.float32),
        lax.psum(parts_vision.astype(jnp.bfloat16), "stream").astype(jnp.float32),
        lax.psum(parts_gains.astype(jnp.bfloat16), "stream").astype(jnp.float32),
    )
    shared_square = (
        jnp.sum(sum_project * sum_project)
        + jnp.sum(sum_output * sum_output)
        + jnp.sum(sum_query * sum_query)
        + jnp.sum(sum_vision * sum_vision)
        + jnp.sum(sum_gains * sum_gains)
    )
    local_square = (
        0.5 * shared_square
        + jnp.sum(parts_expand * parts_expand)
        + jnp.sum(parts_reduce * parts_reduce)
    )
    stat_row = jnp.stack(
        [
            square_rows(source),
            square_rows(branch_self),
            square_rows(branch_feed),
            square_rows(result),
        ]
    )
    stat_local = jnp.where(
        jnp.arange(2, dtype=jnp.int32)[:, None] == stream, stat_row[None, :], 0.0
    )
    total_square, stat_sums = lax.psum((local_square, stat_local), ("stream", "dp"))
    return (
        result, hidden_grad, total_square, stat_sums, parts_expand, parts_reduce,
        (sum_project, sum_output, sum_query, sum_vision, sum_gains),
    )


def direct_body(
    hidden,
    features,
    caption_lengths,
    caption_image,
    out_grad,
    attn_project,
    attn_output,
    cross_query,
    cross_vision,
    feed_expand,
    feed_reduce,
    norm_gains,
    first_project,
    second_project,
    first_output,
    second_output,
    first_query,
    second_query,
    first_vision,
    second_vision,
    first_expand,
    second_expand,
    first_reduce,
    second_reduce,
    first_gains,
    second_gains,
):
    width = attn_project.shape[-1]
    row_count = hidden.shape[1]
    gains = jnp.pad(to_half(norm_gains), ((0, 12), (0, 128 - norm_gains.shape[1])))
    weights = (
        attn_project, attn_output, cross_query, cross_vision, feed_expand[0], feed_reduce[0],
    )
    kept = forward_all(
        weights, gains, hidden[0], out_grad[0], features, caption_lengths, caption_image,
    )
    back = backward_all(kept, hidden[0], caption_lengths, caption_image, features.shape[1])
    own_gains = norm_gains.shape[1]
    begin = lax.axis_index("dp") * own_gains
    sum_gains = lax.dynamic_slice_in_dim(back["gains"][:4], begin, own_gains, axis=1)
    sums = [back[name] for name in ("first", "vision", "expand", "reduce")]
    firsts = (
        first_project, first_output, first_query, first_vision, first_expand[0], first_reduce[0],
    )
    seconds = (
        second_project, second_output, second_query, second_vision, second_expand[0], second_reduce[0],
    )
    amount = row_count * lax.axis_size("dp") * width
    fresh, mean, square, copies, gain_new, grad_norm, rms = update_all(
        amount, back["totals"], sum_gains, (norm_gains, first_gains, second_gains), sums,
        weights, firsts, seconds,
    )
    updated = []
    for n in range(6):
        step = [part[n] if n < 4 else part[n][None] for part in (fresh, mean, square, copies)]
        updated.append(step)
    steps = [value for step in updated for value in step[:3]]
    return (
        back["result"][None],
        back["hidden_grad"][None],
        grad_norm.reshape(()),
        rms.reshape(2, 4),
        *steps,
        *gain_new,
        *[step[3] for step in updated],
    )


def body(
    hidden,
    features,
    caption_lengths,
    caption_image,
    out_grad,
    attn_project,
    attn_output,
    cross_query,
    cross_vision,
    feed_expand,
    feed_reduce,
    norm_gains,
    first_project,
    second_project,
    first_output,
    second_output,
    first_query,
    second_query,
    first_vision,
    second_vision,
    first_expand,
    second_expand,
    first_reduce,
    second_reduce,
    first_gains,
    second_gains,
):
    if lax.axis_size("dp") == 16:
        return direct_body(
            hidden, features, caption_lengths, caption_image, out_grad, attn_project, attn_output, cross_query,
            cross_vision, feed_expand, feed_reduce, norm_gains, first_project, second_project,
            first_output, second_output, first_query, second_query, first_vision, second_vision,
            first_expand, second_expand, first_reduce, second_reduce, first_gains, second_gains,
        )
    row_count = hidden.shape[1]
    result, hidden_grad, total_square, stat_sums, parts_expand, parts_reduce, shared = general_grads(
        hidden, features, caption_lengths, caption_image, out_grad, attn_project,
        attn_output, cross_query, cross_vision, feed_expand, feed_reduce, norm_gains,
    )
    sum_project, sum_output, sum_query, sum_vision, sum_gains = shared
    grad_norm = jnp.sqrt(total_square)
    rms_values = jnp.sqrt(stat_sums / (row_count * lax.axis_size("dp")))
    factor = clip_norm / jnp.maximum(grad_norm, clip_norm)
    clipped_gains = sum_gains * factor
    fresh_expand, mean_expand, square_expand = adam_step(
        feed_expand, parts_expand, first_expand, second_expand, factor, rate_matrix, decay_rate
    )
    fresh_reduce, mean_reduce, square_reduce = adam_step(
        feed_reduce, parts_reduce, first_reduce, second_reduce, factor, rate_matrix, decay_rate
    )
    weights_shared = (attn_project, attn_output, cross_query, cross_vision, norm_gains)
    firsts_shared = (first_project, first_output, first_query, first_vision, first_gains)
    seconds_shared = (second_project, second_output, second_query, second_vision, second_gains)
    summed_shared = (sum_project, sum_output, sum_query, sum_vision, sum_gains)
    updated = []
    for index in range(5):
        rate = rate_gains if index == 4 else rate_matrix
        decay = 0.0 if index == 4 else decay_rate
        weight = weights_shared[index]
        first = firsts_shared[index]
        second = seconds_shared[index]
        updated.append(adam_step(weight, summed_shared[index], first, second, factor, rate, decay))
    fresh_project, mean_project, square_project = updated[0]
    fresh_output, mean_output, square_output = updated[1]
    fresh_query, mean_query, square_query = updated[2]
    fresh_vision, mean_vision, square_vision = updated[3]
    fresh_gains, mean_gains, square_gains = updated[4]
    return (
        result[None],
        hidden_grad[None],
        grad_norm,
        rms_values,
        fresh_project,
        mean_project,
        square_project,
        fresh_output,
        mean_output,
        square_output,
        fresh_query,
        mean_query,
        square_query,
        fresh_vision,
        mean_vision,
        square_vision,
        fresh_expand,
        mean_expand,
        square_expand,
        fresh_reduce,
        mean_reduce,
        square_reduce,
        fresh_gains,
        mean_gains,
        square_gains,
        clipped_gains,
        to_half(fresh_project),
        to_half(fresh_output),
        to_half(fresh_query),
        to_half(fresh_vision),
        to_half(fresh_expand),
        to_half(fresh_reduce),
    )


def solution(mesh):
    return jax.shard_map(
        body,
        mesh=mesh,
        in_specs=(
            P("stream", "dp", None),
            P("dp", None, None),
            P("dp", None),
            P("dp", None),
            P("stream", "dp", None),
            P(None, "dp", None),
            P(None, "dp", None),
            P("dp", None),
            P(None, "dp", None),
            P("stream", "dp", None),
            P("stream", "dp", None),
            P(None, "dp"),
            P(None, "dp", None),
            P(None, "dp", None),
            P(None, "dp", None),
            P(None, "dp", None),
            P("dp", None),
            P("dp", None),
            P(None, "dp", None),
            P(None, "dp", None),
            P("stream", "dp", None),
            P("stream", "dp", None),
            P("stream", "dp", None),
            P("stream", "dp", None),
            P(None, "dp"),
            P(None, "dp"),
        ),
        out_specs=(
            P("stream", "dp", None),
            P("stream", "dp", None),
            P(),
            P(),
            P(None, "dp", None),
            P(None, "dp", None),
            P(None, "dp", None),
            P(None, "dp", None),
            P(None, "dp", None),
            P(None, "dp", None),
            P("dp", None),
            P("dp", None),
            P("dp", None),
            P(None, "dp", None),
            P(None, "dp", None),
            P(None, "dp", None),
            P("stream", "dp", None),
            P("stream", "dp", None),
            P("stream", "dp", None),
            P("stream", "dp", None),
            P("stream", "dp", None),
            P("stream", "dp", None),
            P(None, "dp"),
            P(None, "dp"),
            P(None, "dp"),
            P(None, "dp"),
            P(None, "dp", None),
            P(None, "dp", None),
            P("dp", None),
            P(None, "dp", None),
            P("stream", "dp", None),
            P("stream", "dp", None),
        ),
        check_vma=False,
    )
```

```python
import functools

import jax
import jax.numpy as jnp
from jax import lax
from jax.experimental import pallas as pl
from jax.experimental.pallas import tpu as pltpu
from jax.sharding import PartitionSpec as P

HEADS = 12
HD = 64
NQ = 32
STEP = 10


epsilon = 1e-06
masked_value = -1e30
beta_first = 0.9
beta_second = 0.999
rate_matrix = 0.05
rate_gains = 1.0
decay_rate = 0.01
adam_floor = 1e-08
clip_norm = 1.0


def shifted(block, axis, distance):
    devices = range(lax.axis_size(axis))
    route = [(i - distance, i) for i in devices if i - distance in devices]
    return lax.ppermute(block, axis, route)


def to_half(values):
    return values.astype(jnp.bfloat16)


def product(left, right):
    return jnp.dot(left, right, preferred_element_type=jnp.float32)


def left_product(left, right):
    return lax.dot_general(
        left, right, (((0,), (0,)), ((), ())), preferred_element_type=jnp.float32
    )


def right_product(left, right):
    return lax.dot_general(
        left, right, (((1,), (1,)), ((), ())), preferred_element_type=jnp.float32
    )


def norm_rows(values, gain):
    return values * lax.rsqrt(jnp.mean(values * values, axis=-1, keepdims=True) + epsilon) * gain


def exact_gelu(values):
    return jax.nn.gelu(values, approximate=False)


def square_rows(values):
    return jnp.sum(jnp.mean(values * values, axis=-1))


def layout(lengths, owners, row_count, per_image):
    caption_ends = jnp.cumsum(lengths)
    caption_starts = caption_ends - lengths
    row_index = jnp.arange(row_count, dtype=jnp.int32)
    inside = (row_index[:, None] >= caption_starts[None, :]) & (
        row_index[:, None] < caption_ends[None, :]
    )
    caption = jnp.sum(
        jnp.where(inside, jnp.arange(lengths.shape[0], dtype=jnp.int32)[None, :], 0), axis=1
    )
    text_image = jnp.sum(jnp.where(inside, owners[None, :], 0), axis=1)
    query_image = row_index // per_image
    query_allow = query_image[:, None] == query_image[None, :]
    own_caption = (caption[:, None] == caption[None, :]) & (
        row_index[None, :] <= row_index[:, None]
    )
    text_allow = jnp.concatenate([text_image[:, None] == query_image[None, :], own_caption], axis=1)
    return (query_allow, text_allow)


def attention_scores(query_rows, key_rows, allowed):
    batch_count, query_count, width_all = query_rows.shape
    query_heads = query_rows.reshape(batch_count, query_count, HEADS, HD)
    key_heads = key_rows.reshape(batch_count, key_rows.shape[1], HEADS, HD)
    scores = jnp.einsum(
        "bqhd,bkhd->bhqk", query_heads, key_heads, preferred_element_type=jnp.float32
    ) * HD ** (-0.5)
    if allowed is not None:
        scores = jnp.where(allowed[:, None], scores, masked_value)
    return (scores, query_heads, key_heads)


def attend(query_rows, key_rows, value_rows, allowed):
    scores, query_heads, key_heads = attention_scores(query_rows, key_rows, allowed)
    value_heads = value_rows.reshape(key_heads.shape)
    row_max = jnp.max(scores, axis=-1, keepdims=True)
    weights = jnp.exp(scores - row_max)
    denominator = jnp.sum(weights, axis=-1, keepdims=True)
    probability = to_half(weights / denominator)
    context = jnp.einsum(
        "bhqk,bkhd->bqhd", probability, value_heads, preferred_element_type=jnp.float32
    )
    return (context.reshape(query_rows.shape), (row_max + jnp.log(denominator))[..., 0])


def attend_back(query_rows, key_rows, value_rows, allowed, log_total, grad_context):
    scores, query_heads, key_heads = attention_scores(query_rows, key_rows, allowed)
    value_heads = value_rows.reshape(key_heads.shape)
    probability = jnp.exp(scores - log_total[..., None])
    grad_heads = grad_context.reshape(query_heads.shape)
    grad_prob = jnp.einsum(
        "bqhd,bkhd->bhqk", grad_heads, value_heads, preferred_element_type=jnp.float32
    )
    grad_value = jnp.einsum(
        "bhqk,bqhd->bkhd", to_half(probability), grad_heads, preferred_element_type=jnp.float32
    )
    grad_score = to_half(
        probability * (grad_prob - jnp.sum(grad_prob * probability, axis=-1, keepdims=True))
    )
    grad_query = jnp.einsum(
        "bhqk,bkhd->bqhd", grad_score, key_heads, preferred_element_type=jnp.float32
    ) * HD ** (-0.5)
    grad_key = jnp.einsum(
        "bhqk,bqhd->bkhd", grad_score, query_heads, preferred_element_type=jnp.float32
    ) * HD ** (-0.5)
    return (
        grad_query.reshape(query_rows.shape),
        grad_key.reshape(key_rows.shape),
        grad_value.reshape(value_rows.shape),
    )


def project_vision(feature_block, vision_weights):
    return to_half(
        jnp.einsum(
            "inv,kvd->kind", feature_block, vision_weights, preferred_element_type=jnp.float32
        )
    )


def vision_grad(feature_block, grad_pair):
    return jnp.einsum("inv,kind->kvd", feature_block, grad_pair, preferred_element_type=jnp.float32)


def adam_step(weight, gradient, first, second, factor, rate, decay):
    clipped = gradient * factor
    mean_new = beta_first * first + (1.0 - beta_first) * clipped
    square_new = beta_second * second + (1.0 - beta_second) * clipped * clipped
    corrected_mean = mean_new / (1.0 - beta_first**STEP)
    corrected_square = square_new / (1.0 - beta_second**STEP)
    fresh = weight - rate * (
        corrected_mean / (jnp.sqrt(corrected_square) + adam_floor) + decay * weight
    )
    return (fresh, mean_new, square_new)


MESH = pl.DeviceIdType.MESH
VMEM_LIMIT = 62 * 2**20


def coordinates():
    c = lax.axis_index("stream")
    d = lax.axis_index("dp")
    return c, d // 4, (d // 2) % 2, d % 2


def device(c, z, y, x):
    return (c, z * 4 + y * 2 + x)


def meet(c, z, y, x, layer=False):
    barrier = pltpu.get_barrier_semaphore()
    others = [device(1 - c, z, y, x), device(c, z, 1 - y, x), device(c, z, y, 1 - x)]
    others += [device(c, (z + k) % 4, y, x) for k in (1, 2, 3)]
    if layer:
        others += [device(1 - c, z, 1 - y, x), device(1 - c, z, y, 1 - x)]
        others += [device(c, z, 1 - y, 1 - x), device(1 - c, z, 1 - y, 1 - x)]
    for other in others:
        pl.semaphore_signal(barrier, inc=1, device_id=other, device_id_type=MESH)
    pl.semaphore_wait(barrier, len(others))


ORDERS = {
    ("late", 0): ("z", "y", "x"),
    ("late", 1): ("z", "x", "y"),
    ("early", 0): ("x", "z", "y"),
    ("early", 1): ("y", "z", "x"),
    ("feed", 0): ("z", "o"),
    ("feed", 1): ("z", "o"),
}


PARTS = 2
LMAX = 32
GATHER_TICKS = [(0, 3, 6, 9), (2, 5, 8, 11), (4, 7, 10, 13), (6, 9, 12, 15), (8, 11, 14, 17)]
GATHER_TICKS += [(10, 17, 24), (12, 18, 24), (14, 21, 24), (16, 23, 24)]
PLANES = {
    "query": (0, 0), "key": (0, 1), "cross_output": (0, 2),
    "value": (1, 0), "self_output": (1, 1), "cross_query": (1, 2),
}


def wide(block):
    return block.astype(jnp.float32)


def nn(left, right):
    return lax.dot_general(
        left, right, (((1,), (0,)), ((), ())), preferred_element_type=jnp.float32
    )


def nt(left, right):
    return lax.dot_general(
        left, right, (((1,), (1,)), ((), ())), preferred_element_type=jnp.float32
    )


def tn(left, right):
    return lax.dot_general(
        left, right, (((0,), (0,)), ((), ())), preferred_element_type=jnp.float32
    )


def span(index, size):
    return pl.ds(pl.multiple_of(index * size, size), size)


def loop(count, step):
    def body(index, carry):
        step(index)
        return carry

    lax.fori_loop(0, count, body, 0)


def row_sum(values):
    return jnp.sum(values, axis=0, keepdims=True)


def norm_back(values, gain, grad):
    scale = lax.rsqrt(jnp.mean(values * values, axis=-1, keepdims=True) + epsilon)
    unit = values * scale
    grad_unit = grad * gain
    mean = jnp.mean(grad_unit * unit, axis=-1, keepdims=True)
    return scale * (grad_unit - unit * mean), row_sum(grad * unit)


def lane_masks(rows):
    lane = lax.broadcasted_iota(jnp.int32, (rows, 2 * HD), 1)
    left = jnp.where(lane < HD, 1.0, 0.0)
    return to_half(left), to_half(1.0 - left)


def head_pair(block, masks):
    return jnp.concatenate([block * masks[0], block * masks[1]], axis=0)


def pair_join(both):
    rows = both.shape[0] // 2
    lane = lax.broadcasted_iota(jnp.int32, (rows, 2 * HD), 1)
    return jnp.where(lane < HD, both[:rows], both[rows:])


def diagonal(full, rows):
    lane = lax.broadcasted_iota(jnp.int32, (rows, 2 * HD), 1)
    tiles = []
    for t in range(HEADS // 2):
        tile = full[:, t * 2 * HD : (t + 1) * 2 * HD]
        left = tile[2 * t * rows : (2 * t + 1) * rows]
        right = tile[(2 * t + 1) * rows : (2 * t + 2) * rows]
        tiles.append(jnp.where(lane < HD, left, right))
    return jnp.concatenate(tiles, axis=1)


def head_mask(rows, width):
    row = lax.broadcasted_iota(jnp.int32, (HEADS * rows, width), 0) // rows
    lane = lax.broadcasted_iota(jnp.int32, (HEADS * rows, width), 1) // HD
    return to_half(jnp.where(row == lane, 1.0, 0.0))


def caption_layout(lengths, owners, row_count):
    count = lengths.shape[1]
    size = wide(lengths)
    owner = wide(owners)
    sub = lax.broadcasted_iota(jnp.int32, (count, count), 0)
    lane = lax.broadcasted_iota(jnp.int32, (count, count), 1)
    starts = jnp.sum(jnp.where(lane < sub, size, 0.0), axis=1, keepdims=True)
    owner_down = jnp.sum(jnp.where(lane == sub, owner, 0.0), axis=1, keepdims=True)
    row = wide(lax.broadcasted_iota(jnp.int32, (count, row_count), 1))
    begun = starts <= row
    start = jnp.max(jnp.where(begun, starts, 0.0), axis=0, keepdims=True)
    image = jnp.max(jnp.where(begun, owner_down, 0.0), axis=0, keepdims=True)
    return start, image


def text_bias(rb, start, image, far_rows, window, bias):
    begin = jnp.maximum(rb * 128 - LMAX, 0)
    far = lax.broadcasted_iota(jnp.int32, (far_rows, 128), 0) // NQ
    far_bias = jnp.where(wide(far) == image, 0.0, masked_value)
    key = lax.broadcasted_iota(jnp.int32, (window, 128), 0) + begin
    row = lax.broadcasted_iota(jnp.int32, (window, 128), 1) + rb * 128
    seen = (wide(key) >= start) & (key <= row)
    own_bias = jnp.where(seen, 0.0, masked_value)
    bias[0:far_rows] = jnp.concatenate([far_bias, far_bias], axis=1)
    bias[far_rows : far_rows + window] = jnp.concatenate([own_bias, own_bias], axis=1)


def query_bias(bias):
    key = lax.broadcasted_iota(jnp.int32, (128, 256), 0) // NQ
    row = (lax.broadcasted_iota(jnp.int32, (128, 256), 1) % 128) // NQ
    bias[0:128] = jnp.where(key == row, 0.0, masked_value)


def forward_kernel(
    attn_project, attn_output, cross_query_weight, cross_vision, feed_expand, feed_reduce, gains,
    hidden_in, out_grad_in, features, lengths, owners,
    keep_branch, keep_after_cross, keep_mate_branch, out_grad_cross, part_expand, part_reduce, gain_feed_out, stats,
    keep_first, keep_gains, keep_normed, keep_query, keep_key, keep_value, keep_far_key, keep_far_value,
    keep_context, keep_after_self, keep_cross_query, keep_cross_context, keep_vision, keep_images, total_self, total_cross,
    all_first, raw_vision, all_vision, all_expand, all_reduce, all_gains, gain_rows,
    hidden, out_grad, images, vision_pair, normed, query, key, value, far_key, far_value, context, after_self,
    cross_query, cross_context, after_cross, normed_feed, grad_feed, sum_branch, sum_normed, got_normed, bias, mask,
    first, vision, expand, reduce, layout_rows, send_sem, recv_sem, local_sem,
):
    c, z, y, x = coordinates()
    row_count, width = hidden.shape
    image_count = total_cross.shape[0]
    padded = vision_pair.shape[0] // image_count
    feature_rows = features.shape[0] // (2 * image_count)
    feature_width = features.shape[1]
    part_rows = expand.shape[0] // PARTS
    far_rows, window = far_key.shape[0], 128 + LMAX
    cross_rows = image_count * NQ

    across_at = jnp.where(c == 0, y, x)
    own_at = {"z": z, "y": y, "x": x, "o": across_at}
    mate = (c, z * 4 + jnp.where(c == 0, y, 1 - y) * 2 + jnp.where(c == 0, 1 - x, x))
    beyond = (c, z * 4 + jnp.where(c == 0, 1 - y, y) * 2 + jnp.where(c == 0, x, 1 - x))

    chunks = [(gains, lambda *at: all_gains.at[at], "late", False)]
    chunks.append((vision, lambda *at: raw_vision.at[(c,) + at], "late", True))
    for j in range(3):
        chunks.append((first.at[j], lambda *at, j=j: all_first.at[(c, j) + at], "late", True))
    for p in range(PARTS):
        rows = pl.ds(p * part_rows, part_rows)
        for source, whole in ((expand, all_expand), (reduce, all_reduce)):
            target = lambda *at, p=p, whole=whole: whole.at[(p,) + at]
            chunks.append((source.at[rows], target, "feed", False))
    count = len(chunks)
    events = [
        (when, -stage, number)
        for number, times in enumerate(GATHER_TICKS)
        for stage, when in enumerate(times)
    ]
    last_tick = max(events)[0]

    def axes_of(number):
        return "zo" if chunks[number][2] == "feed" else "zyx"

    def stages_of(number):
        return 2 if chunks[number][2] == "feed" else 3

    def remote(source, target, index, where):
        return pltpu.make_async_remote_copy(
            src_ref=source, dst_ref=target, send_sem=send_sem.at[index],
            recv_sem=recv_sem.at[index], device_id=where, device_id_type=MESH,
        )

    def sends(number, stage, core):
        source, target, kind = chunks[number][:3]
        order = ORDERS[kind, core]
        done, axis = order[:stage], order[stage]
        at = tuple(slice(None) if a in done else own_at[a] for a in axes_of(number))
        block = target(*at)
        here = source if stage == 0 else block
        base = (number * 3 + stage) * 3
        if axis == "z":
            return [
                remote(here, block, base + k - 1, device(c, (z + k) % 4, y, x)) for k in (1, 2, 3)
            ]
        where = {"y": device(c, z, 1 - y, x), "x": device(c, z, y, 1 - x), "o": beyond}[axis]
        return [remote(here, block, base, where)]

    def place(number):
        source, target = chunks[number][:2]
        at = [own_at[a] for a in axes_of(number)]
        return pltpu.make_async_copy(source, target(*at), local_sem.at[number])

    pair = device(1 - c, z, y, x)

    def across(number):
        target = chunks[number][1]
        block = target(slice(None), slice(None), slice(None))
        return remote(block, block, count * 9 + number, pair)

    def tick_core(tick, core):
        for when, negative, number in sorted(events):
            stage = -negative
            if when != tick:
                continue
            if stage > 0:
                for copy in sends(number, stage - 1, core):
                    copy.wait_recv()
            if stage == 1:
                place(number).wait()
            if stage < stages_of(number):
                for copy in sends(number, stage, core):
                    copy.start()
                if stage == 0:
                    place(number).start()
            elif chunks[number][3]:
                across(number).start()

    def both(step):
        @pl.when(c == 0)
        def _():
            step(0)

        @pl.when(c == 1)
        def _():
            step(1)

    def tick(number):
        both(lambda core: tick_core(number, core))

    def sent(number):
        def step(core):
            for stage in range(stages_of(number)):
                for copy in sends(number, stage, core):
                    copy.wait_send()

        both(step)

    swap_base = count * 10
    near_rows, far_away = pl.ds(0, row_count), pl.ds(row_count, row_count)
    active, grad_before = vision_pair.at[pl.ds(0, 2 * row_count)], vision_pair.at[pl.ds(2 * row_count, 2 * row_count)]
    send_normed = images.at[pl.ds(0, row_count), pl.ds(0, width)]
    send_branch = images.at[pl.ds(row_count, row_count), pl.ds(0, width)]
    swaps = {
        "key": (key, far_key),
        "value": (value, far_value),
        "query": (cross_query.at[pl.ds(cross_rows, cross_rows)], cross_query.at[pl.ds(0, cross_rows)]),
        "context": (cross_context.at[pl.ds(0, cross_rows)], cross_context.at[pl.ds(cross_rows, cross_rows)]),
        "grad_feed": (grad_feed.at[near_rows], grad_feed.at[far_away]),
        "normed_feed": (normed_feed.at[near_rows], normed_feed.at[far_away]),
        "sum_normed": (send_normed, got_normed),
    }
    with_mate = ("grad_feed", "normed_feed", "sum_normed")

    def swap(name):
        source, target = swaps[name]
        where = mate if name in with_mate else pair
        return remote(source, target, swap_base + list(swaps).index(name), where)

    local_base = count
    loads = [
        (hidden_in, hidden),
        (out_grad_in, out_grad),
    ]
    step_rows = 2 * image_count * 32
    whole_steps = feature_rows // 32
    half_rows = whole_steps // 2 * step_rows
    for begin, size in ((0, half_rows), (half_rows, features.shape[0] - half_rows)):
        staged = vision_pair.at[pl.ds(0, size), pl.ds(0, feature_width)]
        loads.append((features.at[pl.ds(begin, size)], staged))
    keeps = {
        "first": (all_first, keep_first),
        "gains": (gain_rows, keep_gains),
        "normed": (normed, keep_normed),
        "query": (query, keep_query),
        "key": (key, keep_key),
        "value": (value, keep_value),
        "far_key": (far_key, keep_far_key),
        "far_value": (far_value, keep_far_value),
        "context": (context, keep_context),
        "after_self": (after_self, keep_after_self),
        "cross_query": (cross_query.at[pl.ds(0, cross_rows)], keep_cross_query),
        "cross_context": (cross_context, keep_cross_context),
        "vision": (vision_pair, keep_vision),
        "images": (images, keep_images),
        "branch": (sum_branch.at[pl.ds(0, row_count)], keep_branch),
        "after_cross": (after_cross, keep_after_cross),
        "mate_branch": (images.at[pl.ds(row_count, row_count), pl.ds(0, width)], keep_mate_branch),
        "grad_cross": (sum_normed.at[pl.ds(0, row_count)], out_grad_cross),
    }
    for p in range(PARTS):
        keeps["expand", p] = (all_expand.at[p], part_expand.at[p])
        keeps["reduce", p] = (all_reduce.at[p], part_reduce.at[p])

    shard_rows = first.shape[1]
    sources = {
        0: [attn_project.at[0], attn_project.at[1], attn_output.at[1]],
        1: [attn_project.at[2], attn_output.at[0], cross_query_weight],
    }
    shard_base = local_base + len(loads) + len(keeps)

    def shard_place(k):
        size = (shard_rows, shard_rows, shard_rows, vision.shape[0], expand.shape[0], reduce.shape[0])
        return pl.ds(sum(size[:k]), size[k])

    def shard_load(k, core):
        sources_now = sources[core] + [cross_vision.at[core], feed_expand, feed_reduce]
        target = sum_branch.at[shard_place(k)]
        return pltpu.make_async_copy(sources_now[k], target, local_sem.at[shard_base + k])

    def shard_start():
        both(lambda core: [shard_load(k, core).start() for k in range(6)] and None)

    def shard_round(k):
        both(lambda core: shard_load(k, core).wait())
        value = to_half(sum_branch[shard_place(k), :])
        if k < 3:
            first[k] = value
        else:
            (vision, expand, reduce)[k - 3][...] = value

    def load(k):
        source, target = loads[k]
        return pltpu.make_async_copy(source, target, local_sem.at[local_base + k])

    def keep(name):
        source, target = keeps[name]
        index = local_base + len(loads) + list(keeps).index(name)
        return pltpu.make_async_copy(source, target, local_sem.at[index])

    def weight(name):
        plane, j = PLANES[name]
        return all_first[plane, j].reshape(width, width)

    def gain(k):
        return gain_rows[pl.ds(k, 1), :]

    def stat(k, amount):
        row = pl.ds(c * 4 + k, 1)
        stats[row, :] = stats[row, :] + amount


    def start():
        stats[...] = jnp.zeros_like(stats)
        mask[...] = head_mask(NQ, width)
        first_row, image = caption_layout(lengths[...], owners[...], row_count)
        layout_rows[0:1] = first_row
        layout_rows[1:2] = image

    def read_gains():
        total = jnp.zeros(gain_rows.shape, jnp.float32)
        per = width // 16
        for k in range(16):
            lane = lax.broadcasted_iota(jnp.int32, (128, width), 0)
            column = lax.broadcasted_iota(jnp.int32, (128, width), 1)
            pick = to_half(jnp.where((column == lane + k * per) & (lane < per), 1.0, 0.0))
            total = total + nn(all_gains[k // 4, (k // 2) % 2, k % 2], pick)
        gain_rows[...] = total

    def self_in():
        def step(i):
            rows = span(i, 256)
            source = hidden[rows, :]
            stat(0, row_sum(source * source))
            part = to_half(norm_rows(source, gain(0)))
            normed[rows, :] = part
            query[rows, :] = to_half(nn(part, weight("query"))) * jnp.bfloat16(HD**-0.5)
            key[rows, :] = to_half(nn(part, weight("key")))
            value[rows, :] = to_half(nn(part, weight("value")))

        loop(row_count // 256, step)

    def attend_pair(rb, t, parts):
        lanes, rows = span(t, 128), span(rb, 128)
        queries = head_pair(query[rows, lanes], lane_masks(128))
        scores, most = [], None
        for keys, _, where, _ in parts:
            score = nt(keys, queries) + bias[where, :]
            scores.append(score)
            top = jnp.max(score, axis=0, keepdims=True)
            most = top if most is None else jnp.maximum(most, top)
        weights = [jnp.exp(score - most) for score in scores]
        total = sum(row_sum(part) for part in weights)
        inverse = 1.0 / total
        result = sum(
            tn(to_half(part * inverse), values) for part, (_, values, _, _) in zip(weights, parts)
        )
        context[rows, lanes] = to_half(pair_join(result))
        total_self[rb, t] = most + jnp.log(total)

    def self_query():
        query_bias(bias)

        def step(i):
            rb, t = i // 6, i % 6
            rows, lanes = span(rb, 128), span(t, 128)
            attend_pair(rb, t, [(key[rows, lanes], value[rows, lanes], pl.ds(0, 128), None)])

        loop(row_count // 128 * 6, step)

    def self_text(begin, end):
        def outer(rb):
            rb = rb + begin
            rows = span(rb, 128)
            text_bias(rb, layout_rows[0:1, rows], layout_rows[1:2, rows], far_rows, window, bias)
            near = pl.ds(pl.multiple_of(jnp.maximum(rb * 128 - LMAX, 0), LMAX), window)

            def inner(t):
                lanes = span(t, 128)
                attend_pair(rb, t, [
                    (far_key[:, lanes], far_value[:, lanes], pl.ds(0, far_rows), None),
                    (key[near, lanes], value[near, lanes], pl.ds(far_rows, window), None),
                ])

            loop(6, inner)

        loop(end - begin, outer)

    def self_out():
        def step(i):
            rows = span(i, 256)
            branch = nn(context[rows, :], weight("self_output"))
            stat(1, row_sum(branch * branch))
            after_self[rows, :] = hidden[rows, :] + branch

        loop(row_count // 256, step)

    def cross_in():
        def step(i):
            rows = span(i, 256)
            part = to_half(norm_rows(after_self[rows, :], gain(1)))
            result = to_half(nn(part, weight("cross_query"))) * jnp.bfloat16(HD**-0.5)
            cross_query[rows, :] = result

        loop(row_count // 256, step)

    def pack_vision():
        def step(i):
            plane, z_at, y_at = i // 8, (i // 2) % 4, i % 2
            left = wide(raw_vision[plane, z_at, y_at, 0])
            right = wide(raw_vision[plane, z_at, y_at, 1])
            size = 2 * left.shape[0]
            all_vision[plane, span(z_at * 2 + y_at, size), :] = to_half(
                jnp.concatenate([left, right], axis=0)
            )

        loop(16, step)

    def sort_rows(begin, rows, base):
        size = rows // (2 * image_count)
        block = max(size, 16)
        out = lax.broadcasted_iota(jnp.int32, (image_count * block, rows), 0)
        column = lax.broadcasted_iota(jnp.int32, (image_count * block, rows), 1)
        source = (out % block) * (2 * image_count) + c * image_count + out // block
        pick = to_half(jnp.where((column == source) & (out % block < size), 1.0, 0.0))
        sorted_rows = to_half(nn(pick, vision_pair[begin, 0:feature_width]))
        for j in range(image_count):
            where = pl.ds(pl.multiple_of(j * padded + base, 16), block)
            images[where, :] = sorted_rows[j * block : (j + 1) * block]

    def sort_images(part):
        def step(i):
            sort_rows(span(i, step_rows), step_rows, 32 * (i + part * (whole_steps // 2)))

        loop(whole_steps // 2, step)
        if part == 1:
            rest = feature_rows % 32 * 2 * image_count
            sort_rows(pl.ds(whole_steps // 2 * step_rows, rest), rest, whole_steps * 32)

    def project_images(begin, end):
        def step(i):
            rows = pl.ds(pl.multiple_of((i + begin) * padded, 16), padded)
            image = images[rows, :]
            vision_pair[rows, 0:width] = to_half(nn(image, all_vision[0]))
            vision_pair[rows, width : 2 * width] = to_half(nn(image, all_vision[1]))

        loop(end - begin, step)

    def cross_attend(begin, end):
        def step(i):
            i = i + begin
            rows = pl.ds(pl.multiple_of(i * padded, 16), padded)
            own_rows = span(i, NQ)
            part = cross_query[own_rows, :]
            queries = jnp.concatenate([part] * HEADS, axis=0) * mask[...]
            score = nt(vision_pair[rows, 0:width], queries)
            key_row = lax.broadcasted_iota(jnp.int32, score.shape, 0)
            score = jnp.where(key_row < feature_rows, score, masked_value)
            most = jnp.max(score, axis=0, keepdims=True)
            weights = jnp.exp(score - most)
            total = row_sum(weights)
            total_cross[i] = most + jnp.log(total)
            full = tn(to_half(weights * (1.0 / total)), vision_pair[rows, width : 2 * width])
            cross_context[own_rows, :] = to_half(diagonal(full, NQ))

        loop(end - begin, step)

    def cross_out():
        def step(i):
            rows = span(i, 256)
            after_cross[rows, :] = after_self[rows, :] + nn(cross_context[rows, :], weight("cross_output"))

        loop(row_count // 256, step)

    def round_out_grad():
        def step(i):
            rows = span(i, 128)
            grad_feed[rows, :] = to_half(out_grad[rows, :])

        loop(row_count // 128, step)

    def feed_in():
        def step(i):
            rows = span(i, 128)
            normed_feed[rows, :] = to_half(norm_rows(after_cross[rows, :], gain(2 + c)))

        loop(row_count // 128, step)

    half_parts = 2 * PARTS
    block = all_expand.shape[1] * all_expand.shape[2] * part_rows // 2

    def feed_weights(b):
        p, at = b // 2, pl.ds(all_expand.shape[1] // 2 * (b % 2), all_expand.shape[1] // 2)
        return p, at, all_expand[p, at].reshape(block, width), all_reduce[p, at].reshape(block, width)

    def feed_rows(side, b):
        rows = pl.ds(side * row_count, row_count)
        lanes = pl.ds(b * block, block)
        _, _, up, down = feed_weights(b)
        before = nt(normed_feed[rows, :], up)
        share = 0.5 * (1.0 + lax.erf(before * (0.5**0.5)))
        density = jnp.exp(before * before * -0.5) * (0.5 / jnp.pi) ** 0.5
        result = to_half(before * share)
        slope = share + before * density
        active[rows, lanes] = result
        total = nn(result, down)
        back = to_half(nt(grad_feed[rows, :], down) * slope)
        grad_before[rows, lanes] = back
        total_normed = nn(back, up)
        if b == 0:
            sum_branch[rows, :] = total
            sum_normed[rows, :] = total_normed
        else:
            sum_branch[rows, :] = sum_branch[rows, :] + total
            sum_normed[rows, :] = sum_normed[rows, :] + total_normed

    def feed_grads(b):
        lanes = pl.ds(b * block, block)
        p, at = b // 2, pl.ds(all_expand.shape[1] // 2 * (b % 2), all_expand.shape[1] // 2)
        shape = (all_expand.shape[1] // 2,) + all_expand.shape[2:]
        all_expand[p, at] = to_half(tn(grad_before[:, lanes], normed_feed[...])).reshape(shape)
        all_reduce[p, at] = to_half(tn(active[:, lanes], grad_feed[...])).reshape(shape)

    def round_partial(total, buffer):
        def step(i):
            rows = span(i, 128)
            buffer[rows, :] = to_half(total[pl.ds(pl.multiple_of(row_count + i * 128, 128), 128), :])

        loop(row_count // 128, step)

    def feed_back():
        gain_feed_out[...] = jnp.zeros_like(gain_feed_out)

        def step(i):
            rows = span(i, 128)
            grad = sum_normed[rows, :] + wide(got_normed[rows, :])
            back, gain_part = norm_back(after_cross[rows, :], gain(2 + c), grad)
            gain_feed_out[0:1, :] = gain_feed_out[0:1, :] + gain_part
            sum_normed[rows, :] = out_grad[rows, :] + back

        loop(row_count // 128, step)

    half_tick = [0]

    def ticks(until):
        while half_tick[0] <= until:
            tick(half_tick[0])
            half_tick[0] += 1

    shard_start()
    for k in range(3):
        load(k).start()
    meet(c, z, y, x)
    ticks(0)
    for k in (3, 0, 1, 2, 4, 5):
        shard_round(k)
    ticks(1)
    start()
    ticks(2)
    load(1).wait()
    round_out_grad()
    swap("grad_feed").start()
    ticks(4)
    load(2).wait()
    sort_images(0)
    load(3).start()
    ticks(7)
    load(3).wait()
    sort_images(1)
    keep("images").start()
    ticks(9)
    read_gains()
    keep("gains").start()
    ticks(11)
    across(1).wait_recv()
    pack_vision()
    quarter = image_count // 4
    project_images(0, quarter)
    ticks(13)
    project_images(quarter, 2 * quarter)
    ticks(15)
    project_images(2 * quarter, 3 * quarter)
    ticks(17)
    for number in (2, 3, 4):
        across(number).wait_recv()
    load(0).wait()
    self_in()
    for name in ("normed", "query", "key", "value"):
        keep(name).start()

    @pl.when(c == 0)
    def _():
        swap("key").start()
        swap("value").start()

    project_images(3 * quarter, image_count)
    keep("vision").start()
    ticks(18)
    keep("first").start()
    blocks = row_count // 128

    @pl.when(c == 0)
    def _():
        self_query()
        self_out()
        cross_in()
        swap("query").start()

    @pl.when(c == 1)
    def _():
        swap("key").wait_recv()
        swap("value").wait_recv()
        self_text(0, blocks // 2)
        keep("far_key").start()
        keep("far_value").start()

    ticks(20)

    @pl.when(c == 1)
    def _():
        self_text(blocks // 2, blocks)
        self_out()

    @pl.when(c == 0)
    def _():
        cross_attend(0, image_count // 2)

    ticks(21)

    @pl.when(c == 1)
    def _():
        swap("query").wait_recv()
        cross_attend(0, image_count // 2)

    @pl.when(c == 0)
    def _():
        cross_attend(image_count // 2, image_count)

    keep("context").start()
    keep("after_self").start()
    ticks(22)

    @pl.when(c == 1)
    def _():
        cross_attend(image_count // 2, image_count)
        swap("context").start()
        after_cross[...] = after_self[...]

    ticks(23)

    @pl.when(c == 0)
    def _():
        swap("context").wait_recv()
        cross_out()

    keep("cross_query").start()
    keep("cross_context").start()
    keep("after_cross").start()
    feed_in()
    swap("normed_feed").start()
    ticks(last_tick)
    for name in ("vision", "images"):
        keep(name).wait()
    for b in range(half_parts):
        feed_rows(0, b)
    swap("grad_feed").wait_recv()
    swap("normed_feed").wait_recv()
    for b in range(half_parts):
        feed_rows(1, b)
    round_partial(sum_normed, send_normed)
    swap("sum_normed").start()
    round_partial(sum_branch, send_branch)
    keep("mate_branch").start()
    keep("branch").start()
    for p in range(PARTS):
        sent(5 + 2 * p)
        sent(6 + 2 * p)
        feed_grads(2 * p)
        feed_grads(2 * p + 1)
        keep(("expand", p)).start()
        keep(("reduce", p)).start()
    swap("sum_normed").wait_recv()
    feed_back()
    keep("grad_cross").start()
    for number in range(5):
        sent(number)
    for number in range(1, 5):
        across(number).wait_send()
    for name in with_mate:
        swap(name).wait_send()

    @pl.when(c == 0)
    def _():
        swap("key").wait_send()
        swap("value").wait_send()
        swap("query").wait_send()

    @pl.when(c == 1)
    def _():
        swap("context").wait_send()

    for name in keeps:
        if name in ("vision", "images"):
            continue
        if name in ("far_key", "far_value"):

            @pl.when(c == 1)
            def _(name=name):
                keep(name).wait()

        else:
            keep(name).wait()


def forward_all(weights, gains, hidden, out_grad, features, lengths, owners):
    project, _, _, vision, expand, reduce = weights
    first = jax.ShapeDtypeStruct((3,) + project.shape[1:], project.dtype)
    vision = jax.ShapeDtypeStruct(vision.shape[1:], vision.dtype)
    half, single = jnp.bfloat16, jnp.float32
    row_count, width = hidden.shape
    image_count, feature_rows, feature_width = features.shape
    image_count = image_count // 2
    features = features.transpose(1, 0, 2).reshape(-1, feature_width)
    padded = -(-feature_rows // 16) * 16
    cross_rows = image_count * NQ
    part_rows = expand.shape[0] // PARTS
    anywhere = pl.BlockSpec(memory_space=pl.ANY)
    vmem = pl.BlockSpec(memory_space=pltpu.VMEM)
    rows_half = jax.ShapeDtypeStruct((row_count, width), half)
    rows_single = jax.ShapeDtypeStruct((row_count, width), single)
    all_first = (2,) + first.shape[:1] + (4, 2, 2) + first.shape[1:]
    all_feed = (PARTS, 4, 2, part_rows, width)
    gain_shape = (16, width)
    pair_shape = (image_count * padded, 2 * width)
    outs = {
        "branch": (rows_single, anywhere),
        "after_cross": (rows_single, anywhere),
        "mate_branch": (rows_half, anywhere),
        "grad_cross": (rows_single, anywhere),
        "part_expand": (jax.ShapeDtypeStruct(all_feed, half), anywhere),
        "part_reduce": (jax.ShapeDtypeStruct(all_feed, half), anywhere),
        "gain_feed": (jax.ShapeDtypeStruct((8, width), single), vmem),
        "stats": (jax.ShapeDtypeStruct((8, width), single), vmem),
        "first": (jax.ShapeDtypeStruct(all_first, half), anywhere),
        "gains": (jax.ShapeDtypeStruct(gain_shape, single), anywhere),
        "normed": (rows_half, anywhere),
        "query": (rows_half, anywhere),
        "key": (rows_half, anywhere),
        "value": (rows_half, anywhere),
        "far_key": (rows_half, anywhere),
        "far_value": (rows_half, anywhere),
        "context": (rows_half, anywhere),
        "after_self": (rows_single, anywhere),
        "cross_query": (jax.ShapeDtypeStruct((cross_rows, width), half), anywhere),
        "cross_context": (rows_half, anywhere),
        "vision": (jax.ShapeDtypeStruct(pair_shape, half), anywhere),
        "images": (jax.ShapeDtypeStruct((image_count * padded, feature_width), half), anywhere),
        "total_self": (jax.ShapeDtypeStruct((row_count // 128, HEADS // 2, 1, 256), single), vmem),
        "total_cross": (jax.ShapeDtypeStruct((image_count, 1, HEADS * NQ), single), vmem),
    }
    halves = (row_count, width)
    scratch = [
        pltpu.VMEM(all_first, half),
        pltpu.VMEM((2, 4, 2, 2) + vision.shape, half),
        pltpu.VMEM((2, feature_width, width), half),
        pltpu.VMEM(all_feed, half),
        pltpu.VMEM(all_feed, half),
        pltpu.VMEM((4, 2, 2) + gains.shape, half),
        pltpu.VMEM(gain_shape, single),
        pltpu.VMEM(halves, single),
        pltpu.VMEM(halves, single),
        pltpu.VMEM((image_count * padded, feature_width), half),
        pltpu.VMEM(pair_shape, half),
    ]
    scratch += [pltpu.VMEM(halves, half)] * 7
    scratch += [
        pltpu.VMEM(halves, single),
        pltpu.VMEM(halves, half),
        pltpu.VMEM(halves, half),
        pltpu.VMEM(halves, single),
        pltpu.VMEM((2 * row_count, width), half),
        pltpu.VMEM((2 * row_count, width), half),
        pltpu.VMEM((2 * row_count, width), single),
        pltpu.VMEM((2 * row_count, width), single),
        pltpu.VMEM(halves, half),
        pltpu.VMEM((row_count + 128 + LMAX, 256), single),
        pltpu.VMEM((HEADS * NQ, width), half),
        pltpu.VMEM(first.shape, half),
        pltpu.VMEM(vision.shape, half),
        pltpu.VMEM(expand.shape, half),
        pltpu.VMEM(reduce.shape, half),
        pltpu.VMEM((8, row_count), single),
        pltpu.SemaphoreType.DMA(((5 + 2 * PARTS) * 10 + 8,)),
        pltpu.SemaphoreType.DMA(((5 + 2 * PARTS) * 10 + 8,)),
        pltpu.SemaphoreType.DMA((5 + 4 + 18 + 4 * PARTS + 6,)),
    ]
    values = pl.pallas_call(
        forward_kernel,
        out_shape=[shape for shape, _ in outs.values()],
        in_specs=[anywhere] * 10 + [vmem] * 2,
        out_specs=[spec for _, spec in outs.values()],
        scratch_shapes=scratch,
        compiler_params=pltpu.CompilerParams(
            collective_id=2, has_side_effects=True, vmem_limit_bytes=VMEM_LIMIT
        ),
        name="forward_layer",
    )(*weights, gains, hidden, out_grad, features, lengths, owners)
    return dict(zip(outs, values))


def scatter_engine(chunks, send_sem, recv_sem):
    c, z, y, x = coordinates()
    own = {"z": z, "y": y, "x": x, "o": jnp.where(c == 0, y, x)}
    beyond = (c, z * 4 + jnp.where(c == 0, 1 - y, y) * 2 + jnp.where(c == 0, x, 1 - x))

    def axes_of(chunk):
        return "zo" if chunk["kind"] == "feed" else "zyx"

    def remote(source, target, index, where):
        return pltpu.make_async_remote_copy(
            src_ref=source, dst_ref=target, send_sem=send_sem.at[index],
            recv_sem=recv_sem.at[index], device_id=where, device_id_type=MESH,
        )

    def sends(number, stage, core):
        chunk = chunks[number]
        held, got = chunk["held"], chunk["got"][stage]
        order = ORDERS[chunk["kind"], core][::-1]
        done, axis = order[:stage], order[stage]
        base = (number * 3 + stage) * 3

        def block(there):
            return held.at[
                tuple(
                    there if a == axis else own[a] if a in done else slice(None)
                    for a in axes_of(chunk)
                )
            ]

        if axis == "z":
            return [
                remote(
                    block((z + k) % 4), got.at[k - 1], base + k - 1, device(c, (z + k) % 4, y, x)
                )
                for k in (1, 2, 3)
            ]
        where = {"y": device(c, z, 1 - y, x), "x": device(c, z, y, 1 - x), "o": beyond}[axis]
        return [remote(block(1 - own[axis]), got, base, where)]

    def absorb(number, stage, core):
        chunk = chunks[number]
        held, got = chunk["held"], chunk["got"][stage]
        order = ORDERS[chunk["kind"], core][::-1]
        done, axis = order[: stage + 1], order[stage]
        free = [a for a in axes_of(chunk) if a not in done]
        sizes = [4 if a == "z" else 2 for a in free]
        steps = 1
        for size in sizes:
            steps *= size

        def step(i):
            index = {}
            for a, size in reversed(list(zip(free, sizes))):
                index[a] = i % size
                i = i // size
            at = tuple(index[a] if a in index else own[a] for a in axes_of(chunk))
            inner = tuple(index[a] for a in free)
            value = wide(held[at])
            if axis == "z":
                for k in range(3):
                    value = value + wide(got[(k,) + inner])
            else:
                value = value + wide(got[inner] if inner else got[...])
            if stage == len(order) - 1:
                chunk["total"][...] = value
            else:
                held[at] = to_half(value)

        if steps == 1:
            step(0)
        else:
            loop(steps, step)

    def tick_core(now, core):
        for number, stage in [
            (number, stage)
            for stage in (3, 2, 1, 0)
            for number, chunk in enumerate(chunks)
            if stage < len(chunk["ticks"][core]) and chunk["ticks"][core][stage] == now
        ]:
            if stage == 0:
                chunks[number]["ready"](core)
            else:
                for copy in sends(number, stage - 1, core):
                    copy.wait_recv()
                absorb(number, stage - 1, core)
            if stage < len(chunks[number]["ticks"][core]) - 1:
                for copy in sends(number, stage, core):
                    copy.start()

    def each_core(step):
        @pl.when(c == 0)
        def _():
            step(0)

        @pl.when(c == 1)
        def _():
            step(1)

    def tick(now):
        each_core(lambda core: tick_core(now, core))

    def wait_sent():
        def step(core):
            for number, chunk in enumerate(chunks):
                for stage in range(len(chunk["ticks"][core]) - 1):
                    for copy in sends(number, stage, core):
                        copy.wait_send()

        each_core(step)

    last = max(max(ticks) for chunk in chunks for ticks in chunk["ticks"])
    return tick, wait_sent, remote, last


def got_shapes(kind, rows, width):
    if kind == "feed":
        return [(4, rows, width), (3, rows, width)]
    if kind == "late":
        return [(4, 2, rows, width), (4, rows, width), (3, rows, width)]
    return [(4, 2, rows, width), (3, 2, rows, width), (rows, width)]


FEED_CHUNKS = 2 * PARTS
FEED_TICKS = [(0, 2, 19), (1, 4, 19), (3, 6, 19), (5, 8, 19)]
PLANE_TICKS = (
    [(15, 17, 19, 21), (16, 18, 20, 21), (3, 5, 8, 19)],
    [(16, 18, 20, 21), (10, 15, 18, 21), (10, 15, 18, 21)],
)
VISION_TICKS = ((9, 13, 17, 21), (9, 13, 17, 21))


def backward_kernel(
    feature_rows,
    part_expand, part_reduce, grad_cross_in, hidden_in, after_self_in, first_in, gains_in,
    normed_in, query_in, key_in, value_in, far_key_in, far_value_in, context_in,
    cross_query_in, cross_context_in, vision_in, images_in, branch_in, after_cross_in, mate_branch_in, lengths, owners, total_self, total_cross, gain_feed,
    part_stats, result_out, hidden_grad_out, sum_expand, sum_reduce, sum_first, sum_vision, sum_gains, totals,
    held_expand, held_reduce, got_f0, got_f1, got_p0, got_p1, got_p2, got_v0, got_v1, got_v2,
    pair_first, pair_vision, held_vision, gains_now, gains_got, gains_z, stats_now, stats_got, stats_z,
    first, pair, images, grad_vision, cross_context, after_self, hidden, grad_after, gain_rows,
    cross_query, grad_context, grad_query, far_grad, bias, mask, sum_far_key, sum_far_value, sum_key, sum_value,
    layout_rows, gain_parts, stats, send_sem, recv_sem, local_sem,
):
    c, z, y, x = coordinates()
    row_count, width = hidden.shape
    image_count = total_cross.shape[0]
    padded = pair.shape[0] // image_count
    feature_width = images.shape[1]
    cross_rows = image_count * NQ
    part_rows = held_expand.shape[-2]
    rows_vision = held_vision.shape[-2]
    grad_normed = after_self
    far_rows, window = row_count, 128 + LMAX
    scale = HD**-0.5
    other = device(1 - c, z, y, x)

    def shelf(buffer, number):
        at = pl.ds(number // 2 * row_count, row_count), pl.ds(number % 2 * width, width)
        return buffer.at[at[0], at[1]]

    names = ("normed", "query", "key", "value", "far_key", "far_value", "context", "grad_context")
    normed, query, key, value, far_key, far_value, context, grad_context_self = (
        shelf(pair, number) for number in range(len(names))
    )
    own_query, own_key, own_value = (shelf(images, 2 * number) for number in range(3))

    loads = {
        "expand": (part_expand, held_expand),
        "reduce": (part_reduce, held_reduce),
        "grad_cross": (grad_cross_in, grad_after),
        "first": (first_in, first),
        "gains": (gains_in, gain_rows),
        "cross_context": (cross_context_in, cross_context),
        "cross_query": (cross_query_in, cross_query),
        "vision": (vision_in, pair),
        "images": (images_in, images),
        "after_self": (after_self_in, after_self),
        "hidden": (hidden_in, hidden),
        "normed": (normed_in, normed),
        "query": (query_in, query),
        "key": (key_in, key),
        "value": (value_in, value),
        "far_key": (far_key_in, far_key),
        "far_value": (far_value_in, far_value),
        "context": (context_in, context),
        "out_hidden": (grad_after, hidden_grad_out),
        "branch": (branch_in, hidden),
        "after_cross": (after_cross_in, after_self),
        "mate_branch": (mate_branch_in, grad_vision.at[1, pl.ds(0, row_count)]),
        "out_result": (hidden, result_out),
    }

    def local(name):
        source, target = loads[name]
        return pltpu.make_async_copy(source, target, local_sem.at[list(loads).index(name)])

    def pair_copy(k):
        if k == 3:
            return remote(grad_vision.at[1 - c], pair_vision, pair_base + k, other)
        return remote(first.at[1 - c, k], pair_first.at[k], pair_base + k, other)

    def ready_first(j, core):
        pair_copy(j).wait_recv()

        def step(i):
            at = (i // 4, (i // 2) % 2, i % 2)
            value = wide(first[(core, j) + at]) + wide(pair_first[(j,) + at])
            first[(core, j) + at] = to_half(value)

        loop(16, step)

    def ready_vision(core):
        pair_copy(3).wait_recv()

        def step(i):
            rows = span(i, 2 * rows_vision)
            value = wide(grad_vision[core, rows, :]) + wide(pair_vision[rows, :])
            held_vision[i // 2, i % 2, 0] = to_half(value[:rows_vision])
            held_vision[i // 2, i % 2, 1] = to_half(value[rows_vision:])

        loop(8, step)

    chunks = []
    for number in range(FEED_CHUNKS):
        p = number // 2
        held, total, name = (
            (held_expand, sum_expand, "expand"), (held_reduce, sum_reduce, "reduce")
        )[number % 2]
        chunks.append({
            "held": held.at[p], "got": [got_f0.at[number], got_f1.at[number]], "kind": "feed",
            "total": total.at[pl.ds(p * part_rows, part_rows)], "ticks": (FEED_TICKS[number],) * 2,
            "ready": (lambda core, name=name: local(name).wait()) if p == 0 else (lambda core: None),
        })
    for j in range(3):
        chunks.append({
            "held": first.at[c, j], "got": [got_p0.at[j], got_p1.at[j], got_p2.at[j]], "kind": "late",
            "total": sum_first.at[c, j], "ticks": (PLANE_TICKS[0][j], PLANE_TICKS[1][j]),
            "ready": lambda core, j=j: ready_first(j, core),
        })
    chunks.append({
        "held": held_vision, "got": [got_v0, got_v1, got_v2], "kind": "late",
        "total": sum_vision.at[c], "ticks": VISION_TICKS, "ready": ready_vision,
    })
    tick, wait_sent, remote, last = scatter_engine(chunks, send_sem, recv_sem)
    pair_base = len(chunks) * 9
    gains_base, stats_base = pair_base + 4, pair_base + 14
    back_base = stats_base + 10
    swap_base = back_base + 2

    layer = c * 4 + y * 2 + x

    def small(stage, now, got, got_z, base):
        if stage == 0:
            return [
                remote(now.at[0], got.at[layer], base + k - 1, layer_device(layer, k))
                for k in range(1, 8)
            ]
        return [
            remote(now.at[1], got_z.at[z], base + 6 + k, device(c, (z + k) % 4, y, x))
            for k in (1, 2, 3)
        ]

    def layer_device(at, k):
        c_at, y_at, x_at = k // 4, (k // 2) % 2, k % 2
        flip = lambda value, bit: 1 - value if bit else value
        return device(flip(c, c_at), z, flip(y, y_at), flip(x, x_at))

    def small_step(stage, now, got, got_z, base):
        if stage > 0:
            for copy in small(stage - 1, now, got, got_z, base):
                copy.wait()
            if stage == 1:
                got[layer] = now[0]
                now[1] = sum(got[k] for k in range(8))
            else:
                got_z[z] = now[1]
                now[2] = (got_z[0] + got_z[1]) + (got_z[2] + got_z[3])
        if stage < 2:
            for copy in small(stage, now, got, got_z, base):
                copy.start()

    def folded(values):
        total = values[:, 0:128]
        for k in range(1, values.shape[1] // 128):
            total = total + values[:, k * 128 : (k + 1) * 128]
        return total

    def squares(block):
        return jnp.sum((block * block).reshape(-1, 8, block.shape[1]), axis=0)

    own_rows, other_rows = pl.ds(0, cross_rows), pl.ds(cross_rows, cross_rows)
    swaps = {
        "context": (grad_context.at[other_rows], grad_context.at[own_rows]),
        "query": (grad_query.at[own_rows], grad_query.at[other_rows]),
        "far_key": (far_grad.at[0], far_grad.at[0]),
        "far_value": (far_grad.at[1], far_grad.at[1]),
        "branch": (grad_vision.at[1, pl.ds(0, row_count)], grad_vision.at[0, pl.ds(0, row_count)]),
    }
    mate = (c, z * 4 + jnp.where(c == 0, y, 1 - y) * 2 + jnp.where(c == 0, 1 - x, x))

    def swap(name):
        source, target = swaps[name]
        where = mate if name == "branch" else other
        return remote(source, target, swap_base + list(swaps).index(name), where)

    def weight(name):
        plane, j = PLANES[name]
        return first[plane, j].reshape(width, width)

    def gain(k):
        return gain_rows[pl.ds(k, 1), :]

    def store_weight_grad(name, value):
        plane, j = PLANES[name]
        first[plane, j] = to_half(value).reshape(first.shape[2:])


    def start():
        gain_parts[...] = jnp.zeros_like(gain_parts)
        gain_parts[pl.ds(2 + c, 1), :] = gain_feed[0:1, :]
        mask[...] = head_mask(NQ, width)
        first_row, image = caption_layout(lengths[...], owners[...], row_count)
        layout_rows[0:1] = first_row
        layout_rows[1:2] = image

    def feed_out():
        stats[...] = part_stats[...]

        def step(i):
            rows = span(i, 128)
            branch = hidden[rows, :] + wide(grad_vision[0, rows, :])
            result = after_self[rows, :] + branch
            for k, amount in ((2, branch), (3, result)):
                at = pl.ds(c * 4 + k, 1)
                stats[at, :] = stats[at, :] + row_sum(amount * amount)
            hidden[rows, :] = result

        loop(row_count // 128, step)

    def cross_out_back():
        def step(i):
            rows = span(i, 256)
            part = to_half(grad_after[rows, :])
            grad_query[rows, :] = part
            grad_context[rows, :] = to_half(nt(part, weight("cross_output")))

        loop(row_count // 256, step)
        store_weight_grad("cross_output", tn(cross_context[...], grad_query[...]))
        swap("context").start()

    def cross_back(begin, end):
        def step(i):
            i = i + begin
            rows = pl.ds(pl.multiple_of(i * padded, 16), padded)
            at = span(i, NQ)
            queries = jnp.concatenate([cross_query[at, :]] * HEADS, axis=0) * mask[...]
            grads = jnp.concatenate([grad_context[at, :]] * HEADS, axis=0) * mask[...]
            keys, values = pair[rows, 0:width], pair[rows, width : 2 * width]
            score = nt(keys, queries)
            key_row = lax.broadcasted_iota(jnp.int32, score.shape, 0)
            seen = key_row < feature_rows
            probability = jnp.exp(jnp.where(seen, score, masked_value) - total_cross[i])
            grad_prob = nt(values, grads)
            inner = row_sum(grad_prob * probability)
            grad_score = to_half(probability * (grad_prob - inner))
            full = tn(grad_score, keys)
            pair[rows, 0:width] = to_half(nn(grad_score, queries))
            pair[rows, width : 2 * width] = to_half(nn(to_half(probability), grads))
            grad_query[at, :] = to_half(diagonal(full, NQ) * scale)

        loop(end - begin, step)


    def vision_back(begin, end):
        def step(i):
            i = i + begin
            lanes = span(i, 128)
            both = to_half(tn(images[:, lanes], pair[...]))
            grad_vision[0, lanes, :] = both[:, 0:width]
            grad_vision[1, lanes, :] = both[:, width : 2 * width]

        loop(end - begin, step)

    def cross_in_back():
        def step(i):
            rows = span(i, 128)
            source = after_self[rows, :]
            grad = nt(grad_query[rows, :], weight("cross_query"))
            back, part = norm_back(source, gain(1), grad)
            gain_parts[1:2, :] = gain_parts[1:2, :] + part
            grad_after[rows, :] = grad_after[rows, :] + back
            grad_context[rows, :] = to_half(norm_rows(source, gain(1)))

        loop(row_count // 128, step)
        store_weight_grad("cross_query", tn(grad_context[...], grad_query[...]))

    def self_out_back():
        def step(i):
            rows = span(i, 256)
            part = to_half(grad_after[rows, :])
            grad_context[rows, :] = part
            grad_context_self[rows, :] = to_half(nt(part, weight("self_output")))

        loop(row_count // 256, step)
        store_weight_grad("self_output", tn(context[...], grad_context[...]))

    def attend_pair_back(rb, t, parts):
        rows, lanes = span(rb, 128), span(t, 128)
        masks = lane_masks(128)
        queries = head_pair(query[rows, lanes], masks)
        grads = head_pair(grad_context_self[rows, lanes], masks)
        kept, inner = [], 0.0
        for keys, values, where in parts:
            score = nt(keys, queries) + wide(where)
            probability = jnp.exp(score - total_self[rb, t])
            grad_prob = nt(values, grads)
            inner = inner + row_sum(grad_prob * probability)
            kept.append((probability, grad_prob))
        result, back = [], 0.0
        for (keys, values, _), (probability, grad_prob) in zip(parts, kept):
            grad_score = to_half(probability * (grad_prob - inner))
            result.append((nn(grad_score, queries), nn(to_half(probability), grads)))
            back = back + tn(grad_score, keys)
        own_query[rows, lanes] = to_half(pair_join(back) * scale)
        return result

    def self_query_back(begin, end):
        def step(i):
            rb, t = i // 6, i % 6
            rows, lanes = span(rb, 128), span(t, 128)
            parts = [(key[rows, lanes], value[rows, lanes], bias[0, 0:128])]
            ((grad_key, grad_value),) = attend_pair_back(rb, t, parts)
            own_key[rows, lanes] = to_half(grad_key)
            own_value[rows, lanes] = to_half(grad_value)

        blocks = row_count // 128

        def shifted_step(i):
            step(i + begin * blocks)

        loop((end - begin) * blocks, shifted_step)

    def text_biases():
        def step(rb):
            rows = span(rb, 128)
            start_row, image = layout_rows[0:1, rows], layout_rows[1:2, rows]
            begin = jnp.maximum(rb * 128 - LMAX, 0)
            far = lax.broadcasted_iota(jnp.int32, (far_rows, 128), 0) // NQ
            far_bias = jnp.where(wide(far) == image, 0.0, masked_value)
            key_row = lax.broadcasted_iota(jnp.int32, (window, 128), 0) + begin
            row = lax.broadcasted_iota(jnp.int32, (window, 128), 1) + rb * 128
            seen = (wide(key_row) >= start_row) & (key_row <= row)
            own_bias = jnp.where(seen, 0.0, masked_value)
            bias[rb, 0:far_rows] = to_half(jnp.concatenate([far_bias, far_bias], axis=1))
            bias[rb, far_rows : far_rows + window] = to_half(
                jnp.concatenate([own_bias, own_bias], axis=1)
            )

        loop(row_count // 128, step)

    def query_biases():
        key_row = lax.broadcasted_iota(jnp.int32, (128, 256), 0) // NQ
        row = (lax.broadcasted_iota(jnp.int32, (128, 256), 1) % 128) // NQ
        bias[0, 0:128] = to_half(jnp.where(key_row == row, 0.0, masked_value))

    def self_text_back(begin, end):
        def outer(t):
            t = t + begin
            lanes = span(t, 128)
            for total in (sum_far_key, sum_far_value, sum_key, sum_value):
                total[...] = jnp.zeros_like(total)

            def inner(rb):
                near = pl.ds(pl.multiple_of(jnp.maximum(rb * 128 - LMAX, 0), LMAX), window)
                parts = [
                    (far_key[:, lanes], far_value[:, lanes], bias[rb, 0:far_rows]),
                    (key[near, lanes], value[near, lanes], bias[rb, far_rows : far_rows + window]),
                ]
                far_part, near_part = attend_pair_back(rb, t, parts)
                sum_far_key[...] += far_part[0]
                sum_far_value[...] += far_part[1]
                sum_key[near, :] = sum_key[near, :] + near_part[0]
                sum_value[near, :] = sum_value[near, :] + near_part[1]

            loop(row_count // 128, inner)
            far_grad[0, :, lanes] = to_half(sum_far_key[...])
            far_grad[1, :, lanes] = to_half(sum_far_value[...])
            own_key[:, lanes] = to_half(sum_key[...])
            own_value[:, lanes] = to_half(sum_value[...])

        loop(end - begin, outer)

    def self_in_back(name, own, far):
        def step(i):
            rows = span(i, 256)
            grad = nt(own[rows, :], weight(name))
            if far is not None:
                grad = grad + nt(far_grad[far, rows, :], weight(name))
            if name != "query":
                grad = grad_normed[rows, :] + grad
            grad_normed[rows, :] = grad

        loop(row_count // 256, step)

    def project_back(name, own, far):
        self_in_back(name, own, far)
        grad = tn(normed[...], own[...])
        if far is not None:
            grad = grad + tn(normed[...], far_grad[far])
        store_weight_grad(name, grad)

    def hidden_back():
        def step(i):
            rows = span(i, 128)
            back, part = norm_back(hidden[rows, :], gain(0), grad_normed[rows, :])
            gain_parts[0:1, :] = gain_parts[0:1, :] + part
            grad_after[rows, :] = grad_after[rows, :] + back

        loop(row_count // 128, step)

    def send_pair(core, *names):
        @pl.when(c == core)
        def _():
            for name in names:
                plane, j = PLANES[name]
                if plane != core:
                    pair_copy(j).start()

    for name in ("mate_branch", "grad_cross", "first", "cross_context", "expand", "reduce", "cross_query",
                 "vision", "branch", "after_cross", "images", "gains"):
        local(name).start()
    meet(c, z, y, x, layer=True)
    local("mate_branch").wait()
    swap("branch").start()
    tick(0)
    start()
    local("grad_cross").wait()
    local("first").wait()
    local("cross_context").wait()

    @pl.when(c == 0)
    def _():
        cross_out_back()

    @pl.when(c == 1)
    def _():
        plane, j = PLANES["cross_output"]
        first[plane, j] = jnp.zeros(first.shape[2:], jnp.bfloat16)
        plane, j = PLANES["cross_query"]
        first[plane, j] = jnp.zeros(first.shape[2:], jnp.bfloat16)
        swap("context").wait_recv()

    send_pair(1, "cross_output")
    tick(1)
    local("vision").wait()
    local("cross_query").wait()
    quarter = image_count // 4
    for k in range(4):
        cross_back(k * quarter, (k + 1) * quarter)
        if k == 1:
            local("branch").wait()
            local("after_cross").wait()
            swap("branch").wait_recv()
            feed_out()
            local("out_result").start()
            local("after_self").start()
        tick(2 + k)

    @pl.when(c == 1)
    def _():
        swap("query").start()

    local("images").wait()
    swap("branch").wait_send()
    local("out_result").wait()
    local("hidden").start()
    tiles = feature_width // 128
    vision_back(0, tiles // 3)
    tick(6)
    vision_back(tiles // 3, 2 * tiles // 3)
    tick(7)
    vision_back(2 * tiles // 3, tiles)
    pair_copy(3).start()
    for name in names[:-1]:
        local(name).start()
    tick(8)
    local("after_self").wait()
    local("gains").wait()

    @pl.when(c == 0)
    def _():
        swap("query").wait_recv()
        swap("context").wait_send()
        cross_in_back()

    send_pair(0, "cross_query")
    for name in names[:-1]:
        local(name).wait()
    self_out_back()
    send_pair(0, "self_output")
    tick(9)

    @pl.when(c == 0)
    def _():
        query_biases()
        self_query_back(0, 3)

    @pl.when(c == 1)
    def _():
        text_biases()

    for t in range(6):

        @pl.when(c == 1)
        def _(t=t):
            self_text_back(t, t + 1)

        if t == 1:

            @pl.when(c == 0)
            def _():
                self_query_back(3, 6)

        if t < 5:
            tick(10 + t)

    @pl.when(c == 1)
    def _():
        swap("far_key").start()
        swap("far_value").start()

    project_back("query", own_query, None)
    send_pair(1, "query")

    @pl.when(c == 0)
    def _():
        swap("far_key").wait_recv()
        swap("far_value").wait_recv()
        project_back("value", own_value, 1)

    @pl.when(c == 1)
    def _():
        project_back("key", own_key, None)

    send_pair(0, "value")
    send_pair(1, "key")
    tick(15)

    @pl.when(c == 0)
    def _():
        project_back("key", own_key, 0)

    @pl.when(c == 1)
    def _():
        project_back("value", own_value, None)

    tick(16)
    local("hidden").wait()
    hidden_back()
    local("out_hidden").start()
    gains_now[0] = gain_parts[...]
    for now in range(17, 21):
        if now < 20:
            small_step(now - 17, gains_now, gains_got, gains_z, gains_base)
        tick(now)
    gains = gains_now[2]
    sum_gains[...] = gains
    mass = jnp.where((c == 0) & (z + y + x == 0), 1.0, 0.0) * (gains * gains)
    mass = mass + squares(sum_expand[...]) + squares(sum_reduce[...])
    tick(21)
    back = [
        remote(sum_first.at[c], sum_first.at[c], back_base, other),
        remote(sum_vision.at[c], sum_vision.at[c], back_base + 1, other),
    ]
    for copy in back:
        copy.start()
    for j in range(3):
        mass = mass + squares(sum_first[c, j])
    mass = mass + squares(sum_vision[c])
    stats_now[0, 0:8] = folded(mass)
    stats_now[0, 8:16] = folded(stats[...])
    for stage in range(3):
        small_step(stage, stats_now, stats_got, stats_z, stats_base)
    totals[...] = stats_now[2]
    for copy in back:
        copy.wait()
    assert last == 21
    wait_sent()
    for k in range(4):
        pair_copy(k).wait_send()

    @pl.when(c == 1)
    def _():
        swap("query").wait_send()
        swap("far_key").wait_send()
        swap("far_value").wait_send()

    local("out_hidden").wait()


def backward_all(kept, hidden, lengths, owners, feature_rows):
    half, single = jnp.bfloat16, jnp.float32
    row_count, width = hidden.shape
    feature_width = kept["images"].shape[1]
    parts = kept["part_expand"].shape
    part_rows = parts[-2]
    rows_first = kept["first"].shape[-2]
    rows_vision = feature_width // 16
    cross_rows = kept["cross_query"].shape[0]
    anywhere = pl.BlockSpec(memory_space=pl.ANY)
    vmem = pl.BlockSpec(memory_space=pltpu.VMEM)
    rows_half, rows_single = pltpu.VMEM((row_count, width), half), pltpu.VMEM((row_count, width), single)
    outs = {
        "result": (jax.ShapeDtypeStruct((row_count, width), single), anywhere),
        "hidden_grad": (jax.ShapeDtypeStruct((row_count, width), single), anywhere),
        "expand": (jax.ShapeDtypeStruct((PARTS * part_rows, width), single), vmem),
        "reduce": (jax.ShapeDtypeStruct((PARTS * part_rows, width), single), vmem),
        "first": (jax.ShapeDtypeStruct((2, 3, rows_first, width), single), vmem),
        "vision": (jax.ShapeDtypeStruct((2, rows_vision, width), single), vmem),
        "gains": (jax.ShapeDtypeStruct((8, width), single), vmem),
        "totals": (jax.ShapeDtypeStruct((16, 128), single), vmem),
    }
    scratch = [pltpu.VMEM(parts, half)] * 2
    scratch += [
        pltpu.VMEM((FEED_CHUNKS,) + shape, half) for shape in got_shapes("feed", part_rows, width)
    ]
    scratch += [pltpu.VMEM((3,) + shape, half) for shape in got_shapes("late", rows_first, width)]
    scratch += [pltpu.VMEM(shape, half) for shape in got_shapes("late", rows_vision, width)]
    scratch += [
        pltpu.VMEM(kept["first"].shape[1:], half),
        pltpu.VMEM((feature_width, width), half),
        pltpu.VMEM((4, 2, 2, rows_vision, width), half),
    ]
    for shape in ((8, width), (16, 128)):
        scratch += [pltpu.VMEM((number,) + shape, single) for number in (3, 8, 4)]
    scratch += [
        pltpu.VMEM(kept["first"].shape, half),
        pltpu.VMEM(kept["vision"].shape, half),
        pltpu.VMEM(kept["images"].shape, half),
        pltpu.VMEM((2, feature_width, width), half),
        rows_half,
        rows_single,
        rows_single,
        rows_single,
        pltpu.VMEM((16, width), single),
        pltpu.VMEM((cross_rows, width), half),
        rows_half,
        rows_half,
        pltpu.VMEM((2, row_count, width), half),
        pltpu.VMEM((row_count // 128, row_count + 128 + LMAX, 256), half),
        pltpu.VMEM((HEADS * NQ, width), half),
    ]
    scratch += [pltpu.VMEM((row_count, 128), single)] * 4
    scratch += [
        pltpu.VMEM((8, row_count), single),
        pltpu.VMEM((8, width), single),
        pltpu.VMEM((8, width), single),
        pltpu.SemaphoreType.DMA(((FEED_CHUNKS + 4) * 9 + 4 + 22 + 5,)),
        pltpu.SemaphoreType.DMA(((FEED_CHUNKS + 4) * 9 + 4 + 22 + 5,)),
        pltpu.SemaphoreType.DMA((23,)),
    ]
    order = ("part_expand", "part_reduce", "grad_cross", None, "after_self", "first", "gains", "normed",
             "query", "key", "value", "far_key", "far_value", "context", "cross_query", "cross_context",
             "vision", "images", "branch", "after_cross", "mate_branch")
    values = pl.pallas_call(
        functools.partial(backward_kernel, feature_rows),
        out_shape=[shape for shape, _ in outs.values()],
        in_specs=[anywhere] * len(order) + [vmem] * 6,
        out_specs=[spec for _, spec in outs.values()],
        scratch_shapes=scratch,
        compiler_params=pltpu.CompilerParams(
            collective_id=3, has_side_effects=True, vmem_limit_bytes=VMEM_LIMIT
        ),
        name="backward_layer",
    )(
        *[hidden if name is None else kept[name] for name in order],
        lengths, owners, kept["total_self"], kept["total_cross"], kept["gain_feed"], kept["stats"],
    )
    return dict(zip(outs, values))


NAMES = ("project", "output", "query", "vision", "expand", "reduce")
SUM_OF = {
    "project": ("query", "key", "value"), "output": ("self_output", "cross_output"), "query": ("cross_query",),
}


def update_kernel(amount, totals, sum_gains, gains, first_gains, second_gains, *refs):
    count = len(NAMES)
    sums, refs = refs[:4], refs[4:]
    inputs, refs = [refs[k * count : (k + 1) * count] for k in range(3)], refs[3 * count :]
    outputs, refs = [refs[k * count : (k + 1) * count] for k in range(4)], refs[4 * count :]
    gain_outs, norm_out, rms_out, refs = refs[:4], refs[4], refs[5], refs[6:]
    held_sums, refs = refs[:4], refs[4:]
    held, refs = [refs[k * count : (k + 1) * count] for k in range(3)], refs[3 * count :]
    half, sems = refs[:count], refs[count]

    def load_sum(k):
        return pltpu.make_async_copy(sums[k], held_sums[k], sems.at[k])

    def load(k, n):
        return pltpu.make_async_copy(inputs[k][n], held[k][n], sems.at[4 + k * count + n])

    def store(k, n):
        source = half[n] if k == 3 else held[k][n]
        return pltpu.make_async_copy(source, outputs[k][n], sems.at[4 + (3 + k) * count + n])

    for k in range(4):
        load_sum(k).start()
    for n in range(count):
        for k in range(3):
            load(k, n).start()
    lanes = jnp.sum(totals[0:8], axis=1, keepdims=True)
    grad_norm = jnp.sqrt(jnp.sum(lanes, axis=0, keepdims=True))
    norm_out[...] = grad_norm
    factor = clip_norm / jnp.maximum(grad_norm, clip_norm)
    rms_out[...] = jnp.sqrt(jnp.sum(totals[8:16], axis=1, keepdims=True) / amount)
    clipped = sum_gains[...] * factor
    fresh, mean, square = adam_step(
        gains[...], sum_gains[...], first_gains[...], second_gains[...], factor, rate_gains, 0.0
    )
    for target, value in zip(gain_outs, (fresh, mean, square, clipped)):
        target[...] = value
    for k in range(4):
        load_sum(k).wait()
    for n, name in enumerate(NAMES):
        for k in range(3):
            load(k, n).wait()
        weight, first, second = (held[k][n] for k in range(3))
        pieces = weight.shape[0] if len(weight.shape) == 3 else 1
        for j in range(pieces):
            at = (j,) if len(weight.shape) == 3 else (Ellipsis,)
            if name in SUM_OF:
                gradient = held_sums[0][PLANES[SUM_OF[name][j]]]
            else:
                gradient = held_sums[NAMES.index(name) - 2][at]
            fresh, mean, square = adam_step(
                weight[at], gradient, first[at], second[at], factor, rate_matrix, decay_rate
            )
            weight[at], first[at], second[at] = fresh, mean, square
            half[n][at] = to_half(fresh)
        for k in range(4):
            store(k, n).start()
    for n in range(count):
        for k in range(4):
            store(k, n).wait()


def update_all(amount, totals, sum_gains, gain_state, sums, weights, firsts, seconds):
    single, half = jnp.float32, jnp.bfloat16
    anywhere, vmem = pl.BlockSpec(memory_space=pl.ANY), pl.BlockSpec(memory_space=pltpu.VMEM)
    count = len(NAMES)
    shapes = [weight.shape for weight in weights]
    out_shape = [jax.ShapeDtypeStruct(shape, single) for _ in range(3) for shape in shapes]
    out_shape += [jax.ShapeDtypeStruct(shape, half) for shape in shapes]
    out_shape += [jax.ShapeDtypeStruct(sum_gains.shape, single)] * 4
    out_shape += [jax.ShapeDtypeStruct((1, 1), single), jax.ShapeDtypeStruct((8, 1), single)]
    scratch = [pltpu.VMEM(value.shape, single) for value in sums]
    scratch += [pltpu.VMEM(shape, single) for _ in range(3) for shape in shapes]
    scratch += [pltpu.VMEM(shape, half) for shape in shapes]
    scratch += [pltpu.SemaphoreType.DMA((4 + 7 * count,))]
    values = pl.pallas_call(
        functools.partial(update_kernel, amount),
        out_shape=out_shape,
        in_specs=[vmem] * 5 + [anywhere] * (4 + 3 * count),
        out_specs=[anywhere] * (4 * count) + [vmem] * 6,
        scratch_shapes=scratch,
        compiler_params=pltpu.CompilerParams(vmem_limit_bytes=VMEM_LIMIT),
        name="update_weights",
    )(totals, sum_gains, *gain_state, *sums, *weights, *firsts, *seconds)
    fresh, mean, square, copies = (values[k * count : (k + 1) * count] for k in range(4))
    return fresh, mean, square, copies, values[4 * count : 4 * count + 4], values[-2], values[-1]


def general_grads(
    hidden,
    features,
    caption_lengths,
    caption_image,
    out_grad,
    attn_project,
    attn_output,
    cross_query,
    cross_vision,
    feed_expand,
    feed_reduce,
    norm_gains,
):
    stream = lax.axis_index("stream")
    full_project, full_output, full_query, full_vision, full_expand, full_reduce, full_gains = (
        lax.all_gather(to_half(attn_project), "dp", axis=1, tiled=True),
        lax.all_gather(to_half(attn_output), "dp", axis=1, tiled=True),
        lax.all_gather(to_half(cross_query), "dp", axis=0, tiled=True),
        lax.all_gather(to_half(cross_vision), "dp", axis=1, tiled=True),
        lax.all_gather(to_half(feed_expand), "dp", axis=1, tiled=True),
        lax.all_gather(to_half(feed_reduce), "dp", axis=1, tiled=True),
        lax.all_gather(to_half(norm_gains), "dp", axis=1, tiled=True),
    )
    gain_rows = full_gains.astype(jnp.float32)
    gain_self = gain_rows[0]
    gain_cross = gain_rows[1]
    gain_feed = lax.dynamic_index_in_dim(gain_rows, 2 + stream, 0, keepdims=False)
    source = hidden[0]
    row_count = source.shape[0]
    feature_width = source.shape[1]
    image_count = features.shape[0]
    query_allow, text_allow = layout(caption_lengths[0], caption_image[0], row_count, NQ)
    normed_self = to_half(norm_rows(source, gain_self))
    query_half = to_half(product(normed_self, full_project[0]))
    key_half = to_half(product(normed_self, full_project[1]))
    value_half = to_half(product(normed_self, full_project[2]))
    empty_half = jnp.zeros((row_count, feature_width), jnp.bfloat16)
    far_key, far_value = shifted((key_half, value_half), "stream", 1)
    text_keys = jnp.concatenate([far_key, key_half], axis=0)
    text_values = jnp.concatenate([far_value, value_half], axis=0)

    def self_query():
        return attend(query_half[None], key_half[None], value_half[None], query_allow[None])

    def self_text():
        return attend(query_half[None], text_keys[None], text_values[None], text_allow[None])

    context_self, total_self = lax.cond(stream == 0, self_query, self_text)
    context_half = to_half(context_self[0])
    branch_self = product(context_half, full_output[0])
    after_self = source + branch_self

    def cross_on():
        normed_cross = to_half(norm_rows(after_self, gain_cross))
        cross_half = to_half(product(normed_cross, full_query))
        vision_pair = project_vision(features, full_vision)
        context_cross, total_cross = attend(
            cross_half.reshape(image_count, NQ, feature_width), vision_pair[0], vision_pair[1], None
        )
        context_cross_half = to_half(context_cross.reshape(row_count, feature_width))
        branch = product(context_cross_half, full_output[1])
        return (branch, total_cross, vision_pair, normed_cross, cross_half, context_cross_half)

    def cross_off():
        return (
            jnp.zeros((row_count, feature_width), jnp.float32),
            jnp.zeros((image_count, HEADS, NQ), jnp.float32),
            jnp.zeros((2, image_count, features.shape[1], feature_width), jnp.bfloat16),
            empty_half,
            empty_half,
            empty_half,
        )

    branch_cross, total_cross, vision_pair, normed_cross, cross_half, context_cross_half = lax.cond(
        stream == 0, cross_on, cross_off
    )
    after_cross = after_self + branch_cross
    normed_feed = to_half(norm_rows(after_cross, gain_feed))
    before = right_product(normed_feed, full_expand[0])
    active_half = to_half(exact_gelu(before))
    branch_feed = product(active_half, full_reduce[0])
    result = after_cross + branch_feed
    grad_result = out_grad[0]
    grad_feed_half = to_half(grad_result)
    grad_reduce = left_product(active_half, grad_feed_half)
    grad_active = right_product(grad_feed_half, full_reduce[0])
    grad_before = to_half(jax.vjp(exact_gelu, before)[1](grad_active)[0])
    grad_expand = left_product(grad_before, normed_feed)
    grad_normed_feed = product(grad_before, full_expand[0])
    feed_in, grad_gain_feed = jax.vjp(norm_rows, after_cross, gain_feed)[1](grad_normed_feed)
    grad_cross = grad_result + feed_in

    def cross_back_on():
        grad_branch_half = to_half(grad_cross)
        grad_out_cross = left_product(context_cross_half, grad_branch_half)
        grad_context = to_half(right_product(grad_branch_half, full_output[1]))
        grad_cq, grad_ck, grad_cv = attend_back(
            cross_half.reshape(image_count, NQ, feature_width),
            vision_pair[0],
            vision_pair[1],
            None,
            total_cross,
            grad_context.reshape(image_count, NQ, feature_width),
        )
        grad_cq_half = to_half(grad_cq.reshape(row_count, feature_width))
        grad_pair = to_half(jnp.stack([grad_ck, grad_cv]))
        grad_cross_weight = left_product(normed_cross, grad_cq_half)
        grad_normed_cross = right_product(grad_cq_half, full_query)
        cross_in, grad_gain_cross = jax.vjp(norm_rows, after_self, gain_cross)[1](grad_normed_cross)
        vision_term = vision_grad(features, grad_pair)
        return (cross_in, grad_gain_cross, grad_out_cross, grad_cross_weight, vision_term)

    def cross_back_off():
        square_zero = jnp.zeros((feature_width, feature_width), jnp.float32)
        vision_term = jnp.zeros((2, features.shape[2], feature_width), jnp.float32)
        return (
            jnp.zeros((row_count, feature_width), jnp.float32),
            jnp.zeros((feature_width,), jnp.float32),
            square_zero,
            square_zero,
            vision_term,
        )

    cross_in, grad_gain_cross, grad_out_cross, grad_cross_weight, vision_term = lax.cond(
        stream == 0, cross_back_on, cross_back_off
    )
    grad_after_self = grad_cross + cross_in
    grad_branch_half = to_half(grad_after_self)
    grad_out_self = left_product(context_half, grad_branch_half)
    grad_context_self = to_half(right_product(grad_branch_half, full_output[0]))

    def self_back_query():
        grad_sq, grad_sk, grad_sv = attend_back(
            query_half[None],
            key_half[None],
            value_half[None],
            query_allow[None],
            total_self,
            grad_context_self[None],
        )
        empty_rows = jnp.zeros((row_count, feature_width), jnp.float32)
        return (grad_sq[0], grad_sk[0], grad_sv[0], empty_rows, empty_rows)

    def self_back_text():
        grad_sq, grad_sk, grad_sv = attend_back(
            query_half[None],
            text_keys[None],
            text_values[None],
            text_allow[None],
            total_self,
            grad_context_self[None],
        )
        return (
            grad_sq[0],
            grad_sk[0, row_count:],
            grad_sv[0, row_count:],
            grad_sk[0, :row_count],
            grad_sv[0, :row_count],
        )

    own_query, own_key, own_value, far_grad_key, far_grad_value = lax.cond(
        stream == 0, self_back_query, self_back_text
    )
    own_query = to_half(own_query)
    own_key = to_half(own_key)
    own_value = to_half(own_value)
    far_key_half = to_half(far_grad_key)
    far_value_half = to_half(far_grad_value)
    grad_normed = (
        right_product(own_query, full_project[0])
        + right_product(own_key, full_project[1])
        + right_product(own_value, full_project[2])
    )
    grad_key_weight = left_product(normed_self, own_key)
    grad_value_weight = left_product(normed_self, own_value)
    back_key, back_value = shifted((far_key_half, far_value_half), "stream", -1)
    grad_normed = (
        grad_normed
        + right_product(back_key, full_project[1])
        + right_product(back_value, full_project[2])
    )
    grad_key_weight = grad_key_weight + left_product(normed_self, back_key)
    grad_value_weight = grad_value_weight + left_product(normed_self, back_value)
    grad_project = jnp.stack(
        [left_product(normed_self, own_query), grad_key_weight, grad_value_weight]
    )
    source_in, grad_gain_self = jax.vjp(norm_rows, source, gain_self)[1](grad_normed)
    hidden_grad = grad_after_self + source_in
    zero_row = jnp.zeros_like(grad_gain_feed)
    gain_grads = jnp.stack(
        [
            grad_gain_self,
            grad_gain_cross,
            jnp.where(stream == 0, grad_gain_feed, zero_row),
            jnp.where(stream == 1, grad_gain_feed, zero_row),
        ]
    )
    shared_grads = (
        grad_project,
        jnp.stack([grad_out_self, grad_out_cross]),
        grad_cross_weight,
        vision_term,
        gain_grads,
    )
    (
        parts_project,
        parts_output,
        parts_query,
        parts_vision,
        parts_expand,
        parts_reduce,
        parts_gains,
    ) = (
        lax.psum_scatter(shared_grads[0], "dp", scatter_dimension=1, tiled=True),
        lax.psum_scatter(shared_grads[1], "dp", scatter_dimension=1, tiled=True),
        lax.psum_scatter(shared_grads[2], "dp", scatter_dimension=0, tiled=True),
        lax.psum_scatter(shared_grads[3], "dp", scatter_dimension=1, tiled=True),
        lax.psum_scatter(grad_expand[None], "dp", scatter_dimension=1, tiled=True),
        lax.psum_scatter(grad_reduce[None], "dp", scatter_dimension=1, tiled=True),
        lax.psum_scatter(shared_grads[4], "dp", scatter_dimension=1, tiled=True),
    )
    sum_project, sum_output, sum_query, sum_vision, sum_gains = (
        lax.psum(parts_project.astype(jnp.bfloat16), "stream").astype(jnp.float32),
        lax.psum(parts_output.astype(jnp.bfloat16), "stream").astype(jnp.float32),
        lax.psum(parts_query.astype(jnp.bfloat16), "stream").astype(jnp.float32),
        lax.psum(parts_vision.astype(jnp.bfloat16), "stream").astype(jnp.float32),
        lax.psum(parts_gains.astype(jnp.bfloat16), "stream").astype(jnp.float32),
    )
    shared_square = (
        jnp.sum(sum_project * sum_project)
        + jnp.sum(sum_output * sum_output)
        + jnp.sum(sum_query * sum_query)
        + jnp.sum(sum_vision * sum_vision)
        + jnp.sum(sum_gains * sum_gains)
    )
    local_square = (
        0.5 * shared_square
        + jnp.sum(parts_expand * parts_expand)
        + jnp.sum(parts_reduce * parts_reduce)
    )
    stat_row = jnp.stack(
        [
            square_rows(source),
            square_rows(branch_self),
            square_rows(branch_feed),
            square_rows(result),
        ]
    )
    stat_local = jnp.where(
        jnp.arange(2, dtype=jnp.int32)[:, None] == stream, stat_row[None, :], 0.0
    )
    total_square, stat_sums = lax.psum((local_square, stat_local), ("stream", "dp"))
    return (
        result, hidden_grad, total_square, stat_sums, parts_expand, parts_reduce,
        (sum_project, sum_output, sum_query, sum_vision, sum_gains),
    )


def direct_body(
    hidden,
    features,
    caption_lengths,
    caption_image,
    out_grad,
    attn_project,
    attn_output,
    cross_query,
    cross_vision,
    feed_expand,
    feed_reduce,
    norm_gains,
    first_project,
    second_project,
    first_output,
    second_output,
    first_query,
    second_query,
    first_vision,
    second_vision,
    first_expand,
    second_expand,
    first_reduce,
    second_reduce,
    first_gains,
    second_gains,
):
    width = attn_project.shape[-1]
    row_count = hidden.shape[1]
    gains = jnp.pad(to_half(norm_gains), ((0, 12), (0, 128 - norm_gains.shape[1])))
    weights = (
        attn_project, attn_output, cross_query, cross_vision, feed_expand[0], feed_reduce[0],
    )
    kept = forward_all(
        weights, gains, hidden[0], out_grad[0], features, caption_lengths, caption_image,
    )
    back = backward_all(kept, hidden[0], caption_lengths, caption_image, features.shape[1])
    own_gains = norm_gains.shape[1]
    begin = lax.axis_index("dp") * own_gains
    sum_gains = lax.dynamic_slice_in_dim(back["gains"][:4], begin, own_gains, axis=1)
    sums = [back[name] for name in ("first", "vision", "expand", "reduce")]
    firsts = (
        first_project, first_output, first_query, first_vision, first_expand[0], first_reduce[0],
    )
    seconds = (
        second_project, second_output, second_query, second_vision, second_expand[0], second_reduce[0],
    )
    amount = row_count * lax.axis_size("dp") * width
    fresh, mean, square, copies, gain_new, grad_norm, rms = update_all(
        amount, back["totals"], sum_gains, (norm_gains, first_gains, second_gains), sums,
        weights, firsts, seconds,
    )
    updated = []
    for n in range(6):
        step = [part[n] if n < 4 else part[n][None] for part in (fresh, mean, square, copies)]
        updated.append(step)
    steps = [value for step in updated for value in step[:3]]
    return (
        back["result"][None],
        back["hidden_grad"][None],
        grad_norm.reshape(()),
        rms.reshape(2, 4),
        *steps,
        *gain_new,
        *[step[3] for step in updated],
    )


def body(
    hidden,
    features,
    caption_lengths,
    caption_image,
    out_grad,
    attn_project,
    attn_output,
    cross_query,
    cross_vision,
    feed_expand,
    feed_reduce,
    norm_gains,
    first_project,
    second_project,
    first_output,
    second_output,
    first_query,
    second_query,
    first_vision,
    second_vision,
    first_expand,
    second_expand,
    first_reduce,
    second_reduce,
    first_gains,
    second_gains,
):
    if lax.axis_size("dp") == 16:
        return direct_body(
            hidden, features, caption_lengths, caption_image, out_grad, attn_project, attn_output, cross_query,
            cross_vision, feed_expand, feed_reduce, norm_gains, first_project, second_project,
            first_output, second_output, first_query, second_query, first_vision, second_vision,
            first_expand, second_expand, first_reduce, second_reduce, first_gains, second_gains,
        )
    row_count = hidden.shape[1]
    result, hidden_grad, total_square, stat_sums, parts_expand, parts_reduce, shared = general_grads(
        hidden, features, caption_lengths, caption_image, out_grad, attn_project,
        attn_output, cross_query, cross_vision, feed_expand, feed_reduce, norm_gains,
    )
    sum_project, sum_output, sum_query, sum_vision, sum_gains = shared
    grad_norm = jnp.sqrt(total_square)
    rms_values = jnp.sqrt(stat_sums / (row_count * lax.axis_size("dp")))
    factor = clip_norm / jnp.maximum(grad_norm, clip_norm)
    clipped_gains = sum_gains * factor
    fresh_expand, mean_expand, square_expand = adam_step(
        feed_expand, parts_expand, first_expand, second_expand, factor, rate_matrix, decay_rate
    )
    fresh_reduce, mean_reduce, square_reduce = adam_step(
        feed_reduce, parts_reduce, first_reduce, second_reduce, factor, rate_matrix, decay_rate
    )
    weights_shared = (attn_project, attn_output, cross_query, cross_vision, norm_gains)
    firsts_shared = (first_project, first_output, first_query, first_vision, first_gains)
    seconds_shared = (second_project, second_output, second_query, second_vision, second_gains)
    summed_shared = (sum_project, sum_output, sum_query, sum_vision, sum_gains)
    updated = []
    for index in range(5):
        rate = rate_gains if index == 4 else rate_matrix
        decay = 0.0 if index == 4 else decay_rate
        weight = weights_shared[index]
        first = firsts_shared[index]
        second = seconds_shared[index]
        updated.append(adam_step(weight, summed_shared[index], first, second, factor, rate, decay))
    fresh_project, mean_project, square_project = updated[0]
    fresh_output, mean_output, square_output = updated[1]
    fresh_query, mean_query, square_query = updated[2]
    fresh_vision, mean_vision, square_vision = updated[3]
    fresh_gains, mean_gains, square_gains = updated[4]
    return (
        result[None],
        hidden_grad[None],
        grad_norm,
        rms_values,
        fresh_project,
        mean_project,
        square_project,
        fresh_output,
        mean_output,
        square_output,
        fresh_query,
        mean_query,
        square_query,
        fresh_vision,
        mean_vision,
        square_vision,
        fresh_expand,
        mean_expand,
        square_expand,
        fresh_reduce,
        mean_reduce,
        square_reduce,
        fresh_gains,
        mean_gains,
        square_gains,
        clipped_gains,
        to_half(fresh_project),
        to_half(fresh_output),
        to_half(fresh_query),
        to_half(fresh_vision),
        to_half(fresh_expand),
        to_half(fresh_reduce),
    )


def solution(mesh):
    return jax.shard_map(
        body,
        mesh=mesh,
        in_specs=(
            P("stream", "dp", None),
            P("dp", None, None),
            P("dp", None),
            P("dp", None),
            P("stream", "dp", None),
            P(None, "dp", None),
            P(None, "dp", None),
            P("dp", None),
            P(None, "dp", None),
            P("stream", "dp", None),
            P("stream", "dp", None),
            P(None, "dp"),
            P(None, "dp", None),
            P(None, "dp", None),
            P(None, "dp", None),
            P(None, "dp", None),
            P("dp", None),
            P("dp", None),
            P(None, "dp", None),
            P(None, "dp", None),
            P("stream", "dp", None),
            P("stream", "dp", None),
            P("stream", "dp", None),
            P("stream", "dp", None),
            P(None, "dp"),
            P(None, "dp"),
        ),
        out_specs=(
            P("stream", "dp", None),
            P("stream", "dp", None),
            P(),
            P(),
            P(None, "dp", None),
            P(None, "dp", None),
            P(None, "dp", None),
            P(None, "dp", None),
            P(None, "dp", None),
            P(None, "dp", None),
            P("dp", None),
            P("dp", None),
            P("dp", None),
            P(None, "dp", None),
            P(None, "dp", None),
            P(None, "dp", None),
            P("stream", "dp", None),
            P("stream", "dp", None),
            P("stream", "dp", None),
            P("stream", "dp", None),
            P("stream", "dp", None),
            P("stream", "dp", None),
            P(None, "dp"),
            P(None, "dp"),
            P(None, "dp"),
            P(None, "dp"),
            P(None, "dp", None),
            P(None, "dp", None),
            P("dp", None),
            P(None, "dp", None),
            P("stream", "dp", None),
            P("stream", "dp", None),
        ),
        check_vma=False,
    )
```
